32 devices in a mesh: tile: 8 (over z, x), sub: 4 (over y, core).
Axes of the slice: x: 2, y: 2, z: 4, core: 2. Of those that a mesh axis runs over, the one named last changes fastest.
Arguments:
- outer_image: bfloat16 [1, 256, 256, 256], P(None, 'tile', 'sub'), may hold values from -6 to 6
- inner_image: bfloat16 [1, 4096, 1024], P(None, 'tile', 'sub'), may hold values from -6 to 6
- text_states: bfloat16 [1, 128, 4096], replicated, may hold values from -6 to 6
- time_steps: int32 [1], replicated, may hold values from 0 to 999
- text_lengths: int32 [1], replicated, may hold values from 32 to 128
- first_gain: float32 [256], replicated, may hold values from 0.1 to 1.9
- first_bias: float32 [256], replicated, may hold values from -3 to 3
- conv_first: bfloat16 [3, 3, 256, 256], replicated, may hold values from -0.125 to 0.125
- time_weight: bfloat16 [256, 256], replicated, may hold values from -0.75 to 0.75
- second_gain: float32 [256], replicated, may hold values from 0.1 to 1.9
- second_bias: float32 [256], replicated, may hold values from -3 to 3
- conv_second: bfloat16 [3, 3, 256, 256], replicated, may hold values from -0.125 to 0.125
- lift_weight: bfloat16 [256, 1024], replicated, may hold values from -1.5 to 1.5
- attn_gain: float32 [1024], P('sub'), may hold values from 0.1 to 1.9
- query_weight: bfloat16 [1024, 1024], P(None, 'sub'), may hold values from -0.1875 to 0.1875
- key_weight: bfloat16 [1024, 1024], P(None, 'sub'), may hold values from -0.1875 to 0.1875
- value_weight: bfloat16 [1024, 1024], P(None, 'sub'), may hold values from -0.1875 to 0.1875
- out_weight: bfloat16 [1024, 1024], P('sub'), may hold values from -1.5 to 1.5
- cross_gain: float32 [1024], P('sub'), may hold values from 0.1 to 1.9
- cross_query: bfloat16 [1024, 1024], P(None, 'sub'), may hold values from -0.1875 to 0.1875
- cross_key: bfloat16 [4096, 1024], P(None, 'sub'), may hold values from -0.09375 to 0.09375
- cross_value: bfloat16 [4096, 1024], P(None, 'sub'), may hold values from -0.09375 to 0.09375
- cross_out: bfloat16 [1024, 1024], P('sub'), may hold values from -0.75 to 0.75
- mlp_gain: float32 [1024], P('sub'), may hold values from 0.1 to 1.9
- up_weight: bfloat16 [1024, 4096], P(None, 'sub'), may hold values from -0.1875 to 0.1875
- down_weight: bfloat16 [4096, 1024], P('sub'), may hold values from -0.1875 to 0.1875
- outer_cotan: bfloat16 [1, 256, 256, 256], P(None, 'tile', 'sub'), may hold values from -6 to 6
- inner_cotan: bfloat16 [1, 4096, 1024], P(None, 'tile', 'sub'), may hold values from -6 to 6
Outputs:
- outer_out: bfloat16 [1, 256, 256, 256], P(None, 'tile', 'sub')
- inner_out: bfloat16 [1, 4096, 1024], P(None, 'tile', 'sub')
- outer_grad: float32 [1, 256, 256, 256], P(None, 'tile', 'sub')
- inner_grad: float32 [1, 4096, 1024], P(None, 'tile', 'sub')
- first_gain_grad: float32 [256], replicated
- first_bias_grad: float32 [256], replicated
- conv_first_grad: float32 [3, 3, 256, 256], replicated
- time_weight_grad: float32 [256, 256], replicated
- second_gain_grad: float32 [256], replicated
- second_bias_grad: float32 [256], replicated
- conv_second_grad: float32 [3, 3, 256, 256], replicated
- lift_weight_grad: float32 [256, 1024], replicated
- attn_gain_grad: float32 [1024], P('sub')
- query_weight_grad: float32 [1024, 1024], P(None, 'sub')
- key_weight_grad: float32 [1024, 1024], P(None, 'sub')
- value_weight_grad: float32 [1024, 1024], P(None, 'sub')
- out_weight_grad: float32 [1024, 1024], P('sub')
- cross_gain_grad: float32 [1024], P('sub')
- cross_query_grad: float32 [1024, 1024], P(None, 'sub')
- cross_key_grad: float32 [4096, 1024], P(None, 'sub')
- cross_value_grad: float32 [4096, 1024], P(None, 'sub')
- cross_out_grad: float32 [1024, 1024], P('sub')
- mlp_gain_grad: float32 [1024], P('sub')
- up_weight_grad: float32 [1024, 4096], P(None, 'sub')
- down_weight_grad: float32 [4096, 1024], P('sub')
The draws below stay inside these ranges and needn't reach their ends.
All inputs are finite; a program needn't handle non-finite values.
Results may differ from the reference program's by a relative error of at most 0.033.
Values may be sent and summed in bfloat16 or wider, within the bound.
A program may use at most 256 MiB of HBM per device.

```python
import math
import jax
import jax.numpy as jnp
from jax import lax

C = 256
G = 32
H = 16
HD = 64
D = 1024
FF = 4096
TW = 4096
TXT = 128
S = 256
POOL = 4
L = 64
B = 1


def shard_levels(stream_key, dims, cuts, least, high):
    def one(dim, parts):
        steps = jax.random.uniform(jax.random.fold_in(jax.random.fold_in(stream_key, 6), dim), (parts,), jnp.float32, least / len(cuts), high / len(cuts))
        return jnp.repeat(jnp.exp(steps), dims[dim] // parts).reshape((-1,) + (1,) * (len(dims) - dim - 1))

    loudness = one(*cuts[0])
    for cut in cuts[1:]:
        loudness = loudness * one(*cut)
    return loudness


def scatter_about(rng, extent, scale, bound, pieces=(), dtype=jnp.bfloat16):
    entries = scale * jax.random.normal(rng, extent, jnp.float32)
    if pieces:
        entries = entries * shard_levels(rng, extent, pieces, -0.22, 0.18)
    return jnp.clip(entries, -bound, bound).astype(dtype)


def setup_inputs(seed: int = 0) -> dict:
    seeds = jax.random.split(jax.random.key(seed), 29)
    return {
        "outer_image": scatter_about(seeds[0], (B, S, S, C), 1.0, 6.0, ((1, 8), (2, 4))),
        "inner_image": scatter_about(seeds[1], (B, L * L, D), 1.0, 6.0, ((1, 8), (2, 4))),
        "text_states": scatter_about(seeds[2], (B, TXT, TW), 1.0, 6.0),
        "time_steps": jax.random.randint(seeds[3], (B,), 0, 1000).astype(jnp.int32),
        "text_lengths": jax.random.randint(seeds[4], (B,), TXT // 4, TXT + 1).astype(jnp.int32),
        "first_gain": jnp.clip(1.0 + 0.18 * jax.random.normal(seeds[5], (C,), jnp.float32), 0.1, 1.9),
        "first_bias": scatter_about(seeds[6], (C,), 0.5, 3.0, (), jnp.float32),
        "conv_first": scatter_about(seeds[7], (3, 3, C, C), (9 * C) ** -0.5, 0.125),
        "time_weight": scatter_about(seeds[8], (C, C), (C // 4) ** -0.5, 0.75),
        "second_gain": jnp.clip(1.0 + 0.18 * jax.random.normal(seeds[9], (C,), jnp.float32), 0.1, 1.9),
        "second_bias": scatter_about(seeds[10], (C,), 0.5, 3.0, (), jnp.float32),
        "conv_second": scatter_about(seeds[11], (3, 3, C, C), (9 * C) ** -0.5, 0.125),
        "lift_weight": scatter_about(seeds[12], (C, D), (C // 16) ** -0.5, 1.5),
        "attn_gain": jnp.clip(1.0 + 0.18 * jax.random.normal(seeds[13], (D,), jnp.float32), 0.1, 1.9),
        "query_weight": scatter_about(seeds[14], (D, D), D ** -0.5, 0.1875, ((1, 4),)),
        "key_weight": scatter_about(seeds[15], (D, D), D ** -0.5, 0.1875, ((1, 4),)),
        "value_weight": scatter_about(seeds[16], (D, D), D ** -0.5, 0.1875, ((1, 4),)),
        "out_weight": scatter_about(seeds[17], (D, D), (D // 64) ** -0.5, 1.5, ((0, 4),)),
        "cross_gain": jnp.clip(1.0 + 0.18 * jax.random.normal(seeds[18], (D,), jnp.float32), 0.1, 1.9),
        "cross_query": scatter_about(seeds[19], (D, D), D ** -0.5, 0.1875, ((1, 4),)),
        "cross_key": scatter_about(seeds[20], (TW, D), TW ** -0.5, 0.09375, ((1, 4),)),
        "cross_value": scatter_about(seeds[21], (TW, D), TW ** -0.5, 0.09375, ((1, 4),)),
        "cross_out": scatter_about(seeds[22], (D, D), (D // 16) ** -0.5, 0.75, ((0, 4),)),
        "mlp_gain": jnp.clip(1.0 + 0.18 * jax.random.normal(seeds[23], (D,), jnp.float32), 0.1, 1.9),
        "up_weight": scatter_about(seeds[24], (D, FF), D ** -0.5, 0.1875, ((1, 4),)),
        "down_weight": scatter_about(seeds[25], (FF, D), (FF // 4) ** -0.5, 0.1875, ((0, 4),)),
        "outer_cotan": scatter_about(seeds[26], (B, S, S, C), 1.0, 6.0, ((1, 8), (2, 4))),
        "inner_cotan": scatter_about(seeds[27], (B, L * L, D), 1.0, 6.0, ((1, 8), (2, 4))),
    }


EPSILON = 1e-05
precise = lax.Precision.HIGHEST

@jax.custom_vjp
def low(v):
    return lax.optimization_barrier(v.astype(jnp.bfloat16)).astype(jnp.float32)

@jax.custom_vjp
def low_back(v):
    return v

def low_keep(v):
    return (low(v), None)

def low_pass(kept, grad):
    return (grad,)

def back_keep(v):
    return (v, None)

def back_low(kept, grad):
    return (low(grad),)
low.defvjp(low_keep, low_pass)
low_back.defvjp(back_keep, back_low)

def time_embed(time_steps):
    half_width = C // 2
    frequency = jnp.exp(-math.log(10000.0) * jnp.arange(half_width).astype(jnp.float32) / half_width)
    angles = time_steps.astype(jnp.float32)[:, None] * frequency[None, :]
    return jnp.concatenate([jnp.sin(angles), jnp.cos(angles)], axis=1)

def group_norm(values, norm_gain, norm_bias):
    grouped = values.reshape(B, S, S, G, C // G)
    center = lax.optimization_barrier(jnp.mean(grouped, axis=(1, 2, 4), keepdims=True))
    spread = lax.optimization_barrier(jnp.mean(jnp.square(grouped - center), axis=(1, 2, 4), keepdims=True))
    normed = (grouped - center) * lax.rsqrt(spread + EPSILON)
    return normed.reshape(B, S, S, C) * norm_gain + norm_bias

def layer_norm(values, norm_gain):
    center = lax.optimization_barrier(jnp.mean(values, axis=-1, keepdims=True))
    spread = lax.optimization_barrier(jnp.mean(jnp.square(values - center), axis=-1, keepdims=True))
    return (values - center) * lax.rsqrt(spread + EPSILON) * norm_gain

def conv_same(values, kernel):
    return lax.conv_general_dilated(values, kernel, (1, 1), 'SAME', dimension_numbers=('NHWC', 'HWIO', 'NHWC'), precision=precise)

def softmax_rows(scores):
    maximum = lax.optimization_barrier(jnp.max(scores, axis=-1, keepdims=True))
    raised = jnp.exp(scores - maximum)
    return raised / lax.optimization_barrier(jnp.sum(raised, axis=-1, keepdims=True))

def project(values, weight):
    return jnp.einsum('btd,de->bte', values, weight, precision=precise)

def attend_item(items):
    query_rows, key_rows, value_rows = items
    scores = low_back(jnp.dot(query_rows, key_rows.T, precision=precise) * HD ** (-0.5))
    weights = low(softmax_rows(scores))
    return jnp.dot(weights, value_rows, precision=precise)

def heads_first(values):
    return values.reshape(B, L * L, H, HD).transpose(0, 2, 1, 3).reshape(B * H, L * L, HD)

def self_attention(normed, query_weight, key_weight, value_weight, out_weight):
    query_all = low_back(low(project(normed, query_weight)))
    key_all = low_back(low(project(normed, key_weight)))
    value_all = low_back(low(project(normed, value_weight)))
    mixed_rows = lax.map(jax.checkpoint(attend_item), (heads_first(query_all), heads_first(key_all), heads_first(value_all)))
    mixed_rows = mixed_rows.reshape(B, H, L * L, HD).transpose(0, 2, 1, 3).reshape(B, L * L, D)
    return project(low_back(low(mixed_rows)), out_weight)

def cross_attention(normed, text_f, text_mask, cross_query, cross_key, cross_value, cross_out):
    query_all = low_back(low(project(normed, cross_query))).reshape(B, L * L, H, HD)
    key_all = low(project(text_f, cross_key)).reshape(B, TXT, H, HD)
    value_all = low(project(text_f, cross_value)).reshape(B, TXT, H, HD)
    scores = low_back(jnp.einsum('bqhd,bkhd->bhqk', query_all, key_all, precision=precise) * HD ** (-0.5))
    scores = jnp.where(text_mask[:, None, None, :], scores, -1000000000.0)
    weights = low(softmax_rows(scores))
    mixed_rows = jnp.einsum('bhqk,bkhd->bqhd', weights, value_all, precision=precise).reshape(B, L * L, D)
    return project(low_back(low(mixed_rows)), cross_out)

def feed_forward(normed, up_weight, down_weight):
    lifted_up = low_back(project(normed, up_weight))
    return project(low(jax.nn.gelu(lifted_up, approximate=True)), down_weight)

def reference(outer_image, inner_image, text_states, time_steps, text_lengths, first_gain, first_bias, conv_first, time_weight, second_gain, second_bias, conv_second, lift_weight, attn_gain, query_weight, key_weight, value_weight, out_weight, cross_gain, cross_query, cross_key, cross_value, cross_out, mlp_gain, up_weight, down_weight, outer_cotan, inner_cotan):
    time_act = jax.nn.silu(time_embed(time_steps))
    text_f = text_states.astype(jnp.float32)
    text_mask = jnp.arange(TXT)[None, :] < text_lengths[:, None]

    def whole(outer_f, inner_f, first_gain, first_bias, conv_first, time_weight, second_gain, second_bias, conv_second, lift_weight, attn_gain, query_weight, key_weight, value_weight, out_weight, cross_gain, cross_query, cross_key, cross_value, cross_out, mlp_gain, up_weight, down_weight):
        first_act = low(jax.nn.silu(group_norm(outer_f, first_gain, first_bias)))
        time_shift = jnp.dot(time_act, time_weight, precision=precise)
        hidden = low_back(conv_same(first_act, conv_first)) + time_shift[:, None, None, :]
        second_act = low(jax.nn.silu(group_norm(hidden, second_gain, second_bias)))
        outer_sum = outer_f + low_back(conv_same(second_act, conv_second))
        pooled = low(lax.optimization_barrier(jnp.mean(outer_sum.reshape(B, L, POOL, L, POOL, C), axis=(2, 4))))
        lifted = low_back(low(jnp.einsum('bijc,cd->bijd', pooled, lift_weight, precision=precise))).reshape(B, L * L, D)
        stream_in = inner_f + lifted
        attn_in = low(layer_norm(stream_in, attn_gain))
        after_attn = stream_in + low_back(self_attention(attn_in, query_weight, key_weight, value_weight, out_weight))
        cross_in = low(layer_norm(after_attn, cross_gain))
        after_cross = after_attn + low_back(cross_attention(cross_in, text_f, text_mask, cross_query, cross_key, cross_value, cross_out))
        mlp_in = low(layer_norm(after_cross, mlp_gain))
        inner_sum = after_cross + low_back(feed_forward(mlp_in, up_weight, down_weight))
        return (outer_sum, inner_sum)
    floats = (outer_image, inner_image, first_gain, first_bias, conv_first, time_weight, second_gain, second_bias, conv_second, lift_weight, attn_gain, query_weight, key_weight, value_weight, out_weight, cross_gain, cross_query, cross_key, cross_value, cross_out, mlp_gain, up_weight, down_weight)
    floats = tuple((item.astype(jnp.float32) for item in floats))
    results, pullback = jax.vjp(whole, *floats)
    grads = pullback((outer_cotan.astype(jnp.float32), inner_cotan.astype(jnp.float32)))
    return (results[0].astype(jnp.bfloat16), results[1].astype(jnp.bfloat16), grads[0], grads[1], grads[2], grads[3], grads[4], grads[5], grads[6], grads[7], grads[8], grads[9], grads[10], grads[11], grads[12], grads[13], grads[14], grads[15], grads[16], grads[17], grads[18], grads[19], grads[20], grads[21], grads[22])
```

```python
import functools
import math

import jax
import jax.numpy as jnp
from jax import lax
from jax.experimental import pallas as pl
from jax.experimental.pallas import tpu as pltpu
from jax.sharding import PartitionSpec as P

G = 32
HD = 64
POOL = 4
EPSILON = 1e-05
MESH = pl.DeviceIdType.MESH
precise = lax.Precision.HIGHEST
f32 = jnp.float32
bf16 = jnp.bfloat16


def params(cid=None, vmem=56):
    if cid is None:
        return pltpu.CompilerParams(vmem_limit_bytes=vmem << 20)
    return pltpu.CompilerParams(
        collective_id=cid, has_side_effects=True, vmem_limit_bytes=vmem << 20
    )


def in_vmem():
    return pl.BlockSpec(memory_space=pltpu.VMEM)


def anywhere():
    return pl.BlockSpec(memory_space=pl.ANY)


def dma(*shape):
    return pltpu.SemaphoreType.DMA(shape)


def remote(src, dst, send_sem, recv_sem, where):
    return pltpu.make_async_remote_copy(
        src_ref=src,
        dst_ref=dst,
        send_sem=send_sem,
        recv_sem=recv_sem,
        device_id=where,
        device_id_type=MESH,
    )


def arrived(dst, send_sem, recv_sem, me):
    remote(dst, dst, send_sem, recv_sem, me).wait_recv()


def greet(peers):
    barrier = pltpu.get_barrier_semaphore()
    for peer in peers:
        pl.semaphore_signal(barrier, inc=1, device_id=peer, device_id_type=MESH)
    pl.semaphore_wait(barrier, len(peers))


def total_kernel(nt, ns, x_ref, o_ref, first, second, ss1, rs1, ss2, rs2):
    t, s = lax.axis_index("tile"), lax.axis_index("sub")
    near = [lax.rem(s + k, ns) for k in range(1, ns)]
    far = [lax.rem(t + k, nt) for k in range(1, nt)]
    first[s] = x_ref[...]
    greet([(t, p) for p in near] + [(p, s) for p in far])
    copies = []
    for k, p in enumerate(near):
        copies.append(remote(first.at[s], first.at[s], ss1.at[k], rs1.at[s], (t, p)))
        copies[-1].start()
    for k, p in enumerate(near):
        arrived(first.at[p], ss1.at[k], rs1.at[p], (t, s))
    total = first[0]
    for k in range(1, ns):
        total = total + first[k]
    second[t] = total
    for k, p in enumerate(far):
        copies.append(remote(second.at[t], second.at[t], ss2.at[k], rs2.at[t], (p, s)))
        copies[-1].start()
    for k, p in enumerate(far):
        arrived(second.at[p], ss2.at[k], rs2.at[p], (t, s))
    total = second[0]
    for k in range(1, nt):
        total = total + second[k]
    o_ref[...] = total
    for copy in copies:
        copy.wait_send()


def total_all(values, cid):
    nt, ns = lax.axis_size("tile"), lax.axis_size("sub")
    flat = values.reshape(-1, 128)
    out = pl.pallas_call(
        functools.partial(total_kernel, nt, ns),
        out_shape=jax.ShapeDtypeStruct(flat.shape, f32),
        in_specs=[in_vmem()],
        out_specs=in_vmem(),
        scratch_shapes=[
            pltpu.VMEM((ns,) + flat.shape, f32),
            pltpu.VMEM((nt,) + flat.shape, f32),
            dma(ns),
            dma(ns),
            dma(nt),
            dma(nt),
        ],
        compiler_params=params(cid),
        name="total_all",
    )(flat)
    return out.reshape(values.shape)


def chunks_of(rows):
    return max(1, min(4, rows // 16))


def gather_kernel(ns, count, x_ref, o_ref, s1, r1, s2, r2, own):
    far = ns // 2
    t, s = lax.axis_index("tile"), lax.axis_index("sub")
    r, c = s // 2, lax.rem(s, 2)
    me, twin = (t, s), (t, r * 2 + 1 - c)
    size = x_ref.shape[0] // count
    greet([twin] + [(t, lax.rem(r + k, far) * 2 + c) for k in range(1, far)])
    local = pltpu.make_async_copy(x_ref, o_ref.at[s], own)
    local.start()
    copies = []

    def send(src, dst, send_sem, recv_sem, where):
        copies.append(remote(src, dst, send_sem, recv_sem, where))
        copies[-1].start()

    for j in range(count):
        part = pl.ds(j * size, size)
        for k in range(1, far):
            peer = (t, lax.rem(r + k, far) * 2 + c)
            send(x_ref.at[part], o_ref.at[s, part], s1.at[k, j], r1.at[k, j], peer)
    for j in range(count):
        part = pl.ds(j * size, size)
        send(x_ref.at[part], o_ref.at[s, part], s2.at[0, j], r2.at[0, j], twin)
    for j in range(count):
        part = pl.ds(j * size, size)
        for k in range(1, far):
            block = o_ref.at[lax.rem(r + far - k, far) * 2 + c, part]
            arrived(block, s1.at[k, j], r1.at[k, j], me)
            send(block, block, s2.at[k, j], r2.at[k, j], twin)
    for j in range(count):
        part = pl.ds(j * size, size)
        for k in range(far):
            block = o_ref.at[lax.rem(r + far - k, far) * 2 + 1 - c, part]
            arrived(block, s2.at[k, j], r2.at[k, j], me)
    for copy in copies:
        copy.wait_send()
    local.wait()


def gather_sub(x, cid):
    ns = lax.axis_size("sub")
    far, count = ns // 2, chunks_of(x.shape[0])
    return pl.pallas_call(
        functools.partial(gather_kernel, ns, count),
        out_shape=jax.ShapeDtypeStruct((ns,) + x.shape, x.dtype),
        in_specs=[anywhere()],
        out_specs=anywhere(),
        scratch_shapes=[dma(far, count) for _ in range(4)] + [pltpu.SemaphoreType.DMA],
        compiler_params=params(cid),
        name="gather_sub",
    )(x)


def scatter_kernel(ns, count, x_ref, o_ref, got, stage, last, s1, r1, s2, r2):
    far = ns // 2
    t, s = lax.axis_index("tile"), lax.axis_index("sub")
    r, c = s // 2, lax.rem(s, 2)
    me, twin = (t, s), (t, r * 2 + 1 - c)
    size = x_ref.shape[1] // count
    greet([twin] + [(t, lax.rem(r + k, far) * 2 + c) for k in range(1, far)])
    copies = []

    def send(src, dst, send_sem, recv_sem, where):
        copies.append(remote(src, dst, send_sem, recv_sem, where))
        copies[-1].start()

    for k in list(range(1, far)) + [0]:
        for j in range(count):
            part = pl.ds(j * size, size)
            block = x_ref.at[lax.rem(r + k, far) * 2 + 1 - c, part]
            send(block, got.at[k, part], s1.at[k, j], r1.at[k, j], twin)
    for j in range(count):
        part = pl.ds(j * size, size)
        for k in range(1, far):
            p = lax.rem(r + k, far) * 2 + c
            arrived(got.at[k, part], s1.at[k, j], r1.at[k, j], me)
            stage[k, part] = (x_ref[p, part].astype(f32) + got[k, part].astype(f32)).astype(bf16)
            send(stage.at[k, part], last.at[k, part], s2.at[k, j], r2.at[k, j], (t, p))
    for j in range(count):
        part = pl.ds(j * size, size)
        arrived(got.at[0, part], s1.at[0, j], r1.at[0, j], me)
        total = x_ref[s, part].astype(f32) + got[0, part].astype(f32)
        for k in range(1, far):
            arrived(last.at[k, part], s2.at[k, j], r2.at[k, j], me)
            total = total + last[k, part].astype(f32)
        o_ref[part] = total
    for copy in copies:
        copy.wait_send()


def scatter_sub(x, cid):
    ns = lax.axis_size("sub")
    x = x.astype(bf16).reshape(ns, x.shape[0] // ns, x.shape[1])
    block = x.shape[1:]
    far, count = ns // 2, chunks_of(block[0])
    return pl.pallas_call(
        functools.partial(scatter_kernel, ns, count),
        out_shape=jax.ShapeDtypeStruct(block, f32),
        in_specs=[in_vmem()],
        out_specs=in_vmem(),
        scratch_shapes=[pltpu.VMEM((far,) + block, bf16) for _ in range(3)]
        + [dma(far, count) for _ in range(4)],
        compiler_params=params(cid),
        name="scatter_sub",
    )(x)


def deal(nt, u):
    t, s = lax.axis_index("tile"), lax.axis_index("sub")
    nb = nt // u
    a, b = t // nb, lax.rem(t, nb)
    a_peer = lambda k: (lax.rem(a + k, u) * nb + b, s)
    b_peer = lambda k: (a * nb + lax.rem(b + k, nb), s)
    peers = [a_peer(k) for k in range(1, u)] + [b_peer(k) for k in range(1, nb)]
    return t, s, nb, a, b, a_peer, b_peer, peers


def rows_of(ref, i, size):
    return ref.at[:, pl.ds(pl.multiple_of(i * size, size), size), :]


def lanes_of(ref, i, size):
    return ref.at[:, :, pl.ds(pl.multiple_of(i * size, size), size)]


def qkv_out_kernel(nt, u, q_ref, kv_ref, qo, kvo, qs, qr, ks, kr, fs, fr, own):
    t, s, nb, a, b, a_peer, b_peer, peers = deal(nt, u)
    me = (t, s)
    greet(peers)
    local = [
        pltpu.make_async_copy(rows_of(q_ref, a, HD), qo.at[a], own.at[0]),
        pltpu.make_async_copy(lanes_of(kv_ref, a, 2 * HD), kvo.at[t], own.at[1]),
    ]
    for copy in local:
        copy.start()
    copies = []

    def send(src, dst, send_sem, recv_sem, where):
        copies.append(remote(src, dst, send_sem, recv_sem, where))
        copies[-1].start()

    for k in range(1, u):
        block = lanes_of(kv_ref, lax.rem(a + k, u), 2 * HD)
        send(block, kvo.at[t], ks.at[k], kr.at[k], a_peer(k))
    for m in range(1, nb):
        send(lanes_of(kv_ref, a, 2 * HD), kvo.at[t], fs.at[0, m], fr.at[0, m], b_peer(m))
    for k in range(1, u):
        block = rows_of(q_ref, lax.rem(a + k, u), HD)
        send(block, qo.at[a], qs.at[k], qr.at[k], a_peer(k))
    for k in range(1, u):
        block = kvo.at[lax.rem(a + u - k, u) * nb + b]
        arrived(block, ks.at[k], kr.at[k], me)
        for m in range(1, nb):
            send(block, block, fs.at[k, m], fr.at[k, m], b_peer(m))
    for k in range(1, u):
        arrived(qo.at[lax.rem(a + u - k, u)], qs.at[k], qr.at[k], me)
    for k in range(u):
        for m in range(1, nb):
            block = kvo.at[lax.rem(a + u - k, u) * nb + lax.rem(b + nb - m, nb)]
            arrived(block, fs.at[k, m], fr.at[k, m], me)
    for copy in copies:
        copy.wait_send()
    for copy in local:
        copy.wait()


def qkv_out(q, kv, cid):
    nt = lax.axis_size("tile")
    batch, width, length = q.shape
    u = width // HD
    nb = nt // u
    return pl.pallas_call(
        functools.partial(qkv_out_kernel, nt, u),
        out_shape=(
            jax.ShapeDtypeStruct((u, batch, HD, length), bf16),
            jax.ShapeDtypeStruct((nt, batch, length, 2 * HD), bf16),
        ),
        in_specs=[anywhere()] * 2,
        out_specs=(anywhere(), anywhere()),
        scratch_shapes=[dma(u), dma(u), dma(u), dma(u), dma(u, nb), dma(u, nb), dma(2)],
        compiler_params=params(cid),
        name="qkv_out",
    )(q, kv)


def swap_kernel(nt, u, home, x_ref, o_ref, ss, rs, own):
    t, s, nb, a, b, a_peer, b_peer, peers = deal(nt, u)
    greet([a_peer(k) for k in range(1, u)])
    taken = lambda i: x_ref.at[i] if home else rows_of(x_ref, i, HD)
    placed = lambda i: rows_of(o_ref, i, HD) if home else o_ref.at[i]
    local = pltpu.make_async_copy(taken(a), placed(a), own)
    local.start()
    copies = []
    for k in range(1, u):
        copies.append(
            remote(taken(lax.rem(a + k, u)), placed(a), ss.at[k], rs.at[k], a_peer(k))
        )
        copies[-1].start()
    for k in range(1, u):
        arrived(placed(lax.rem(a + u - k, u)), ss.at[k], rs.at[k], (t, s))
    for copy in copies:
        copy.wait_send()
    local.wait()


def swap_heads(x, home, cid):
    nt = lax.axis_size("tile")
    if home:
        u, batch, _, length = x.shape
        shape = (batch, u * HD, length)
    else:
        batch, width, length = x.shape
        u = width // HD
        shape = (u, batch, HD, length)
    if u == 1:
        return x.reshape(shape)
    return pl.pallas_call(
        functools.partial(swap_kernel, nt, u, home),
        out_shape=jax.ShapeDtypeStruct(shape, bf16),
        in_specs=[anywhere()],
        out_specs=anywhere(),
        scratch_shapes=[dma(u), dma(u), pltpu.SemaphoreType.DMA],
        compiler_params=params(cid),
        name="swap_heads",
    )(x)


def dqkv_home_kernel(nt, u, dq_ref, dkv_ref, qo, kvo, got, stage, qs, qr, fs, fr, ks, kr, own):
    t, s, nb, a, b, a_peer, b_peer, peers = deal(nt, u)
    me = (t, s)
    greet(peers)
    copies = []

    def send(src, dst, send_sem, recv_sem, where):
        copies.append(remote(src, dst, send_sem, recv_sem, where))
        copies[-1].start()

    order = list(range(1, u)) + [0]
    for k in order:
        for m in range(1, nb):
            block = dkv_ref.at[lax.rem(a + k, u) * nb + lax.rem(b + m, nb)]
            send(block, got.at[m, k], fs.at[k, m], fr.at[k, m], b_peer(m))
    for k in range(1, u):
        send(dq_ref.at[lax.rem(a + k, u)], rows_of(qo, a, HD), qs.at[k], qr.at[k], a_peer(k))
    local = [pltpu.make_async_copy(dq_ref.at[a], rows_of(qo, a, HD), own.at[0])]
    local[0].start()
    for k in order:
        total = dkv_ref[lax.rem(a + k, u) * nb + b].astype(f32)
        for m in range(1, nb):
            arrived(got.at[m, k], fs.at[k, m], fr.at[k, m], me)
            total = total + got[m, k].astype(f32)
        stage[k] = total.astype(bf16)
        if k:
            send(stage.at[k], lanes_of(kvo, a, 2 * HD), ks.at[k], kr.at[k], a_peer(k))
        else:
            local.append(pltpu.make_async_copy(stage.at[0], lanes_of(kvo, a, 2 * HD), own.at[1]))
            local[1].start()
    for k in range(1, u):
        i = lax.rem(a + u - k, u)
        arrived(rows_of(qo, i, HD), qs.at[k], qr.at[k], me)
        arrived(lanes_of(kvo, i, 2 * HD), ks.at[k], kr.at[k], me)
    for copy in copies:
        copy.wait_send()
    for copy in local:
        copy.wait()


def dqkv_home(dq, dkv, cid):
    nt = lax.axis_size("tile")
    u, batch, _, length = dq.shape
    nb = nt // u
    block = (batch, length, 2 * HD)
    return pl.pallas_call(
        functools.partial(dqkv_home_kernel, nt, u),
        out_shape=(
            jax.ShapeDtypeStruct((batch, u * HD, length), bf16),
            jax.ShapeDtypeStruct((batch, length, u * 2 * HD), bf16),
        ),
        in_specs=[in_vmem()] * 2,
        out_specs=(anywhere(), anywhere()),
        scratch_shapes=[
            pltpu.VMEM((nb, u) + block, bf16),
            pltpu.VMEM((u,) + block, bf16),
            dma(u),
            dma(u),
            dma(u, nb),
            dma(u, nb),
            dma(u),
            dma(u),
            dma(2),
        ],
        compiler_params=params(cid),
        name="dqkv_home",
    )(dq, dkv)


def dot(left, right):
    return jnp.dot(left, right, preferred_element_type=f32)


def flash_kernel(q_ref, kv_ref, o_ref, of_ref, lse_ref, vt):
    count, length = kv_ref.shape[0], kv_ref.shape[2]

    @pl.when(pl.program_id(1) == 0)
    def _():
        for j in range(count):
            vt[j] = kv_ref[j, 0].T[HD:]

    q = q_ref[0, 0] * 0.125
    padded = jnp.concatenate([q, jnp.zeros_like(q)], axis=0)
    top = jnp.full((1, q.shape[1]), -jnp.inf, f32)
    total = jnp.zeros((1, q.shape[1]), f32)
    mixed = jnp.zeros(q.shape, f32)
    for j in range(count):
        scores = dot(kv_ref[j, 0], padded)
        new = jnp.maximum(top, jnp.max(scores, axis=0, keepdims=True))
        raised = jnp.exp(scores - new)
        scale = jnp.exp(top - new)
        total = total * scale + jnp.sum(raised, axis=0, keepdims=True)
        mixed = mixed * scale + dot(vt[j], raised.astype(bf16))
        top = new
    mixed = mixed / total
    o_ref[0, 0] = mixed.astype(bf16)
    of_ref[0, 0] = mixed
    lse_ref[0, 0] = top + jnp.log(total)


def flash(q, kv):
    u, batch, _, length = q.shape
    nt = kv.shape[0]
    rows = pl.BlockSpec((1, 1, HD, length), lambda b, i: (i, b, 0, 0))
    return pl.pallas_call(
        flash_kernel,
        grid=(batch, u),
        out_shape=(
            jax.ShapeDtypeStruct(q.shape, bf16),
            jax.ShapeDtypeStruct(q.shape, f32),
            jax.ShapeDtypeStruct((u, batch, 1, length), f32),
        ),
        in_specs=[rows, pl.BlockSpec((nt, 1, length, 2 * HD), lambda b, i: (0, b, 0, 0))],
        out_specs=(rows, rows, pl.BlockSpec((1, 1, 1, length), lambda b, i: (i, b, 0, 0))),
        scratch_shapes=[pltpu.VMEM((nt, HD, length), bf16)],
        compiler_params=params(),
        name="flash",
    )(q, kv)


def flash_back_kernel(q_ref, d_ref, of_ref, lse_ref, kv_ref, dq_ref, dkv_ref, qd, rows, delta, acc):
    u, length = q_ref.shape[0], q_ref.shape[3]
    j = pl.program_id(1)

    @pl.when(j == 0)
    def _():
        for i in range(u):
            q, d = q_ref[i, 0], d_ref[i, 0]
            zero = jnp.zeros_like(q)
            qd[i, 0] = jnp.concatenate([q * 0.125, zero], axis=0)
            qd[i, 1] = jnp.concatenate([zero, d], axis=0)
            rows[i, 0] = qd[i, 0].T
            rows[i, 1] = qd[i, 1].T
            delta[i] = jnp.sum(d.astype(f32) * of_ref[i, 0], axis=0, keepdims=True)
            acc[i] = jnp.zeros_like(acc[i])

    kv = kv_ref[0, 0]
    kt = kv.T[:HD]
    total = jnp.zeros(kv.shape, f32)
    for i in range(u):
        probs = jnp.exp(dot(kv, qd[i, 0]) - lse_ref[i, 0])
        slope = dot(kv, qd[i, 1])
        grads = (probs * (slope - delta[i])).astype(bf16)
        total = total + dot(probs.astype(bf16), rows[i, 1]) + dot(grads, rows[i, 0])
        acc[i] += dot(kt, grads)
    dkv_ref[0, 0] = total.astype(bf16)

    @pl.when(j == pl.num_programs(1) - 1)
    def _():
        for i in range(u):
            dq_ref[i, 0] = (acc[i] * 0.125).astype(bf16)


def flash_back(q, d, of, lse, kv):
    u, batch, _, length = q.shape
    nt = kv.shape[0]
    whole = pl.BlockSpec((u, 1, HD, length), lambda b, j: (0, b, 0, 0))
    part = pl.BlockSpec((1, 1, length, 2 * HD), lambda b, j: (j, b, 0, 0))
    return pl.pallas_call(
        flash_back_kernel,
        grid=(batch, nt),
        out_shape=(jax.ShapeDtypeStruct(q.shape, bf16), jax.ShapeDtypeStruct(kv.shape, bf16)),
        in_specs=[
            whole,
            whole,
            whole,
            pl.BlockSpec((u, 1, 1, length), lambda b, j: (0, b, 0, 0)),
            part,
        ],
        out_specs=(whole, part),
        scratch_shapes=[
            pltpu.VMEM((u, 2, 2 * HD, length), bf16),
            pltpu.VMEM((u, 2, length, 2 * HD), bf16),
            pltpu.VMEM((u, 1, length), f32),
            pltpu.VMEM((u, HD, length), f32),
        ],
        compiler_params=params(),
        name="flash_back",
    )(q, d, of, lse, kv)


def bordered(block, width):
    for axis, dim in (("tile", 1), ("sub", 2)):
        count = lax.axis_size(axis)
        forward = [(i, i + 1) for i in range(count - 1)]
        backward = [(target, source) for source, target in forward]
        low = lax.ppermute(
            lax.slice_in_dim(block, block.shape[dim] - width, None, axis=dim), axis, forward
        )
        high = lax.ppermute(lax.slice_in_dim(block, 0, width, axis=dim), axis, backward)
        block = jnp.concatenate([low, block, high], axis=dim)
    return block


def inside(shape, width):
    rows, cols = shape[1] - 2 * width, shape[2] - 2 * width
    y = lax.axis_index("tile") * rows - width + jnp.arange(shape[1])
    x = lax.axis_index("sub") * cols - width + jnp.arange(shape[2])
    good_y = (y >= 0) & (y < rows * lax.axis_size("tile"))
    good_x = (x >= 0) & (x < cols * lax.axis_size("sub"))
    return (good_y[:, None] & good_x[None, :])[None, :, :, None]


def trim(values, width):
    return values[:, width:-width, width:-width]


def time_embed(time_steps, channels):
    half_width = channels // 2
    frequency = jnp.exp(
        -math.log(10000.0) * jnp.arange(half_width).astype(f32) / half_width
    )
    angles = time_steps.astype(f32)[:, None] * frequency[None, :]
    return jnp.concatenate([jnp.sin(angles), jnp.cos(angles)], axis=1)


def conv_valid(padded, kernel):
    return lax.conv_general_dilated(
        padded,
        kernel,
        (1, 1),
        "VALID",
        dimension_numbers=("NHWC", "HWIO", "NHWC"),
        preferred_element_type=f32,
    )


def conv_transposed(padded, kernel):
    return conv_valid(padded, jnp.transpose(kernel[::-1, ::-1], (0, 1, 3, 2)))


def conv_kernel_grad(padded_in, grad_out):
    rows, cols = grad_out.shape[1], grad_out.shape[2]
    taps = []
    for y in range(3):
        for x in range(3):
            window = padded_in[:, y : y + rows, x : x + cols, :]
            taps.append(
                jnp.einsum("bhwc,bhwd->cd", window, grad_out, preferred_element_type=f32)
            )
    return jnp.stack(taps).reshape(3, 3, padded_in.shape[3], grad_out.shape[3])


def by_group(values):
    channels = values.shape[-1]
    grouped = values.reshape(values.shape[:-1] + (G, channels // G))
    return jnp.repeat(jnp.sum(grouped, axis=-1), channels // G, axis=-1)


def pixel_sums(first, second):
    return jnp.stack([jnp.sum(first, axis=(1, 2)), jnp.sum(second, axis=(1, 2))], axis=1)


def group_stats(sums, group_size):
    center = by_group(sums[:, 0]) / group_size
    inv_std = lax.rsqrt(by_group(sums[:, 1]) / group_size - center * center + EPSILON)
    return center[:, None, None, :], inv_std[:, None, None, :]


def layer_stats(values, gain):
    width = values.shape[1]
    center = jnp.sum(values, axis=1, keepdims=True) / width
    moved = values - center
    inv_std = lax.rsqrt(jnp.sum(moved * moved, axis=1, keepdims=True) / width + EPSILON)
    normed = moved * inv_std
    return (normed * gain).astype(bf16), normed, inv_std


def layer_back(grad_out, normed, inv_std, gain):
    width = normed.shape[1]
    scaled = grad_out * gain
    mean_grad = jnp.sum(scaled, axis=1, keepdims=True) / width
    mean_cross = jnp.sum(scaled * normed, axis=1, keepdims=True) / width
    grad_in = inv_std * (scaled - mean_grad - normed * mean_cross)
    return grad_in, jnp.sum(grad_out * normed, axis=0)


def silu_grad(values):
    sigma = jax.nn.sigmoid(values)
    return sigma * (1.0 + values * (1.0 - sigma))


def gelu_tanh(values):
    return jax.nn.gelu(values, approximate=True)


def weight_grad(inputs, grads):
    return lax.dot_general(inputs, grads, (((0,), (0,)), ((), ())), preferred_element_type=f32)


def dot_t(left, right):
    return lax.dot_general(left, right, (((1,), (1,)), ((), ())), preferred_element_type=f32)


def cross_scores(queries, keys, text_mask):
    scores = jnp.einsum("sbqhd,bkhd->sbhqk", queries, keys, preferred_element_type=f32)
    return jnp.where(text_mask[None, :, None, None, :], scores * HD ** (-0.5), -1000000000.0)


def local(
    outer_image,
    inner_image,
    text_states,
    time_steps,
    text_lengths,
    first_gain,
    first_bias,
    conv_first,
    time_weight,
    second_gain,
    second_bias,
    conv_second,
    lift_weight,
    attn_gain,
    query_weight,
    key_weight,
    value_weight,
    out_weight,
    cross_gain,
    cross_query,
    cross_key,
    cross_value,
    cross_out,
    mlp_gain,
    up_weight,
    down_weight,
    outer_cotan,
    inner_cotan,
):
    nt, ns = lax.axis_size("tile"), lax.axis_size("sub")
    s = lax.axis_index("sub")
    batch, rows, cols, channels = outer_image.shape
    lr, lc = rows // POOL, cols // POOL
    width = inner_image.shape[2] * ns
    features = inner_image.shape[2]
    heads = features // HD
    own = batch * lr * lc
    length = ns * lr * lc
    pixels = rows * cols * nt * ns
    group_size = pixels * (channels // G)

    image_ext = bordered(outer_image, 2)
    cotan_ext = bordered(outer_cotan, 2)

    def whole_tokens(values):
        full = lax.all_gather(values, "sub", axis=2, tiled=True)
        full = full.reshape(batch, lr, ns, lc, width)
        mine = lax.dynamic_index_in_dim(full, s, 2, keepdims=False).reshape(own, width)
        return full, mine

    _, inner_own = whole_tokens(inner_image)
    cotan_full, cotan_own = whole_tokens(inner_cotan)
    cotan_full = jnp.transpose(cotan_full, (2, 0, 1, 3, 4)).reshape(ns * own, width)
    gains = lax.all_gather(
        jnp.stack([attn_gain, cross_gain, mlp_gain]), "sub", axis=1, tiled=True
    )

    time_act = jax.nn.silu(time_embed(time_steps, channels))
    time_shift = jnp.dot(time_act, time_weight.astype(f32), precision=precise)
    outer_f = outer_image.astype(f32)
    center1, std1 = group_stats(
        total_all(pixel_sums(outer_f, outer_f * outer_f), 0), group_size
    )
    hat1 = lambda v: (v.astype(f32) - center1) * std1
    norm1 = lambda v: hat1(v) * first_gain + first_bias
    act1 = jnp.where(
        inside(image_ext.shape, 2), jax.nn.silu(norm1(image_ext)), 0.0
    ).astype(bf16)
    hidden = conv_valid(act1, conv_first) + time_shift[:, None, None, :]
    middle = trim(hidden, 1)
    sums2 = total_all(pixel_sums(middle, middle * middle), 1)
    center2, std2 = group_stats(sums2, group_size)
    hat2 = lambda v: (v - center2) * std2
    norm2 = lambda v: hat2(v) * second_gain + second_bias
    act2 = jnp.where(inside(hidden.shape, 1), jax.nn.silu(norm2(hidden)), 0.0).astype(bf16)
    outer_sum = outer_f + conv_valid(act2, conv_second)
    pooled = jnp.mean(
        outer_sum.reshape(batch, lr, POOL, lc, POOL, channels), axis=(2, 4)
    ).astype(bf16)
    pooled = pooled.reshape(own, channels)

    stream_in = inner_own.astype(f32) + dot(pooled, lift_weight).astype(bf16).astype(f32)
    attn_low, attn_hat, attn_std = layer_stats(stream_in, gains[0])
    attn_in = gather_sub(attn_low, 2).reshape(ns * own, width)

    def per_sample(values, tokens_last):
        if tokens_last:
            values = values.reshape(-1, ns, batch, lr * lc)
            return jnp.transpose(values, (2, 0, 1, 3)).reshape(batch, -1, length)
        values = values.reshape(ns, batch, lr * lc, -1)
        return jnp.transpose(values, (1, 0, 2, 3)).reshape(batch, length, -1)

    def all_samples(values, tokens_last):
        if tokens_last:
            values = values.reshape(batch, -1, ns, lr * lc)
            return jnp.transpose(values, (1, 2, 0, 3)).reshape(-1, ns * own)
        values = values.reshape(batch, ns, lr * lc, -1)
        return jnp.transpose(values, (1, 0, 2, 3)).reshape(ns * own, -1)

    pair = lambda k, v: jnp.concatenate(
        [k.reshape(-1, heads, HD), v.reshape(-1, heads, HD)], axis=2
    ).reshape(-1, heads * 2 * HD)
    kv_weight = pair(key_weight, value_weight)
    query_t = lax.dot_general(
        query_weight, attn_in, (((0,), (1,)), ((), ())), preferred_element_type=f32
    ).astype(bf16)
    kv = dot(attn_in, kv_weight).astype(bf16)
    head_q, head_kv = qkv_out(per_sample(query_t, True), per_sample(kv, False), 3)
    head_mixed, head_mixed_f, head_lse = flash(head_q, head_kv)
    mixed_t = all_samples(swap_heads(head_mixed, True, 4), True)
    after_attn = stream_in + scatter_sub(weight_grad(mixed_t, out_weight), 5)

    cross_low, cross_hat, cross_std = layer_stats(after_attn, gains[1])
    cross_in = gather_sub(cross_low, 6).reshape(ns * own, width)
    text_split = lambda w: jnp.einsum(
        "bsw,we->bse", text_states, w, preferred_element_type=f32
    ).astype(bf16).reshape(batch, -1, heads, HD)
    cross_k, cross_v = text_split(cross_key), text_split(cross_value)
    text_mask = jnp.arange(text_states.shape[1])[None, :] < text_lengths[:, None]
    split = lambda v: v.reshape(ns, batch, lr * lc, heads, HD)
    cross_q = split(dot(cross_in, cross_query).astype(bf16))
    scores = cross_scores(cross_q, cross_k, text_mask)
    cross_probs = jax.nn.softmax(scores, axis=-1)
    cross_probs_low = cross_probs.astype(bf16)
    cross_mixed = (
        jnp.einsum("sbhqk,bkhd->sbqhd", cross_probs_low, cross_v, preferred_element_type=f32)
        .astype(bf16)
        .reshape(ns * own, features)
    )
    after_cross = after_attn + scatter_sub(dot(cross_mixed, cross_out), 7)

    mlp_low, mlp_hat, mlp_std = layer_stats(after_cross, gains[2])
    mlp_in = gather_sub(mlp_low, 8).reshape(ns * own, width)
    lifted_up = dot(mlp_in, up_weight)
    activated_f, gelu_pull = jax.vjp(gelu_tanh, lifted_up)
    activated = activated_f.astype(bf16)

    grad_act = dot_t(cotan_full, down_weight)
    grad_lift_up = gelu_pull(grad_act)[0].astype(bf16)
    grad_mid, grad_mlp_gain = layer_back(
        scatter_sub(dot_t(grad_lift_up, up_weight), 9), mlp_hat, mlp_std, gains[2]
    )
    grad_after_cross = cotan_own.astype(f32) + grad_mid
    grad_cross_full = gather_sub(grad_after_cross.astype(bf16), 10).reshape(ns * own, width)
    grad_cross_mixed = split(dot_t(grad_cross_full, cross_out).astype(bf16))
    grad_cv = jnp.einsum(
        "sbhqk,sbqhd->bkhd", cross_probs_low, grad_cross_mixed, preferred_element_type=f32
    )
    grad_probs = jnp.einsum(
        "sbqhd,bkhd->sbhqk", grad_cross_mixed, cross_v, preferred_element_type=f32
    )
    grad_scores = (
        cross_probs
        * (grad_probs - jnp.sum(cross_probs * grad_probs, axis=-1, keepdims=True))
    ).astype(bf16)
    grad_cq = (
        jnp.einsum("sbhqk,bkhd->sbqhd", grad_scores, cross_k, preferred_element_type=f32)
        * HD ** (-0.5)
    ).astype(bf16).reshape(ns * own, features)
    grad_ck = jnp.einsum(
        "sbhqk,sbqhd->bkhd", grad_scores, cross_q, preferred_element_type=f32
    ) * HD ** (-0.5)
    grad_mid, grad_cross_gain = layer_back(
        scatter_sub(dot_t(grad_cq, cross_query), 11), cross_hat, cross_std, gains[1]
    )
    grad_after_attn = grad_after_cross + grad_mid
    grad_attn_full = gather_sub(grad_after_attn.astype(bf16), 12).reshape(ns * own, width)
    grad_mixed_t = dot_t(out_weight, grad_attn_full).astype(bf16)
    head_d = swap_heads(per_sample(grad_mixed_t, True), False, 13)
    head_dq, head_dkv = flash_back(head_q, head_d, head_mixed_f, head_lse, head_kv)
    grad_q_t, grad_kv = dqkv_home(head_dq, head_dkv, 14)
    grad_q_t, grad_kv = all_samples(grad_q_t, True), all_samples(grad_kv, False)
    grad_attn_in = weight_grad(grad_q_t, query_weight.T) + dot_t(grad_kv, kv_weight)
    grad_mid, grad_attn_gain = layer_back(
        scatter_sub(grad_attn_in, 15), attn_hat, attn_std, gains[0]
    )
    inner_grad = grad_after_attn + grad_mid
    grad_lifted = inner_grad.astype(bf16)

    grad_lift = weight_grad(pooled, grad_lifted)
    grad_pooled = dot_t(grad_lifted, lift_weight) / (POOL * POOL)
    pooled_ext = bordered(grad_pooled.reshape(batch, lr, lc, channels), 1)
    spread = jnp.repeat(jnp.repeat(pooled_ext, POOL, axis=1), POOL, axis=2)
    grad_outer = cotan_ext.astype(f32) + trim(spread, POOL - 2)
    grad_conv2 = jnp.where(inside(grad_outer.shape, 2), grad_outer, 0.0).astype(bf16)
    slope2 = conv_transposed(grad_conv2, conv_second) * silu_grad(norm2(hidden))
    back2 = total_all(pixel_sums(trim(slope2, 1), trim(slope2 * hat2(hidden), 1)), 16)

    def group_means(back, gain):
        spread_out = lambda v: (by_group(v * gain) / group_size)[:, None, None, :]
        return spread_out(back[:, 0]), spread_out(back[:, 1])

    mean_grad2, mean_cross2 = group_means(back2, second_gain)
    grad_hidden = std2 * (slope2 * second_gain - mean_grad2 - hat2(hidden) * mean_cross2)
    grad_conv1 = jnp.where(inside(grad_hidden.shape, 1), grad_hidden, 0.0).astype(bf16)
    flat = lambda v: v[:, 0, 0, :]
    hat2_sum = flat(std2) * (sums2[:, 0] - pixels * flat(center2))
    hidden_sum = flat(std2) * (
        second_gain * back2[:, 0] - pixels * flat(mean_grad2) - flat(mean_cross2) * hat2_sum
    )
    grad_time = jnp.dot(time_act.T, hidden_sum, precision=precise)
    slope1 = conv_transposed(grad_conv1, conv_first) * silu_grad(norm1(outer_image))
    back1 = total_all(pixel_sums(slope1, slope1 * hat1(outer_image)), 17)
    mean_grad1, mean_cross1 = group_means(back1, first_gain)
    outer_grad = trim(grad_outer, 2) + std1 * (
        slope1 * first_gain - mean_grad1 - hat1(outer_image) * mean_cross1
    )

    down = dot(activated, down_weight).astype(bf16)
    inner_sum = after_cross + lax.psum_scatter(
        down, "sub", scatter_dimension=0, tiled=True
    ).astype(f32)

    def by_feature(values):
        full = lax.all_gather(values.astype(bf16), "sub", axis=0)
        mine = lax.dynamic_slice_in_dim(full, s * features, features, axis=2)
        mine = mine.reshape(ns, batch, lr, lc, features)
        return jnp.transpose(mine, (1, 2, 0, 3, 4)).reshape(batch, length, features)

    inner_out = by_feature(inner_sum)
    inner_grad = by_feature(inner_grad).astype(f32)

    over_tile = lambda *values: tuple(
        v.astype(f32) for v in lax.psum(tuple(v.astype(bf16) for v in values), "tile")
    )
    grad_down = weight_grad(activated, cotan_full)
    grad_up = weight_grad(mlp_in, grad_lift_up)
    grad_down, grad_up = over_tile(grad_down, grad_up)
    grad_cq_w = weight_grad(cross_in, grad_cq)
    grad_co_w = weight_grad(cross_mixed, grad_cross_full)
    grad_ck, grad_cv = lax.psum((grad_ck, grad_cv), "tile")

    def text_grad(grads):
        grads = grads.reshape(batch, -1, features)
        high = grads.astype(bf16)
        rest = (grads - high.astype(f32)).astype(bf16)
        both = jnp.concatenate([high, rest], axis=1)
        text = jnp.concatenate([text_states, text_states], axis=1)
        return jnp.einsum("bsw,bse->we", text, both, preferred_element_type=f32)

    grad_ck_w, grad_cv_w = text_grad(grad_ck), text_grad(grad_cv)
    grad_o_w = lax.dot_general(
        mixed_t, grad_attn_full, (((1,), (0,)), ((), ())), preferred_element_type=f32
    )
    grad_q_w = lax.dot_general(
        attn_in, grad_q_t, (((0,), (1,)), ((), ())), preferred_element_type=f32
    )
    grad_kv_w = weight_grad(attn_in, grad_kv)
    grad_cq_w, grad_co_w, grad_o_w, grad_q_w, grad_kv_w = over_tile(
        grad_cq_w, grad_co_w, grad_o_w, grad_q_w, grad_kv_w
    )
    grad_kv_w = grad_kv_w.reshape(width, heads, 2, HD)
    grad_k_w = grad_kv_w[:, :, 0].reshape(width, features)
    grad_v_w = grad_kv_w[:, :, 1].reshape(width, features)

    grad_conv_second = conv_kernel_grad(act2, trim(grad_conv2, 2))
    grad_conv_first = conv_kernel_grad(trim(act1, 1), trim(grad_conv1, 1))
    grad_gains = jnp.stack([grad_attn_gain, grad_cross_gain, grad_mlp_gain])
    everywhere = lax.psum(
        tuple(
            v.astype(bf16) for v in (grad_conv_first, grad_conv_second, grad_lift, grad_gains)
        ),
        ("tile", "sub"),
    )
    grad_conv_first, grad_conv_second, grad_lift, grad_gains = (
        v.astype(f32) for v in everywhere
    )
    grad_gains = lax.dynamic_slice_in_dim(grad_gains, s * features, features, axis=1)
    back1, back2 = jnp.sum(back1, axis=0), jnp.sum(back2, axis=0)
    return (
        outer_sum.astype(bf16),
        inner_out,
        outer_grad,
        inner_grad,
        back1[1],
        back1[0],
        grad_conv_first,
        grad_time,
        back2[1],
        back2[0],
        grad_conv_second,
        grad_lift,
        grad_gains[0],
        grad_q_w,
        grad_k_w,
        grad_v_w,
        grad_o_w,
        grad_gains[1],
        grad_cq_w,
        grad_ck_w,
        grad_cv_w,
        grad_co_w,
        grad_gains[2],
        grad_up,
        grad_down,
    )


def solution(mesh):
    pixels = P(None, "tile", "sub", None)
    tokens = P(None, "tile", "sub")
    columns, rows, vector = P(None, "sub"), P("sub", None), P("sub")
    return jax.shard_map(
        local,
        mesh=mesh,
        in_specs=(pixels, tokens)
        + (P(),) * 11
        + (vector, columns, columns, columns, rows)
        + (vector, columns, columns, columns, rows)
        + (vector, columns, rows)
        + (pixels, tokens),
        out_specs=(pixels, tokens, pixels, tokens)
        + (P(),) * 8
        + (vector, columns, columns, columns, rows)
        + (vector, columns, columns, columns, rows)
        + (vector, columns, rows),
        check_vma=False,
    )
```

```python
import functools
import math

import jax
import jax.numpy as jnp
from jax import lax
from jax.experimental import pallas as pl
from jax.experimental.pallas import tpu as pltpu
from jax.sharding import PartitionSpec as P

G = 32
HD = 64
POOL = 4
EPSILON = 1e-05
MESH = pl.DeviceIdType.MESH
precise = lax.Precision.HIGHEST
f32 = jnp.float32
bf16 = jnp.bfloat16


def params(cid=None, vmem=56):
    if cid is None:
        return pltpu.CompilerParams(vmem_limit_bytes=vmem << 20)
    return pltpu.CompilerParams(
        collective_id=cid, has_side_effects=True, vmem_limit_bytes=vmem << 20
    )


SHORT = pl.CostEstimate(flops=1, transcendentals=0, bytes_accessed=1)


def in_vmem():
    return pl.BlockSpec(memory_space=pltpu.VMEM)


def anywhere():
    return pl.BlockSpec(memory_space=pl.ANY)


def dma(*shape):
    return pltpu.SemaphoreType.DMA(shape)


def remote(src, dst, send_sem, recv_sem, where):
    return pltpu.make_async_remote_copy(
        src_ref=src,
        dst_ref=dst,
        send_sem=send_sem,
        recv_sem=recv_sem,
        device_id=where,
        device_id_type=MESH,
    )


def arrived(dst, send_sem, recv_sem, me):
    remote(dst, dst, send_sem, recv_sem, me).wait_recv()


def greet(peers):
    barrier = pltpu.get_barrier_semaphore()
    for peer in peers:
        pl.semaphore_signal(barrier, inc=1, device_id=peer, device_id_type=MESH)
    pl.semaphore_wait(barrier, len(peers))


def dot(left, right):
    return jnp.dot(left, right, preferred_element_type=f32)


def round_up(rows, step):
    return (rows + step - 1) // step * step


def chunks_of(rows):
    return max(1, min(4, rows // 16))


def gather_kernel(ns, count, x_ref, o_ref, s1, r1, s2, r2, own):
    far = ns // 2
    t, s = lax.axis_index("tile"), lax.axis_index("sub")
    r, c = s // 2, lax.rem(s, 2)
    me, twin = (t, s), (t, r * 2 + 1 - c)
    size = x_ref.shape[0] // count
    greet([twin] + [(t, lax.rem(r + k, far) * 2 + c) for k in range(1, far)])
    local = pltpu.make_async_copy(x_ref, o_ref.at[s], own)
    local.start()
    copies = []

    def send(src, dst, send_sem, recv_sem, where):
        copies.append(remote(src, dst, send_sem, recv_sem, where))
        copies[-1].start()

    for j in range(count):
        part = pl.ds(j * size, size)
        for k in range(1, far):
            peer = (t, lax.rem(r + k, far) * 2 + c)
            send(x_ref.at[part], o_ref.at[s, part], s1.at[k, j], r1.at[k, j], peer)
    for j in range(count):
        part = pl.ds(j * size, size)
        send(x_ref.at[part], o_ref.at[s, part], s2.at[0, j], r2.at[0, j], twin)
    for j in range(count):
        part = pl.ds(j * size, size)
        for k in range(1, far):
            block = o_ref.at[lax.rem(r + far - k, far) * 2 + c, part]
            arrived(block, s1.at[k, j], r1.at[k, j], me)
            send(block, block, s2.at[k, j], r2.at[k, j], twin)
    for j in range(count):
        part = pl.ds(j * size, size)
        for k in range(far):
            block = o_ref.at[lax.rem(r + far - k, far) * 2 + 1 - c, part]
            arrived(block, s2.at[k, j], r2.at[k, j], me)
    for copy in copies:
        copy.wait_send()
    local.wait()


def gather_sub(x, cid):
    ns = lax.axis_size("sub")
    far, count = ns // 2, chunks_of(x.shape[0])
    return pl.pallas_call(
        functools.partial(gather_kernel, ns, count),
        out_shape=jax.ShapeDtypeStruct((ns,) + x.shape, x.dtype),
        in_specs=[anywhere()],
        out_specs=anywhere(),
        scratch_shapes=[dma(far, count) for _ in range(4)] + [pltpu.SemaphoreType.DMA],
        cost_estimate=SHORT,
        compiler_params=params(cid),
        name="gather_sub",
    )(x)


class Copies:
    def __init__(self):
        self.started = []

    def send(self, src, dst, send_sem, recv_sem, where, when=None):
        copy = remote(src, dst, send_sem, recv_sem, where)
        if when is None:
            copy.start()
        else:
            pl.when(when)(copy.start)
        self.started.append((when, copy))

    def finish(self):
        for when, copy in self.started:
            if when is None:
                copy.wait_send()
            else:
                pl.when(when)(copy.wait_send)


class SubScatter:
    def __init__(self, ns, copies, x, got, stage, last, sems):
        t, s = lax.axis_index("tile"), lax.axis_index("sub")
        self.far, self.copies, self.x, self.s, self.t = ns // 2, copies, x, s, t
        self.got, self.stage, self.last = got, stage, last
        self.r, self.c = s // 2, lax.rem(s, 2)
        self.me, self.twin = (t, s), (t, self.r * 2 + 1 - self.c)
        self.count = chunks_of(x.shape[1])
        self.size = x.shape[1] // self.count
        self.s1, self.r1, self.s2, self.r2 = sems

    @staticmethod
    def scratch(ns, rows, width):
        far, count = ns // 2, chunks_of(rows)
        blocks = [pltpu.VMEM((far, rows, width), bf16) for _ in range(3)]
        return blocks + [dma(far, count) for _ in range(4)]

    def peers(self):
        return [self.twin] + [self.peer(k) for k in range(1, self.far)]

    def peer(self, k):
        return (self.t, lax.rem(self.r + k, self.far) * 2 + self.c)

    def part(self, j):
        return pl.ds(j * self.size, self.size)

    def start(self):
        for k in list(range(1, self.far)) + [0]:
            for j in range(self.count):
                block = self.x.at[lax.rem(self.r + k, self.far) * 2 + 1 - self.c, self.part(j)]
                got = self.got.at[k, self.part(j)]
                self.copies.send(block, got, self.s1.at[k, j], self.r1.at[k, j], self.twin)

    def cross(self):
        for j in range(self.count):
            part = self.part(j)
            for k in range(1, self.far):
                arrived(self.got.at[k, part], self.s1.at[k, j], self.r1.at[k, j], self.me)
                own = self.x[self.peer(k)[1], part].astype(f32)
                self.stage[k, part] = (own + self.got[k, part].astype(f32)).astype(bf16)
                src, dst = self.stage.at[k, part], self.last.at[k, part]
                self.copies.send(src, dst, self.s2.at[k, j], self.r2.at[k, j], self.peer(k))

    def end(self, out):
        for j in range(self.count):
            part = self.part(j)
            arrived(self.got.at[0, part], self.s1.at[0, j], self.r1.at[0, j], self.me)
            total = self.x[self.s, part].astype(f32) + self.got[0, part].astype(f32)
            for k in range(1, self.far):
                arrived(self.last.at[k, part], self.s2.at[k, j], self.r2.at[k, j], self.me)
                total = total + self.last[k, part].astype(f32)
            out[part] = total


def scatter_kernel(ns, x_ref, o_ref, got, stage, last, *sems):
    copies = Copies()
    scatter = SubScatter(ns, copies, x_ref, got, stage, last, sems)
    greet(scatter.peers())
    scatter.start()
    scatter.cross()
    scatter.end(o_ref)
    copies.finish()


def scatter_sub(x, cid):
    ns = lax.axis_size("sub")
    x = x.astype(bf16).reshape(ns, x.shape[0] // ns, x.shape[1])
    block = x.shape[1:]
    return pl.pallas_call(
        functools.partial(scatter_kernel, ns),
        out_shape=jax.ShapeDtypeStruct(block, f32),
        in_specs=[in_vmem()],
        out_specs=in_vmem(),
        scratch_shapes=SubScatter.scratch(ns, *block),
        cost_estimate=SHORT,
        compiler_params=params(cid),
        name="scatter_sub",
    )(x)


def deal(nt, u):
    t, s = lax.axis_index("tile"), lax.axis_index("sub")
    nb = nt // u
    a, b = t // nb, lax.rem(t, nb)
    a_peer = lambda k: (lax.rem(a + k, u) * nb + b, s)
    b_peer = lambda k: (a * nb + lax.rem(b + k, nb), s)
    peers = [a_peer(k) for k in range(1, u)] + [b_peer(k) for k in range(1, nb)]
    return t, s, nb, a, b, a_peer, b_peer, peers


def rows_of(ref, i, size):
    return ref.at[:, pl.ds(pl.multiple_of(i * size, size), size), :]


def lanes_of(ref, i, size):
    return ref.at[:, :, pl.ds(pl.multiple_of(i * size, size), size)]


def qkv_out_kernel(nt, u, q_ref, kv_ref, qo, kvo, qs, qr, ks, kr, fs, fr, own):
    t, s, nb, a, b, a_peer, b_peer, peers = deal(nt, u)
    me = (t, s)
    greet(peers)
    local = [
        pltpu.make_async_copy(rows_of(q_ref, a, HD), qo.at[a], own.at[0]),
        pltpu.make_async_copy(lanes_of(kv_ref, a, 2 * HD), kvo.at[t], own.at[1]),
    ]
    for copy in local:
        copy.start()
    copies = []

    def send(src, dst, send_sem, recv_sem, where):
        copies.append(remote(src, dst, send_sem, recv_sem, where))
        copies[-1].start()

    for k in range(1, u):
        block = lanes_of(kv_ref, lax.rem(a + k, u), 2 * HD)
        send(block, kvo.at[t], ks.at[k], kr.at[k], a_peer(k))
    for m in range(1, nb):
        send(lanes_of(kv_ref, a, 2 * HD), kvo.at[t], fs.at[0, m], fr.at[0, m], b_peer(m))
    for k in range(1, u):
        block = rows_of(q_ref, lax.rem(a + k, u), HD)
        send(block, qo.at[a], qs.at[k], qr.at[k], a_peer(k))
    for k in range(1, u):
        block = kvo.at[lax.rem(a + u - k, u) * nb + b]
        arrived(block, ks.at[k], kr.at[k], me)
        for m in range(1, nb):
            send(block, block, fs.at[k, m], fr.at[k, m], b_peer(m))
    for k in range(1, u):
        arrived(qo.at[lax.rem(a + u - k, u)], qs.at[k], qr.at[k], me)
    for k in range(u):
        for m in range(1, nb):
            block = kvo.at[lax.rem(a + u - k, u) * nb + lax.rem(b + nb - m, nb)]
            arrived(block, fs.at[k, m], fr.at[k, m], me)
    for copy in copies:
        copy.wait_send()
    for copy in local:
        copy.wait()


def qkv_out(q, kv, cid):
    nt = lax.axis_size("tile")
    batch, width, length = q.shape
    u = width // HD
    nb = nt // u
    return pl.pallas_call(
        functools.partial(qkv_out_kernel, nt, u),
        out_shape=(
            jax.ShapeDtypeStruct((u, batch, HD, length), bf16),
            jax.ShapeDtypeStruct((nt, batch, length, 2 * HD), bf16),
        ),
        in_specs=[anywhere()] * 2,
        out_specs=(anywhere(), anywhere()),
        scratch_shapes=[dma(u), dma(u), dma(u), dma(u), dma(u, nb), dma(u, nb), dma(2)],
        cost_estimate=SHORT,
        compiler_params=params(cid),
        name="qkv_out",
    )(q, kv)


def swap_kernel(nt, u, home, x_ref, o_ref, ss, rs, own):
    t, s, nb, a, b, a_peer, b_peer, peers = deal(nt, u)
    greet([a_peer(k) for k in range(1, u)])
    taken = lambda i: x_ref.at[i] if home else rows_of(x_ref, i, HD)
    placed = lambda i: rows_of(o_ref, i, HD) if home else o_ref.at[i]
    local = pltpu.make_async_copy(taken(a), placed(a), own)
    local.start()
    copies = []
    for k in range(1, u):
        copies.append(
            remote(taken(lax.rem(a + k, u)), placed(a), ss.at[k], rs.at[k], a_peer(k))
        )
        copies[-1].start()
    for k in range(1, u):
        arrived(placed(lax.rem(a + u - k, u)), ss.at[k], rs.at[k], (t, s))
    for copy in copies:
        copy.wait_send()
    local.wait()


def swap_heads(x, home, cid):
    nt = lax.axis_size("tile")
    if home:
        u, batch, _, length = x.shape
        shape = (batch, u * HD, length)
    else:
        batch, width, length = x.shape
        u = width // HD
        shape = (u, batch, HD, length)
    if u == 1:
        return x.reshape(shape)
    return pl.pallas_call(
        functools.partial(swap_kernel, nt, u, home),
        out_shape=jax.ShapeDtypeStruct(shape, bf16),
        in_specs=[anywhere()],
        out_specs=anywhere(),
        scratch_shapes=[dma(u), dma(u), pltpu.SemaphoreType.DMA],
        cost_estimate=SHORT,
        compiler_params=params(cid),
        name="swap_heads",
    )(x)


def dqkv_home_kernel(
    nt, ns, u, dq_ref, dkv_ref, beside_ref, mixed_t, grad_attn, cross_mixed, grad_cross, cross_in,
    grad_cq, qo, kvo, beside_out, wide, cq_out, got, stage, qs, qr, fs, fr, ks, kr, own, *scratch
):
    t, s, nb, a, b, a_peer, b_peer, peers = deal(nt, u)
    me = (t, s)
    copies = Copies()
    beside = SubScatter(ns, copies, beside_ref, *scratch[:3], scratch[3:])
    greet(peers + beside.peers())
    order = list(range(1, u)) + [0]
    for k in order:
        for m in range(1, nb):
            block = dkv_ref.at[lax.rem(a + k, u) * nb + lax.rem(b + m, nb)]
            copies.send(block, got.at[m, k], fs.at[k, m], fr.at[k, m], b_peer(m))
    beside.start()
    for k in range(1, u):
        block = dq_ref.at[lax.rem(a + k, u)]
        copies.send(block, rows_of(qo, a, HD), qs.at[k], qr.at[k], a_peer(k))
    local = [pltpu.make_async_copy(dq_ref.at[a], rows_of(qo, a, HD), own.at[0])]
    local[0].start()
    features = mixed_t.shape[0]
    wide[pl.ds(0, features), :] = dot(mixed_t[...], grad_attn[...]).astype(bf16)
    beside.cross()
    turned = cross_mixed[...].T
    wide[pl.ds(features, features), :] = dot(turned, grad_cross[...]).astype(bf16)
    if 2 * features < wide.shape[0]:
        spare = wide.shape[0] - 2 * features
        wide[pl.ds(2 * features, spare), :] = jnp.zeros((spare, wide.shape[1]), bf16)
    for k in order:
        total = dkv_ref[lax.rem(a + k, u) * nb + b].astype(f32)
        for m in range(1, nb):
            arrived(got.at[m, k], fs.at[k, m], fr.at[k, m], me)
            total = total + got[m, k].astype(f32)
        stage[k] = total.astype(bf16)
        if k:
            copies.send(stage.at[k], lanes_of(kvo, a, 2 * HD), ks.at[k], kr.at[k], a_peer(k))
        else:
            local.append(pltpu.make_async_copy(stage.at[0], lanes_of(kvo, a, 2 * HD), own.at[1]))
            local[1].start()
    beside.end(beside_out)
    cq_out[...] = dot(cross_in[...].T, grad_cq[...]).astype(bf16)
    for k in range(1, u):
        i = lax.rem(a + u - k, u)
        arrived(rows_of(qo, i, HD), qs.at[k], qr.at[k], me)
        arrived(lanes_of(kvo, i, 2 * HD), ks.at[k], kr.at[k], me)
    copies.finish()
    for copy in local:
        copy.wait()


def dqkv_home(dq, dkv, beside, mixed_t, grad_attn, cross_mixed, grad_cross, cross_in, grad_cq, cid):
    nt, ns = lax.axis_size("tile"), lax.axis_size("sub")
    u, batch, _, length = dq.shape
    nb = nt // u
    block = (batch, length, 2 * HD)
    beside = beside.reshape(ns, -1, beside.shape[1])
    return pl.pallas_call(
        functools.partial(dqkv_home_kernel, nt, ns, u),
        out_shape=(
            jax.ShapeDtypeStruct((batch, u * HD, length), bf16),
            jax.ShapeDtypeStruct((batch, length, u * 2 * HD), bf16),
            jax.ShapeDtypeStruct(beside.shape[1:], f32),
            jax.ShapeDtypeStruct((round_up(2 * u * HD, 16 * nt), grad_attn.shape[1]), bf16),
            jax.ShapeDtypeStruct((cross_in.shape[1], u * HD), bf16),
        ),
        in_specs=[in_vmem()] * 9,
        out_specs=(anywhere(), anywhere()) + (in_vmem(),) * 3,
        scratch_shapes=[
            pltpu.VMEM((nb, u) + block, bf16),
            pltpu.VMEM((u,) + block, bf16),
            dma(u),
            dma(u),
            dma(u, nb),
            dma(u, nb),
            dma(u),
            dma(u),
            dma(2),
        ]
        + SubScatter.scratch(ns, *beside.shape[1:]),
        cost_estimate=SHORT,
        compiler_params=params(cid),
        name="dqkv_home",
    )(dq, dkv, beside, mixed_t, grad_attn, cross_mixed, grad_cross, cross_in, grad_cq)


def flash_kernel(q_ref, kv_ref, o_ref, of_ref, lse_ref, vt):
    count, length = kv_ref.shape[0], kv_ref.shape[2]

    @pl.when(pl.program_id(1) == 0)
    def _():
        for j in range(count):
            vt[j] = kv_ref[j, 0].T[HD:]

    q = q_ref[0, 0] * 0.125
    padded = jnp.concatenate([q, jnp.zeros_like(q)], axis=0)
    top = jnp.full((1, q.shape[1]), -jnp.inf, f32)
    total = jnp.zeros((1, q.shape[1]), f32)
    mixed = jnp.zeros(q.shape, f32)
    for j in range(count):
        scores = dot(kv_ref[j, 0], padded)
        new = jnp.maximum(top, jnp.max(scores, axis=0, keepdims=True))
        raised = jnp.exp(scores - new)
        scale = jnp.exp(top - new)
        total = total * scale + jnp.sum(raised, axis=0, keepdims=True)
        mixed = mixed * scale + dot(vt[j], raised.astype(bf16))
        top = new
    mixed = mixed / total
    o_ref[0, 0] = mixed.astype(bf16)
    of_ref[0, 0] = mixed
    lse_ref[0, 0] = top + jnp.log(total)


def flash(q, kv):
    u, batch, _, length = q.shape
    nt = kv.shape[0]
    rows = pl.BlockSpec((1, 1, HD, length), lambda b, i: (i, b, 0, 0))
    return pl.pallas_call(
        flash_kernel,
        grid=(batch, u),
        out_shape=(
            jax.ShapeDtypeStruct(q.shape, bf16),
            jax.ShapeDtypeStruct(q.shape, f32),
            jax.ShapeDtypeStruct((u, batch, 1, length), f32),
        ),
        in_specs=[rows, pl.BlockSpec((nt, 1, length, 2 * HD), lambda b, i: (0, b, 0, 0))],
        out_specs=(rows, rows, pl.BlockSpec((1, 1, 1, length), lambda b, i: (i, b, 0, 0))),
        scratch_shapes=[pltpu.VMEM((nt, HD, length), bf16)],
        cost_estimate=SHORT,
        compiler_params=params(),
        name="flash",
    )(q, kv)


def flash_back_kernel(q_ref, d_ref, of_ref, lse_ref, kv_ref, dq_ref, dkv_ref, qd, rows, delta, acc):
    u, length = q_ref.shape[0], q_ref.shape[3]
    j = pl.program_id(1)

    @pl.when(j == 0)
    def _():
        for i in range(u):
            q, d = q_ref[i, 0], d_ref[i, 0]
            zero = jnp.zeros_like(q)
            qd[i, 0] = jnp.concatenate([q * 0.125, zero], axis=0)
            qd[i, 1] = jnp.concatenate([zero, d], axis=0)
            rows[i, 0] = qd[i, 0].T
            rows[i, 1] = qd[i, 1].T
            delta[i] = jnp.sum(d.astype(f32) * of_ref[i, 0], axis=0, keepdims=True)
            acc[i] = jnp.zeros_like(acc[i])

    kv = kv_ref[0, 0]
    kt = kv.T[:HD]
    total = jnp.zeros(kv.shape, f32)
    for i in range(u):
        probs = jnp.exp(dot(kv, qd[i, 0]) - lse_ref[i, 0])
        slope = dot(kv, qd[i, 1])
        grads = (probs * (slope - delta[i])).astype(bf16)
        total = total + dot(probs.astype(bf16), rows[i, 1]) + dot(grads, rows[i, 0])
        acc[i] += dot(kt, grads)
    dkv_ref[0, 0] = total.astype(bf16)

    @pl.when(j == pl.num_programs(1) - 1)
    def _():
        for i in range(u):
            dq_ref[i, 0] = (acc[i] * 0.125).astype(bf16)


def flash_back(q, d, of, lse, kv):
    u, batch, _, length = q.shape
    nt = kv.shape[0]
    whole = pl.BlockSpec((u, 1, HD, length), lambda b, j: (0, b, 0, 0))
    part = pl.BlockSpec((1, 1, length, 2 * HD), lambda b, j: (j, b, 0, 0))
    return pl.pallas_call(
        flash_back_kernel,
        grid=(batch, nt),
        out_shape=(jax.ShapeDtypeStruct(q.shape, bf16), jax.ShapeDtypeStruct(kv.shape, bf16)),
        in_specs=[
            whole,
            whole,
            whole,
            pl.BlockSpec((u, 1, 1, length), lambda b, j: (0, b, 0, 0)),
            part,
        ],
        out_specs=(whole, part),
        scratch_shapes=[
            pltpu.VMEM((u, 2, 2 * HD, length), bf16),
            pltpu.VMEM((u, 2, length, 2 * HD), bf16),
            pltpu.VMEM((u, 1, length), f32),
            pltpu.VMEM((u, HD, length), f32),
        ],
        cost_estimate=SHORT,
        compiler_params=params(),
        name="flash_back",
    )(q, d, of, lse, kv)


class TileSum:
    PARTS = 4

    def __init__(self, nt, copies, x, out, got1, stage, got2, sems):
        t, s = lax.axis_index("tile"), lax.axis_index("sub")
        self.na, self.copies, self.x, self.out = nt // 2, copies, x, out
        self.got1, self.stage, self.got2 = got1, stage, got2
        self.a, self.b, self.s = t // 2, lax.rem(t, 2), s
        self.me, self.pair = (t, s), (self.a * 2 + 1 - self.b, s)
        self.half = x.shape[0] // 2
        self.piece = self.half // 2 // self.PARTS
        (self.s1, self.r1, self.s2, self.r2, self.s3, self.r3, self.s4, self.r4) = sems

    @staticmethod
    def scratch(nt, rows, width):
        return [pltpu.VMEM((rows // 2, width), bf16) for _ in range(3)] + [
            dma(2, TileSum.PARTS) for _ in range(8)
        ]

    def rows(self, b, e, j):
        start = b * self.half + (j * 2 + e) * self.piece
        return pl.ds(pl.multiple_of(start, 16), self.piece)

    def along(self, e):
        up, down = (self.a * 2 + 2 + self.b, self.s), (self.a * 2 - 2 + self.b, self.s)
        return (down, up, self.a) if e else (up, down, self.na - 1 - self.a)

    def start(self):
        for j in range(self.PARTS):
            for e in range(2):
                src, dst = self.x.at[self.rows(1 - self.b, e, j)], self.got1.at[self.rows(0, e, j)]
                self.copies.send(src, dst, self.s1.at[e, j], self.r1.at[e, j], self.pair)

    def steps(self):
        return range(self.PARTS + self.na - 1)

    def step_of(self, way, step, action):
        j = step - way
        pl.when((j >= 0) & (j < self.PARTS))(lambda: action(jnp.clip(j, 0, self.PARTS - 1)))

    def add(self, steps):
        for step in steps:
            for e in range(2):
                self.step_of(self.along(e)[2], step, functools.partial(self.add_one, e))

    def add_one(self, e, j):
        _, after, way = self.along(e)
        here, mine = self.rows(0, e, j), self.rows(self.b, e, j)
        arrived(self.got1.at[here], self.s1.at[e, j], self.r1.at[e, j], self.me)
        both = self.x[mine].astype(f32) + self.got1[here].astype(f32)

        @pl.when(way == 0)
        def _():
            self.stage[here] = both.astype(bf16)

        @pl.when(way > 0)
        def _():
            arrived(self.got2.at[here], self.s2.at[e, j], self.r2.at[e, j], self.me)
            self.stage[here] = (both + self.got2[here].astype(f32)).astype(bf16)

        @pl.when(way < self.na - 1)
        def _():
            src, dst = self.stage.at[here], self.got2.at[here]
            remote(src, dst, self.s2.at[e, j], self.r2.at[e, j], after).start()

        @pl.when(way == self.na - 1)
        def _():
            self.out[mine] = self.stage[here]

    def share(self, steps):
        for step in steps:
            for e in range(2):
                way = self.na - 1 - self.along(e)[2]
                self.step_of(way, step, functools.partial(self.share_one, e))

    def share_one(self, e, j):
        before, _, way = self.along(e)
        block = self.out.at[self.rows(self.b, e, j)]

        @pl.when(way < self.na - 1)
        def _():
            arrived(block, self.s3.at[e, j], self.r3.at[e, j], self.me)

        @pl.when(way > 0)
        def _():
            remote(block, block, self.s3.at[e, j], self.r3.at[e, j], before).start()

        remote(block, block, self.s4.at[e, j], self.r4.at[e, j], self.pair).start()

    def end(self):
        for j in range(self.PARTS):
            for e in range(2):
                block = self.out.at[self.rows(1 - self.b, e, j)]
                arrived(block, self.s4.at[e, j], self.r4.at[e, j], self.me)
        for j in range(self.PARTS):
            for e in range(2):
                before, after, way = self.along(e)
                block = self.out.at[self.rows(self.b, e, j)]
                stage = self.stage.at[self.rows(0, e, j)]
                sent = remote(stage, stage, self.s2.at[e, j], self.r2.at[e, j], after)
                pl.when(way < self.na - 1)(sent.wait_send)
                sent = remote(block, block, self.s3.at[e, j], self.r3.at[e, j], before)
                pl.when(way > 0)(sent.wait_send)
                remote(block, block, self.s4.at[e, j], self.r4.at[e, j], self.pair).wait_send()


class FullSum:
    def __init__(self, nt, ns, copies, x, out, got1, stage, got2, mine, got3, sems):
        t, s = lax.axis_index("tile"), lax.axis_index("sub")
        self.nt, self.far, self.copies, self.x, self.out = nt, ns // 2, copies, x, out
        self.got1, self.stage, self.got2, self.mine, self.got3 = got1, stage, got2, mine, got3
        self.t, self.s, self.r, self.c = t, s, s // 2, lax.rem(s, 2)
        self.me, self.twin = (t, s), (t, self.r * 2 + 1 - self.c)
        self.part = x.shape[0] // ns
        self.piece = self.part // nt
        (self.s1, self.r1, self.s2, self.r2, self.s3, self.r3) = sems[:6]
        (self.s4, self.r4, self.s5, self.r5, self.s6, self.r6) = sems[6:]

    @staticmethod
    def scratch(nt, ns, rows, width):
        far, part = ns // 2, rows // ns
        return (
            [pltpu.VMEM((far, part, width), bf16) for _ in range(3)]
            + [pltpu.VMEM((part, width), bf16), pltpu.VMEM((nt, part // nt, width), bf16)]
            + [dma(far) for _ in range(4)]
            + [dma(nt) for _ in range(4)]
            + [dma(far) for _ in range(4)]
        )

    def rows(self, r, c):
        return pl.ds(pl.multiple_of((c * self.far + r) * self.part, 16), self.part)

    def slot(self, t):
        return pl.ds(pl.multiple_of(t * self.piece, 16), self.piece)

    def other(self, k):
        return lax.rem(self.r + k, self.far)

    def tile(self, k):
        return lax.rem(self.t + k, self.nt)

    def start(self):
        for k in list(range(1, self.far)) + [0]:
            src = self.x.at[self.rows(self.other(k), 1 - self.c)]
            self.copies.send(src, self.got1.at[k], self.s1.at[k], self.r1.at[k], self.twin)

    def cross(self):
        for k in range(1, self.far):
            arrived(self.got1.at[k], self.s1.at[k], self.r1.at[k], self.me)
            own = self.x[self.rows(self.other(k), self.c)].astype(f32)
            self.stage[k] = (own + self.got1[k].astype(f32)).astype(bf16)
            peer = (self.t, self.other(k) * 2 + self.c)
            self.copies.send(self.stage.at[k], self.got2.at[k], self.s2.at[k], self.r2.at[k], peer)

    def spread(self):
        arrived(self.got1.at[0], self.s1.at[0], self.r1.at[0], self.me)
        total = self.x[self.rows(self.r, self.c)].astype(f32) + self.got1[0].astype(f32)
        for k in range(1, self.far):
            arrived(self.got2.at[k], self.s2.at[k], self.r2.at[k], self.me)
            total = total + self.got2[k].astype(f32)
        self.mine[...] = total.astype(bf16)
        for k in range(1, self.nt):
            p = self.tile(k)
            src = self.mine.at[self.slot(p)]
            self.copies.send(src, self.got3.at[k], self.s3.at[k], self.r3.at[k], (p, self.s))

    def place(self, t, r, c):
        start = (c * self.far + r) * self.part + t * self.piece
        return pl.ds(pl.multiple_of(start, 16), self.piece)

    def settle(self):
        total = self.mine[self.slot(self.t)].astype(f32)
        for k in range(1, self.nt):
            arrived(self.got3.at[k], self.s3.at[k], self.r3.at[k], self.me)
            total = total + self.got3[k].astype(f32)
        here = self.place(self.t, self.r, self.c)
        self.out[here] = total.astype(bf16)
        block = self.out.at[here]
        for k in range(1, self.nt):
            self.copies.send(block, block, self.s4.at[k], self.r4.at[k], (self.tile(k), self.s))

    def share(self):
        for k in range(1, self.nt):
            block = self.out.at[self.place(self.tile(self.nt - k), self.r, self.c)]
            arrived(block, self.s4.at[k], self.r4.at[k], self.me)
        block = self.out.at[self.rows(self.r, self.c)]
        for k in range(1, self.far):
            peer = (self.t, self.other(k) * 2 + self.c)
            self.copies.send(block, block, self.s5.at[k], self.r5.at[k], peer)
        self.copies.send(block, block, self.s6.at[0], self.r6.at[0], self.twin)

    def relay(self):
        for k in range(1, self.far):
            block = self.out.at[self.rows(self.other(self.far - k), self.c)]
            arrived(block, self.s5.at[k], self.r5.at[k], self.me)
            self.copies.send(block, block, self.s6.at[k], self.r6.at[k], self.twin)

    def end(self):
        for k in range(self.far):
            block = self.out.at[self.rows(self.other(self.far - k), 1 - self.c)]
            arrived(block, self.s6.at[k], self.r6.at[k], self.me)


AROUND = [(-1, 0), (1, 0), (0, -1), (0, 1), (-1, -1), (-1, 1), (1, -1), (1, 1)]
DIAGONAL = AROUND[4:]


def present(nt, ns, t, s, dt, ds):
    y, x = t + dt, s + ds
    return (y >= 0) & (y < nt) & (x >= 0) & (x < ns)


def greet_all(nt, ns):
    t, s = lax.axis_index("tile"), lax.axis_index("sub")
    barrier = pltpu.get_barrier_semaphore()
    for k in range(1, ns):
        peer = (t, lax.rem(s + k, ns))
        pl.semaphore_signal(barrier, inc=1, device_id=peer, device_id_type=MESH)
    for k in range(1, nt):
        peer = (lax.rem(t + k, nt), s)
        pl.semaphore_signal(barrier, inc=1, device_id=peer, device_id_type=MESH)
    count = ns + nt - 2
    for dt, ds in DIAGONAL:
        there = present(nt, ns, t, s, dt, ds)
        count = count + jnp.where(there, 1, 0)

        @pl.when(there)
        def _():
            pl.semaphore_signal(
                barrier, inc=1, device_id=(t + dt, s + ds), device_id_type=MESH
            )

    pl.semaphore_wait(barrier, count)


def border_copies(nt, ns, src, top, bottom, left, right, ss, rs):
    t, s = lax.axis_index("tile"), lax.axis_index("sub")
    rows, cols = src.shape[0], src.shape[1]
    high, low = pl.ds(0, 2), pl.ds(rows - 2, 2)
    first, last = pl.ds(0, 16), pl.ds(cols - 16, 16)
    inner, before, after = pl.ds(2, rows), pl.ds(0, 2), pl.ds(rows + 2, 2)
    pairs = [
        (src.at[high], bottom),
        (src.at[low], top),
        (src.at[:, first], right.at[inner]),
        (src.at[:, last], left.at[inner]),
        (src.at[high, first], right.at[after]),
        (src.at[high, last], left.at[after]),
        (src.at[low, first], right.at[before]),
        (src.at[low, last], left.at[before]),
    ]
    copies = []
    for i, (dt, ds) in enumerate(AROUND):
        out = present(nt, ns, t, s, dt, ds)
        back = present(nt, ns, t, s, -dt, -ds)
        copies.append((out, back, remote(*pairs[i], ss.at[i], rs.at[i], (t + dt, s + ds))))
    return copies


def begin(copies):
    for out, _, copy in copies:
        pl.when(out)(copy.start)


def finish(copies):
    for out, back, copy in copies:
        pl.when(back)(copy.wait_recv)
        pl.when(out)(copy.wait_send)


def sum_near(nt, ns, value, first, ss, rs):
    t, s = lax.axis_index("tile"), lax.axis_index("sub")
    first[s] = value
    copies = []
    for k in range(1, ns):
        peer = (t, lax.rem(s + k, ns))
        copies.append(remote(first.at[s], first.at[s], ss.at[k], rs.at[s], peer))
        copies[-1].start()
    return copies


def sum_far(nt, ns, first, second, ss1, rs1, ss2, rs2):
    t, s = lax.axis_index("tile"), lax.axis_index("sub")
    for k in range(1, ns):
        p = lax.rem(s + k, ns)
        arrived(first.at[p], ss1.at[k], rs1.at[p], (t, s))
    total = first[0]
    for k in range(1, ns):
        total = total + first[k]
    second[t] = total
    copies = []
    for k in range(1, nt):
        peer = (lax.rem(t + k, nt), s)
        copies.append(remote(second.at[t], second.at[t], ss2.at[k], rs2.at[t], peer))
        copies[-1].start()
    return copies


def sum_end(nt, second, ss2, rs2):
    t, s = lax.axis_index("tile"), lax.axis_index("sub")
    for k in range(1, nt):
        p = lax.rem(t + k, nt)
        arrived(second.at[p], ss2.at[k], rs2.at[p], (t, s))
    total = second[0]
    for k in range(1, nt):
        total = total + second[k]
    return total


def sum_scratch(nt, ns, channels, rows=2):
    return [
        pltpu.VMEM((ns, rows, channels), f32),
        pltpu.VMEM((nt, rows, channels), f32),
        dma(ns),
        dma(ns),
        dma(nt),
        dma(nt),
    ]


def in_groups(values):
    count, channels = values.shape
    per = channels // G
    row = lax.broadcasted_iota(jnp.int32, (channels, channels), 0) // per
    col = lax.broadcasted_iota(jnp.int32, (channels, channels), 1) // per
    same = jnp.where(row == col, 1.0, 0.0).astype(bf16)
    parts, rest = [], values
    for _ in range(3):
        parts.append(rest.astype(bf16))
        rest = rest - parts[-1].astype(f32)
    out = [dot(part, same) for part in parts]
    return out[0] + out[1] + out[2]


def fold(values):
    return jnp.sum(values.reshape(-1, 8, values.shape[-1]), axis=0)


def row_sums(count, channels, pair):
    def step(i, carry):
        first, second = pair(i)
        return carry[0] + fold(first), carry[1] + fold(second)

    zero = jnp.zeros((8, channels), f32)
    first, second = lax.fori_loop(0, count, step, (zero, zero), unroll=2)
    return jnp.concatenate(
        [jnp.sum(first, axis=0, keepdims=True), jnp.sum(second, axis=0, keepdims=True)], axis=0
    )


def sigmoid(values):
    return 1.0 / (1.0 + jnp.exp(-values))


def silu_slope(values):
    sigma = sigmoid(values)
    return sigma * (1.0 + values * (1.0 - sigma))


def block_of(total, step, limit):
    return max(n for n in range(step, limit + 1, step) if total % n == 0)


def put_left_to_right(flat, triple):
    total, channels = triple.shape[0], flat.shape[1]
    size = block_of(total, 16, 256)
    for start in range(0, total, size):
        for j in range(3):
            piece = flat[pl.ds(8 + start + j - 1, size), :]
            triple[pl.ds(start, size), pl.ds(j * channels, channels)] = piece.astype(bf16)


def conv_rows(triple, weight, start, size, pitch, multiply=dot):
    taps = [triple[pl.ds(start + i * pitch, size), :] for i in range(3)]
    return multiply(jnp.concatenate(taps, axis=1), weight)


def dot_t(left, right):
    return lax.dot_general(left, right, (((1,), (1,)), ((), ())), preferred_element_type=f32)


def turned_taps(weight):
    return jnp.concatenate([weight[8 - k] for k in range(9)], axis=1)


def list_length(rows, pitch):
    return 16 + rows * pitch + 16


def fill(flat, rows, cols, row_ok, left_ok, right_ok, body, ending, opening):
    pitch = cols + 16
    channels = flat.shape[1]
    place = lax.broadcasted_iota(jnp.int32, (16, channels), 0)
    flat[pl.ds(0, 8), :] = jnp.zeros((8, channels), f32)
    end = 8 + 16 + rows * pitch
    flat[pl.ds(end, 24), :] = jnp.zeros((24, channels), f32)

    def places(right_good, left_good):
        good = jnp.where(place < 8, jnp.where(right_good, 1, 0), jnp.where(left_good, 1, 0))
        return good > 0

    flat[pl.ds(8, 16), :] = jnp.where(
        places(False, left_ok & row_ok(0)), opening(), 0.0
    )

    def step(i, carry):
        start = pl.multiple_of(24 + i * pitch, 8)
        value = body(i)
        good = jnp.full(value.shape, jnp.where(row_ok(i), 1, 0), jnp.int32)
        flat[pl.ds(start, cols), :] = jnp.where(good > 0, value, 0.0)
        good = places(right_ok & row_ok(i), left_ok & row_ok(i + 1))
        flat[pl.ds(start + cols, 16), :] = jnp.where(good, ending(i), 0.0)
        return carry

    lax.fori_loop(0, rows, step, 0)


def sides(left, right, i):
    place = lax.broadcasted_iota(jnp.int32, right.shape[1:], 0)
    return jnp.where(place < 8, right[i].astype(f32), left[i + 1].astype(f32))


def clear(*refs):
    for ref in refs:
        ref[...] = jnp.zeros_like(ref)


def outer_forward_kernel(
    nt, ns, img, w1, w2, vec, gains, out, pooled, act1_out, act2_out, hidden, stats, gains_out,
    body, left, right, flat, act1, act2, rowsum, border_ss, border_rs, keep, gain_ss, gain_rs, *sums
):
    rows, cols, channels = img.shape
    pitch = cols + 16
    t, s = lax.axis_index("tile"), lax.axis_index("sub")
    sums1, sums2 = sums[:6], sums[6:]
    count = float(nt * ns * rows * cols * (channels // G))
    clear(body, left, right)
    greet_all(nt, ns)
    top, bottom = body.at[pl.ds(0, 2)], body.at[pl.ds(rows + 2, 2)]
    border = border_copies(nt, ns, img, top, bottom, left, right, border_ss, border_rs)
    begin(border)
    pixel = lambda i: img[i].astype(f32)
    local1 = row_sums(rows, channels, lambda i: (pixel(i), pixel(i) * pixel(i)))
    copies = sum_near(nt, ns, local1, sums1[0], sums1[2], sums1[3])
    copies += sum_far(nt, ns, sums1[0], sums1[1], *sums1[2:])
    gains_out[s] = gains[...]
    for k in range(1, ns):
        block, peer = gains_out.at[s], (t, lax.rem(s + k, ns))
        copies.append(remote(block, block, gain_ss.at[k], gain_rs.at[s], peer))
        copies[-1].start()

    def inner(i, carry):
        body[i + 2] = img[i]
        return carry

    lax.fori_loop(0, rows, inner, 0)
    total1 = sum_end(nt, sums1[1], sums1[4], sums1[5])

    def moments(total):
        grouped = in_groups(total) / count
        center = grouped[0:1]
        return center, lax.rsqrt(grouped[1:2] - center * center + EPSILON)

    center1, std1 = moments(total1)
    scale1 = std1 * vec[0:1]
    shift1 = vec[1:2] - center1 * scale1
    finish(border)

    def first_act(values):
        normed = values.astype(f32) * scale1 + shift1
        return normed * sigmoid(normed)

    ok = lambda lift: (
        lambda i: (t * rows + i - lift >= 0) & (t * rows + i - lift < nt * rows)
    )
    fill(
        flat, rows + 4, cols, ok(2), s > 0, s < ns - 1,
        lambda i: first_act(body[i]),
        lambda i: first_act(sides(left, right, i)),
        lambda: first_act(left[0]),
    )
    put_left_to_right(flat, act1)
    saved = [pltpu.make_async_copy(act1, act1_out, keep.at[0])]
    saved[0].start()
    length = list_length(rows + 2, pitch)
    size = block_of(length, 16, 700)
    for start in range(0, length, size):
        hidden[pl.ds(start, size), :] = conv_rows(act1, w1[...], start, size, pitch) + vec[4:5]

    def hidden_row(i):
        return hidden[pl.ds(pl.multiple_of(16 + (i + 1) * pitch, 16), cols), :]

    local2 = row_sums(rows, channels, lambda i: (hidden_row(i), hidden_row(i) * hidden_row(i)))
    copies += sum_near(nt, ns, local2, sums2[0], sums2[2], sums2[3])
    copies += sum_far(nt, ns, sums2[0], sums2[1], *sums2[2:])
    total2 = sum_end(nt, sums2[1], sums2[4], sums2[5])
    center2, std2 = moments(total2)
    scale2 = std2 * vec[2:3]
    shift2 = vec[3:4] - center2 * scale2
    stats[...] = jnp.concatenate(
        [center1, std1, center2, std2, total2, jnp.zeros_like(total2)], axis=0
    )

    def second_act(start, amount):
        normed = hidden[pl.ds(start, amount), :] * scale2 + shift2
        return normed * sigmoid(normed)

    at = lambda i: pl.multiple_of(16 + i * pitch, 16)
    fill(
        flat, rows + 2, cols, ok(1), s > 0, s < ns - 1,
        lambda i: second_act(at(i), cols),
        lambda i: second_act(at(i) + cols, 16),
        lambda: second_act(0, 16),
    )
    put_left_to_right(flat, act2)
    saved.append(pltpu.make_async_copy(act2, act2_out, keep.at[1]))
    saved[1].start()
    lc = cols // POOL
    for start in range(0, rows, 2 * POOL):
        grown = conv_rows(act2, w2[...], 16 + start * pitch, 2 * POOL * pitch, pitch)
        grown = grown.reshape(2 * POOL, pitch, channels)[:, :cols]
        grown = grown + img[pl.ds(start, 2 * POOL)].astype(f32)
        out[pl.ds(start, 2 * POOL)] = grown.astype(bf16)
        for half in range(2):
            added = jnp.sum(grown[half * POOL : (half + 1) * POOL], axis=0)
            means = []
            for n in range(channels // 128):
                rowsum[n] = added[:, n * 128 : (n + 1) * 128]
                mean = rowsum[n, pl.ds(0, lc, stride=POOL), :]
                for k in range(1, POOL):
                    mean = mean + rowsum[n, pl.ds(k, lc, stride=POOL), :]
                means.append(mean * (1.0 / (POOL * POOL)))
            pooled[start // POOL + half] = jnp.concatenate(means, axis=1)
    for k in range(1, ns):
        p = lax.rem(s + k, ns)
        arrived(gains_out.at[p], gain_ss.at[k], gain_rs.at[p], (t, s))
    for copy in copies:
        copy.wait_send()
    for copy in saved:
        copy.wait()


def outer_forward(img, w1, w2, vec, gains, cid):
    nt, ns = lax.axis_size("tile"), lax.axis_size("sub")
    rows, cols, channels = img.shape
    pitch = cols + 16
    long1, long2 = list_length(rows + 4, pitch), list_length(rows + 2, pitch)
    shape = jax.ShapeDtypeStruct
    return pl.pallas_call(
        functools.partial(outer_forward_kernel, nt, ns),
        out_shape=(
            shape(img.shape, bf16),
            shape((rows // POOL, cols // POOL, channels), f32),
            shape((long1, 3 * channels), bf16),
            shape((long2, 3 * channels), bf16),
            shape((long2, channels), f32),
            shape((8, channels), f32),
            shape((ns,) + gains.shape, f32),
        ),
        in_specs=[in_vmem()] * 5,
        out_specs=(in_vmem(),) * 2 + (anywhere(),) * 2 + (in_vmem(),) * 3,
        scratch_shapes=[
            pltpu.VMEM((rows + 4, cols, channels), bf16),
            pltpu.VMEM((rows + 5, 16, channels), bf16),
            pltpu.VMEM((rows + 5, 16, channels), bf16),
            pltpu.VMEM((long1 + 16, channels), f32),
            pltpu.VMEM((long1, 3 * channels), bf16),
            pltpu.VMEM((long2, 3 * channels), bf16),
            pltpu.VMEM((channels // 128, cols, 128), f32),
            dma(8),
            dma(8),
            dma(2),
            dma(ns),
            dma(ns),
        ]
        + sum_scratch(nt, ns, channels) * 2,
        cost_estimate=SHORT,
        compiler_params=params(cid),
        name="outer_forward",
    )(img, w1, w2, vec, gains)


def kernel_grads(triple, grads_t, start, size, pitch, out, between=()):
    for i in range(3):
        rows = triple[pl.ds(start + i * pitch, size), :]
        taps = dot(grads_t[...], rows).T.astype(bf16)
        out[pl.ds(i * taps.shape[0], taps.shape[0]), :] = taps
        for action in between[i : i + 1]:
            action()


def outer_backward_kernel(
    nt, ns, cot, img, w2, w1, vec, stats, hidden, wide, tokens, gains, pooled, lifted, lift_weight,
    attn_in, grad_q_t, grad_kv, grad_cq_w, grad_ck, grad_cv, act1_in, act2_in, outer_grad, tall_out, wide_out, tokens_out, sum2_out, sum1_out, back_out,
    spread, grad2, body, left, right, flat, act1, act2, triple, inner_t, slope, own2, own1, tall,
    border_ss, border_rs, keep, token_ss, token_rs, *scratch
):
    rows, cols, channels = img.shape
    pitch = cols + 16
    lr, lc = rows // POOL, cols // POOL
    t, s = lax.axis_index("tile"), lax.axis_index("sub")
    sums2, sums1, scratch = scratch[:6], scratch[6:12], scratch[12:]
    copies = Copies()
    weights = []
    for x, out in ((wide, wide_out), (tall, tall_out)):
        weights.append(TileSum(nt, copies, x, out, *scratch[:3], scratch[3:11]))
        scratch = scratch[11:]
    second = FullSum(nt, ns, copies, own2, sum2_out, *scratch[:5], scratch[5:17])
    scratch = scratch[17:]
    first = FullSum(nt, ns, copies, own1, sum1_out, *scratch[:5], scratch[5:17])
    count = float(nt * ns * rows * cols * (channels // G))
    held = [
        pltpu.make_async_copy(act2_in, act2, keep.at[0]),
        pltpu.make_async_copy(act1_in, act1, keep.at[1]),
    ]
    for copy in held:
        copy.start()
    clear(body, left, right)
    greet_all(nt, ns)
    weights[0].start()
    width = lifted.shape[1]
    shrunk = dot_t(lifted[...], lift_weight[...]) * (1.0 / (POOL * POOL))

    def widen(i):
        for n in range(channels // 128):
            part = shrunk[i * lc : (i + 1) * lc, n * 128 : (n + 1) * 128]
            for k in range(POOL):
                spread[i, n, pl.ds(k, lc, stride=POOL), :] = part

    for i in range(lr):
        widen(i)

    def outer(i):
        parts = [spread[i // POOL, n] for n in range(channels // 128)]
        return cot[i].astype(f32) + jnp.concatenate(parts, axis=1)

    def round_outer(i, carry):
        value = outer(i).astype(bf16)
        grad2[i] = value
        body[i + 2] = value
        return carry

    lax.fori_loop(0, rows, round_outer, 0)
    top, bottom = body.at[pl.ds(0, 2)], body.at[pl.ds(rows + 2, 2)]
    border = border_copies(nt, ns, grad2, top, bottom, left, right, border_ss, border_rs)
    begin(border)
    tokens_out[s] = tokens[s]
    for k in range(1, ns):
        p = lax.rem(s + k, ns)
        copies.send(tokens.at[p], tokens_out.at[s], token_ss.at[k], token_rs.at[k], (t, p))
    features = grad_q_t.shape[0]
    heads = features // HD
    attn_t = attn_in[...].T
    tall[pl.ds(0, width), :] = dot_t(attn_t, grad_q_t[...]).astype(bf16)
    both = dot(attn_t, grad_kv[...])
    for n in range(2):
        lanes = [both[:, (2 * h + n) * HD : (2 * h + n + 1) * HD] for h in range(heads)]
        part = jnp.concatenate(lanes, axis=1) if heads > 1 else lanes[0]
        tall[pl.ds((1 + n) * width, width), :] = part.astype(bf16)
    used = 3 * width
    for ref in (grad_cq_w, grad_ck, grad_cv):
        tall[pl.ds(used, ref.shape[0]), :] = ref[...]
        used += ref.shape[0]
    if used < tall.shape[0]:
        tall[pl.ds(used, tall.shape[0] - used), :] = jnp.zeros(
            (tall.shape[0] - used, features), bf16
        )
    weights[1].start()
    total = rows * pitch

    def turned(row):
        for start in range(0, rows, 8):
            block = [row(start + k) for k in range(8)]
            gap = jnp.zeros((16, channels), bf16)
            piece = jnp.concatenate([p for b in block for p in (b, gap)], axis=0)
            inner_t[:, pl.ds(start * pitch, 8 * pitch)] = piece.T

    def pad_below(ref, used):
        if used < ref.shape[0]:
            ref[pl.ds(used, ref.shape[0] - used), :] = jnp.zeros(
                (ref.shape[0] - used, channels), bf16
            )

    taps = 9 * channels
    turned(lambda i: grad2[i])
    held[0].wait()
    kernel_grads(act2, inner_t, 16, total, pitch, own2)
    lift_grad = dot(pooled[...].T, lifted[...]).astype(bf16)
    for n in range(width // channels):
        own2[pl.ds(taps + n * channels, channels), :] = lift_grad[
            :, n * channels : (n + 1) * channels
        ]
    pad_below(own2, taps + width)
    second.start()
    finish(border)
    ok = lambda lift_by: (
        lambda i: (t * rows + i - lift_by >= 0) & (t * rows + i - lift_by < nt * rows)
    )
    fill(
        flat, rows + 4, cols, ok(2), s > 0, s < ns - 1,
        lambda i: body[i].astype(f32),
        lambda i: sides(left, right, i),
        lambda: left[0].astype(f32),
    )
    put_left_to_right(flat, triple)
    second.cross()
    center1, std1, center2, std2 = (stats[k : k + 1] for k in range(4))
    gain1, bias1, gain2, bias2 = (vec[k : k + 1] for k in range(4))
    length = list_length(rows + 2, pitch)
    size = block_of(length, 16, 700)
    w2t = turned_taps(w2)
    for start in range(0, length, size):
        hat = (hidden[pl.ds(start, size), :] - center2) * std2
        slope[pl.ds(start, size), :] = conv_rows(
            triple, w2t, start, size, pitch, dot_t
        ) * silu_slope(hat * gain2 + bias2)
        if start == size:
            weights[0].add([0])
    weights[0].add([1])

    at = lambda i: pl.multiple_of(16 + i * pitch, 16)

    def pair2(i):
        place = pl.ds(at(i + 1), cols)
        value = slope[place, :]
        return value, value * ((hidden[place, :] - center2) * std2)

    local2 = jnp.concatenate([row_sums(rows, channels, pair2), gains[...]], axis=0)
    plain = sum_near(nt, ns, local2, sums2[0], sums2[2], sums2[3])
    plain += sum_far(nt, ns, sums2[0], sums2[1], *sums2[2:])
    second.spread()
    steps = weights[0].steps()
    weights[0].add(steps[2:5])
    back2 = sum_end(nt, sums2[1], sums2[4], sums2[5])
    back2, gains_total = back2[:2], back2[2:]
    means2 = in_groups(back2 * gain2) / count

    def grad_hidden(start, amount):
        hat = (hidden[pl.ds(start, amount), :] - center2) * std2
        value = slope[pl.ds(start, amount), :] * gain2 - means2[0:1] - hat * means2[1:2]
        return std2 * value

    fill(
        flat, rows + 2, cols, ok(1), s > 0, s < ns - 1,
        lambda i: grad_hidden(at(i), cols),
        lambda i: grad_hidden(at(i) + cols, 16),
        lambda: grad_hidden(0, 16),
    )
    weights[0].add(steps[5:6])
    turned(lambda i: flat[pl.ds(24 + (i + 1) * pitch, cols), :].astype(bf16))
    held[1].wait()
    between = [
        lambda: weights[0].add(steps[6:]),
        lambda: weights[1].add([0]),
        lambda: weights[1].add([1]),
    ]
    kernel_grads(act1, inner_t, 16 + pitch, total, pitch, own1, between)
    pad_below(own1, taps)
    first.start()
    second.settle()
    put_left_to_right(flat, triple.at[pl.ds(0, length)])
    first.cross()
    hat1 = lambda i: (img[i].astype(f32) - center1) * std1
    step = 2 * POOL
    w1t = turned_taps(w1)
    for start in range(0, rows, step):
        value = conv_rows(triple, w1t, 16 + start * pitch, step * pitch, pitch, dot_t)
        value = value.reshape(step, pitch, channels)[:, :cols]
        hat = (img[pl.ds(start, step)].astype(f32) - center1) * std1
        outer_grad[pl.ds(start, step)] = value * silu_slope(hat * gain1 + bias1)
        if start == step:
            weights[1].add([2])
            weights[0].share([0])
    weights[1].add([3])
    weights[0].share([1])
    local1 = row_sums(rows, channels, lambda i: (outer_grad[i], outer_grad[i] * hat1(i)))
    plain += sum_near(nt, ns, local1, sums1[0], sums1[2], sums1[3])
    first.spread()
    plain += sum_far(nt, ns, sums1[0], sums1[1], *sums1[2:])
    weights[1].add([4])
    weights[0].share([2])
    back1 = sum_end(nt, sums1[1], sums1[4], sums1[5])
    means1 = in_groups(back1 * gain1) / count
    weights[1].add([5])
    weights[0].share([3])

    def last(i, carry):
        value = outer_grad[i] * gain1 - means1[0:1] - hat1(i) * means1[1:2]
        outer_grad[i] = outer(i) + std1 * value
        return carry

    lax.fori_loop(0, rows, last, 0)
    back_out[...] = jnp.concatenate(
        [back1, back2, means2, jnp.zeros_like(means2), gains_total], axis=0
    )
    for step in steps[6:]:
        weights[1].add([step])
    weights[1].share([0])
    first.settle()
    second.share()
    for i, step in enumerate(steps[4:]):
        weights[0].share([step])
        weights[1].share([1 + i])
    first.share()
    second.relay()
    weights[1].share(steps[1 + len(steps[4:]) :])
    for k in range(1, ns):
        block = tokens_out.at[lax.rem(s + ns - k, ns)]
        arrived(block, token_ss.at[k], token_rs.at[k], (t, s))
    first.relay()
    second.end()
    for each in weights:
        each.end()
    first.end()
    copies.finish()
    for copy in plain:
        copy.wait_send()


def outer_backward(
    cot, img, w2, w1, vec, stats, hidden, wide, tokens, gains, pooled, lifted, lift_weight,
    attn_in, grad_q_t, grad_kv, grad_cq_w, grad_ck, grad_cv, act1, act2, cid
):
    nt, ns = lax.axis_size("tile"), lax.axis_size("sub")
    rows, cols, channels = img.shape
    pitch = cols + 16
    long1, long2 = list_length(rows + 4, pitch), list_length(rows + 2, pitch)
    shape = jax.ShapeDtypeStruct
    step = 16 * nt * ns
    width, features = attn_in.shape[1], grad_q_t.shape[0]
    rows2 = round_up(9 * channels + width, step)
    tall = (round_up(4 * width + 2 * grad_ck.shape[0], 16 * nt), features)
    rows1 = round_up(9 * channels, step)
    return pl.pallas_call(
        functools.partial(outer_backward_kernel, nt, ns),
        out_shape=(
            shape(img.shape, f32),
            shape(tall, bf16),
            shape(wide.shape, bf16),
            shape(tokens.shape, bf16),
            shape((rows2, channels), bf16),
            shape((rows1, channels), bf16),
            shape((8 + gains.shape[0], channels), f32),
        ),
        in_specs=[in_vmem()] * 19 + [anywhere()] * 2,
        out_specs=(in_vmem(),) * 7,
        scratch_shapes=[
            pltpu.VMEM((rows // POOL, channels // 128, cols, 128), f32),
            pltpu.VMEM((rows, cols, channels), bf16),
            pltpu.VMEM((rows + 4, cols, channels), bf16),
            pltpu.VMEM((rows + 5, 16, channels), bf16),
            pltpu.VMEM((rows + 5, 16, channels), bf16),
            pltpu.VMEM((long1 + 16, channels), f32),
            pltpu.VMEM((long1, 3 * channels), bf16),
            pltpu.VMEM((long2, 3 * channels), bf16),
            pltpu.VMEM((long1, 3 * channels), bf16),
            pltpu.VMEM((channels, rows * pitch), bf16),
            pltpu.VMEM((long2, channels), f32),
            pltpu.VMEM((rows2, channels), bf16),
            pltpu.VMEM((rows1, channels), bf16),
            pltpu.VMEM(tall, bf16),
            dma(8),
            dma(8),
            dma(2),
            dma(ns),
            dma(ns),
        ]
        + sum_scratch(nt, ns, channels, 2 + gains.shape[0])
        + sum_scratch(nt, ns, channels)
        + TileSum.scratch(nt, *wide.shape)
        + TileSum.scratch(nt, *tall)
        + FullSum.scratch(nt, ns, rows2, channels)
        + FullSum.scratch(nt, ns, rows1, channels),
        cost_estimate=SHORT,
        compiler_params=params(cid, 62),
        name="outer_backward",
    )(
        cot, img, w2, w1, vec, stats, hidden, wide, tokens, gains, pooled, lifted, lift_weight,
        attn_in, grad_q_t, grad_kv, grad_cq_w, grad_ck, grad_cv, act1, act2,
    )


def finish_kernel(text, up, down, *refs):
    q, k, v, cq, ck, cv, o, co, second, first = refs[:10]
    lift, refs = refs[10:-13], refs[-13:]
    for src, dst in zip((q, k, v, cq, o, co, second, first, up, down), refs[:10]):
        dst[...] = src[...].astype(f32)
    turned = text[...].T
    refs[10][...] = dot(turned, ck[...])
    refs[11][...] = dot(turned, cv[...])
    refs[12][...] = jnp.concatenate([part[...].astype(f32) for part in lift], axis=1)


def finish_grads(text, up, down, tall, wide, second, first, taps, text_rows):
    features, width = tall.shape[1], wide.shape[1]
    channels = first.shape[1]
    steps = features // 16
    row = lambda size, lanes, skip=0: pl.BlockSpec((size, lanes), lambda i: (skip + i, 0))
    size = width // steps
    tall_specs = [row(size, features, n * steps) for n in range(4)]
    start = 4 * width // text_rows
    tall_specs += [
        pl.BlockSpec((text_rows, features), lambda i, n=n: (start + n, 0)) for n in range(2)
    ]
    wide_specs = [row(16, width, n * steps) for n in range(2)]
    size = taps // steps
    lift_size = channels // steps
    lift_specs = [
        row(lift_size, channels, taps // lift_size + n * steps) for n in range(width // channels)
    ]
    full = text.shape[1]
    up_specs = [row(w.shape[0] // steps, w.shape[1]) for w in (up, down)]
    in_specs = [pl.BlockSpec((text.shape[0], full // steps), lambda i: (0, i))] + up_specs
    in_specs += tall_specs + wide_specs + [row(size, channels)] * 2 + lift_specs
    shape = lambda *dims: jax.ShapeDtypeStruct(dims, f32)
    return pl.pallas_call(
        finish_kernel,
        grid=(steps,),
        out_shape=(shape(width, features),) * 4
        + (shape(features, width),) * 2
        + (shape(taps, channels),) * 2
        + (shape(*up.shape), shape(*down.shape))
        + (shape(full, features), shape(full, features), shape(channels, width)),
        in_specs=in_specs,
        out_specs=[row(width // steps, features)] * 4
        + [row(16, width)] * 2
        + [row(size, channels)] * 2
        + up_specs
        + [row(full // steps, features)] * 2
        + [row(lift_size, width)],
        cost_estimate=SHORT,
        compiler_params=params(),
        name="finish_grads",
    )(text, up, down, *[tall] * 6, *[wide] * 2, second, first, *[second] * len(lift_specs))


def time_embed(time_steps, channels):
    half_width = channels // 2
    frequency = jnp.exp(
        -math.log(10000.0) * jnp.arange(half_width).astype(f32) / half_width
    )
    angles = time_steps.astype(f32)[:, None] * frequency[None, :]
    return jnp.concatenate([jnp.sin(angles), jnp.cos(angles)], axis=1)


def layer_stats(values, gain):
    width = values.shape[1]
    center = jnp.sum(values, axis=1, keepdims=True) / width
    moved = values - center
    inv_std = lax.rsqrt(jnp.sum(moved * moved, axis=1, keepdims=True) / width + EPSILON)
    normed = moved * inv_std
    return (normed * gain).astype(bf16), normed, inv_std


def layer_back(grad_out, normed, inv_std, gain):
    width = normed.shape[1]
    scaled = grad_out * gain
    mean_grad = jnp.sum(scaled, axis=1, keepdims=True) / width
    mean_cross = jnp.sum(scaled * normed, axis=1, keepdims=True) / width
    grad_in = inv_std * (scaled - mean_grad - normed * mean_cross)
    return grad_in, jnp.sum(grad_out * normed, axis=0)


def gelu_tanh(values):
    return jax.nn.gelu(values, approximate=True)


def weight_grad(inputs, grads):
    return lax.dot_general(inputs, grads, (((0,), (0,)), ((), ())), preferred_element_type=f32)


def cross_scores(queries, keys, text_mask):
    scores = jnp.einsum("sbqhd,bkhd->sbhqk", queries, keys, preferred_element_type=f32)
    return jnp.where(text_mask[None, :, None, None, :], scores * HD ** (-0.5), -1000000000.0)


def local(
    outer_image,
    inner_image,
    text_states,
    time_steps,
    text_lengths,
    first_gain,
    first_bias,
    conv_first,
    time_weight,
    second_gain,
    second_bias,
    conv_second,
    lift_weight,
    attn_gain,
    query_weight,
    key_weight,
    value_weight,
    out_weight,
    cross_gain,
    cross_query,
    cross_key,
    cross_value,
    cross_out,
    mlp_gain,
    up_weight,
    down_weight,
    outer_cotan,
    inner_cotan,
):
    nt, ns = lax.axis_size("tile"), lax.axis_size("sub")
    s = lax.axis_index("sub")
    batch, rows, cols, channels = outer_image.shape
    lr, lc = rows // POOL, cols // POOL
    width = inner_image.shape[2] * ns
    features = inner_image.shape[2]
    heads = features // HD
    own = batch * lr * lc
    length = ns * lr * lc
    pixels = rows * cols * nt * ns


    def whole_tokens(values):
        full = lax.all_gather(values, "sub", axis=2, tiled=True)
        full = full.reshape(batch, lr, ns, lc, width)
        mine = lax.dynamic_index_in_dim(full, s, 2, keepdims=False).reshape(own, width)
        return full, mine

    _, inner_own = whole_tokens(inner_image)
    cotan_full, cotan_own = whole_tokens(inner_cotan)
    cotan_full = jnp.transpose(cotan_full, (2, 0, 1, 3, 4)).reshape(ns * own, width)
    own_gains = jnp.stack([attn_gain, cross_gain, mlp_gain])

    time_act = jax.nn.silu(time_embed(time_steps, channels))
    time_shift = jnp.dot(time_act, time_weight.astype(f32), precision=precise)
    vectors = jnp.zeros((batch, 8, channels), f32)
    for i, vector in enumerate([first_gain, first_bias, second_gain, second_bias]):
        vectors = vectors.at[:, i].set(vector)
    vectors = vectors.at[:, 4].set(time_shift)
    as_rows = lambda w: w.reshape(9 * channels, channels)
    forward = [
        outer_forward(
            outer_image[b],
            as_rows(conv_first),
            as_rows(conv_second),
            vectors[b],
            own_gains,
            20 + b,
        )
        for b in range(batch)
    ]
    outer_out = jnp.stack([f[0] for f in forward])
    gains = jnp.transpose(forward[0][6], (1, 0, 2)).reshape(3, width)
    pooled = jnp.stack([f[1] for f in forward]).astype(bf16).reshape(own, channels)

    stream_in = inner_own.astype(f32) + dot(pooled, lift_weight).astype(bf16).astype(f32)
    attn_low, attn_hat, attn_std = layer_stats(stream_in, gains[0])
    attn_in = gather_sub(attn_low, 2).reshape(ns * own, width)

    def per_sample(values, tokens_last):
        if tokens_last:
            values = values.reshape(-1, ns, batch, lr * lc)
            return jnp.transpose(values, (2, 0, 1, 3)).reshape(batch, -1, length)
        values = values.reshape(ns, batch, lr * lc, -1)
        return jnp.transpose(values, (1, 0, 2, 3)).reshape(batch, length, -1)

    def all_samples(values, tokens_last):
        if tokens_last:
            values = values.reshape(batch, -1, ns, lr * lc)
            return jnp.transpose(values, (1, 2, 0, 3)).reshape(-1, ns * own)
        values = values.reshape(batch, ns, lr * lc, -1)
        return jnp.transpose(values, (1, 0, 2, 3)).reshape(ns * own, -1)

    pair = lambda k, v: jnp.concatenate(
        [k.reshape(-1, heads, HD), v.reshape(-1, heads, HD)], axis=2
    ).reshape(-1, heads * 2 * HD)
    kv_weight = pair(key_weight, value_weight)
    query_t = lax.dot_general(
        query_weight, attn_in, (((0,), (1,)), ((), ())), preferred_element_type=f32
    ).astype(bf16)
    kv = dot(attn_in, kv_weight).astype(bf16)
    head_q, head_kv = qkv_out(per_sample(query_t, True), per_sample(kv, False), 3)
    head_mixed, head_mixed_f, head_lse = flash(head_q, head_kv)
    mixed_t = all_samples(swap_heads(head_mixed, True, 4), True)
    after_attn = stream_in + scatter_sub(weight_grad(mixed_t, out_weight), 5)

    cross_low, cross_hat, cross_std = layer_stats(after_attn, gains[1])
    cross_in = gather_sub(cross_low, 6).reshape(ns * own, width)
    text_split = lambda w: jnp.einsum(
        "bsw,we->bse", text_states, w, preferred_element_type=f32
    ).astype(bf16).reshape(batch, -1, heads, HD)
    cross_k, cross_v = text_split(cross_key), text_split(cross_value)
    text_mask = jnp.arange(text_states.shape[1])[None, :] < text_lengths[:, None]
    split = lambda v: v.reshape(ns, batch, lr * lc, heads, HD)
    cross_q = split(dot(cross_in, cross_query).astype(bf16))
    scores = cross_scores(cross_q, cross_k, text_mask)
    cross_probs = jax.nn.softmax(scores, axis=-1)
    cross_probs_low = cross_probs.astype(bf16)
    cross_mixed = (
        jnp.einsum("sbhqk,bkhd->sbqhd", cross_probs_low, cross_v, preferred_element_type=f32)
        .astype(bf16)
        .reshape(ns * own, features)
    )
    after_cross = after_attn + scatter_sub(dot(cross_mixed, cross_out), 7)

    mlp_low, mlp_hat, mlp_std = layer_stats(after_cross, gains[2])
    mlp_in = gather_sub(mlp_low, 8).reshape(ns * own, width)
    lifted_up = dot(mlp_in, up_weight)
    activated_f, gelu_pull = jax.vjp(gelu_tanh, lifted_up)
    activated = activated_f.astype(bf16)

    grad_act = dot_t(cotan_full, down_weight)
    grad_lift_up = gelu_pull(grad_act)[0].astype(bf16)
    grad_mlp_in = dot_t(grad_lift_up, up_weight).astype(bf16)
    grad_down = weight_grad(activated, cotan_full).astype(bf16)
    grad_up = weight_grad(mlp_in, grad_lift_up).astype(bf16)
    grad_mlp_in, grad_down, grad_up = lax.optimization_barrier(
        (grad_mlp_in, grad_down, grad_up)
    )
    grad_down, grad_up = lax.psum((grad_down, grad_up), "tile")
    grad_mid, grad_mlp_gain = layer_back(
        scatter_sub(grad_mlp_in, 9), mlp_hat, mlp_std, gains[2]
    )
    grad_after_cross = cotan_own.astype(f32) + grad_mid
    grad_cross_full = gather_sub(grad_after_cross.astype(bf16), 10).reshape(ns * own, width)
    grad_cross_mixed = split(dot_t(grad_cross_full, cross_out).astype(bf16))
    grad_cv = jnp.einsum(
        "sbhqk,sbqhd->bkhd", cross_probs_low, grad_cross_mixed, preferred_element_type=f32
    )
    grad_probs = jnp.einsum(
        "sbqhd,bkhd->sbhqk", grad_cross_mixed, cross_v, preferred_element_type=f32
    )
    grad_scores = (
        cross_probs
        * (grad_probs - jnp.sum(cross_probs * grad_probs, axis=-1, keepdims=True))
    ).astype(bf16)
    grad_cq = (
        jnp.einsum("sbhqk,bkhd->sbqhd", grad_scores, cross_k, preferred_element_type=f32)
        * HD ** (-0.5)
    ).astype(bf16).reshape(ns * own, features)
    grad_ck = jnp.einsum(
        "sbhqk,sbqhd->bkhd", grad_scores, cross_q, preferred_element_type=f32
    ) * HD ** (-0.5)
    grad_mid, grad_cross_gain = layer_back(
        scatter_sub(dot_t(grad_cq, cross_query), 11), cross_hat, cross_std, gains[1]
    )
    grad_after_attn = grad_after_cross + grad_mid
    grad_attn_full = gather_sub(grad_after_attn.astype(bf16), 12).reshape(ns * own, width)
    grad_mixed_t = dot_t(out_weight, grad_attn_full).astype(bf16)
    head_d = swap_heads(per_sample(grad_mixed_t, True), False, 13)
    head_dq, head_dkv = flash_back(head_q, head_d, head_mixed_f, head_lse, head_kv)
    down = dot(activated, down_weight).astype(bf16)
    grad_q_t, grad_kv, down_own, wide, grad_cq_w = dqkv_home(
        head_dq,
        head_dkv,
        down,
        mixed_t,
        grad_attn_full,
        cross_mixed,
        grad_cross_full,
        cross_in,
        grad_cq,
        14,
    )
    grad_q_t, grad_kv = all_samples(grad_q_t, True), all_samples(grad_kv, False)
    grad_attn_in = weight_grad(grad_q_t, query_weight.T) + dot_t(grad_kv, kv_weight)
    grad_mid, grad_attn_gain = layer_back(
        scatter_sub(grad_attn_in, 15), attn_hat, attn_std, gains[0]
    )
    inner_grad = grad_after_attn + grad_mid
    grad_lifted = inner_grad.astype(bf16)

    text_rows = grad_ck.shape[0] * grad_ck.shape[1]
    grad_ck, grad_cv = (v.reshape(text_rows, features).astype(bf16) for v in (grad_ck, grad_cv))
    inner_sum = after_cross + down_own
    tokens = jnp.stack([inner_sum.astype(bf16), grad_lifted])
    tokens = tokens.reshape(2, own, ns, features).transpose(2, 0, 1, 3)
    gain_rows = jnp.stack([grad_attn_gain, grad_cross_gain, grad_mlp_gain]).reshape(-1, channels)
    by_tap = lambda w: w.reshape(9, channels, channels)
    backward = []
    for b in range(batch):
        once = (lambda v: v) if b == 0 else jnp.zeros_like
        sample = lambda v: v.reshape(batch, lr * lc, -1)[b]
        backward.append(
            outer_backward(
                outer_cotan[b],
                outer_image[b],
                by_tap(conv_second),
                by_tap(conv_first),
                vectors[b],
                forward[b][5],
                forward[b][4],
                once(wide),
                once(tokens),
                once(gain_rows),
                sample(pooled),
                sample(grad_lifted),
                lift_weight,
                attn_in,
                once(grad_q_t),
                once(grad_kv),
                once(grad_cq_w),
                once(grad_ck),
                once(grad_cv),
                forward[b][2],
                forward[b][3],
                20 + batch + b,
            )
        )
    outer_grad = jnp.stack([f[0] for f in backward])
    tall, wide, tokens = backward[0][1:4]
    tokens = tokens.reshape(ns, 2, batch, lr, lc, features).transpose(1, 2, 3, 0, 4, 5)
    inner_out, inner_grad = tokens.reshape(2, batch, length, features)
    inner_grad = inner_grad.astype(f32)
    if batch > 1:
        sum2, sum1 = (
            sum(f[k].astype(f32) for f in backward).astype(bf16) for k in (4, 5)
        )
    else:
        sum2, sum1 = backward[0][4:6]
    ends = finish_grads(
        text_states.reshape(text_rows, -1),
        grad_up,
        grad_down,
        tall,
        wide,
        sum2,
        sum1,
        9 * channels,
        text_rows,
    )
    grad_q_w, grad_k_w, grad_v_w, grad_cq_w, grad_o_w, grad_co_w = ends[:6]
    grad_conv_second, grad_conv_first = (v.reshape(conv_first.shape) for v in ends[6:8])
    grad_up, grad_down = ends[8:10]
    grad_ck_w, grad_cv_w, grad_lift = ends[10:]
    stats = jnp.stack([f[5] for f in forward])
    back = jnp.stack([f[6] for f in backward])
    grad_gains = back[0, 8:].reshape(3, width)
    center2, std2, hidden_total = stats[:, 2], stats[:, 3], stats[:, 4]
    hat2_total = std2 * (hidden_total - pixels * center2)
    hidden_sum = std2 * (
        second_gain * back[:, 2] - pixels * back[:, 4] - back[:, 5] * hat2_total
    )
    grad_time = jnp.dot(time_act.T, hidden_sum, precision=precise)
    back = jnp.sum(back, axis=0)
    grad_gains = lax.dynamic_slice_in_dim(grad_gains, s * features, features, axis=1)
    return (
        outer_out,
        inner_out,
        outer_grad,
        inner_grad,
        back[1],
        back[0],
        grad_conv_first,
        grad_time,
        back[3],
        back[2],
        grad_conv_second,
        grad_lift,
        grad_gains[0],
        grad_q_w,
        grad_k_w,
        grad_v_w,
        grad_o_w,
        grad_gains[1],
        grad_cq_w,
        grad_ck_w,
        grad_cv_w,
        grad_co_w,
        grad_gains[2],
        grad_up,
        grad_down,
    )


def solution(mesh):
    pixels = P(None, "tile", "sub", None)
    tokens = P(None, "tile", "sub")
    columns, rows, vector = P(None, "sub"), P("sub", None), P("sub")
    return jax.shard_map(
        local,
        mesh=mesh,
        in_specs=(pixels, tokens)
        + (P(),) * 11
        + (vector, columns, columns, columns, rows)
        + (vector, columns, columns, columns, rows)
        + (vector, columns, rows)
        + (pixels, tokens),
        out_specs=(pixels, tokens, pixels, tokens)
        + (P(),) * 8
        + (vector, columns, columns, columns, rows)
        + (vector, columns, columns, columns, rows)
        + (vector, columns, rows),
        check_vma=False,
    )
```

```python
import functools
import math

import jax
import jax.numpy as jnp
from jax import lax
from jax.experimental import pallas as pl
from jax.experimental.pallas import tpu as pltpu
from jax.sharding import PartitionSpec as P

G = 32
HD = 64
POOL = 4
EPSILON = 1e-05
MESH = pl.DeviceIdType.MESH
precise = lax.Precision.HIGHEST
f32 = jnp.float32
bf16 = jnp.bfloat16


def params(cid=None, vmem=56):
    if cid is None:
        return pltpu.CompilerParams(vmem_limit_bytes=vmem << 20)
    return pltpu.CompilerParams(
        collective_id=cid, has_side_effects=True, vmem_limit_bytes=vmem << 20
    )


SHORT = pl.CostEstimate(flops=1, transcendentals=0, bytes_accessed=1)


def in_vmem():
    return pl.BlockSpec(memory_space=pltpu.VMEM)


def anywhere():
    return pl.BlockSpec(memory_space=pl.ANY)


def dma(*shape):
    return pltpu.SemaphoreType.DMA(shape)


def remote(src, dst, send_sem, recv_sem, where):
    return pltpu.make_async_remote_copy(
        src_ref=src,
        dst_ref=dst,
        send_sem=send_sem,
        recv_sem=recv_sem,
        device_id=where,
        device_id_type=MESH,
    )


def arrived(dst, send_sem, recv_sem, me):
    remote(dst, dst, send_sem, recv_sem, me).wait_recv()


def greet(peers):
    barrier = pltpu.get_barrier_semaphore()
    for peer in peers:
        pl.semaphore_signal(barrier, inc=1, device_id=peer, device_id_type=MESH)
    pl.semaphore_wait(barrier, len(peers))


def dot(left, right):
    return jnp.dot(left, right, preferred_element_type=f32)


def dot_t(left, right):
    return lax.dot_general(left, right, (((1,), (1,)), ((), ())), preferred_element_type=f32)


def clear(*refs):
    for ref in refs:
        ref[...] = jnp.zeros_like(ref)


def round_up(rows, step):
    return (rows + step - 1) // step * step


def chunks_of(rows):
    return max(1, min(4, rows // 16))


class Copies:
    def __init__(self):
        self.started = []

    def send(self, src, dst, send_sem, recv_sem, where, when=None):
        copy = remote(src, dst, send_sem, recv_sem, where)
        if when is None:
            copy.start()
        else:
            pl.when(when)(copy.start)
        self.started.append((when, copy))

    def finish(self):
        for when, copy in self.started:
            if when is None:
                copy.wait_send()
            else:
                pl.when(when)(copy.wait_send)


class SubScatter:
    def __init__(self, ns, copies, x, got, stage, last, sems):
        t, s = lax.axis_index("tile"), lax.axis_index("sub")
        self.far, self.copies, self.x, self.s, self.t = ns // 2, copies, x, s, t
        self.got, self.stage, self.last = got, stage, last
        self.r, self.c = s // 2, lax.rem(s, 2)
        self.me, self.twin = (t, s), (t, self.r * 2 + 1 - self.c)
        self.count = chunks_of(x.shape[1])
        self.size = x.shape[1] // self.count
        self.s1, self.r1, self.s2, self.r2 = sems

    @staticmethod
    def scratch(ns, rows, width):
        far, count = ns // 2, chunks_of(rows)
        blocks = [pltpu.VMEM((far, rows, width), bf16) for _ in range(3)]
        return blocks + [dma(far, count) for _ in range(4)]

    def peers(self):
        return [self.twin] + [self.peer(k) for k in range(1, self.far)]

    def peer(self, k):
        return (self.t, lax.rem(self.r + k, self.far) * 2 + self.c)

    def part(self, j):
        return pl.ds(j * self.size, self.size)

    def over(self, k):
        return lax.rem(self.r + k, self.far) * 2 + 1 - self.c

    def start_one(self, k):
        for j in range(self.count):
            block, got = self.x.at[self.over(k), self.part(j)], self.got.at[k, self.part(j)]
            self.copies.send(block, got, self.s1.at[k, j], self.r1.at[k, j], self.twin)

    def start(self):
        for k in list(range(1, self.far)) + [0]:
            self.start_one(k)

    def run(self, make, out, meanwhile=None, then=None):
        for k in range(1, self.far):
            make(self.over(k))
            self.start_one(k)
        for k in range(1, self.far):
            make(self.peer(k)[1])
        make(self.over(0))
        self.start_one(0)
        self.cross()
        make(self.s)
        if meanwhile is not None:
            meanwhile()
        self.end(out, then)

    def cross(self):
        for j in range(self.count):
            part = self.part(j)
            for k in range(1, self.far):
                arrived(self.got.at[k, part], self.s1.at[k, j], self.r1.at[k, j], self.me)
                own = self.x[self.peer(k)[1], part].astype(f32)
                self.stage[k, part] = (own + self.got[k, part].astype(f32)).astype(bf16)
                src, dst = self.stage.at[k, part], self.last.at[k, part]
                self.copies.send(src, dst, self.s2.at[k, j], self.r2.at[k, j], self.peer(k))

    def end(self, out, then=None):
        for j in range(self.count):
            part = self.part(j)
            arrived(self.got.at[0, part], self.s1.at[0, j], self.r1.at[0, j], self.me)
            total = self.x[self.s, part].astype(f32) + self.got[0, part].astype(f32)
            for k in range(1, self.far):
                arrived(self.last.at[k, part], self.s2.at[k, j], self.r2.at[k, j], self.me)
                total = total + self.last[k, part].astype(f32)
            out[part] = total
            if then is not None:
                then(j, part)


class SubGather:
    def __init__(self, ns, copies, out, sems):
        t, s = lax.axis_index("tile"), lax.axis_index("sub")
        self.far, self.copies, self.out, self.t, self.s = ns // 2, copies, out, t, s
        self.r, self.c = s // 2, lax.rem(s, 2)
        self.me, self.twin = (t, s), (t, self.r * 2 + 1 - self.c)
        self.count = chunks_of(out.shape[1])
        self.size = out.shape[1] // self.count
        self.s1, self.r1, self.s2, self.r2 = sems

    @staticmethod
    def scratch(ns, rows):
        return [dma(ns // 2, chunks_of(rows)) for _ in range(4)]

    def block(self, r, c, j):
        return self.out.at[lax.rem(r, self.far) * 2 + c, pl.ds(j * self.size, self.size)]

    def start(self):
        for j in range(self.count):
            self.start_one(j)

    def start_one(self, j):
        block = self.block(self.r, self.c, j)
        for k in range(1, self.far):
            peer = (self.t, lax.rem(self.r + k, self.far) * 2 + self.c)
            self.copies.send(block, block, self.s1.at[k, j], self.r1.at[k, j], peer)
        self.copies.send(block, block, self.s2.at[0, j], self.r2.at[0, j], self.twin)

    def relay(self):
        for j in range(self.count):
            for k in range(1, self.far):
                block = self.block(self.r + self.far - k, self.c, j)
                arrived(block, self.s1.at[k, j], self.r1.at[k, j], self.me)
                self.copies.send(block, block, self.s2.at[k, j], self.r2.at[k, j], self.twin)

    def end(self):
        for j in range(self.count):
            for k in range(self.far):
                block = self.block(self.r + self.far - k, 1 - self.c, j)
                arrived(block, self.s2.at[k, j], self.r2.at[k, j], self.me)


def sub_peers(ns):
    t, s = lax.axis_index("tile"), lax.axis_index("sub")
    far, r, c = ns // 2, s // 2, lax.rem(s, 2)
    return [(t, r * 2 + 1 - c)] + [(t, lax.rem(r + k, far) * 2 + c) for k in range(1, far)]


def layer_hat(values):
    width = values.shape[1]
    center = jnp.sum(values, axis=1, keepdims=True) / width
    moved = values - center
    inv_std = lax.rsqrt(jnp.sum(moved * moved, axis=1, keepdims=True) / width + EPSILON)
    return moved * inv_std, inv_std


def layer_back(grad_out, values, gain):
    width = values.shape[1]
    hat, inv_std = layer_hat(values)
    scaled = grad_out * gain
    mean_grad = jnp.sum(scaled, axis=1, keepdims=True) / width
    mean_cross = jnp.sum(scaled * hat, axis=1, keepdims=True) / width
    grad_in = inv_std * (scaled - mean_grad - hat * mean_cross)
    return grad_in, jnp.sum(grad_out * hat, axis=0, keepdims=True)


def enter_kernel(ns, inner, pooled, lift, gain, stream, gathered, *sems):
    copies = Copies()
    gather = SubGather(ns, copies, gathered, sems)
    value = inner[...].astype(f32) + dot(pooled[...], lift[...]).astype(bf16).astype(f32)
    stream[...] = value
    gathered[gather.s] = (layer_hat(value)[0] * gain[...]).astype(bf16)
    greet(sub_peers(ns))
    gather.start()
    gather.relay()
    gather.end()
    copies.finish()


def attn_out_kernel(ns, mixed_t, weight, before, gain, after, gathered, turned, *scratch):
    copies = Copies()
    own = before.shape[0]
    scatter = SubScatter(ns, copies, *scratch[:4], scratch[4:8])
    gather = SubGather(ns, copies, gathered, scratch[8:])
    turned[...] = mixed_t[...].T

    def make(p):
        rows = turned[pl.ds(pl.multiple_of(p * own, 16), own), :]
        scatter.x[p] = dot(rows, weight[...]).astype(bf16)

    greet(sub_peers(ns))

    def normalize(j, part):
        value = before[part, :] + after[part, :]
        after[part, :] = value
        gathered[gather.s, part] = (layer_hat(value)[0] * gain[...]).astype(bf16)
        gather.start_one(j)

    scatter.run(make, after, None, normalize)
    gather.relay()
    gather.end()
    copies.finish()


def head_of(values, h):
    return values[:, h * HD : (h + 1) * HD]


def head_probs(queries, keys, mask, h):
    scores = dot_t(head_of(queries, h), head_of(keys, h)) * HD ** (-0.5)
    scores = jnp.where(mask > 0.5, scores, -1000000000.0)
    raised = jnp.exp(scores - jnp.max(scores, axis=1, keepdims=True))
    return raised / jnp.sum(raised, axis=1, keepdims=True)


def side_by_side(parts):
    return jnp.concatenate(parts, axis=1) if len(parts) > 1 else parts[0]


def cross_kernel(
    ns, cross_in, wq, ck, cv, mask, wo, before, gain, after, gathered, queries, mixed, *scratch
):
    copies = Copies()
    scatter = SubScatter(ns, copies, *scratch[:4], scratch[4:8])
    gather = SubGather(ns, copies, gathered, scratch[8:])
    heads = wq.shape[1] // HD

    def make(p):
        q = dot(cross_in[p], wq[...]).astype(bf16)
        queries[p] = q
        keys, values, masked = ck[...], cv[...], mask[...]
        parts = [
            dot(head_probs(q, keys, masked, h).astype(bf16), head_of(values, h))
            for h in range(heads)
        ]
        mixed[p] = side_by_side(parts).astype(bf16)
        scatter.x[p] = dot(mixed[p], wo[...]).astype(bf16)

    greet(sub_peers(ns))

    def normalize(j, part):
        value = before[part, :] + after[part, :]
        after[part, :] = value
        gathered[gather.s, part] = (layer_hat(value)[0] * gain[...]).astype(bf16)
        gather.start_one(j)

    scatter.run(make, after, None, normalize)
    gather.relay()
    gather.end()
    copies.finish()


def mlp_kernel(
    ns, mlp_in, cotan, w_up, w_down, before, gain,
    grad, gathered, gain_grad, down, up_grad, down_grad, activated, grad_up, *scratch
):
    copies = Copies()
    scatter = SubScatter(ns, copies, *scratch[:4], scratch[4:8])
    gather = SubGather(ns, copies, gathered, scratch[8:])
    own = before.shape[0]
    rate = math.sqrt(2.0 / math.pi)

    def make(p):
        up = dot(mlp_in[p], w_up[...])
        square = up * up
        bent = jnp.tanh(rate * (up + 0.044715 * up * square))
        rows = pl.ds(pl.multiple_of(p * own, 16), own)
        activated[rows, :] = (0.5 * up * (1.0 + bent)).astype(bf16)
        slope = 0.5 * (1.0 + bent) + 0.5 * up * (1.0 - bent * bent) * (
            rate * (1.0 + 3.0 * 0.044715 * square)
        )
        turned = (slope * dot_t(cotan[p], w_down[...])).astype(bf16)
        grad_up[rows, :] = turned
        scatter.x[p] = dot_t(turned, w_up[...]).astype(bf16)

    greet(sub_peers(ns))
    whole = lambda ref: ref[...].reshape(ns * own, ref.shape[2])

    def meanwhile():
        up_grad[...] = dot(whole(mlp_in).T, grad_up[...]).astype(bf16)

    gain_grad[...] = jnp.zeros_like(gain_grad)

    def normalize(j, part):
        back, gains = layer_back(grad[part, :], before[part, :], gain[...])
        gain_grad[...] += gains
        value = cotan[gather.s, part].astype(f32) + back
        grad[part, :] = value
        gathered[gather.s, part] = value.astype(bf16)
        gather.start_one(j)

    scatter.run(make, grad, meanwhile, normalize)
    down_grad[...] = dot(activated[...].T, whole(cotan)).astype(bf16)
    gather.relay()
    down[...] = dot(activated[...], w_down[...]).astype(bf16)
    gather.end()
    copies.finish()


def cross_back_kernel(
    ns, incoming, wo, queries, ck, cv, mask, wq, before, gain, residual, cross_in, mixed,
    grad, gathered, gain_grad, dk_out, dv_out, weights, dk, dv, dq, *scratch
):
    copies = Copies()
    scatter = SubScatter(ns, copies, *scratch[:4], scratch[4:8])
    gather = SubGather(ns, copies, gathered, scratch[8:])
    heads = wq.shape[1] // HD
    own = before.shape[0]
    clear(dk, dv)

    def make(p):
        grad_mixed = dot_t(incoming[p], wo[...]).astype(bf16)
        q, keys, values, masked = queries[p], ck[...], cv[...], mask[...]
        parts_q, parts_k, parts_v = [], [], []
        for h in range(heads):
            probs = head_probs(q, keys, masked, h)
            slope = dot_t(head_of(grad_mixed, h), head_of(values, h))
            lean = probs * (slope - jnp.sum(probs * slope, axis=1, keepdims=True))
            lean = lean.astype(bf16)
            parts_q.append(dot(lean, head_of(keys, h)))
            parts_k.append(dot(lean.T, head_of(q, h)))
            parts_v.append(dot(probs.astype(bf16).T, head_of(grad_mixed, h)))
        part = (side_by_side(parts_q) * HD ** (-0.5)).astype(bf16)
        dq[pl.ds(pl.multiple_of(p * own, 16), own), :] = part
        dk[...] += side_by_side(parts_k)
        dv[...] += side_by_side(parts_v)
        scatter.x[p] = dot_t(part, wq[...]).astype(bf16)

    greet(sub_peers(ns))
    whole = lambda ref: ref[...].reshape(ns * own, ref.shape[2])

    def meanwhile():
        weights[0] = dot(whole(mixed).T, whole(incoming)).astype(bf16)
        dk_out[...] = (dk[...] * HD ** (-0.5)).astype(bf16)
        dv_out[...] = dv[...].astype(bf16)

    gain_grad[...] = jnp.zeros_like(gain_grad)

    def normalize(j, part):
        back, gains = layer_back(grad[part, :], before[part, :], gain[...])
        gain_grad[...] += gains
        value = residual[part, :] + back
        grad[part, :] = value
        gathered[gather.s, part] = value.astype(bf16)
        gather.start_one(j)

    scatter.run(make, grad, meanwhile, normalize)
    weights[1] = dot(dq[...].T, whole(cross_in)).astype(bf16)
    gather.relay()
    gather.end()
    copies.finish()


def attn_back_kernel(
    ns, dq_t, dkv, wq, wkv, before, gain, residual, out, gain_grad, turned, *scratch
):
    copies = Copies()
    scatter = SubScatter(ns, copies, *scratch[1:5], scratch[5:9])
    total = scratch[0]
    own = before.shape[0]
    turned[...] = dq_t[...].T

    def make(p):
        rows = pl.ds(pl.multiple_of(p * own, 16), own)
        value = dot_t(turned[rows, :], wq[...]) + dot_t(dkv[rows, :], wkv[...])
        scatter.x[p] = value.astype(bf16)

    greet(sub_peers(ns))
    scatter.run(make, total)
    back, gains = layer_back(total[...], before[...], gain[...])
    gain_grad[...] = gains
    out[...] = (residual[...] + back).astype(bf16)
    copies.finish()


def chain_call(kernel, name, cid, outs, args, extra, scatter, gather=True):
    ns = lax.axis_size("sub")
    own, width = outs[0][0]
    scratch = list(extra)
    if scatter:
        scratch += [pltpu.VMEM((ns, own, width), bf16)] + SubScatter.scratch(ns, own, width)
    if gather:
        scratch += SubGather.scratch(ns, own)
    return pl.pallas_call(
        functools.partial(kernel, ns),
        out_shape=tuple(jax.ShapeDtypeStruct(*out) for out in outs),
        in_specs=[in_vmem()] * len(args),
        out_specs=(in_vmem(),) * len(outs),
        scratch_shapes=scratch,
        cost_estimate=SHORT,
        compiler_params=params(cid),
        name=name,
    )(*args)


def deal(nt, u):
    t, s = lax.axis_index("tile"), lax.axis_index("sub")
    nb = nt // u
    a, b = t // nb, lax.rem(t, nb)
    a_peer = lambda k: (lax.rem(a + k, u) * nb + b, s)
    b_peer = lambda k: (a * nb + lax.rem(b + k, nb), s)
    peers = [a_peer(k) for k in range(1, u)] + [b_peer(k) for k in range(1, nb)]
    return t, s, nb, a, b, a_peer, b_peer, peers


def rows_of(ref, i, size):
    return ref.at[:, pl.ds(pl.multiple_of(i * size, size), size), :]


def lanes_of(ref, i, size):
    return ref.at[:, :, pl.ds(pl.multiple_of(i * size, size), size)]


def swap_kernel(nt, u, home, x_ref, o_ref, ss, rs, own):
    t, s, nb, a, b, a_peer, b_peer, peers = deal(nt, u)
    greet([a_peer(k) for k in range(1, u)])
    taken = lambda i: x_ref.at[i] if home else rows_of(x_ref, i, HD)
    placed = lambda i: rows_of(o_ref, i, HD) if home else o_ref.at[i]
    local = pltpu.make_async_copy(taken(a), placed(a), own)
    local.start()
    copies = []
    for k in range(1, u):
        copies.append(
            remote(taken(lax.rem(a + k, u)), placed(a), ss.at[k], rs.at[k], a_peer(k))
        )
        copies[-1].start()
    for k in range(1, u):
        arrived(placed(lax.rem(a + u - k, u)), ss.at[k], rs.at[k], (t, s))
    for copy in copies:
        copy.wait_send()
    local.wait()


def swap_heads(x, home, cid):
    nt = lax.axis_size("tile")
    if home:
        u, batch, _, length = x.shape
        shape = (batch, u * HD, length)
    else:
        batch, width, length = x.shape
        u = width // HD
        shape = (u, batch, HD, length)
    if u == 1:
        return x.reshape(shape)
    return pl.pallas_call(
        functools.partial(swap_kernel, nt, u, home),
        out_shape=jax.ShapeDtypeStruct(shape, bf16),
        in_specs=[anywhere()],
        out_specs=anywhere(),
        scratch_shapes=[dma(u), dma(u), pltpu.SemaphoreType.DMA],
        cost_estimate=SHORT,
        compiler_params=params(cid),
        name="swap_heads",
    )(x)


def dqkv_home_kernel(
    nt, ns, u, dq_ref, dkv_ref, beside_ref, qo, kvo, beside_out, got, stage, qs, qr, fs, fr, ks, kr, own, *scratch
):
    t, s, nb, a, b, a_peer, b_peer, peers = deal(nt, u)
    me = (t, s)
    copies = Copies()
    beside = SubScatter(ns, copies, beside_ref, *scratch[:3], scratch[3:])
    greet(peers + beside.peers())
    order = list(range(1, u)) + [0]
    for k in order:
        for m in range(1, nb):
            block = dkv_ref.at[lax.rem(a + k, u) * nb + lax.rem(b + m, nb)]
            copies.send(block, got.at[m, k], fs.at[k, m], fr.at[k, m], b_peer(m))
    beside.start()
    for k in range(1, u):
        block = dq_ref.at[lax.rem(a + k, u)]
        copies.send(block, rows_of(qo, a, HD), qs.at[k], qr.at[k], a_peer(k))
    local = [pltpu.make_async_copy(dq_ref.at[a], rows_of(qo, a, HD), own.at[0])]
    local[0].start()
    beside.cross()
    for k in order:
        total = dkv_ref[lax.rem(a + k, u) * nb + b].astype(f32)
        for m in range(1, nb):
            arrived(got.at[m, k], fs.at[k, m], fr.at[k, m], me)
            total = total + got[m, k].astype(f32)
        stage[k] = total.astype(bf16)
        if k:
            copies.send(stage.at[k], lanes_of(kvo, a, 2 * HD), ks.at[k], kr.at[k], a_peer(k))
        else:
            local.append(pltpu.make_async_copy(stage.at[0], lanes_of(kvo, a, 2 * HD), own.at[1]))
            local[1].start()
    beside.end(beside_out)
    for k in range(1, u):
        i = lax.rem(a + u - k, u)
        arrived(rows_of(qo, i, HD), qs.at[k], qr.at[k], me)
        arrived(lanes_of(kvo, i, 2 * HD), ks.at[k], kr.at[k], me)
    copies.finish()
    for copy in local:
        copy.wait()


def dqkv_home(dq, dkv, beside, cid):
    nt, ns = lax.axis_size("tile"), lax.axis_size("sub")
    u, batch, _, length = dq.shape
    nb = nt // u
    block = (batch, length, 2 * HD)
    beside = beside.reshape(ns, -1, beside.shape[1])
    return pl.pallas_call(
        functools.partial(dqkv_home_kernel, nt, ns, u),
        out_shape=(
            jax.ShapeDtypeStruct((batch, u * HD, length), bf16),
            jax.ShapeDtypeStruct((batch, length, u * 2 * HD), bf16),
            jax.ShapeDtypeStruct(beside.shape[1:], f32),
        ),
        in_specs=[in_vmem()] * 3,
        out_specs=(anywhere(), anywhere(), in_vmem()),
        scratch_shapes=[
            pltpu.VMEM((nb, u) + block, bf16),
            pltpu.VMEM((u,) + block, bf16),
            dma(u),
            dma(u),
            dma(u, nb),
            dma(u, nb),
            dma(u),
            dma(u),
            dma(2),
        ]
        + SubScatter.scratch(ns, *beside.shape[1:]),
        cost_estimate=SHORT,
        compiler_params=params(cid),
        name="dqkv_home",
    )(dq, dkv, beside)


class TileSum:
    PARTS = 4

    def __init__(self, nt, x, out, buffers, add_sems, share_sems):
        t, s = lax.axis_index("tile"), lax.axis_index("sub")
        self.na, self.x, self.out = nt // 2, x, out
        self.a, self.b, self.s = t // 2, lax.rem(t, 2), s
        self.me, self.pair = (t, s), (self.a * 2 + 1 - self.b, s)
        self.half = out.shape[0] // 2
        self.piece = self.half // 2 // self.PARTS
        if add_sems:
            self.got1, self.stage, self.got2 = buffers
            self.s1, self.r1, self.s2, self.r2 = add_sems
        if share_sems:
            self.s3, self.r3, self.s4, self.r4 = share_sems

    @staticmethod
    def buffers(rows, width):
        return [pltpu.VMEM((rows // 2, width), bf16) for _ in range(3)]

    @staticmethod
    def sems():
        return [dma(2, TileSum.PARTS) for _ in range(4)]

    def rows(self, b, e, j):
        start = b * self.half + (j * 2 + e) * self.piece
        return pl.ds(pl.multiple_of(start, 16), self.piece)

    def along(self, e):
        up, down = (self.a * 2 + 2 + self.b, self.s), (self.a * 2 - 2 + self.b, self.s)
        return (down, up, self.a) if e else (up, down, self.na - 1 - self.a)

    def start(self):
        for j in range(self.PARTS):
            for e in range(2):
                self.to_pair(e, j).start()

    def to_pair(self, e, j):
        src, dst = self.x.at[self.rows(1 - self.b, e, j)], self.got1.at[self.rows(0, e, j)]
        return remote(src, dst, self.s1.at[e, j], self.r1.at[e, j], self.pair)

    def steps(self):
        return range(self.PARTS + self.na - 1)

    def step_of(self, way, step, action):
        j = step - way
        pl.when((j >= 0) & (j < self.PARTS))(lambda: action(jnp.clip(j, 0, self.PARTS - 1)))

    def add(self, steps):
        for step in steps:
            for e in range(2):
                self.step_of(self.along(e)[2], step, functools.partial(self.add_one, e))

    def add_one(self, e, j):
        _, after, way = self.along(e)
        here, mine = self.rows(0, e, j), self.rows(self.b, e, j)
        arrived(self.got1.at[here], self.s1.at[e, j], self.r1.at[e, j], self.me)
        both = self.x[mine].astype(f32) + self.got1[here].astype(f32)

        @pl.when(way == 0)
        def _():
            self.stage[here] = both.astype(bf16)

        @pl.when(way > 0)
        def _():
            arrived(self.got2.at[here], self.s2.at[e, j], self.r2.at[e, j], self.me)
            self.stage[here] = (both + self.got2[here].astype(f32)).astype(bf16)

        @pl.when(way < self.na - 1)
        def _():
            src, dst = self.stage.at[here], self.got2.at[here]
            remote(src, dst, self.s2.at[e, j], self.r2.at[e, j], after).start()

        @pl.when(way == self.na - 1)
        def _():
            self.out[mine] = self.stage[here]

    def share(self, steps):
        for step in steps:
            for e in range(2):
                way = self.na - 1 - self.along(e)[2]
                self.step_of(way, step, functools.partial(self.share_one, e))

    def share_one(self, e, j):
        before, _, way = self.along(e)
        block = self.out.at[self.rows(self.b, e, j)]

        @pl.when(way < self.na - 1)
        def _():
            arrived(block, self.s3.at[e, j], self.r3.at[e, j], self.me)

        @pl.when(way > 0)
        def _():
            remote(block, block, self.s3.at[e, j], self.r3.at[e, j], before).start()

        remote(block, block, self.s4.at[e, j], self.r4.at[e, j], self.pair).start()

    def end_add(self):
        for j in range(self.PARTS):
            for e in range(2):
                _, after, way = self.along(e)
                self.to_pair(e, j).wait_send()
                stage = self.stage.at[self.rows(0, e, j)]
                sent = remote(stage, stage, self.s2.at[e, j], self.r2.at[e, j], after)
                pl.when(way < self.na - 1)(sent.wait_send)

    def end_share(self):
        for j in range(self.PARTS):
            for e in range(2):
                block = self.out.at[self.rows(1 - self.b, e, j)]
                arrived(block, self.s4.at[e, j], self.r4.at[e, j], self.me)
        for j in range(self.PARTS):
            for e in range(2):
                before, _, way = self.along(e)
                block = self.out.at[self.rows(self.b, e, j)]
                sent = remote(block, block, self.s3.at[e, j], self.r3.at[e, j], before)
                pl.when(way > 0)(sent.wait_send)
                remote(block, block, self.s4.at[e, j], self.r4.at[e, j], self.pair).wait_send()


def self_attention_kernel(
    nt, u, q_ref, kv_ref, home, qo, kvo, mixed_out, lse, top, total, mixed, low,
    qs, qr, ks, kr, fs, fr, hs, hr, own
):
    t, s, nb, a, b, a_peer, b_peer, peers = deal(nt, u)
    me = (t, s)
    batch, length = q_ref.shape[0], q_ref.shape[2]
    copies = Copies()
    qo[a] = q_ref[:, pl.ds(pl.multiple_of(a * HD, HD), HD), :]
    local = [pltpu.make_async_copy(lanes_of(kv_ref, a, 2 * HD), kvo.at[t], own.at[0])]
    local[0].start()
    greet(peers)
    for k in range(1, u):
        block = rows_of(q_ref, lax.rem(a + k, u), HD)
        copies.send(block, qo.at[a], qs.at[k], qr.at[k], a_peer(k))
    for k in range(1, u):
        block = lanes_of(kv_ref, lax.rem(a + k, u), 2 * HD)
        copies.send(block, kvo.at[t], ks.at[k], kr.at[k], a_peer(k))
    for m in range(1, nb):
        block = lanes_of(kv_ref, a, 2 * HD)
        copies.send(block, kvo.at[t], fs.at[0, m], fr.at[0, m], b_peer(m))
    clear(total, mixed)
    top[...] = jnp.full(top.shape, -jnp.inf, f32)

    def take(tile, i, n):
        q = qo[i, n] * 0.125
        padded = jnp.concatenate([q, jnp.zeros_like(q)], axis=0)
        keys = kvo[tile, n]
        scores = dot(keys, padded)
        new = jnp.maximum(top[i, n], jnp.max(scores, axis=0, keepdims=True))
        raised = jnp.exp(scores - new)
        scale = jnp.exp(top[i, n] - new)
        added = dot(keys.T[HD:], raised.astype(bf16))
        return (
            new,
            total[i, n] * scale + jnp.sum(raised, axis=0, keepdims=True),
            mixed[i, n] * scale + added,
        )

    def take_all(tile):
        for n in range(batch):
            for i in range(u):
                top[i, n], total[i, n], mixed[i, n] = take(tile, i, n)

    def tile_of(k, m):
        return lax.rem(a + u - k, u) * nb + lax.rem(b + nb - m, nb)

    for k in range(1, u):
        arrived(qo.at[lax.rem(a + u - k, u)], qs.at[k], qr.at[k], me)
    local[0].wait()
    order = [(0, 0)] + [(k, 0) for k in range(1, u)]
    order += [(k, m) for k in range(u) for m in range(1, nb)]
    for k, m in order[:-1]:
        tile = tile_of(k, m)
        if m:
            arrived(kvo.at[tile], fs.at[k, m], fr.at[k, m], me)
        elif k:
            arrived(kvo.at[tile], ks.at[k], kr.at[k], me)
            for n in range(1, nb):
                block = kvo.at[tile]
                copies.send(block, block, fs.at[k, n], fr.at[k, n], b_peer(n))
        take_all(tile)
    k, m = order[-1]
    tile = tile_of(k, m)
    if m:
        arrived(kvo.at[tile], fs.at[k, m], fr.at[k, m], me)
    elif k:
        arrived(kvo.at[tile], ks.at[k], kr.at[k], me)
    for k in list(range(1, u)) + [0]:
        i = lax.rem(a + k, u)
        for n in range(batch):
            peak, weight, value = take(tile, i, n)
            value = value / weight
            mixed_out[i, n] = value
            low[i, n] = value.astype(bf16)
            lse[i, n] = peak + jnp.log(weight)
        if k:
            copies.send(low.at[i], rows_of(home, a, HD), hs.at[k], hr.at[k], a_peer(k))
        else:
            local.append(pltpu.make_async_copy(low.at[i], rows_of(home, a, HD), own.at[1]))
            local[1].start()
    for k in range(1, u):
        arrived(rows_of(home, lax.rem(a + u - k, u), HD), hs.at[k], hr.at[k], me)
    local[1].wait()
    copies.finish()


def self_attention(q, kv, cid):
    nt = lax.axis_size("tile")
    batch, width, length = q.shape
    u = width // HD
    nb = nt // u
    shape = jax.ShapeDtypeStruct
    dealt = (u, batch, HD, length)
    return pl.pallas_call(
        functools.partial(self_attention_kernel, nt, u),
        out_shape=(
            shape(q.shape, bf16),
            shape(dealt, bf16),
            shape((nt, batch, length, 2 * HD), bf16),
            shape(dealt, f32),
            shape((u, batch, 1, length), f32),
        ),
        in_specs=[in_vmem()] * 2,
        out_specs=(in_vmem(),) * 5,
        scratch_shapes=[
            pltpu.VMEM((u, batch, 1, length), f32),
            pltpu.VMEM((u, batch, 1, length), f32),
            pltpu.VMEM(dealt, f32),
            pltpu.VMEM(dealt, bf16),
        ]
        + [dma(u) for _ in range(4)]
        + [dma(u, nb) for _ in range(2)]
        + [dma(u) for _ in range(2)]
        + [dma(2)],
        cost_estimate=SHORT,
        compiler_params=params(cid),
        name="self_attention",
    )(q, kv)


def flash_back_kernel(
    nt, q_ref, d_ref, of_ref, lse_ref, kv_ref, mixed_t, grad_attn, early_ref, dq_ref, dkv_ref, early,
    qd, rows, delta, acc, mine, *scratch
):
    u, length = q_ref.shape[0], q_ref.shape[3]
    j = pl.program_id(1)
    last_j = pl.num_programs(1) - 1
    at = lambda step: (pl.program_id(0) == 0) & (j == step)
    sums = TileSum(nt, mine, early, scratch[:3], scratch[3:], None)
    steps = list(sums.steps())

    @pl.when(at(0))
    def _():
        features = mixed_t.shape[0]
        mine[pl.ds(0, features), :] = dot(mixed_t[...], grad_attn[...]).astype(bf16)
        mine[pl.ds(features, 2 * features), :] = early_ref[...]
        spare = mine.shape[0] - 3 * features
        if spare:
            mine[pl.ds(3 * features, spare), :] = jnp.zeros((spare, mine.shape[1]), bf16)
        clear(early)
        a, b, s = sums.a, sums.b, sums.s
        barrier = pltpu.get_barrier_semaphore()
        up, down = a + 1 < nt // 2, a > 0
        for there, peer in ((up, (a + 1) * 2 + b), (down, (a - 1) * 2 + b)):

            @pl.when(there)
            def _():
                pl.semaphore_signal(barrier, inc=1, device_id=(peer, s), device_id_type=MESH)

        pl.semaphore_signal(barrier, inc=1, device_id=sums.pair, device_id_type=MESH)
        pl.semaphore_wait(barrier, 1 + jnp.where(up, 1, 0) + jnp.where(down, 1, 0))
        sums.start()

    @pl.when(j == 0)
    def _():
        for i in range(u):
            q, d = q_ref[i, 0], d_ref[i, 0]
            zero = jnp.zeros_like(q)
            qd[i, 0] = jnp.concatenate([q * 0.125, zero], axis=0)
            qd[i, 1] = jnp.concatenate([zero, d], axis=0)
            rows[i, 0] = qd[i, 0].T
            rows[i, 1] = qd[i, 1].T
            delta[i] = jnp.sum(d.astype(f32) * of_ref[i, 0], axis=0, keepdims=True)
            acc[i] = jnp.zeros_like(acc[i])

    kv = kv_ref[0, 0]
    kt = kv.T[:HD]
    total = jnp.zeros(kv.shape, f32)
    for i in range(u):
        probs = jnp.exp(dot(kv, qd[i, 0]) - lse_ref[i, 0])
        slope = dot(kv, qd[i, 1])
        grads = (probs * (slope - delta[i])).astype(bf16)
        total = total + dot(probs.astype(bf16), rows[i, 1]) + dot(grads, rows[i, 0])
        acc[i] += dot(kt, grads)
    dkv_ref[0, 0] = total.astype(bf16)

    for before in range(3, 0, -1):

        @pl.when(at(last_j - before))
        def _():
            sums.add(steps[2 * (3 - before) : 2 * (4 - before)])

    @pl.when(at(last_j))
    def _():
        sums.add(steps[6:])
        sums.end_add()

    @pl.when(j == last_j)
    def _():
        for i in range(u):
            dq_ref[i, 0] = (acc[i] * 0.125).astype(bf16)


def flash_back(q, d, of, lse, kv, mixed_t, grad_attn, early, cid):
    u, batch, _, length = q.shape
    nt = kv.shape[0]
    whole = pl.BlockSpec((u, 1, HD, length), lambda b, j: (0, b, 0, 0))
    part = pl.BlockSpec((1, 1, length, 2 * HD), lambda b, j: (j, b, 0, 0))
    sums = (round_up(3 * u * HD, 16 * nt), grad_attn.shape[1])
    return pl.pallas_call(
        functools.partial(flash_back_kernel, nt),
        grid=(batch, nt),
        out_shape=(
            jax.ShapeDtypeStruct(q.shape, bf16),
            jax.ShapeDtypeStruct(kv.shape, bf16),
            jax.ShapeDtypeStruct(sums, bf16),
        ),
        in_specs=[
            whole,
            whole,
            whole,
            pl.BlockSpec((u, 1, 1, length), lambda b, j: (0, b, 0, 0)),
            part,
        ]
        + [in_vmem()] * 3,
        out_specs=(whole, part, in_vmem()),
        scratch_shapes=[
            pltpu.VMEM((u, 2, 2 * HD, length), bf16),
            pltpu.VMEM((u, 2, length, 2 * HD), bf16),
            pltpu.VMEM((u, 1, length), f32),
            pltpu.VMEM((u, HD, length), f32),
            pltpu.VMEM(sums, bf16),
        ]
        + TileSum.buffers(*sums)
        + TileSum.sems(),
        cost_estimate=SHORT,
        compiler_params=params(cid),
        name="flash_back",
    )(q, d, of, lse, kv, mixed_t, grad_attn, early)


class Nothing:
    def __getattr__(self, name):
        return lambda *args: None


class FullSum:
    def __init__(self, nt, ns, copies, x, out, got1, stage, got2, mine, got3, sems):
        t, s = lax.axis_index("tile"), lax.axis_index("sub")
        self.nt, self.far, self.copies, self.x, self.out = nt, ns // 2, copies, x, out
        self.got1, self.stage, self.got2, self.mine, self.got3 = got1, stage, got2, mine, got3
        self.t, self.s, self.r, self.c = t, s, s // 2, lax.rem(s, 2)
        self.me, self.twin = (t, s), (t, self.r * 2 + 1 - self.c)
        self.part = x.shape[0] // ns
        self.piece = self.part // nt
        (self.s1, self.r1, self.s2, self.r2, self.s3, self.r3) = sems[:6]
        (self.s4, self.r4, self.s5, self.r5, self.s6, self.r6) = sems[6:]

    @staticmethod
    def scratch(nt, ns, rows, width):
        far, part = ns // 2, rows // ns
        return (
            [pltpu.VMEM((far, part, width), bf16) for _ in range(3)]
            + [pltpu.VMEM((part, width), bf16), pltpu.VMEM((nt, part // nt, width), bf16)]
            + [dma(far) for _ in range(4)]
            + [dma(nt) for _ in range(4)]
            + [dma(far) for _ in range(4)]
        )

    def rows(self, r, c):
        return pl.ds(pl.multiple_of((c * self.far + r) * self.part, 16), self.part)

    def slot(self, t):
        return pl.ds(pl.multiple_of(t * self.piece, 16), self.piece)

    def other(self, k):
        return lax.rem(self.r + k, self.far)

    def tile(self, k):
        return lax.rem(self.t + k, self.nt)

    def start(self):
        for k in list(range(1, self.far)) + [0]:
            src = self.x.at[self.rows(self.other(k), 1 - self.c)]
            self.copies.send(src, self.got1.at[k], self.s1.at[k], self.r1.at[k], self.twin)

    def cross(self):
        for k in range(1, self.far):
            arrived(self.got1.at[k], self.s1.at[k], self.r1.at[k], self.me)
            own = self.x[self.rows(self.other(k), self.c)].astype(f32)
            self.stage[k] = (own + self.got1[k].astype(f32)).astype(bf16)
            peer = (self.t, self.other(k) * 2 + self.c)
            self.copies.send(self.stage.at[k], self.got2.at[k], self.s2.at[k], self.r2.at[k], peer)

    def spread(self):
        arrived(self.got1.at[0], self.s1.at[0], self.r1.at[0], self.me)
        total = self.x[self.rows(self.r, self.c)].astype(f32) + self.got1[0].astype(f32)
        for k in range(1, self.far):
            arrived(self.got2.at[k], self.s2.at[k], self.r2.at[k], self.me)
            total = total + self.got2[k].astype(f32)
        self.mine[...] = total.astype(bf16)
        for k in range(1, self.nt):
            p = self.tile(k)
            src = self.mine.at[self.slot(p)]
            self.copies.send(src, self.got3.at[k], self.s3.at[k], self.r3.at[k], (p, self.s))

    def place(self, t, r, c):
        start = (c * self.far + r) * self.part + t * self.piece
        return pl.ds(pl.multiple_of(start, 16), self.piece)

    def settle(self):
        total = self.mine[self.slot(self.t)].astype(f32)
        for k in range(1, self.nt):
            arrived(self.got3.at[k], self.s3.at[k], self.r3.at[k], self.me)
            total = total + self.got3[k].astype(f32)
        here = self.place(self.t, self.r, self.c)
        self.out[here] = total.astype(bf16)
        block = self.out.at[here]
        for k in range(1, self.nt):
            self.copies.send(block, block, self.s4.at[k], self.r4.at[k], (self.tile(k), self.s))

    def share(self):
        for k in range(1, self.nt):
            block = self.out.at[self.place(self.tile(self.nt - k), self.r, self.c)]
            arrived(block, self.s4.at[k], self.r4.at[k], self.me)
        block = self.out.at[self.rows(self.r, self.c)]
        for k in range(1, self.far):
            peer = (self.t, self.other(k) * 2 + self.c)
            self.copies.send(block, block, self.s5.at[k], self.r5.at[k], peer)
        self.copies.send(block, block, self.s6.at[0], self.r6.at[0], self.twin)

    def relay(self):
        for k in range(1, self.far):
            block = self.out.at[self.rows(self.other(self.far - k), self.c)]
            arrived(block, self.s5.at[k], self.r5.at[k], self.me)
            self.copies.send(block, block, self.s6.at[k], self.r6.at[k], self.twin)

    def end(self):
        for k in range(self.far):
            block = self.out.at[self.rows(self.other(self.far - k), 1 - self.c)]
            arrived(block, self.s6.at[k], self.r6.at[k], self.me)


AROUND = [(-1, 0), (1, 0), (0, -1), (0, 1), (-1, -1), (-1, 1), (1, -1), (1, 1)]
DIAGONAL = AROUND[4:]


def present(nt, ns, t, s, dt, ds):
    y, x = t + dt, s + ds
    return (y >= 0) & (y < nt) & (x >= 0) & (x < ns)


def greet_all(nt, ns):
    t, s = lax.axis_index("tile"), lax.axis_index("sub")
    barrier = pltpu.get_barrier_semaphore()
    for k in range(1, ns):
        peer = (t, lax.rem(s + k, ns))
        pl.semaphore_signal(barrier, inc=1, device_id=peer, device_id_type=MESH)
    for k in range(1, nt):
        peer = (lax.rem(t + k, nt), s)
        pl.semaphore_signal(barrier, inc=1, device_id=peer, device_id_type=MESH)
    count = ns + nt - 2
    for dt, ds in DIAGONAL:
        there = present(nt, ns, t, s, dt, ds)
        count = count + jnp.where(there, 1, 0)

        @pl.when(there)
        def _():
            pl.semaphore_signal(
                barrier, inc=1, device_id=(t + dt, s + ds), device_id_type=MESH
            )

    pl.semaphore_wait(barrier, count)


def border_copies(nt, ns, src, top, bottom, left, right, ss, rs):
    t, s = lax.axis_index("tile"), lax.axis_index("sub")
    rows, cols = src.shape[0], src.shape[1]
    high, low = pl.ds(0, 2), pl.ds(rows - 2, 2)
    first, last = pl.ds(0, 16), pl.ds(cols - 16, 16)
    inner, before, after = pl.ds(2, rows), pl.ds(0, 2), pl.ds(rows + 2, 2)
    pairs = [
        (src.at[high], bottom),
        (src.at[low], top),
        (src.at[:, first], right.at[inner]),
        (src.at[:, last], left.at[inner]),
        (src.at[high, first], right.at[after]),
        (src.at[high, last], left.at[after]),
        (src.at[low, first], right.at[before]),
        (src.at[low, last], left.at[before]),
    ]
    copies = []
    for i, (dt, ds) in enumerate(AROUND):
        out = present(nt, ns, t, s, dt, ds)
        back = present(nt, ns, t, s, -dt, -ds)
        copies.append((out, back, remote(*pairs[i], ss.at[i], rs.at[i], (t + dt, s + ds))))
    return copies


def begin(copies):
    for out, _, copy in copies:
        pl.when(out)(copy.start)


def finish(copies):
    for out, back, copy in copies:
        pl.when(back)(copy.wait_recv)
        pl.when(out)(copy.wait_send)


def sum_near(nt, ns, value, first, ss, rs):
    t, s = lax.axis_index("tile"), lax.axis_index("sub")
    first[s] = value
    copies = []
    for k in range(1, ns):
        peer = (t, lax.rem(s + k, ns))
        copies.append(remote(first.at[s], first.at[s], ss.at[k], rs.at[s], peer))
        copies[-1].start()
    return copies


def sum_far(nt, ns, first, second, ss1, rs1, ss2, rs2):
    t, s = lax.axis_index("tile"), lax.axis_index("sub")
    for k in range(1, ns):
        p = lax.rem(s + k, ns)
        arrived(first.at[p], ss1.at[k], rs1.at[p], (t, s))
    total = first[0]
    for k in range(1, ns):
        total = total + first[k]
    second[t] = total
    copies = []
    for k in range(1, nt):
        peer = (lax.rem(t + k, nt), s)
        copies.append(remote(second.at[t], second.at[t], ss2.at[k], rs2.at[t], peer))
        copies[-1].start()
    return copies


def sum_end(nt, second, ss2, rs2):
    t, s = lax.axis_index("tile"), lax.axis_index("sub")
    for k in range(1, nt):
        p = lax.rem(t + k, nt)
        arrived(second.at[p], ss2.at[k], rs2.at[p], (t, s))
    total = second[0]
    for k in range(1, nt):
        total = total + second[k]
    return total


def sum_scratch(nt, ns, channels, rows=2):
    return [
        pltpu.VMEM((ns, rows, channels), f32),
        pltpu.VMEM((nt, rows, channels), f32),
        dma(ns),
        dma(ns),
        dma(nt),
        dma(nt),
    ]


def in_groups(values):
    count, channels = values.shape
    per = channels // G
    row = lax.broadcasted_iota(jnp.int32, (channels, channels), 0) // per
    col = lax.broadcasted_iota(jnp.int32, (channels, channels), 1) // per
    same = jnp.where(row == col, 1.0, 0.0).astype(bf16)
    parts, rest = [], values
    for _ in range(3):
        parts.append(rest.astype(bf16))
        rest = rest - parts[-1].astype(f32)
    out = [dot(part, same) for part in parts]
    return out[0] + out[1] + out[2]


def fold(values):
    return jnp.sum(values.reshape(-1, 8, values.shape[-1]), axis=0)


def row_sums(count, channels, pair):
    def step(i, carry):
        first, second = pair(i)
        return carry[0] + fold(first), carry[1] + fold(second)

    zero = jnp.zeros((8, channels), f32)
    first, second = lax.fori_loop(0, count, step, (zero, zero), unroll=2)
    return jnp.concatenate(
        [jnp.sum(first, axis=0, keepdims=True), jnp.sum(second, axis=0, keepdims=True)], axis=0
    )


def sigmoid(values):
    return 1.0 / (1.0 + jnp.exp(-values))


def silu_slope(values):
    sigma = sigmoid(values)
    return sigma * (1.0 + values * (1.0 - sigma))


def block_of(total, step, limit):
    return max(n for n in range(step, limit + 1, step) if total % n == 0)


def put_left_to_right(flat, triple):
    total, channels = triple.shape[0], flat.shape[1]
    size = block_of(total, 16, 256)
    for start in range(0, total, size):
        for j in range(3):
            piece = flat[pl.ds(8 + start + j - 1, size), :]
            triple[pl.ds(start, size), pl.ds(j * channels, channels)] = piece.astype(bf16)


def conv_rows(triple, weight, start, size, pitch, multiply=dot):
    taps = [triple[pl.ds(start + i * pitch, size), :] for i in range(3)]
    return multiply(jnp.concatenate(taps, axis=1), weight)


def turned_taps(weight):
    return jnp.concatenate([weight[8 - k] for k in range(9)], axis=1)


def list_length(rows, pitch):
    return 16 + rows * pitch + 16


def fill(flat, rows, cols, row_ok, left_ok, right_ok, body, ending, opening):
    pitch = cols + 16
    channels = flat.shape[1]
    place = lax.broadcasted_iota(jnp.int32, (16, channels), 0)
    flat[pl.ds(0, 8), :] = jnp.zeros((8, channels), f32)
    end = 8 + 16 + rows * pitch
    flat[pl.ds(end, 24), :] = jnp.zeros((24, channels), f32)

    def places(right_good, left_good):
        good = jnp.where(place < 8, jnp.where(right_good, 1, 0), jnp.where(left_good, 1, 0))
        return good > 0

    flat[pl.ds(8, 16), :] = jnp.where(
        places(False, left_ok & row_ok(0)), opening(), 0.0
    )

    def step(i, carry):
        start = pl.multiple_of(24 + i * pitch, 8)
        value = body(i)
        good = jnp.full(value.shape, jnp.where(row_ok(i), 1, 0), jnp.int32)
        flat[pl.ds(start, cols), :] = jnp.where(good > 0, value, 0.0)
        good = places(right_ok & row_ok(i), left_ok & row_ok(i + 1))
        flat[pl.ds(start + cols, 16), :] = jnp.where(good, ending(i), 0.0)
        return carry

    lax.fori_loop(0, rows, step, 0)


def sides(left, right, i):
    place = lax.broadcasted_iota(jnp.int32, right.shape[1:], 0)
    return jnp.where(place < 8, right[i].astype(f32), left[i + 1].astype(f32))


def outer_forward_kernel(
    nt, ns, img, w1, w2, vec, gains, out, pooled, act1_out, act2_out, hidden, stats, gains_out,
    body, left, right, flat, act1, act2, rowsum, border_ss, border_rs, keep, gain_ss, gain_rs, *sums
):
    rows, cols, channels = img.shape
    pitch = cols + 16
    t, s = lax.axis_index("tile"), lax.axis_index("sub")
    sums1, sums2 = sums[:6], sums[6:]
    count = float(nt * ns * rows * cols * (channels // G))
    clear(body, left, right)
    greet_all(nt, ns)
    top, bottom = body.at[pl.ds(0, 2)], body.at[pl.ds(rows + 2, 2)]
    border = border_copies(nt, ns, img, top, bottom, left, right, border_ss, border_rs)
    begin(border)
    pixel = lambda i: img[i].astype(f32)
    local1 = row_sums(rows, channels, lambda i: (pixel(i), pixel(i) * pixel(i)))
    copies = sum_near(nt, ns, local1, sums1[0], sums1[2], sums1[3])
    copies += sum_far(nt, ns, sums1[0], sums1[1], *sums1[2:])
    gains_out[s] = gains[...]
    for k in range(1, ns):
        block, peer = gains_out.at[s], (t, lax.rem(s + k, ns))
        copies.append(remote(block, block, gain_ss.at[k], gain_rs.at[s], peer))
        copies[-1].start()

    def inner(i, carry):
        body[i + 2] = img[i]
        return carry

    lax.fori_loop(0, rows, inner, 0)
    total1 = sum_end(nt, sums1[1], sums1[4], sums1[5])

    def moments(total):
        grouped = in_groups(total) / count
        center = grouped[0:1]
        return center, lax.rsqrt(grouped[1:2] - center * center + EPSILON)

    center1, std1 = moments(total1)
    scale1 = std1 * vec[0:1]
    shift1 = vec[1:2] - center1 * scale1
    finish(border)

    def first_act(values):
        normed = values.astype(f32) * scale1 + shift1
        return normed * sigmoid(normed)

    ok = lambda lift: (
        lambda i: (t * rows + i - lift >= 0) & (t * rows + i - lift < nt * rows)
    )
    fill(
        flat, rows + 4, cols, ok(2), s > 0, s < ns - 1,
        lambda i: first_act(body[i]),
        lambda i: first_act(sides(left, right, i)),
        lambda: first_act(left[0]),
    )
    put_left_to_right(flat, act1)
    saved = [pltpu.make_async_copy(act1, act1_out, keep.at[0])]
    saved[0].start()
    length = list_length(rows + 2, pitch)
    size = block_of(length, 16, 700)
    for start in range(0, length, size):
        hidden[pl.ds(start, size), :] = conv_rows(act1, w1[...], start, size, pitch) + vec[4:5]

    def hidden_row(i):
        return hidden[pl.ds(pl.multiple_of(16 + (i + 1) * pitch, 16), cols), :]

    local2 = row_sums(rows, channels, lambda i: (hidden_row(i), hidden_row(i) * hidden_row(i)))
    copies += sum_near(nt, ns, local2, sums2[0], sums2[2], sums2[3])
    copies += sum_far(nt, ns, sums2[0], sums2[1], *sums2[2:])
    total2 = sum_end(nt, sums2[1], sums2[4], sums2[5])
    center2, std2 = moments(total2)
    scale2 = std2 * vec[2:3]
    shift2 = vec[3:4] - center2 * scale2
    stats[...] = jnp.concatenate(
        [center1, std1, center2, std2, total2, jnp.zeros_like(total2)], axis=0
    )

    def second_act(start, amount):
        normed = hidden[pl.ds(start, amount), :] * scale2 + shift2
        return normed * sigmoid(normed)

    at = lambda i: pl.multiple_of(16 + i * pitch, 16)
    fill(
        flat, rows + 2, cols, ok(1), s > 0, s < ns - 1,
        lambda i: second_act(at(i), cols),
        lambda i: second_act(at(i) + cols, 16),
        lambda: second_act(0, 16),
    )
    put_left_to_right(flat, act2)
    saved.append(pltpu.make_async_copy(act2, act2_out, keep.at[1]))
    saved[1].start()
    lc = cols // POOL
    for start in range(0, rows, 2 * POOL):
        grown = conv_rows(act2, w2[...], 16 + start * pitch, 2 * POOL * pitch, pitch)
        grown = grown.reshape(2 * POOL, pitch, channels)[:, :cols]
        grown = grown + img[pl.ds(start, 2 * POOL)].astype(f32)
        out[pl.ds(start, 2 * POOL)] = grown.astype(bf16)
        for half in range(2):
            added = jnp.sum(grown[half * POOL : (half + 1) * POOL], axis=0)
            means = []
            for n in range(channels // 128):
                rowsum[n] = added[:, n * 128 : (n + 1) * 128]
                mean = rowsum[n, pl.ds(0, lc, stride=POOL), :]
                for k in range(1, POOL):
                    mean = mean + rowsum[n, pl.ds(k, lc, stride=POOL), :]
                means.append(mean * (1.0 / (POOL * POOL)))
            place = pl.ds((start // POOL + half) * lc, lc)
            pooled[place, :] = jnp.concatenate(means, axis=1).astype(bf16)
    for k in range(1, ns):
        p = lax.rem(s + k, ns)
        arrived(gains_out.at[p], gain_ss.at[k], gain_rs.at[p], (t, s))
    for copy in copies:
        copy.wait_send()
    for copy in saved:
        copy.wait()


def outer_forward(img, w1, w2, vec, gains, cid):
    nt, ns = lax.axis_size("tile"), lax.axis_size("sub")
    rows, cols, channels = img.shape
    pitch = cols + 16
    long1, long2 = list_length(rows + 4, pitch), list_length(rows + 2, pitch)
    shape = jax.ShapeDtypeStruct
    return pl.pallas_call(
        functools.partial(outer_forward_kernel, nt, ns),
        out_shape=(
            shape(img.shape, bf16),
            shape((rows // POOL * (cols // POOL), channels), bf16),
            shape((long1, 3 * channels), bf16),
            shape((long2, 3 * channels), bf16),
            shape((long2, channels), f32),
            shape((8, channels), f32),
            shape((ns,) + gains.shape, f32),
        ),
        in_specs=[in_vmem()] * 5,
        out_specs=(in_vmem(),) * 2 + (anywhere(),) * 2 + (in_vmem(),) * 3,
        scratch_shapes=[
            pltpu.VMEM((rows + 4, cols, channels), bf16),
            pltpu.VMEM((rows + 5, 16, channels), bf16),
            pltpu.VMEM((rows + 5, 16, channels), bf16),
            pltpu.VMEM((long1 + 16, channels), f32),
            pltpu.VMEM((long1, 3 * channels), bf16),
            pltpu.VMEM((long2, 3 * channels), bf16),
            pltpu.VMEM((channels // 128, cols, 128), f32),
            dma(8),
            dma(8),
            dma(2),
            dma(ns),
            dma(ns),
        ]
        + sum_scratch(nt, ns, channels) * 2,
        cost_estimate=SHORT,
        compiler_params=params(cid),
        name="outer_forward",
    )(img, w1, w2, vec, gains)


def kernel_grads(triple, grads_t, start, size, pitch, out, between=()):
    for i in range(3):
        rows = triple[pl.ds(start + i * pitch, size), :]
        taps = dot(grads_t[...], rows).T.astype(bf16)
        out[pl.ds(i * taps.shape[0], taps.shape[0]), :] = taps
        for action in between[i : i + 1]:
            action()


def outer_backward_kernel(
    nt, ns, cut, cot, img, w2, w1, vec, stats, hidden, wide, tokens, gains, pooled, lifted, lift_weight,
    attn_in, grad_q_t, grad_kv, grad_ck, grad_cv, act1_in, act2_in, outer_grad, tall_out, wide_out, tokens_out, sum2_out, sum1_out, back_out,
    spread, grad2, body, left, right, flat, act1, act2, triple, inner_t, slope, own2, own1, tall,
    border_ss, border_rs, keep, token_ss, token_rs, *scratch
):
    rows, cols, channels = img.shape
    pitch = cols + 16
    lr, lc = rows // POOL, cols // POOL
    t, s = lax.axis_index("tile"), lax.axis_index("sub")
    sums2, sums1, scratch = scratch[:6], scratch[6:12], scratch[12:]
    copies = Copies()
    early = TileSum(nt, None, wide_out, None, None, scratch[:4])
    late = TileSum(nt, tall, tall_out, scratch[4:7], scratch[7:11], scratch[11:15])
    scratch = scratch[15:]
    wide_out[...] = wide[...]
    second = FullSum(nt, ns, copies, own2, sum2_out, *scratch[:5], scratch[5:17])
    scratch = scratch[17:]
    first, rest = Nothing(), []
    for skip, rows_of_sum in ((0, cut), (cut, own1.shape[0] - cut)):
        if rows_of_sum:
            part = pl.ds(skip, rows_of_sum)
            views = own1.at[part], sum1_out.at[part]
            rest.append(FullSum(nt, ns, copies, *views, *scratch[:5], scratch[5:17]))
            scratch = scratch[17:]
    if len(rest) > 1:
        first = rest[0]
    rest = rest[-1]
    count = float(nt * ns * rows * cols * (channels // G))
    held = [
        pltpu.make_async_copy(act2_in, act2, keep.at[0]),
        pltpu.make_async_copy(act1_in, act1, keep.at[1]),
    ]
    for copy in held:
        copy.start()
    clear(body, left, right)
    greet_all(nt, ns)
    width = lifted.shape[1]
    shrunk = dot_t(lifted[...], lift_weight[...]) * (1.0 / (POOL * POOL))

    def widen(i):
        for n in range(channels // 128):
            part = shrunk[i * lc : (i + 1) * lc, n * 128 : (n + 1) * 128]
            for k in range(POOL):
                spread[i, n, pl.ds(k, lc, stride=POOL), :] = part

    for i in range(lr):
        widen(i)

    def outer(i):
        parts = [spread[i // POOL, n] for n in range(channels // 128)]
        return cot[i].astype(f32) + jnp.concatenate(parts, axis=1)

    def round_outer(i, carry):
        value = outer(i).astype(bf16)
        grad2[i] = value
        body[i + 2] = value
        return carry

    lax.fori_loop(0, rows, round_outer, 0)
    top, bottom = body.at[pl.ds(0, 2)], body.at[pl.ds(rows + 2, 2)]
    border = border_copies(nt, ns, grad2, top, bottom, left, right, border_ss, border_rs)
    begin(border)
    tokens_out[s] = tokens[s]
    for k in range(1, ns):
        p = lax.rem(s + k, ns)
        copies.send(tokens.at[p], tokens_out.at[s], token_ss.at[k], token_rs.at[k], (t, p))
    features = grad_q_t.shape[0]
    heads = features // HD
    attn_t = attn_in[...].T
    tall[pl.ds(0, width), :] = dot_t(attn_t, grad_q_t[...]).astype(bf16)
    both = dot(attn_t, grad_kv[...])
    for n in range(2):
        lanes = [both[:, (2 * h + n) * HD : (2 * h + n + 1) * HD] for h in range(heads)]
        part = jnp.concatenate(lanes, axis=1) if heads > 1 else lanes[0]
        tall[pl.ds((1 + n) * width, width), :] = part.astype(bf16)
    used = 3 * width
    for ref in (grad_ck, grad_cv):
        tall[pl.ds(used, ref.shape[0]), :] = ref[...]
        used += ref.shape[0]
    if used < tall.shape[0]:
        tall[pl.ds(used, tall.shape[0] - used), :] = jnp.zeros(
            (tall.shape[0] - used, features), bf16
        )
    late.start()
    steps = list(early.steps())
    early.share(steps[:1])
    total = rows * pitch

    def turned(row):
        for start in range(0, rows, 8):
            block = [row(start + k) for k in range(8)]
            gap = jnp.zeros((16, channels), bf16)
            piece = jnp.concatenate([p for b in block for p in (b, gap)], axis=0)
            inner_t[:, pl.ds(start * pitch, 8 * pitch)] = piece.T

    def pad_below(ref, used):
        if used < ref.shape[0]:
            ref[pl.ds(used, ref.shape[0] - used), :] = jnp.zeros(
                (ref.shape[0] - used, channels), bf16
            )

    taps = 9 * channels
    turned(lambda i: grad2[i])
    held[0].wait()
    between = [lambda k=k: early.share(steps[k : k + 1]) for k in (1, 2, 3)]
    kernel_grads(act2, inner_t, 16, total, pitch, own2, between)
    lift_grad = dot(pooled[...].T, lifted[...]).astype(bf16)
    for n in range(width // channels):
        own2[pl.ds(taps + n * channels, channels), :] = lift_grad[
            :, n * channels : (n + 1) * channels
        ]
    pad_below(own2, taps + width)
    second.start()
    early.share(steps[4:5])
    finish(border)
    ok = lambda lift_by: (
        lambda i: (t * rows + i - lift_by >= 0) & (t * rows + i - lift_by < nt * rows)
    )
    fill(
        flat, rows + 4, cols, ok(2), s > 0, s < ns - 1,
        lambda i: body[i].astype(f32),
        lambda i: sides(left, right, i),
        lambda: left[0].astype(f32),
    )
    put_left_to_right(flat, triple)
    second.cross()
    center1, std1, center2, std2 = (stats[k : k + 1] for k in range(4))
    gain1, bias1, gain2, bias2 = (vec[k : k + 1] for k in range(4))
    length = list_length(rows + 2, pitch)
    size = block_of(length, 16, 700)
    w2t = turned_taps(w2)
    for start in range(0, length, size):
        hat = (hidden[pl.ds(start, size), :] - center2) * std2
        slope[pl.ds(start, size), :] = conv_rows(
            triple, w2t, start, size, pitch, dot_t
        ) * silu_slope(hat * gain2 + bias2)
        if start == size:
            early.share(steps[5:6])
    early.share(steps[6:])

    at = lambda i: pl.multiple_of(16 + i * pitch, 16)

    def pair2(i):
        place = pl.ds(at(i + 1), cols)
        value = slope[place, :]
        return value, value * ((hidden[place, :] - center2) * std2)

    local2 = jnp.concatenate([row_sums(rows, channels, pair2), gains[...]], axis=0)
    plain = sum_near(nt, ns, local2, sums2[0], sums2[2], sums2[3])
    plain += sum_far(nt, ns, sums2[0], sums2[1], *sums2[2:])
    second.spread()
    late.add(steps[:2])
    back2 = sum_end(nt, sums2[1], sums2[4], sums2[5])
    back2, gains_total = back2[:2], back2[2:]
    means2 = in_groups(back2 * gain2) / count

    def grad_hidden(start, amount):
        hat = (hidden[pl.ds(start, amount), :] - center2) * std2
        value = slope[pl.ds(start, amount), :] * gain2 - means2[0:1] - hat * means2[1:2]
        return std2 * value

    fill(
        flat, rows + 2, cols, ok(1), s > 0, s < ns - 1,
        lambda i: grad_hidden(at(i), cols),
        lambda i: grad_hidden(at(i) + cols, 16),
        lambda: grad_hidden(0, 16),
    )
    late.add(steps[2:3])
    turned(lambda i: flat[pl.ds(24 + (i + 1) * pitch, cols), :].astype(bf16))
    held[1].wait()
    between = [lambda: late.add(steps[3:4]), lambda: first.start(), lambda: late.add(steps[4:5])]
    kernel_grads(act1, inner_t, 16 + pitch, total, pitch, own1, between)
    pad_below(own1, taps)
    rest.start()
    second.settle()
    first.cross()
    put_left_to_right(flat, triple.at[pl.ds(0, length)])
    rest.cross()
    hat1 = lambda i: (img[i].astype(f32) - center1) * std1
    step = 2 * POOL
    w1t = turned_taps(w1)
    for start in range(0, rows, step):
        value = conv_rows(triple, w1t, 16 + start * pitch, step * pitch, pitch, dot_t)
        value = value.reshape(step, pitch, channels)[:, :cols]
        hat = (img[pl.ds(start, step)].astype(f32) - center1) * std1
        outer_grad[pl.ds(start, step)] = value * silu_slope(hat * gain1 + bias1)
        if start == step:
            late.add(steps[5:6])
    first.spread()
    late.add(steps[6:])
    late.share(steps[:1])
    local1 = row_sums(rows, channels, lambda i: (outer_grad[i], outer_grad[i] * hat1(i)))
    plain += sum_near(nt, ns, local1, sums1[0], sums1[2], sums1[3])
    rest.spread()
    plain += sum_far(nt, ns, sums1[0], sums1[1], *sums1[2:])
    late.share(steps[1:3])
    second.share()
    back1 = sum_end(nt, sums1[1], sums1[4], sums1[5])
    means1 = in_groups(back1 * gain1) / count
    first.settle()
    late.share(steps[3:4])

    def last(i, carry):
        value = outer_grad[i] * gain1 - means1[0:1] - hat1(i) * means1[1:2]
        outer_grad[i] = outer(i) + std1 * value
        return carry

    lax.fori_loop(0, rows, last, 0)
    back_out[...] = jnp.concatenate(
        [back1, back2, means2, jnp.zeros_like(means2), gains_total], axis=0
    )
    rest.settle()
    late.share(steps[4:5])
    first.share()
    late.share(steps[5:])
    second.relay()
    rest.share()
    first.relay()
    for k in range(1, ns):
        block = tokens_out.at[lax.rem(s + ns - k, ns)]
        arrived(block, token_ss.at[k], token_rs.at[k], (t, s))
    rest.relay()
    early.end_share()
    second.end()
    first.end()
    late.end_add()
    late.end_share()
    rest.end()
    copies.finish()
    for copy in plain:
        copy.wait_send()


def outer_backward(
    cot, img, w2, w1, vec, stats, hidden, wide, tokens, gains, pooled, lifted, lift_weight,
    attn_in, grad_q_t, grad_kv, grad_ck, grad_cv, act1, act2, cid
):
    nt, ns = lax.axis_size("tile"), lax.axis_size("sub")
    rows, cols, channels = img.shape
    pitch = cols + 16
    long1, long2 = list_length(rows + 4, pitch), list_length(rows + 2, pitch)
    shape = jax.ShapeDtypeStruct
    step = 16 * nt * ns
    width, features = attn_in.shape[1], grad_q_t.shape[0]
    rows2 = round_up(9 * channels + width, step)
    tall = (round_up(3 * width + 2 * grad_ck.shape[0], 16 * nt), features)
    cut = 6 * channels // step * step
    rows1 = round_up(9 * channels, step)
    return pl.pallas_call(
        functools.partial(outer_backward_kernel, nt, ns, cut),
        out_shape=(
            shape(img.shape, f32),
            shape(tall, bf16),
            shape(wide.shape, bf16),
            shape(tokens.shape, bf16),
            shape((rows2, channels), bf16),
            shape((rows1, channels), bf16),
            shape((8 + gains.shape[0], channels), f32),
        ),
        in_specs=[in_vmem()] * 18 + [anywhere()] * 2,
        out_specs=(in_vmem(),) * 7,
        scratch_shapes=[
            pltpu.VMEM((rows // POOL, channels // 128, cols, 128), f32),
            pltpu.VMEM((rows, cols, channels), bf16),
            pltpu.VMEM((rows + 4, cols, channels), bf16),
            pltpu.VMEM((rows + 5, 16, channels), bf16),
            pltpu.VMEM((rows + 5, 16, channels), bf16),
            pltpu.VMEM((long1 + 16, channels), f32),
            pltpu.VMEM((long1, 3 * channels), bf16),
            pltpu.VMEM((long2, 3 * channels), bf16),
            pltpu.VMEM((long1, 3 * channels), bf16),
            pltpu.VMEM((channels, rows * pitch), bf16),
            pltpu.VMEM((long2, channels), f32),
            pltpu.VMEM((rows2, channels), bf16),
            pltpu.VMEM((rows1, channels), bf16),
            pltpu.VMEM(tall, bf16),
            dma(8),
            dma(8),
            dma(2),
            dma(ns),
            dma(ns),
        ]
        + sum_scratch(nt, ns, channels, 2 + gains.shape[0])
        + sum_scratch(nt, ns, channels)
        + TileSum.sems()
        + TileSum.buffers(*tall)
        + TileSum.sems()
        + TileSum.sems()
        + FullSum.scratch(nt, ns, rows2, channels)
        + (FullSum.scratch(nt, ns, cut, channels) if cut else [])
        + FullSum.scratch(nt, ns, rows1 - cut, channels),
        cost_estimate=SHORT,
        compiler_params=params(cid, 62),
        name="outer_backward",
    )(
        cot, img, w2, w1, vec, stats, hidden, wide, tokens, gains, pooled, lifted, lift_weight,
        attn_in, grad_q_t, grad_kv, grad_ck, grad_cv, act1, act2,
    )


def finish_kernel(text, up, down, *refs):
    q, k, v, ck, cv, o, co, cq, second, first = refs[:10]
    lift, refs = refs[10:-13], refs[-13:]
    for src, dst in zip((q, k, v, o, co, second, first, up, down), refs[:9]):
        dst[...] = src[...].astype(f32)
    refs[9][...] = cq[...].T.astype(f32)
    turned = text[...].T
    refs[10][...] = dot(turned, ck[...])
    refs[11][...] = dot(turned, cv[...])
    refs[12][...] = jnp.concatenate([part[...].astype(f32) for part in lift], axis=1)


def finish_grads(text, up, down, tall, wide, second, first, taps, text_rows):
    features, width = tall.shape[1], wide.shape[1]
    channels = first.shape[1]
    steps = features // 32
    row = lambda size, lanes, skip=0: pl.BlockSpec((size, lanes), lambda i: (skip + i, 0))
    size = width // steps
    tall_specs = [row(size, features, n * steps) for n in range(3)]
    start = 3 * width // text_rows
    tall_specs += [
        pl.BlockSpec((text_rows, features), lambda i, n=n: (start + n, 0)) for n in range(2)
    ]
    wide_specs = [row(32, width, n * steps) for n in range(2)]
    wide_specs.append(pl.BlockSpec((features, size), lambda i: (2, i)))
    size = taps // steps
    lift_size = channels // steps
    lift_specs = [
        row(lift_size, channels, taps // lift_size + n * steps) for n in range(width // channels)
    ]
    full = text.shape[1]
    up_specs = [row(w.shape[0] // steps, w.shape[1]) for w in (up, down)]
    in_specs = [pl.BlockSpec((text.shape[0], full // steps), lambda i: (0, i))] + up_specs
    in_specs += tall_specs + wide_specs + [row(size, channels)] * 2 + lift_specs
    shape = lambda *dims: jax.ShapeDtypeStruct(dims, f32)
    return pl.pallas_call(
        finish_kernel,
        grid=(steps,),
        out_shape=(shape(width, features),) * 3
        + (shape(features, width),) * 2
        + (shape(taps, channels),) * 2
        + (shape(*up.shape), shape(*down.shape), shape(width, features))
        + (shape(full, features), shape(full, features), shape(channels, width)),
        in_specs=in_specs,
        out_specs=[row(width // steps, features)] * 3
        + [row(32, width)] * 2
        + [row(size, channels)] * 2
        + up_specs
        + [row(width // steps, features)]
        + [row(full // steps, features)] * 2
        + [row(lift_size, width)],
        cost_estimate=SHORT,
        compiler_params=params(),
        name="finish_grads",
    )(text, up, down, *[tall] * 5, *[wide] * 3, second, first, *[second] * len(lift_specs))


def time_embed(time_steps, channels):
    half_width = channels // 2
    frequency = jnp.exp(
        -math.log(10000.0) * jnp.arange(half_width).astype(f32) / half_width
    )
    angles = time_steps.astype(f32)[:, None] * frequency[None, :]
    return jnp.concatenate([jnp.sin(angles), jnp.cos(angles)], axis=1)


def weight_grad(inputs, grads):
    return lax.dot_general(inputs, grads, (((0,), (0,)), ((), ())), preferred_element_type=f32)


def local(
    outer_image,
    inner_image,
    text_states,
    time_steps,
    text_lengths,
    first_gain,
    first_bias,
    conv_first,
    time_weight,
    second_gain,
    second_bias,
    conv_second,
    lift_weight,
    attn_gain,
    query_weight,
    key_weight,
    value_weight,
    out_weight,
    cross_gain,
    cross_query,
    cross_key,
    cross_value,
    cross_out,
    mlp_gain,
    up_weight,
    down_weight,
    outer_cotan,
    inner_cotan,
):
    nt, ns = lax.axis_size("tile"), lax.axis_size("sub")
    s = lax.axis_index("sub")
    batch, rows, cols, channels = outer_image.shape
    lr, lc = rows // POOL, cols // POOL
    width = inner_image.shape[2] * ns
    features = inner_image.shape[2]
    heads = features // HD
    own = batch * lr * lc
    length = ns * lr * lc
    pixels = rows * cols * nt * ns


    def whole_tokens(values):
        full = lax.all_gather(values, "sub", axis=2, tiled=True)
        full = full.reshape(batch, lr, ns, lc, width)
        mine = lax.dynamic_index_in_dim(full, s, 2, keepdims=False).reshape(own, width)
        return full, mine

    _, inner_own = whole_tokens(inner_image)
    cotan_full, _ = whole_tokens(inner_cotan)
    cotan_full = jnp.transpose(cotan_full, (2, 0, 1, 3, 4)).reshape(ns, own, width)
    own_gains = jnp.stack([attn_gain, cross_gain, mlp_gain])

    time_act = jax.nn.silu(time_embed(time_steps, channels))
    time_shift = jnp.dot(time_act, time_weight.astype(f32), precision=precise)
    fixed = jnp.stack([first_gain, first_bias, second_gain, second_bias])
    fixed = jnp.broadcast_to(fixed[None], (batch, 4, channels))
    empty = jnp.zeros((batch, 3, channels), f32)
    vectors = jnp.concatenate([fixed, time_shift[:, None, :], empty], axis=1)
    as_rows = lambda w: w.reshape(9 * channels, channels)
    forward = [
        outer_forward(
            outer_image[b],
            as_rows(conv_first),
            as_rows(conv_second),
            vectors[b],
            own_gains,
            20 + b,
        )
        for b in range(batch)
    ]
    outer_out = jnp.stack([f[0] for f in forward])
    gains = jnp.transpose(forward[0][6], (1, 0, 2)).reshape(3, width)
    pooled = jnp.concatenate([f[1] for f in forward], axis=0)

    flat = lambda v: v.reshape(-1, v.shape[-1])
    block, rows_all = ((own, width), f32), ((ns, own, width), bf16)
    stream_in, attn_in = chain_call(
        enter_kernel,
        "enter",
        2,
        (block, rows_all),
        (inner_own, pooled, lift_weight, gains[0:1]),
        (),
        False,
    )
    attn_in = flat(attn_in)

    def per_sample(values, tokens_last):
        if tokens_last:
            values = values.reshape(-1, ns, batch, lr * lc)
            return jnp.transpose(values, (2, 0, 1, 3)).reshape(batch, -1, length)
        values = values.reshape(ns, batch, lr * lc, -1)
        return jnp.transpose(values, (1, 0, 2, 3)).reshape(batch, length, -1)

    def all_samples(values, tokens_last):
        if tokens_last:
            values = values.reshape(batch, -1, ns, lr * lc)
            return jnp.transpose(values, (1, 2, 0, 3)).reshape(-1, ns * own)
        values = values.reshape(batch, ns, lr * lc, -1)
        return jnp.transpose(values, (1, 0, 2, 3)).reshape(ns * own, -1)

    pair = lambda k, v: jnp.concatenate(
        [k.reshape(-1, heads, HD), v.reshape(-1, heads, HD)], axis=2
    ).reshape(-1, heads * 2 * HD)
    kv_weight = pair(key_weight, value_weight)
    query_t = lax.dot_general(
        query_weight, attn_in, (((0,), (1,)), ((), ())), preferred_element_type=f32
    ).astype(bf16)
    kv = dot(attn_in, kv_weight).astype(bf16)
    mixed_t, head_q, head_kv, head_mixed_f, head_lse = self_attention(
        per_sample(query_t, True), per_sample(kv, False), 3
    )
    mixed_t = all_samples(mixed_t, True)
    after_attn, cross_in = chain_call(
        attn_out_kernel,
        "attn_out",
        5,
        (block, rows_all),
        (mixed_t, out_weight, stream_in, gains[1:2]),
        [pltpu.VMEM((ns * own, features), bf16)],
        True,
    )
    text_rows = batch * text_states.shape[1]
    text = text_states.reshape(text_rows, -1)
    cross_k, cross_v = dot(text, cross_key).astype(bf16), dot(text, cross_value).astype(bf16)
    sample_of = lambda count: jnp.arange(batch * count) // count
    text_at = jnp.tile(jnp.arange(text_states.shape[1]), batch)
    good = text_at < jnp.repeat(text_lengths, text_states.shape[1])
    same = sample_of(lr * lc)[:, None] == sample_of(text_states.shape[1])[None, :]
    mask = jnp.where(same & good[None, :], 1.0, 0.0).astype(f32)
    head_rows = ((ns, own, features), bf16)
    after_cross, mlp_in, cross_q, cross_mixed = chain_call(
        cross_kernel,
        "cross",
        6,
        (block, rows_all, head_rows, head_rows),
        (cross_in, cross_query, cross_k, cross_v, mask, cross_out, after_attn, gains[2:3]),
        (),
        True,
    )

    units = up_weight.shape[1]
    one_row = ((1, width), f32)
    middle = pltpu.VMEM((ns * own, units), bf16)
    grad_after_cross, grad_cross_full, grad_mlp_gain, down, grad_up, grad_down = chain_call(
        mlp_kernel,
        "mlp",
        8,
        (
            block,
            rows_all,
            one_row,
            ((ns * own, width), bf16),
            ((width, units), bf16),
            ((units, width), bf16),
        ),
        (mlp_in, cotan_full, up_weight, down_weight, after_cross, gains[2:3]),
        [middle, middle],
        True,
    )
    grad_down, grad_up = lax.psum((grad_down, grad_up), "tile")
    text_block = ((text_rows, features), bf16)
    (
        grad_after_attn,
        grad_attn_full,
        grad_cross_gain,
        grad_ck,
        grad_cv,
        grad_early,
    ) = chain_call(
        cross_back_kernel,
        "cross_back",
        10,
        (
            block,
            rows_all,
            one_row,
            text_block,
            text_block,
            ((2, features, width), bf16),
        ),
        (
            grad_cross_full,
            cross_out,
            cross_q,
            cross_k,
            cross_v,
            mask,
            cross_query,
            after_attn,
            gains[1:2],
            grad_after_cross,
            cross_in,
            cross_mixed,
        ),
        [pltpu.VMEM((text_rows, features), f32)] * 2
        + [pltpu.VMEM((ns * own, features), bf16)],
        True,
    )
    grad_attn_full = flat(grad_attn_full)
    grad_mixed_t = dot_t(out_weight, grad_attn_full).astype(bf16)
    head_d = swap_heads(per_sample(grad_mixed_t, True), False, 13)
    head_dq, head_dkv, wide = flash_back(
        head_q,
        head_d,
        head_mixed_f,
        head_lse,
        head_kv,
        mixed_t,
        grad_attn_full,
        grad_early.reshape(2 * features, width),
        16,
    )
    grad_q_t, grad_kv, down_own = dqkv_home(head_dq, head_dkv, down, 14)
    grad_q_t, grad_kv = all_samples(grad_q_t, True), all_samples(grad_kv, False)
    grad_lifted, grad_attn_gain = chain_call(
        attn_back_kernel,
        "attn_back",
        15,
        (((own, width), bf16), one_row),
        (grad_q_t, grad_kv, query_weight, kv_weight, stream_in, gains[0:1], grad_after_attn),
        [pltpu.VMEM((ns * own, features), bf16), pltpu.VMEM((own, width), f32)],
        True,
        False,
    )

    inner_sum = after_cross + down_own
    tokens = jnp.stack([inner_sum.astype(bf16), grad_lifted])
    tokens = tokens.reshape(2, own, ns, features).transpose(2, 0, 1, 3)
    gain_rows = jnp.stack([grad_attn_gain, grad_cross_gain, grad_mlp_gain]).reshape(-1, channels)
    by_tap = lambda w: w.reshape(9, channels, channels)
    backward = []
    for b in range(batch):
        once = (lambda v: v) if b == 0 else jnp.zeros_like
        sample = lambda v: v.reshape(batch, lr * lc, -1)[b]
        backward.append(
            outer_backward(
                outer_cotan[b],
                outer_image[b],
                by_tap(conv_second),
                by_tap(conv_first),
                vectors[b],
                forward[b][5],
                forward[b][4],
                once(wide),
                once(tokens),
                once(gain_rows),
                sample(pooled),
                sample(grad_lifted),
                lift_weight,
                attn_in,
                once(grad_q_t),
                once(grad_kv),
                once(grad_ck),
                once(grad_cv),
                forward[b][2],
                forward[b][3],
                20 + batch + b,
            )
        )
    outer_grad = jnp.stack([f[0] for f in backward])
    tall, wide, tokens = backward[0][1:4]
    tokens = tokens.reshape(ns, 2, batch, lr, lc, features).transpose(1, 2, 3, 0, 4, 5)
    inner_out, inner_grad = tokens.reshape(2, batch, length, features)
    inner_grad = inner_grad.astype(f32)
    if batch > 1:
        sum2, sum1 = (
            sum(f[k].astype(f32) for f in backward).astype(bf16) for k in (4, 5)
        )
    else:
        sum2, sum1 = backward[0][4:6]
    ends = finish_grads(
        text,
        grad_up,
        grad_down,
        tall,
        wide,
        sum2,
        sum1,
        9 * channels,
        text_rows,
    )
    grad_q_w, grad_k_w, grad_v_w, grad_o_w, grad_co_w = ends[:5]
    grad_conv_second, grad_conv_first = (v.reshape(conv_first.shape) for v in ends[5:7])
    grad_up, grad_down, grad_cq_w = ends[7:10]
    grad_ck_w, grad_cv_w, grad_lift = ends[10:]
    stats = jnp.stack([f[5] for f in forward])
    back = jnp.stack([f[6] for f in backward])
    grad_gains = back[0, 8:].reshape(3, width)
    center2, std2, hidden_total = stats[:, 2], stats[:, 3], stats[:, 4]
    hat2_total = std2 * (hidden_total - pixels * center2)
    hidden_sum = std2 * (
        second_gain * back[:, 2] - pixels * back[:, 4] - back[:, 5] * hat2_total
    )
    grad_time = jnp.dot(time_act.T, hidden_sum, precision=precise)
    back = jnp.sum(back, axis=0)
    grad_gains = lax.dynamic_slice_in_dim(grad_gains, s * features, features, axis=1)
    return (
        outer_out,
        inner_out,
        outer_grad,
        inner_grad,
        back[1],
        back[0],
        grad_conv_first,
        grad_time,
        back[3],
        back[2],
        grad_conv_second,
        grad_lift,
        grad_gains[0],
        grad_q_w,
        grad_k_w,
        grad_v_w,
        grad_o_w,
        grad_gains[1],
        grad_cq_w,
        grad_ck_w,
        grad_cv_w,
        grad_co_w,
        grad_gains[2],
        grad_up,
        grad_down,
    )


def solution(mesh):
    pixels = P(None, "tile", "sub", None)
    tokens = P(None, "tile", "sub")
    columns, rows, vector = P(None, "sub"), P("sub", None), P("sub")
    return jax.shard_map(
        local,
        mesh=mesh,
        in_specs=(pixels, tokens)
        + (P(),) * 11
        + (vector, columns, columns, columns, rows)
        + (vector, columns, columns, columns, rows)
        + (vector, columns, rows)
        + (pixels, tokens),
        out_specs=(pixels, tokens, pixels, tokens)
        + (P(),) * 8
        + (vector, columns, columns, columns, rows)
        + (vector, columns, columns, columns, rows)
        + (vector, columns, rows),
        check_vma=False,
    )
```

```python
import functools
import math

import jax
import jax.numpy as jnp
from jax import lax
from jax.experimental import pallas as pl
from jax.experimental.pallas import tpu as pltpu
from jax.sharding import PartitionSpec as P

G = 32
HD = 64
POOL = 4
EPSILON = 1e-05
MESH = pl.DeviceIdType.MESH
precise = lax.Precision.HIGHEST
f32 = jnp.float32
bf16 = jnp.bfloat16


def params(cid=None, vmem=56):
    if cid is None:
        return pltpu.CompilerParams(vmem_limit_bytes=vmem << 20)
    return pltpu.CompilerParams(
        collective_id=cid, has_side_effects=True, vmem_limit_bytes=vmem << 20
    )


SHORT = pl.CostEstimate(flops=1, transcendentals=0, bytes_accessed=1)
LONG = pl.CostEstimate(flops=20_000_000_000, transcendentals=0, bytes_accessed=60_000_000)


def in_vmem():
    return pl.BlockSpec(memory_space=pltpu.VMEM)


def anywhere():
    return pl.BlockSpec(memory_space=pl.ANY)


def dma(*shape):
    return pltpu.SemaphoreType.DMA(shape)


def remote(src, dst, send_sem, recv_sem, where):
    return pltpu.make_async_remote_copy(
        src_ref=src,
        dst_ref=dst,
        send_sem=send_sem,
        recv_sem=recv_sem,
        device_id=where,
        device_id_type=MESH,
    )


def arrived(dst, send_sem, recv_sem, me):
    remote(dst, dst, send_sem, recv_sem, me).wait_recv()


def greet(peers):
    barrier = pltpu.get_barrier_semaphore()
    for peer in peers:
        pl.semaphore_signal(barrier, inc=1, device_id=peer, device_id_type=MESH)
    pl.semaphore_wait(barrier, len(peers))


def dot(left, right):
    return jnp.dot(left, right, preferred_element_type=f32)


def dot_t(left, right):
    return lax.dot_general(left, right, (((1,), (1,)), ((), ())), preferred_element_type=f32)


def clear(*refs):
    for ref in refs:
        ref[...] = jnp.zeros_like(ref)


def round_up(rows, step):
    return (rows + step - 1) // step * step


def chunks_of(rows):
    return max(1, min(4, rows // 16))


class Copies:
    def __init__(self):
        self.started = []

    def send(self, src, dst, send_sem, recv_sem, where, when=None):
        copy = remote(src, dst, send_sem, recv_sem, where)
        if when is None:
            copy.start()
        else:
            pl.when(when)(copy.start)
        self.started.append((when, copy))

    def finish(self):
        for when, copy in self.started:
            if when is None:
                copy.wait_send()
            else:
                pl.when(when)(copy.wait_send)


class SubScatter:
    def __init__(self, ns, copies, x, got, stage, last, sems):
        t, s = lax.axis_index("tile"), lax.axis_index("sub")
        self.far, self.copies, self.x, self.s, self.t = ns // 2, copies, x, s, t
        self.got, self.stage, self.last = got, stage, last
        self.r, self.c = s // 2, lax.rem(s, 2)
        self.me, self.twin = (t, s), (t, self.r * 2 + 1 - self.c)
        self.count = chunks_of(x.shape[1])
        self.size = x.shape[1] // self.count
        self.s1, self.r1, self.s2, self.r2 = sems

    @staticmethod
    def scratch(ns, rows, width):
        far, count = ns // 2, chunks_of(rows)
        blocks = [pltpu.VMEM((far, rows, width), bf16) for _ in range(3)]
        return blocks + [dma(far, count) for _ in range(4)]

    def peers(self):
        return [self.twin] + [self.peer(k) for k in range(1, self.far)]

    def peer(self, k):
        return (self.t, lax.rem(self.r + k, self.far) * 2 + self.c)

    def part(self, j):
        return pl.ds(j * self.size, self.size)

    def over(self, k):
        return lax.rem(self.r + k, self.far) * 2 + 1 - self.c

    def start_one(self, k):
        for j in range(self.count):
            block, got = self.x.at[self.over(k), self.part(j)], self.got.at[k, self.part(j)]
            self.copies.send(block, got, self.s1.at[k, j], self.r1.at[k, j], self.twin)

    def start(self):
        for k in list(range(1, self.far)) + [0]:
            self.start_one(k)

    def run(self, make, out, meanwhile=None, then=None):
        for k in range(1, self.far):
            make(self.over(k))
            self.start_one(k)
        for k in range(1, self.far):
            make(self.peer(k)[1])
        make(self.over(0))
        self.start_one(0)
        self.cross()
        make(self.s)
        if meanwhile is not None:
            meanwhile()
        self.end(out, then)

    def cross(self):
        for j in range(self.count):
            part = self.part(j)
            for k in range(1, self.far):
                arrived(self.got.at[k, part], self.s1.at[k, j], self.r1.at[k, j], self.me)
                own = self.x[self.peer(k)[1], part].astype(f32)
                self.stage[k, part] = (own + self.got[k, part].astype(f32)).astype(bf16)
                src, dst = self.stage.at[k, part], self.last.at[k, part]
                self.copies.send(src, dst, self.s2.at[k, j], self.r2.at[k, j], self.peer(k))

    def end(self, out, then=None):
        for j in range(self.count):
            part = self.part(j)
            arrived(self.got.at[0, part], self.s1.at[0, j], self.r1.at[0, j], self.me)
            total = self.x[self.s, part].astype(f32) + self.got[0, part].astype(f32)
            for k in range(1, self.far):
                arrived(self.last.at[k, part], self.s2.at[k, j], self.r2.at[k, j], self.me)
                total = total + self.last[k, part].astype(f32)
            out[part] = total
            if then is not None:
                then(j, part)


class SubGather:
    def __init__(self, ns, copies, out, sems):
        t, s = lax.axis_index("tile"), lax.axis_index("sub")
        self.far, self.copies, self.out, self.t, self.s = ns // 2, copies, out, t, s
        self.r, self.c = s // 2, lax.rem(s, 2)
        self.me, self.twin = (t, s), (t, self.r * 2 + 1 - self.c)
        self.count = chunks_of(out.shape[1])
        self.size = out.shape[1] // self.count
        self.s1, self.r1, self.s2, self.r2 = sems

    @staticmethod
    def scratch(ns, rows):
        return [dma(ns // 2, chunks_of(rows)) for _ in range(4)]

    def block(self, r, c, j):
        return self.out.at[lax.rem(r, self.far) * 2 + c, pl.ds(j * self.size, self.size)]

    def start(self):
        for j in range(self.count):
            self.start_one(j)

    def start_one(self, j):
        block = self.block(self.r, self.c, j)
        for k in range(1, self.far):
            peer = (self.t, lax.rem(self.r + k, self.far) * 2 + self.c)
            self.copies.send(block, block, self.s1.at[k, j], self.r1.at[k, j], peer)
        self.copies.send(block, block, self.s2.at[0, j], self.r2.at[0, j], self.twin)

    def relay(self):
        for j in range(self.count):
            for k in range(1, self.far):
                block = self.block(self.r + self.far - k, self.c, j)
                arrived(block, self.s1.at[k, j], self.r1.at[k, j], self.me)
                self.copies.send(block, block, self.s2.at[k, j], self.r2.at[k, j], self.twin)

    def end(self):
        for j in range(self.count):
            for k in range(self.far):
                block = self.block(self.r + self.far - k, 1 - self.c, j)
                arrived(block, self.s2.at[k, j], self.r2.at[k, j], self.me)


def sub_peers(ns):
    t, s = lax.axis_index("tile"), lax.axis_index("sub")
    far, r, c = ns // 2, s // 2, lax.rem(s, 2)
    return [(t, r * 2 + 1 - c)] + [(t, lax.rem(r + k, far) * 2 + c) for k in range(1, far)]


def layer_hat(values):
    width = values.shape[1]
    center = jnp.sum(values, axis=1, keepdims=True) / width
    moved = values - center
    inv_std = lax.rsqrt(jnp.sum(moved * moved, axis=1, keepdims=True) / width + EPSILON)
    return moved * inv_std, inv_std


def layer_back(grad_out, values, gain):
    width = values.shape[1]
    hat, inv_std = layer_hat(values)
    scaled = grad_out * gain
    mean_grad = jnp.sum(scaled, axis=1, keepdims=True) / width
    mean_cross = jnp.sum(scaled * hat, axis=1, keepdims=True) / width
    grad_in = inv_std * (scaled - mean_grad - hat * mean_cross)
    return grad_in, jnp.sum(grad_out * hat, axis=0, keepdims=True)


def tokens_of(ref, p):
    return ref[:, p].reshape(-1, ref.shape[3]) if len(ref.shape) == 4 else ref[p]


def by_head(first, second):
    parts = []
    for h in range(first.shape[1] // HD):
        parts += [head_of(first, h), head_of(second, h)]
    return side_by_side(parts)


def enter_kernel(
    ns, inner, pooled, lift, gain, wq, wk, wv, stream, gathered, q_out, kv_out, *sems
):
    copies = Copies()
    gather = SubGather(ns, copies, gathered, sems)
    mine = tokens_of(inner, gather.s) if len(inner.shape) == 4 else inner[...]
    value = mine.astype(f32) + dot(pooled[...], lift[...]).astype(bf16).astype(f32)
    stream[...] = value
    gathered[gather.s] = (layer_hat(value)[0] * gain[0:1, :]).astype(bf16)
    greet(sub_peers(ns))
    gather.start()
    turned = wq[...].T
    gather.relay()
    gather.end()
    rows = gathered[...].reshape(-1, gathered.shape[2])
    q_out[...] = dot_t(turned, rows).astype(bf16)
    kv_out[...] = by_head(dot(rows, wk[...]), dot(rows, wv[...])).astype(bf16)
    copies.finish()


def attn_out_kernel(ns, mixed_t, weight, before, gain, after, gathered, turned, *scratch):
    copies = Copies()
    own = before.shape[0]
    scatter = SubScatter(ns, copies, *scratch[:4], scratch[4:8])
    gather = SubGather(ns, copies, gathered, scratch[8:])
    turned[...] = mixed_t[...].T

    def make(p):
        rows = turned[pl.ds(pl.multiple_of(p * own, 16), own), :]
        scatter.x[p] = dot(rows, weight[...]).astype(bf16)

    greet(sub_peers(ns))

    def normalize(j, part):
        value = before[part, :] + after[part, :]
        after[part, :] = value
        gathered[gather.s, part] = (layer_hat(value)[0] * gain[1:2, :]).astype(bf16)
        gather.start_one(j)

    scatter.run(make, after, None, normalize)
    gather.relay()
    gather.end()
    copies.finish()


def head_of(values, h):
    return values[:, h * HD : (h + 1) * HD]


def head_probs(queries, keys, mask, h):
    scores = dot_t(head_of(queries, h), head_of(keys, h)) * HD ** (-0.5)
    scores = jnp.where(mask > 0.5, scores, -1000000000.0)
    raised = jnp.exp(scores - jnp.max(scores, axis=1, keepdims=True))
    return raised / jnp.sum(raised, axis=1, keepdims=True)


def side_by_side(parts):
    return jnp.concatenate(parts, axis=1) if len(parts) > 1 else parts[0]


def cross_kernel(
    ns, cross_in, wq, ck, cv, mask, wo, before, gain, after, gathered, queries, mixed, *scratch
):
    copies = Copies()
    scatter = SubScatter(ns, copies, *scratch[:4], scratch[4:8])
    gather = SubGather(ns, copies, gathered, scratch[8:])
    heads = wq.shape[1] // HD

    def make(p):
        q = dot(cross_in[p], wq[...]).astype(bf16)
        queries[p] = q
        keys, values, masked = ck[...], cv[...], mask[...]
        parts = [
            dot(head_probs(q, keys, masked, h).astype(bf16), head_of(values, h))
            for h in range(heads)
        ]
        mixed[p] = side_by_side(parts).astype(bf16)
        scatter.x[p] = dot(mixed[p], wo[...]).astype(bf16)

    greet(sub_peers(ns))

    def normalize(j, part):
        value = before[part, :] + after[part, :]
        after[part, :] = value
        gathered[gather.s, part] = (layer_hat(value)[0] * gain[2:3, :]).astype(bf16)
        gather.start_one(j)

    scatter.run(make, after, None, normalize)
    gather.relay()
    gather.end()
    copies.finish()


def mlp_kernel(
    ns, mlp_in, cotan, w_up, w_down, before, gain,
    grad, gathered, gain_grad, down, up_grad, down_grad, activated, grad_up, cotans, *scratch
):
    copies = Copies()
    for p in range(ns):
        cotans[p] = tokens_of(cotan, p)
    cotan = cotans
    scatter = SubScatter(ns, copies, *scratch[:4], scratch[4:8])
    gather = SubGather(ns, copies, gathered, scratch[8:])
    own = before.shape[0]
    rate = math.sqrt(2.0 / math.pi)

    def make(p):
        up = dot(mlp_in[p], w_up[...])
        square = up * up
        bent = jnp.tanh(rate * (up + 0.044715 * up * square))
        rows = pl.ds(pl.multiple_of(p * own, 16), own)
        activated[rows, :] = (0.5 * up * (1.0 + bent)).astype(bf16)
        slope = 0.5 * (1.0 + bent) + 0.5 * up * (1.0 - bent * bent) * (
            rate * (1.0 + 3.0 * 0.044715 * square)
        )
        turned = (slope * dot_t(cotan[p], w_down[...])).astype(bf16)
        grad_up[rows, :] = turned
        scatter.x[p] = dot_t(turned, w_up[...]).astype(bf16)

    greet(sub_peers(ns))
    whole = lambda ref: ref[...].reshape(ns * own, ref.shape[2])

    def meanwhile():
        up_grad[...] = dot(whole(mlp_in).T, grad_up[...]).astype(bf16)

    gain_grad[...] = jnp.zeros_like(gain_grad)

    def normalize(j, part):
        back, gains = layer_back(grad[part, :], before[part, :], gain[2:3, :])
        gain_grad[...] += gains
        value = cotan[gather.s, part].astype(f32) + back
        grad[part, :] = value
        gathered[gather.s, part] = value.astype(bf16)
        gather.start_one(j)

    scatter.run(make, grad, meanwhile, normalize)
    down_grad[...] = dot(activated[...].T, whole(cotan)).astype(bf16)
    gather.relay()
    down[...] = dot(activated[...], w_down[...]).astype(bf16)
    gather.end()
    copies.finish()


def cross_back_kernel(
    ns, incoming, wo, queries, ck, cv, mask, wq, before, gain, residual, cross_in, mixed,
    grad, gathered, gain_grad, dk_out, dv_out, weights, dk, dv, dq, *scratch
):
    copies = Copies()
    scatter = SubScatter(ns, copies, *scratch[:4], scratch[4:8])
    gather = SubGather(ns, copies, gathered, scratch[8:])
    heads = wq.shape[1] // HD
    own = before.shape[0]
    clear(dk, dv)

    def make(p):
        grad_mixed = dot_t(incoming[p], wo[...]).astype(bf16)
        q, keys, values, masked = queries[p], ck[...], cv[...], mask[...]
        parts_q, parts_k, parts_v = [], [], []
        for h in range(heads):
            probs = head_probs(q, keys, masked, h)
            slope = dot_t(head_of(grad_mixed, h), head_of(values, h))
            lean = probs * (slope - jnp.sum(probs * slope, axis=1, keepdims=True))
            lean = lean.astype(bf16)
            parts_q.append(dot(lean, head_of(keys, h)))
            parts_k.append(dot(lean.T, head_of(q, h)))
            parts_v.append(dot(probs.astype(bf16).T, head_of(grad_mixed, h)))
        part = (side_by_side(parts_q) * HD ** (-0.5)).astype(bf16)
        dq[pl.ds(pl.multiple_of(p * own, 16), own), :] = part
        dk[...] += side_by_side(parts_k)
        dv[...] += side_by_side(parts_v)
        scatter.x[p] = dot_t(part, wq[...]).astype(bf16)

    greet(sub_peers(ns))
    whole = lambda ref: ref[...].reshape(ns * own, ref.shape[2])

    def meanwhile():
        weights[0] = dot(whole(mixed).T, whole(incoming)).astype(bf16)
        dk_out[...] = (dk[...] * HD ** (-0.5)).astype(bf16)
        dv_out[...] = dv[...].astype(bf16)

    gain_grad[...] = jnp.zeros_like(gain_grad)

    def normalize(j, part):
        back, gains = layer_back(grad[part, :], before[part, :], gain[1:2, :])
        gain_grad[...] += gains
        value = residual[part, :] + back
        grad[part, :] = value
        gathered[gather.s, part] = value.astype(bf16)
        gather.start_one(j)

    scatter.run(make, grad, meanwhile, normalize)
    weights[1] = dot(dq[...].T, whole(cross_in)).astype(bf16)
    gather.relay()
    gather.end()
    copies.finish()


def attn_back_kernel(
    ns, dq_t, dkv, wq, wk, wv, before, gain, residual, out, gain_grad, turned, wkv, *scratch
):
    copies = Copies()
    scatter = SubScatter(ns, copies, *scratch[1:5], scratch[5:9])
    total = scratch[0]
    own = before.shape[0]
    turned[...] = dq_t[...].T
    wkv[...] = by_head(wk[...], wv[...])

    def make(p):
        rows = pl.ds(pl.multiple_of(p * own, 16), own)
        value = dot_t(turned[rows, :], wq[...]) + dot_t(dkv[rows, :], wkv[...])
        scatter.x[p] = value.astype(bf16)

    greet(sub_peers(ns))
    scatter.run(make, total)
    back, gains = layer_back(total[...], before[...], gain[0:1, :])
    gain_grad[...] = gains
    out[...] = (residual[...] + back).astype(bf16)
    copies.finish()


def chain_call(kernel, name, cid, outs, args, extra, scatter, gather=True, vmem=16, cost=SHORT):
    ns = lax.axis_size("sub")
    own, width = outs[0][0]
    scratch = list(extra)
    if scatter:
        scratch += [pltpu.VMEM((ns, own, width), bf16)] + SubScatter.scratch(ns, own, width)
    if gather:
        scratch += SubGather.scratch(ns, own)
    return pl.pallas_call(
        functools.partial(kernel, ns),
        out_shape=tuple(jax.ShapeDtypeStruct(*out) for out in outs),
        in_specs=[in_vmem()] * len(args),
        out_specs=(in_vmem(),) * len(outs),
        scratch_shapes=scratch,
        cost_estimate=cost,
        compiler_params=params(cid, vmem),
        name=name,
    )(*args)


def deal(nt, u):
    t, s = lax.axis_index("tile"), lax.axis_index("sub")
    nb = nt // u
    a, b = t // nb, lax.rem(t, nb)
    a_peer = lambda k: (lax.rem(a + k, u) * nb + b, s)
    b_peer = lambda k: (a * nb + lax.rem(b + k, nb), s)
    peers = [a_peer(k) for k in range(1, u)] + [b_peer(k) for k in range(1, nb)]
    return t, s, nb, a, b, a_peer, b_peer, peers


def rows_of(ref, i, size):
    return ref.at[:, pl.ds(pl.multiple_of(i * size, size), size), :]


def lanes_of(ref, i, size):
    return ref.at[:, :, pl.ds(pl.multiple_of(i * size, size), size)]


class TileSum:
    PARTS = 4

    def __init__(self, nt, x, out, buffers, add_sems, share_sems):
        t, s = lax.axis_index("tile"), lax.axis_index("sub")
        self.na, self.x, self.out = nt // 2, x, out
        self.a, self.b, self.s = t // 2, lax.rem(t, 2), s
        self.me, self.pair = (t, s), (self.a * 2 + 1 - self.b, s)
        self.half = out.shape[0] // 2
        self.piece = self.half // 2 // self.PARTS
        if add_sems:
            self.got1, self.stage, self.got2 = buffers
            self.s1, self.r1, self.s2, self.r2 = add_sems
        if share_sems:
            self.s3, self.r3, self.s4, self.r4 = share_sems

    @staticmethod
    def buffers(rows, width):
        return [pltpu.VMEM((rows // 2, width), bf16) for _ in range(3)]

    @staticmethod
    def sems():
        return [dma(2, TileSum.PARTS) for _ in range(4)]

    def rows(self, b, e, j):
        start = b * self.half + (j * 2 + e) * self.piece
        return pl.ds(pl.multiple_of(start, 16), self.piece)

    def along(self, e):
        up, down = (self.a * 2 + 2 + self.b, self.s), (self.a * 2 - 2 + self.b, self.s)
        return (down, up, self.a) if e else (up, down, self.na - 1 - self.a)

    def start(self):
        for j in range(self.PARTS):
            for e in range(2):
                self.to_pair(e, j).start()

    def to_pair(self, e, j):
        src, dst = self.x.at[self.rows(1 - self.b, e, j)], self.got1.at[self.rows(0, e, j)]
        return remote(src, dst, self.s1.at[e, j], self.r1.at[e, j], self.pair)

    def steps(self):
        return range(self.PARTS + self.na - 1)

    def step_of(self, way, step, action):
        j = step - way
        pl.when((j >= 0) & (j < self.PARTS))(lambda: action(jnp.clip(j, 0, self.PARTS - 1)))

    def add(self, steps):
        for step in steps:
            for e in range(2):
                self.step_of(self.along(e)[2], step, functools.partial(self.add_one, e))

    def add_one(self, e, j):
        _, after, way = self.along(e)
        here, mine = self.rows(0, e, j), self.rows(self.b, e, j)
        arrived(self.got1.at[here], self.s1.at[e, j], self.r1.at[e, j], self.me)
        both = self.x[mine].astype(f32) + self.got1[here].astype(f32)

        @pl.when(way == 0)
        def _():
            self.stage[here] = both.astype(bf16)

        @pl.when(way > 0)
        def _():
            arrived(self.got2.at[here], self.s2.at[e, j], self.r2.at[e, j], self.me)
            self.stage[here] = (both + self.got2[here].astype(f32)).astype(bf16)

        @pl.when(way < self.na - 1)
        def _():
            src, dst = self.stage.at[here], self.got2.at[here]
            remote(src, dst, self.s2.at[e, j], self.r2.at[e, j], after).start()

        @pl.when(way == self.na - 1)
        def _():
            self.out[mine] = self.stage[here]

    def share(self, steps):
        for step in steps:
            for e in range(2):
                way = self.na - 1 - self.along(e)[2]
                self.step_of(way, step, functools.partial(self.share_one, e))

    def share_one(self, e, j):
        before, _, way = self.along(e)
        block = self.out.at[self.rows(self.b, e, j)]

        @pl.when(way < self.na - 1)
        def _():
            arrived(block, self.s3.at[e, j], self.r3.at[e, j], self.me)

        @pl.when(way > 0)
        def _():
            remote(block, block, self.s3.at[e, j], self.r3.at[e, j], before).start()

        remote(block, block, self.s4.at[e, j], self.r4.at[e, j], self.pair).start()

    def end_add(self):
        for j in range(self.PARTS):
            for e in range(2):
                _, after, way = self.along(e)
                self.to_pair(e, j).wait_send()
                stage = self.stage.at[self.rows(0, e, j)]
                sent = remote(stage, stage, self.s2.at[e, j], self.r2.at[e, j], after)
                pl.when(way < self.na - 1)(sent.wait_send)

    def end_share(self):
        for j in range(self.PARTS):
            for e in range(2):
                block = self.out.at[self.rows(1 - self.b, e, j)]
                arrived(block, self.s4.at[e, j], self.r4.at[e, j], self.me)
        for j in range(self.PARTS):
            for e in range(2):
                before, _, way = self.along(e)
                block = self.out.at[self.rows(self.b, e, j)]
                sent = remote(block, block, self.s3.at[e, j], self.r3.at[e, j], before)
                pl.when(way > 0)(sent.wait_send)
                remote(block, block, self.s4.at[e, j], self.r4.at[e, j], self.pair).wait_send()


def self_attention_kernel(
    nt, u, q_ref, kv_ref, home, qo, kvo, mixed_out, lse, top, total, mixed, low,
    qs, qr, ks, kr, fs, fr, hs, hr, own
):
    t, s, nb, a, b, a_peer, b_peer, peers = deal(nt, u)
    me = (t, s)
    batch, length = q_ref.shape[0], q_ref.shape[2]
    copies = Copies()
    qo[a] = q_ref[:, pl.ds(pl.multiple_of(a * HD, HD), HD), :]
    local = [pltpu.make_async_copy(lanes_of(kv_ref, a, 2 * HD), kvo.at[t], own.at[0])]
    local[0].start()
    greet(peers)
    for k in range(1, u):
        block = rows_of(q_ref, lax.rem(a + k, u), HD)
        copies.send(block, qo.at[a], qs.at[k], qr.at[k], a_peer(k))
    for k in range(1, u):
        block = lanes_of(kv_ref, lax.rem(a + k, u), 2 * HD)
        copies.send(block, kvo.at[t], ks.at[k], kr.at[k], a_peer(k))
    for m in range(1, nb):
        block = lanes_of(kv_ref, a, 2 * HD)
        copies.send(block, kvo.at[t], fs.at[0, m], fr.at[0, m], b_peer(m))
    clear(total, mixed)
    top[...] = jnp.full(top.shape, -jnp.inf, f32)

    def take(tile, i, n):
        q = qo[i, n] * 0.125
        padded = jnp.concatenate([q, jnp.zeros_like(q)], axis=0)
        keys = kvo[tile, n]
        scores = dot(keys, padded)
        new = jnp.maximum(top[i, n], jnp.max(scores, axis=0, keepdims=True))
        raised = jnp.exp(scores - new)
        scale = jnp.exp(top[i, n] - new)
        added = dot(keys.T[HD:], raised.astype(bf16))
        return (
            new,
            total[i, n] * scale + jnp.sum(raised, axis=0, keepdims=True),
            mixed[i, n] * scale + added,
        )

    def take_all(tile):
        for n in range(batch):
            for i in range(u):
                top[i, n], total[i, n], mixed[i, n] = take(tile, i, n)

    def tile_of(k, m):
        return lax.rem(a + u - k, u) * nb + lax.rem(b + nb - m, nb)

    for k in range(1, u):
        arrived(qo.at[lax.rem(a + u - k, u)], qs.at[k], qr.at[k], me)
    local[0].wait()
    near_first = sorted(range(1, u), key=lambda k: min(k, u - k))
    order = [(0, m) for m in range(nb)] + [(k, 0) for k in near_first]
    order += [(k, m) for k in near_first for m in range(1, nb)]
    for k, m in order[:-1]:
        tile = tile_of(k, m)
        if m:
            arrived(kvo.at[tile], fs.at[k, m], fr.at[k, m], me)
        elif k:
            arrived(kvo.at[tile], ks.at[k], kr.at[k], me)
            for n in range(1, nb):
                block = kvo.at[tile]
                copies.send(block, block, fs.at[k, n], fr.at[k, n], b_peer(n))
        take_all(tile)
    k, m = order[-1]
    tile = tile_of(k, m)
    if m:
        arrived(kvo.at[tile], fs.at[k, m], fr.at[k, m], me)
    elif k:
        arrived(kvo.at[tile], ks.at[k], kr.at[k], me)
    for k in list(range(1, u)) + [0]:
        i = lax.rem(a + k, u)
        for n in range(batch):
            peak, weight, value = take(tile, i, n)
            value = value / weight
            mixed_out[i, n] = value
            low[i, n] = value.astype(bf16)
            lse[i, n] = peak + jnp.log(weight)
        if k:
            copies.send(low.at[i], rows_of(home, a, HD), hs.at[k], hr.at[k], a_peer(k))
        else:
            local.append(pltpu.make_async_copy(low.at[i], rows_of(home, a, HD), own.at[1]))
            local[1].start()
    for k in range(1, u):
        arrived(rows_of(home, lax.rem(a + u - k, u), HD), hs.at[k], hr.at[k], me)
    local[1].wait()
    copies.finish()


def self_attention(q, kv, cid):
    nt = lax.axis_size("tile")
    batch, width, length = q.shape
    u = width // HD
    nb = nt // u
    shape = jax.ShapeDtypeStruct
    dealt = (u, batch, HD, length)
    return pl.pallas_call(
        functools.partial(self_attention_kernel, nt, u),
        out_shape=(
            shape(q.shape, bf16),
            shape(dealt, bf16),
            shape((nt, batch, length, 2 * HD), bf16),
            shape(dealt, f32),
            shape((u, batch, 1, length), f32),
        ),
        in_specs=[in_vmem()] * 2,
        out_specs=(in_vmem(),) * 5,
        scratch_shapes=[
            pltpu.VMEM((u, batch, 1, length), f32),
            pltpu.VMEM((u, batch, 1, length), f32),
            pltpu.VMEM(dealt, f32),
            pltpu.VMEM(dealt, bf16),
        ]
        + [dma(u) for _ in range(4)]
        + [dma(u, nb) for _ in range(2)]
        + [dma(u) for _ in range(2)]
        + [dma(2)],
        cost_estimate=LONG,
        compiler_params=params(cid, 24),
        name="self_attention",
    )(q, kv)


class Nothing:
    def __getattr__(self, name):
        return lambda *args: None


class FullSum:
    def __init__(self, nt, ns, copies, x, out, got1, stage, got2, mine, got3, sems):
        t, s = lax.axis_index("tile"), lax.axis_index("sub")
        self.nt, self.far, self.copies, self.x, self.out = nt, ns // 2, copies, x, out
        self.got1, self.stage, self.got2, self.mine, self.got3 = got1, stage, got2, mine, got3
        self.t, self.s, self.r, self.c = t, s, s // 2, lax.rem(s, 2)
        self.me, self.twin = (t, s), (t, self.r * 2 + 1 - self.c)
        self.part = x.shape[0] // ns
        self.piece = self.part // nt
        (self.s1, self.r1, self.s2, self.r2, self.s3, self.r3) = sems[:6]
        (self.s4, self.r4, self.s5, self.r5, self.s6, self.r6) = sems[6:]

    @staticmethod
    def scratch(nt, ns, rows, width):
        far, part = ns // 2, rows // ns
        return (
            [pltpu.VMEM((far, part, width), bf16) for _ in range(3)]
            + [pltpu.VMEM((part, width), bf16), pltpu.VMEM((nt, part // nt, width), bf16)]
            + [dma(far) for _ in range(4)]
            + [dma(nt) for _ in range(4)]
            + [dma(far) for _ in range(4)]
        )

    def rows(self, r, c):
        return pl.ds(pl.multiple_of((c * self.far + r) * self.part, 16), self.part)

    def slot(self, t):
        return pl.ds(pl.multiple_of(t * self.piece, 16), self.piece)

    def other(self, k):
        return lax.rem(self.r + k, self.far)

    def tile(self, k):
        return lax.rem(self.t + k, self.nt)

    def start(self):
        for k in list(range(1, self.far)) + [0]:
            src = self.x.at[self.rows(self.other(k), 1 - self.c)]
            self.copies.send(src, self.got1.at[k], self.s1.at[k], self.r1.at[k], self.twin)

    def cross(self):
        for k in range(1, self.far):
            arrived(self.got1.at[k], self.s1.at[k], self.r1.at[k], self.me)
            own = self.x[self.rows(self.other(k), self.c)].astype(f32)
            self.stage[k] = (own + self.got1[k].astype(f32)).astype(bf16)
            peer = (self.t, self.other(k) * 2 + self.c)
            self.copies.send(self.stage.at[k], self.got2.at[k], self.s2.at[k], self.r2.at[k], peer)

    def spread(self):
        arrived(self.got1.at[0], self.s1.at[0], self.r1.at[0], self.me)
        total = self.x[self.rows(self.r, self.c)].astype(f32) + self.got1[0].astype(f32)
        for k in range(1, self.far):
            arrived(self.got2.at[k], self.s2.at[k], self.r2.at[k], self.me)
            total = total + self.got2[k].astype(f32)
        self.mine[...] = total.astype(bf16)
        for k in range(1, self.nt):
            p = self.tile(k)
            src = self.mine.at[self.slot(p)]
            self.copies.send(src, self.got3.at[k], self.s3.at[k], self.r3.at[k], (p, self.s))

    def place(self, t, r, c):
        start = (c * self.far + r) * self.part + t * self.piece
        return pl.ds(pl.multiple_of(start, 16), self.piece)

    def settle(self):
        total = self.mine[self.slot(self.t)].astype(f32)
        for k in range(1, self.nt):
            arrived(self.got3.at[k], self.s3.at[k], self.r3.at[k], self.me)
            total = total + self.got3[k].astype(f32)
        here = self.place(self.t, self.r, self.c)
        self.out[here] = total.astype(bf16)
        block = self.out.at[here]
        for k in range(1, self.nt):
            self.copies.send(block, block, self.s4.at[k], self.r4.at[k], (self.tile(k), self.s))

    def share(self):
        for k in range(1, self.nt):
            block = self.out.at[self.place(self.tile(self.nt - k), self.r, self.c)]
            arrived(block, self.s4.at[k], self.r4.at[k], self.me)
        block = self.out.at[self.rows(self.r, self.c)]
        for k in range(1, self.far):
            peer = (self.t, self.other(k) * 2 + self.c)
            self.copies.send(block, block, self.s5.at[k], self.r5.at[k], peer)
        self.copies.send(block, block, self.s6.at[0], self.r6.at[0], self.twin)

    def relay(self):
        for k in range(1, self.far):
            block = self.out.at[self.rows(self.other(self.far - k), self.c)]
            arrived(block, self.s5.at[k], self.r5.at[k], self.me)
            self.copies.send(block, block, self.s6.at[k], self.r6.at[k], self.twin)

    def end(self):
        for k in range(self.far):
            block = self.out.at[self.rows(self.other(self.far - k), 1 - self.c)]
            arrived(block, self.s6.at[k], self.r6.at[k], self.me)


def attention_back_kernel(
    nt, ns, u, d_ref, q_ref, of_ref, lse_ref, kv_ref, mixed_t, grad_attn, early_ref, beside_ref,
    qo, kvo, early_out, beside_out,
    dealt, qd, rows, delta, acc, low, sent, kept, got, stage, mine,
    ds, dr, fs, fr, ks, kr, qs, qr, own, *scratch
):
    t, s, nb, a, b, a_peer, b_peer, peers = deal(nt, u)
    me = (t, s)
    batch, length = d_ref.shape[0], d_ref.shape[2]
    copies = Copies()
    early = TileSum(nt, mine, early_out, scratch[:3], scratch[3:7], None)
    beside = SubScatter(ns, copies, beside_ref, *scratch[7:10], scratch[10:])
    steps = list(early.steps())
    clear(early_out)
    greet_all(nt, ns)
    dealt[a] = d_ref[:, pl.ds(pl.multiple_of(a * HD, HD), HD), :]
    for k in range(1, u):
        block = rows_of(d_ref, lax.rem(a + k, u), HD)
        copies.send(block, dealt.at[a], ds.at[k], dr.at[k], a_peer(k))
    features = mixed_t.shape[0]
    mine[pl.ds(0, features), :] = dot(mixed_t[...], grad_attn[...]).astype(bf16)
    mine[pl.ds(features, 2 * features), :] = early_ref[...]
    spare = mine.shape[0] - 3 * features
    if spare:
        mine[pl.ds(3 * features, spare), :] = jnp.zeros((spare, mine.shape[1]), bf16)
    early.start()
    beside.start()

    def prepare(i):
        for n in range(batch):
            q, d = q_ref[i, n], dealt[i, n]
            zero = jnp.zeros_like(q)
            qd[i, n, 0] = jnp.concatenate([q * 0.125, zero], axis=0)
            qd[i, n, 1] = jnp.concatenate([zero, d], axis=0)
            rows[i, n, 0] = qd[i, n, 0].T
            rows[i, n, 1] = qd[i, n, 1].T
            delta[i, n] = jnp.sum(d.astype(f32) * of_ref[i, n], axis=0, keepdims=True)

    clear(acc)
    for k in range(u):
        i = lax.rem(a + u - k, u)
        if k:
            arrived(dealt.at[i], ds.at[k], dr.at[k], me)
        prepare(i)

    def work(tile, n):
        kv = kv_ref[tile, n]
        kt = kv.T[:HD]
        total = jnp.zeros(kv.shape, f32)
        for i in range(u):
            probs = jnp.exp(dot(kv, qd[i, n, 0]) - lse_ref[i, n])
            slope = dot(kv, qd[i, n, 1])
            grads = (probs * (slope - delta[i, n])).astype(bf16)
            total = total + dot(probs.astype(bf16), rows[i, n, 1]) + dot(grads, rows[i, n, 0])
            acc[i, n] += dot(kt, grads)
        return total

    def settle(k):
        for n in range(batch):
            total = kept[k, n]
            for m in range(1, nb):
                if n == 0:
                    arrived(got.at[m, k], fs.at[k, m], fr.at[k, m], me)
                total = total + got[m, k, n].astype(f32)
            stage[k, n] = total.astype(bf16)
        if k:
            copies.send(stage.at[k], lanes_of(kvo, a, 2 * HD), ks.at[k], kr.at[k], a_peer(k))

    order = list(range(1, u)) + [0]
    done = 0
    for at, k in enumerate(order):
        for m in range(1, nb):
            tile = lax.rem(a + k, u) * nb + lax.rem(b + m, nb)
            for n in range(batch):
                sent[m, k, n] = work(tile, n).astype(bf16)
            copies.send(sent.at[m, k], got.at[m, k], fs.at[k, m], fr.at[k, m], b_peer(m))
        if at == min(1, u - 1):
            beside.cross()
        for n in range(batch):
            kept[k, n] = work(lax.rem(a + k, u) * nb + b, n)
        if at:
            settle(order[at - 1])
            early.add(steps[done : done + 2])
            done += 2
    for k in list(range(1, u)) + [0]:
        i = lax.rem(a + k, u)
        for n in range(batch):
            low[i, n] = (acc[i, n] * 0.125).astype(bf16)
        if k:
            copies.send(low.at[i], rows_of(qo, a, HD), qs.at[k], qr.at[k], a_peer(k))
    local = [pltpu.make_async_copy(low.at[a], rows_of(qo, a, HD), own.at[0])]
    local[0].start()
    beside.end(beside_out)
    settle(order[-1])
    local.append(pltpu.make_async_copy(stage.at[0], lanes_of(kvo, a, 2 * HD), own.at[1]))
    local[1].start()
    early.add(steps[done:])
    early.end_add()
    for k in range(1, u):
        i = lax.rem(a + u - k, u)
        arrived(rows_of(qo, i, HD), qs.at[k], qr.at[k], me)
        arrived(lanes_of(kvo, i, 2 * HD), ks.at[k], kr.at[k], me)
    for copy in local:
        copy.wait()
    copies.finish()


def attention_back(d, q, of, lse, kv, mixed_t, grad_attn, early, beside, cid):
    nt, ns = lax.axis_size("tile"), lax.axis_size("sub")
    u, batch, _, length = q.shape
    nb = nt // u
    block = (batch, length, 2 * HD)
    sums = (round_up(3 * u * HD, 16 * nt), grad_attn.shape[1])
    beside = beside.reshape(ns, -1, beside.shape[1])
    shape = jax.ShapeDtypeStruct
    return pl.pallas_call(
        functools.partial(attention_back_kernel, nt, ns, u),
        out_shape=(
            shape(d.shape, bf16),
            shape((batch, length, u * 2 * HD), bf16),
            shape(sums, bf16),
            shape(beside.shape[1:], f32),
        ),
        in_specs=[in_vmem()] * 9,
        out_specs=(in_vmem(),) * 4,
        scratch_shapes=[
            pltpu.VMEM(q.shape, bf16),
            pltpu.VMEM((u, batch, 2, 2 * HD, length), bf16),
            pltpu.VMEM((u, batch, 2, length, 2 * HD), bf16),
            pltpu.VMEM((u, batch, 1, length), f32),
            pltpu.VMEM(q.shape, f32),
            pltpu.VMEM(q.shape, bf16),
            pltpu.VMEM((nb, u) + block, bf16),
            pltpu.VMEM((u,) + block, f32),
            pltpu.VMEM((nb, u) + block, bf16),
            pltpu.VMEM((u,) + block, bf16),
            pltpu.VMEM(sums, bf16),
            dma(u),
            dma(u),
            dma(u, nb),
            dma(u, nb),
            dma(u),
            dma(u),
            dma(u),
            dma(u),
            dma(2),
        ]
        + TileSum.buffers(*sums)
        + TileSum.sems()
        + SubScatter.scratch(ns, *beside.shape[1:]),
        cost_estimate=SHORT,
        compiler_params=params(cid, 40),
        name="attention_back",
    )(d, q, of, lse, kv, mixed_t, grad_attn, early, beside)


AROUND = [(-1, 0), (1, 0), (0, -1), (0, 1), (-1, -1), (-1, 1), (1, -1), (1, 1)]
DIAGONAL = AROUND[4:]


def present(nt, ns, t, s, dt, ds):
    y, x = t + dt, s + ds
    return (y >= 0) & (y < nt) & (x >= 0) & (x < ns)


def greet_all(nt, ns):
    t, s = lax.axis_index("tile"), lax.axis_index("sub")
    barrier = pltpu.get_barrier_semaphore()
    for k in range(1, ns):
        peer = (t, lax.rem(s + k, ns))
        pl.semaphore_signal(barrier, inc=1, device_id=peer, device_id_type=MESH)
    for k in range(1, nt):
        peer = (lax.rem(t + k, nt), s)
        pl.semaphore_signal(barrier, inc=1, device_id=peer, device_id_type=MESH)
    count = ns + nt - 2
    for dt, ds in DIAGONAL:
        there = present(nt, ns, t, s, dt, ds)
        count = count + jnp.where(there, 1, 0)

        @pl.when(there)
        def _():
            pl.semaphore_signal(
                barrier, inc=1, device_id=(t + dt, s + ds), device_id_type=MESH
            )

    pl.semaphore_wait(barrier, count)


def border_copies(nt, ns, src, top, bottom, left, right, ss, rs):
    t, s = lax.axis_index("tile"), lax.axis_index("sub")
    rows, cols = src.shape[0], src.shape[1]
    high, low = pl.ds(0, 2), pl.ds(rows - 2, 2)
    first, last = pl.ds(0, 16), pl.ds(cols - 16, 16)
    inner, before, after = pl.ds(2, rows), pl.ds(0, 2), pl.ds(rows + 2, 2)
    pairs = [
        (src.at[high], bottom),
        (src.at[low], top),
        (src.at[:, first], right.at[inner]),
        (src.at[:, last], left.at[inner]),
        (src.at[high, first], right.at[after]),
        (src.at[high, last], left.at[after]),
        (src.at[low, first], right.at[before]),
        (src.at[low, last], left.at[before]),
    ]
    copies = []
    for i, (dt, ds) in enumerate(AROUND):
        out = present(nt, ns, t, s, dt, ds)
        back = present(nt, ns, t, s, -dt, -ds)
        copies.append((out, back, remote(*pairs[i], ss.at[i], rs.at[i], (t + dt, s + ds))))
    return copies


def begin(copies):
    for out, _, copy in copies:
        pl.when(out)(copy.start)


def finish(copies):
    for out, back, copy in copies:
        pl.when(back)(copy.wait_recv)
        pl.when(out)(copy.wait_send)


def sum_near(nt, ns, value, first, ss, rs):
    t, s = lax.axis_index("tile"), lax.axis_index("sub")
    first[s] = value
    copies = []
    for k in range(1, ns):
        peer = (t, lax.rem(s + k, ns))
        copies.append(remote(first.at[s], first.at[s], ss.at[k], rs.at[s], peer))
        copies[-1].start()
    return copies


def sum_far(nt, ns, first, second, ss1, rs1, ss2, rs2):
    t, s = lax.axis_index("tile"), lax.axis_index("sub")
    for k in range(1, ns):
        p = lax.rem(s + k, ns)
        arrived(first.at[p], ss1.at[k], rs1.at[p], (t, s))
    total = first[0]
    for k in range(1, ns):
        total = total + first[k]
    second[t] = total
    copies = []
    for k in range(1, nt):
        peer = (lax.rem(t + k, nt), s)
        copies.append(remote(second.at[t], second.at[t], ss2.at[k], rs2.at[t], peer))
        copies[-1].start()
    return copies


def sum_end(nt, second, ss2, rs2):
    t, s = lax.axis_index("tile"), lax.axis_index("sub")
    for k in range(1, nt):
        p = lax.rem(t + k, nt)
        arrived(second.at[p], ss2.at[k], rs2.at[p], (t, s))
    total = second[0]
    for k in range(1, nt):
        total = total + second[k]
    return total


def sum_scratch(nt, ns, channels, rows=2):
    return [
        pltpu.VMEM((ns, rows, channels), f32),
        pltpu.VMEM((nt, rows, channels), f32),
        dma(ns),
        dma(ns),
        dma(nt),
        dma(nt),
    ]


def in_groups(values):
    count, channels = values.shape
    per = channels // G
    row = lax.broadcasted_iota(jnp.int32, (channels, channels), 0) // per
    col = lax.broadcasted_iota(jnp.int32, (channels, channels), 1) // per
    same = jnp.where(row == col, 1.0, 0.0).astype(bf16)
    parts, rest = [], values
    for _ in range(3):
        parts.append(rest.astype(bf16))
        rest = rest - parts[-1].astype(f32)
    out = [dot(part, same) for part in parts]
    return out[0] + out[1] + out[2]


def fold(values):
    return jnp.sum(values.reshape(-1, 8, values.shape[-1]), axis=0)


def row_sums(count, channels, pair):
    def step(i, carry):
        first, second = pair(i)
        return carry[0] + fold(first), carry[1] + fold(second)

    zero = jnp.zeros((8, channels), f32)
    first, second = lax.fori_loop(0, count, step, (zero, zero), unroll=2)
    return jnp.concatenate(
        [jnp.sum(first, axis=0, keepdims=True), jnp.sum(second, axis=0, keepdims=True)], axis=0
    )


def sigmoid(values):
    return 1.0 / (1.0 + jnp.exp(-values))


def silu_slope(values):
    sigma = sigmoid(values)
    return sigma * (1.0 + values * (1.0 - sigma))


def block_of(total, step, limit):
    return max(n for n in range(step, limit + 1, step) if total % n == 0)


def put_left_to_right(flat, triple):
    total, channels = triple.shape[0], flat.shape[1]
    size = block_of(total, 16, 256)
    for start in range(0, total, size):
        for j in range(3):
            piece = flat[pl.ds(8 + start + j - 1, size), :]
            triple[pl.ds(start, size), pl.ds(j * channels, channels)] = piece.astype(bf16)


def conv_rows(triple, weight, start, size, pitch, multiply=dot):
    taps = [triple[pl.ds(start + i * pitch, size), :] for i in range(3)]
    return multiply(jnp.concatenate(taps, axis=1), weight)


def turned_taps(weight):
    return jnp.concatenate([weight[8 - k] for k in range(9)], axis=1)


def list_length(rows, pitch):
    return 16 + rows * pitch + 16


def fill(flat, rows, cols, row_ok, left_ok, right_ok, body, ending, opening):
    pitch = cols + 16
    channels = flat.shape[1]
    place = lax.broadcasted_iota(jnp.int32, (16, channels), 0)
    flat[pl.ds(0, 8), :] = jnp.zeros((8, channels), f32)
    end = 8 + 16 + rows * pitch
    flat[pl.ds(end, 24), :] = jnp.zeros((24, channels), f32)

    def places(right_good, left_good):
        good = jnp.where(place < 8, jnp.where(right_good, 1, 0), jnp.where(left_good, 1, 0))
        return good > 0

    flat[pl.ds(8, 16), :] = jnp.where(
        places(False, left_ok & row_ok(0)), opening(), 0.0
    )

    def step(i, carry):
        start = pl.multiple_of(24 + i * pitch, 8)
        value = body(i)
        good = jnp.full(value.shape, jnp.where(row_ok(i), 1, 0), jnp.int32)
        flat[pl.ds(start, cols), :] = jnp.where(good > 0, value, 0.0)
        good = places(right_ok & row_ok(i), left_ok & row_ok(i + 1))
        flat[pl.ds(start + cols, 16), :] = jnp.where(good, ending(i), 0.0)
        return carry

    lax.fori_loop(0, rows, step, 0)


def sides(left, right, i):
    place = lax.broadcasted_iota(jnp.int32, right.shape[1:], 0)
    return jnp.where(place < 8, right[i].astype(f32), left[i + 1].astype(f32))


def outer_forward_kernel(
    nt, ns, img, w1, w2, vec, gain1, gain2, gain3, text_in, wk_in, wv_in,
    out, pooled, act1_out, act2_out, hidden, stats, gains_out, keys, values,
    body, left, right, flat, act1, act2, rowsum, gains, text, wk, wv,
    border_ss, border_rs, keep, gain_ss, gain_rs, *sums
):
    rows, cols, channels = img.shape
    pitch = cols + 16
    t, s = lax.axis_index("tile"), lax.axis_index("sub")
    sums1, sums2 = sums[:6], sums[6:]
    count = float(nt * ns * rows * cols * (channels // G))
    pairs = ((text_in, text), (wk_in, wk), (wv_in, wv))
    loads = [pltpu.make_async_copy(*pair, keep.at[2 + i]) for i, pair in enumerate(pairs)]
    clear(body, left, right)
    greet_all(nt, ns)
    top, bottom = body.at[pl.ds(0, 2)], body.at[pl.ds(rows + 2, 2)]
    border = border_copies(nt, ns, img, top, bottom, left, right, border_ss, border_rs)
    begin(border)
    pixel = lambda i: img[i].astype(f32)
    local1 = row_sums(rows, channels, lambda i: (pixel(i), pixel(i) * pixel(i)))
    copies = sum_near(nt, ns, local1, sums1[0], sums1[2], sums1[3])
    copies += sum_far(nt, ns, sums1[0], sums1[1], *sums1[2:])
    for copy in loads:
        copy.start()
    gains[s] = jnp.concatenate([gain1[...], gain2[...], gain3[...]], axis=0)
    for k in range(1, ns):
        block, peer = gains.at[s], (t, lax.rem(s + k, ns))
        copies.append(remote(block, block, gain_ss.at[k], gain_rs.at[s], peer))
        copies[-1].start()

    def inner(i, carry):
        body[i + 2] = img[i]
        return carry

    lax.fori_loop(0, rows, inner, 0)
    total1 = sum_end(nt, sums1[1], sums1[4], sums1[5])

    def moments(total):
        grouped = in_groups(total) / count
        center = grouped[0:1]
        return center, lax.rsqrt(grouped[1:2] - center * center + EPSILON)

    center1, std1 = moments(total1)
    scale1 = std1 * vec[0:1]
    shift1 = vec[1:2] - center1 * scale1
    finish(border)

    def first_act(values):
        normed = values.astype(f32) * scale1 + shift1
        return normed * sigmoid(normed)

    ok = lambda lift: (
        lambda i: (t * rows + i - lift >= 0) & (t * rows + i - lift < nt * rows)
    )
    fill(
        flat, rows + 4, cols, ok(2), s > 0, s < ns - 1,
        lambda i: first_act(body[i]),
        lambda i: first_act(sides(left, right, i)),
        lambda: first_act(left[0]),
    )
    put_left_to_right(flat, act1)
    saved = [pltpu.make_async_copy(act1, act1_out, keep.at[0])]
    saved[0].start()
    length = list_length(rows + 2, pitch)
    size = block_of(length, 16, 700)
    for start in range(0, length, size):
        hidden[pl.ds(start, size), :] = conv_rows(act1, w1[...], start, size, pitch) + vec[4:5]

    def hidden_row(i):
        return hidden[pl.ds(pl.multiple_of(16 + (i + 1) * pitch, 16), cols), :]

    local2 = row_sums(rows, channels, lambda i: (hidden_row(i), hidden_row(i) * hidden_row(i)))
    copies += sum_near(nt, ns, local2, sums2[0], sums2[2], sums2[3])
    copies += sum_far(nt, ns, sums2[0], sums2[1], *sums2[2:])
    for copy in loads:
        copy.wait()
    keys[...] = dot(text[...], wk[...]).astype(bf16)
    values[...] = dot(text[...], wv[...]).astype(bf16)
    total2 = sum_end(nt, sums2[1], sums2[4], sums2[5])
    center2, std2 = moments(total2)
    scale2 = std2 * vec[2:3]
    shift2 = vec[3:4] - center2 * scale2
    stats[...] = jnp.concatenate(
        [center1, std1, center2, std2, total2, jnp.zeros_like(total2)], axis=0
    )

    def second_act(start, amount):
        normed = hidden[pl.ds(start, amount), :] * scale2 + shift2
        return normed * sigmoid(normed)

    at = lambda i: pl.multiple_of(16 + i * pitch, 16)
    fill(
        flat, rows + 2, cols, ok(1), s > 0, s < ns - 1,
        lambda i: second_act(at(i), cols),
        lambda i: second_act(at(i) + cols, 16),
        lambda: second_act(0, 16),
    )
    put_left_to_right(flat, act2)
    saved.append(pltpu.make_async_copy(act2, act2_out, keep.at[1]))
    saved[1].start()
    lc = cols // POOL
    for start in range(0, rows, 2 * POOL):
        grown = conv_rows(act2, w2[...], 16 + start * pitch, 2 * POOL * pitch, pitch)
        grown = grown.reshape(2 * POOL, pitch, channels)[:, :cols]
        grown = grown + img[pl.ds(start, 2 * POOL)].astype(f32)
        out[pl.ds(start, 2 * POOL)] = grown.astype(bf16)
        for half in range(2):
            added = jnp.sum(grown[half * POOL : (half + 1) * POOL], axis=0)
            means = []
            for n in range(channels // 128):
                rowsum[n] = added[:, n * 128 : (n + 1) * 128]
                mean = rowsum[n, pl.ds(0, lc, stride=POOL), :]
                for k in range(1, POOL):
                    mean = mean + rowsum[n, pl.ds(k, lc, stride=POOL), :]
                means.append(mean * (1.0 / (POOL * POOL)))
            place = pl.ds((start // POOL + half) * lc, lc)
            pooled[place, :] = jnp.concatenate(means, axis=1).astype(bf16)
    for k in range(1, ns):
        p = lax.rem(s + k, ns)
        arrived(gains.at[p], gain_ss.at[k], gain_rs.at[p], (t, s))
    gains_out[...] = side_by_side([gains[i] for i in range(ns)])
    for copy in copies:
        copy.wait_send()
    for copy in saved:
        copy.wait()


def outer_forward(img, w1, w2, vec, gains, text, wk, wv, cid):
    nt, ns = lax.axis_size("tile"), lax.axis_size("sub")
    rows, cols, channels = img.shape
    pitch = cols + 16
    long1, long2 = list_length(rows + 4, pitch), list_length(rows + 2, pitch)
    shape = jax.ShapeDtypeStruct
    return pl.pallas_call(
        functools.partial(outer_forward_kernel, nt, ns),
        out_shape=(
            shape(img.shape, bf16),
            shape((rows // POOL * (cols // POOL), channels), bf16),
            shape((long1, 3 * channels), bf16),
            shape((long2, 3 * channels), bf16),
            shape((long2, channels), f32),
            shape((8, channels), f32),
            shape((3, ns * wk.shape[1]), f32),
            shape((text.shape[0], wk.shape[1]), bf16),
            shape((text.shape[0], wk.shape[1]), bf16),
        ),
        in_specs=[in_vmem()] * 7 + [anywhere()] * 3,
        out_specs=(in_vmem(),) * 2 + (anywhere(),) * 2 + (in_vmem(),) * 5,
        scratch_shapes=[
            pltpu.VMEM((rows + 4, cols, channels), bf16),
            pltpu.VMEM((rows + 5, 16, channels), bf16),
            pltpu.VMEM((rows + 5, 16, channels), bf16),
            pltpu.VMEM((long1 + 16, channels), f32),
            pltpu.VMEM((long1, 3 * channels), bf16),
            pltpu.VMEM((long2, 3 * channels), bf16),
            pltpu.VMEM((channels // 128, cols, 128), f32),
            pltpu.VMEM((ns, 3, wk.shape[1]), f32),
            pltpu.VMEM(text.shape, bf16),
            pltpu.VMEM(wk.shape, bf16),
            pltpu.VMEM(wv.shape, bf16),
            dma(8),
            dma(8),
            dma(5),
            dma(ns),
            dma(ns),
        ]
        + sum_scratch(nt, ns, channels) * 2,
        cost_estimate=LONG,
        compiler_params=params(cid),
        name="outer_forward",
    )(img, w1, w2, vec, *gains, text, wk, wv)


def kernel_grads(triple, grads_t, start, size, pitch, out, between=()):
    for i in range(3):
        rows = triple[pl.ds(start + i * pitch, size), :]
        taps = dot(grads_t[...], rows).T.astype(bf16)
        out[pl.ds(i * taps.shape[0], taps.shape[0]), :] = taps
        for action in between[i : i + 1]:
            action()


def outer_backward_kernel(
    nt, ns, cut, cot, img, w2, w1, vec, stats, hidden, wide, tokens, gains, pooled, lifted, lift_weight,
    attn_in, grad_q_t, grad_kv, grad_ck, grad_cv, act1_in, act2_in, outer_grad, tall_out, wide_out, tokens_out, sum2_out, sum1_out, back_out,
    spread, grad2, body, left, right, flat, act1, act2, triple, inner_t, slope, own2, own1, tall,
    border_ss, border_rs, keep, token_ss, token_rs, *scratch
):
    rows, cols, channels = img.shape
    pitch = cols + 16
    lr, lc = rows // POOL, cols // POOL
    t, s = lax.axis_index("tile"), lax.axis_index("sub")
    sums2, sums1, scratch = scratch[:6], scratch[6:12], scratch[12:]
    copies = Copies()
    early = TileSum(nt, None, wide_out, None, None, scratch[:4])
    late = TileSum(nt, tall, tall_out, scratch[4:7], scratch[7:11], scratch[11:15])
    scratch = scratch[15:]
    wide_out[...] = wide[...]
    second = FullSum(nt, ns, copies, own2, sum2_out, *scratch[:5], scratch[5:17])
    scratch = scratch[17:]
    first, rest = Nothing(), []
    for skip, rows_of_sum in ((0, cut), (cut, own1.shape[0] - cut)):
        if rows_of_sum:
            part = pl.ds(skip, rows_of_sum)
            views = own1.at[part], sum1_out.at[part]
            rest.append(FullSum(nt, ns, copies, *views, *scratch[:5], scratch[5:17]))
            scratch = scratch[17:]
    if len(rest) > 1:
        first = rest[0]
    rest = rest[-1]
    count = float(nt * ns * rows * cols * (channels // G))
    held = [
        pltpu.make_async_copy(act2_in, act2, keep.at[0]),
        pltpu.make_async_copy(act1_in, act1, keep.at[1]),
    ]
    for copy in held:
        copy.start()
    clear(body, left, right)
    greet_all(nt, ns)
    width = lifted.shape[1]
    shrunk = dot_t(lifted[...], lift_weight[...]) * (1.0 / (POOL * POOL))

    def widen(i):
        for n in range(channels // 128):
            part = shrunk[i * lc : (i + 1) * lc, n * 128 : (n + 1) * 128]
            for k in range(POOL):
                spread[i, n, pl.ds(k, lc, stride=POOL), :] = part

    for i in range(lr):
        widen(i)

    def outer(i):
        parts = [spread[i // POOL, n] for n in range(channels // 128)]
        return cot[i].astype(f32) + jnp.concatenate(parts, axis=1)

    def round_outer(i, carry):
        value = outer(i).astype(bf16)
        grad2[i] = value
        body[i + 2] = value
        return carry

    lax.fori_loop(0, rows, round_outer, 0)
    top, bottom = body.at[pl.ds(0, 2)], body.at[pl.ds(rows + 2, 2)]
    border = border_copies(nt, ns, grad2, top, bottom, left, right, border_ss, border_rs)
    begin(border)
    tokens_out[s] = tokens[s]
    for k in range(1, ns):
        p = lax.rem(s + k, ns)
        copies.send(tokens.at[p], tokens_out.at[s], token_ss.at[k], token_rs.at[k], (t, p))
    features = grad_q_t.shape[0]
    heads = features // HD
    attn_t = attn_in[...].T
    tall[pl.ds(0, width), :] = dot_t(attn_t, grad_q_t[...]).astype(bf16)
    both = dot(attn_t, grad_kv[...])
    for n in range(2):
        lanes = [both[:, (2 * h + n) * HD : (2 * h + n + 1) * HD] for h in range(heads)]
        part = jnp.concatenate(lanes, axis=1) if heads > 1 else lanes[0]
        tall[pl.ds((1 + n) * width, width), :] = part.astype(bf16)
    used = 3 * width
    for ref in (grad_ck, grad_cv):
        tall[pl.ds(used, ref.shape[0]), :] = ref[...]
        used += ref.shape[0]
    if used < tall.shape[0]:
        tall[pl.ds(used, tall.shape[0] - used), :] = jnp.zeros(
            (tall.shape[0] - used, features), bf16
        )
    late.start()
    steps = list(early.steps())
    early.share(steps[:1])
    total = rows * pitch

    def turned(row):
        for start in range(0, rows, 8):
            block = [row(start + k) for k in range(8)]
            gap = jnp.zeros((16, channels), bf16)
            piece = jnp.concatenate([p for b in block for p in (b, gap)], axis=0)
            inner_t[:, pl.ds(start * pitch, 8 * pitch)] = piece.T

    def pad_below(ref, used):
        if used < ref.shape[0]:
            ref[pl.ds(used, ref.shape[0] - used), :] = jnp.zeros(
                (ref.shape[0] - used, channels), bf16
            )

    taps = 9 * channels
    turned(lambda i: grad2[i])
    held[0].wait()
    between = [lambda k=k: early.share(steps[k : k + 1]) for k in (1, 2, 3)]
    kernel_grads(act2, inner_t, 16, total, pitch, own2, between)
    lift_grad = dot(pooled[...].T, lifted[...]).astype(bf16)
    for n in range(width // channels):
        own2[pl.ds(taps + n * channels, channels), :] = lift_grad[
            :, n * channels : (n + 1) * channels
        ]
    pad_below(own2, taps + width)
    second.start()
    early.share(steps[4:5])
    finish(border)
    ok = lambda lift_by: (
        lambda i: (t * rows + i - lift_by >= 0) & (t * rows + i - lift_by < nt * rows)
    )
    fill(
        flat, rows + 4, cols, ok(2), s > 0, s < ns - 1,
        lambda i: body[i].astype(f32),
        lambda i: sides(left, right, i),
        lambda: left[0].astype(f32),
    )
    put_left_to_right(flat, triple)
    second.cross()
    center1, std1, center2, std2 = (stats[k : k + 1] for k in range(4))
    gain1, bias1, gain2, bias2 = (vec[k : k + 1] for k in range(4))
    length = list_length(rows + 2, pitch)
    size = block_of(length, 16, 700)
    w2t = turned_taps(w2)
    for start in range(0, length, size):
        hat = (hidden[pl.ds(start, size), :] - center2) * std2
        slope[pl.ds(start, size), :] = conv_rows(
            triple, w2t, start, size, pitch, dot_t
        ) * silu_slope(hat * gain2 + bias2)
        if start == size:
            early.share(steps[5:6])
    early.share(steps[6:])

    at = lambda i: pl.multiple_of(16 + i * pitch, 16)

    def pair2(i):
        place = pl.ds(at(i + 1), cols)
        value = slope[place, :]
        return value, value * ((hidden[place, :] - center2) * std2)

    local2 = jnp.concatenate([row_sums(rows, channels, pair2), gains[...]], axis=0)
    plain = sum_near(nt, ns, local2, sums2[0], sums2[2], sums2[3])
    plain += sum_far(nt, ns, sums2[0], sums2[1], *sums2[2:])
    second.spread()
    late.add(steps[:2])
    back2 = sum_end(nt, sums2[1], sums2[4], sums2[5])
    back2, gains_total = back2[:2], back2[2:]
    means2 = in_groups(back2 * gain2) / count

    def grad_hidden(start, amount):
        hat = (hidden[pl.ds(start, amount), :] - center2) * std2
        value = slope[pl.ds(start, amount), :] * gain2 - means2[0:1] - hat * means2[1:2]
        return std2 * value

    fill(
        flat, rows + 2, cols, ok(1), s > 0, s < ns - 1,
        lambda i: grad_hidden(at(i), cols),
        lambda i: grad_hidden(at(i) + cols, 16),
        lambda: grad_hidden(0, 16),
    )
    late.add(steps[2:3])
    turned(lambda i: flat[pl.ds(24 + (i + 1) * pitch, cols), :].astype(bf16))
    held[1].wait()
    between = [lambda: late.add(steps[3:4]), lambda: first.start(), lambda: late.add(steps[4:5])]
    kernel_grads(act1, inner_t, 16 + pitch, total, pitch, own1, between)
    pad_below(own1, taps)
    rest.start()
    second.settle()
    first.cross()
    put_left_to_right(flat, triple.at[pl.ds(0, length)])
    rest.cross()
    hat1 = lambda i: (img[i].astype(f32) - center1) * std1
    step = 2 * POOL
    w1t = turned_taps(w1)
    for start in range(0, rows, step):
        value = conv_rows(triple, w1t, 16 + start * pitch, step * pitch, pitch, dot_t)
        value = value.reshape(step, pitch, channels)[:, :cols]
        hat = (img[pl.ds(start, step)].astype(f32) - center1) * std1
        outer_grad[pl.ds(start, step)] = value * silu_slope(hat * gain1 + bias1)
        if start == step:
            late.add(steps[5:6])
    first.spread()
    late.add(steps[6:])
    late.share(steps[:1])
    local1 = row_sums(rows, channels, lambda i: (outer_grad[i], outer_grad[i] * hat1(i)))
    plain += sum_near(nt, ns, local1, sums1[0], sums1[2], sums1[3])
    rest.spread()
    plain += sum_far(nt, ns, sums1[0], sums1[1], *sums1[2:])
    late.share(steps[1:3])
    second.share()
    back1 = sum_end(nt, sums1[1], sums1[4], sums1[5])
    means1 = in_groups(back1 * gain1) / count
    first.settle()
    late.share(steps[3:4])

    def last(i, carry):
        value = outer_grad[i] * gain1 - means1[0:1] - hat1(i) * means1[1:2]
        outer_grad[i] = outer(i) + std1 * value
        return carry

    lax.fori_loop(0, rows, last, 0)
    back_out[...] = jnp.concatenate(
        [back1, back2, means2, jnp.zeros_like(means2), gains_total], axis=0
    )
    rest.settle()
    late.share(steps[4:5])
    first.share()
    late.share(steps[5:])
    second.relay()
    rest.share()
    first.relay()
    for k in range(1, ns):
        block = tokens_out.at[lax.rem(s + ns - k, ns)]
        arrived(block, token_ss.at[k], token_rs.at[k], (t, s))
    rest.relay()
    early.end_share()
    second.end()
    first.end()
    late.end_add()
    late.end_share()
    rest.end()
    copies.finish()
    for copy in plain:
        copy.wait_send()


def outer_backward(
    cot, img, w2, w1, vec, stats, hidden, wide, tokens, gains, pooled, lifted, lift_weight,
    attn_in, grad_q_t, grad_kv, grad_ck, grad_cv, act1, act2, cid
):
    nt, ns = lax.axis_size("tile"), lax.axis_size("sub")
    rows, cols, channels = img.shape
    pitch = cols + 16
    long1, long2 = list_length(rows + 4, pitch), list_length(rows + 2, pitch)
    shape = jax.ShapeDtypeStruct
    step = 16 * nt * ns
    width, features = attn_in.shape[1], grad_q_t.shape[0]
    rows2 = round_up(9 * channels + width, step)
    tall = (round_up(3 * width + 2 * grad_ck.shape[0], 16 * nt), features)
    cut = 6 * channels // step * step
    rows1 = round_up(9 * channels, step)
    return pl.pallas_call(
        functools.partial(outer_backward_kernel, nt, ns, cut),
        out_shape=(
            shape(img.shape, f32),
            shape(tall, bf16),
            shape(wide.shape, bf16),
            shape(tokens.shape, bf16),
            shape((rows2, channels), bf16),
            shape((rows1, channels), bf16),
            shape((8 + gains.shape[0], channels), f32),
        ),
        in_specs=[in_vmem()] * 18 + [anywhere()] * 2,
        out_specs=(in_vmem(),) * 7,
        scratch_shapes=[
            pltpu.VMEM((rows // POOL, channels // 128, cols, 128), f32),
            pltpu.VMEM((rows, cols, channels), bf16),
            pltpu.VMEM((rows + 4, cols, channels), bf16),
            pltpu.VMEM((rows + 5, 16, channels), bf16),
            pltpu.VMEM((rows + 5, 16, channels), bf16),
            pltpu.VMEM((long1 + 16, channels), f32),
            pltpu.VMEM((long1, 3 * channels), bf16),
            pltpu.VMEM((long2, 3 * channels), bf16),
            pltpu.VMEM((long1, 3 * channels), bf16),
            pltpu.VMEM((channels, rows * pitch), bf16),
            pltpu.VMEM((long2, channels), f32),
            pltpu.VMEM((rows2, channels), bf16),
            pltpu.VMEM((rows1, channels), bf16),
            pltpu.VMEM(tall, bf16),
            dma(8),
            dma(8),
            dma(2),
            dma(ns),
            dma(ns),
        ]
        + sum_scratch(nt, ns, channels, 2 + gains.shape[0])
        + sum_scratch(nt, ns, channels)
        + TileSum.sems()
        + TileSum.buffers(*tall)
        + TileSum.sems()
        + TileSum.sems()
        + FullSum.scratch(nt, ns, rows2, channels)
        + (FullSum.scratch(nt, ns, cut, channels) if cut else [])
        + FullSum.scratch(nt, ns, rows1 - cut, channels),
        cost_estimate=SHORT,
        compiler_params=params(cid, 62),
        name="outer_backward",
    )(
        cot, img, w2, w1, vec, stats, hidden, wide, tokens, gains, pooled, lifted, lift_weight,
        attn_in, grad_q_t, grad_kv, grad_ck, grad_cv, act1, act2,
    )


def finish_kernel(text, up, down, *refs):
    q, k, v, ck, cv, o, co, cq, second, first = refs[:10]
    lift, refs = refs[10:-13], refs[-13:]
    for src, dst in zip((q, k, v, o, co, second, first, up, down), refs[:9]):
        dst[...] = src[...].astype(f32)
    refs[9][...] = cq[...].T.astype(f32)
    turned = text[...].T
    refs[10][...] = dot(turned, ck[...])
    refs[11][...] = dot(turned, cv[...])
    refs[12][...] = jnp.concatenate([part[...].astype(f32) for part in lift], axis=1)


def finish_grads(text, up, down, tall, wide, second, first, taps, text_rows):
    features, width = tall.shape[1], wide.shape[1]
    channels = first.shape[1]
    steps = features // 32
    row = lambda size, lanes, skip=0: pl.BlockSpec((size, lanes), lambda i: (skip + i, 0))
    size = width // steps
    tall_specs = [row(size, features, n * steps) for n in range(3)]
    start = 3 * width // text_rows
    tall_specs += [
        pl.BlockSpec((text_rows, features), lambda i, n=n: (start + n, 0)) for n in range(2)
    ]
    wide_specs = [row(32, width, n * steps) for n in range(2)]
    wide_specs.append(pl.BlockSpec((features, size), lambda i: (2, i)))
    size = taps // steps
    lift_size = channels // steps
    lift_specs = [
        row(lift_size, channels, taps // lift_size + n * steps) for n in range(width // channels)
    ]
    full = text.shape[1]
    up_specs = [row(w.shape[0] // steps, w.shape[1]) for w in (up, down)]
    in_specs = [pl.BlockSpec((text.shape[0], full // steps), lambda i: (0, i))] + up_specs
    in_specs += tall_specs + wide_specs + [row(size, channels)] * 2 + lift_specs
    shape = lambda *dims: jax.ShapeDtypeStruct(dims, f32)
    return pl.pallas_call(
        finish_kernel,
        grid=(steps,),
        out_shape=(shape(width, features),) * 3
        + (shape(features, width),) * 2
        + (shape(taps, channels),) * 2
        + (shape(*up.shape), shape(*down.shape), shape(width, features))
        + (shape(full, features), shape(full, features), shape(channels, width)),
        in_specs=in_specs,
        out_specs=[row(width // steps, features)] * 3
        + [row(32, width)] * 2
        + [row(size, channels)] * 2
        + up_specs
        + [row(width // steps, features)]
        + [row(full // steps, features)] * 2
        + [row(lift_size, width)],
        cost_estimate=SHORT,
        compiler_params=params(),
        name="finish_grads",
    )(text, up, down, *[tall] * 5, *[wide] * 3, second, first, *[second] * len(lift_specs))


def time_embed(time_steps, channels):
    half_width = channels // 2
    frequency = jnp.exp(
        -math.log(10000.0) * jnp.arange(half_width).astype(f32) / half_width
    )
    angles = time_steps.astype(f32)[:, None] * frequency[None, :]
    return jnp.concatenate([jnp.sin(angles), jnp.cos(angles)], axis=1)


def weight_grad(inputs, grads):
    return lax.dot_general(inputs, grads, (((0,), (0,)), ((), ())), preferred_element_type=f32)


def local(
    outer_image,
    inner_image,
    text_states,
    time_steps,
    text_lengths,
    first_gain,
    first_bias,
    conv_first,
    time_weight,
    second_gain,
    second_bias,
    conv_second,
    lift_weight,
    attn_gain,
    query_weight,
    key_weight,
    value_weight,
    out_weight,
    cross_gain,
    cross_query,
    cross_key,
    cross_value,
    cross_out,
    mlp_gain,
    up_weight,
    down_weight,
    outer_cotan,
    inner_cotan,
):
    nt, ns = lax.axis_size("tile"), lax.axis_size("sub")
    s = lax.axis_index("sub")
    batch, rows, cols, channels = outer_image.shape
    lr, lc = rows // POOL, cols // POOL
    width = inner_image.shape[2] * ns
    features = inner_image.shape[2]
    heads = features // HD
    own = batch * lr * lc
    length = ns * lr * lc
    pixels = rows * cols * nt * ns


    def whole_tokens(values):
        full = lax.all_gather(values, "sub", axis=2, tiled=True)
        return full.reshape(batch, lr, ns, lc, width)

    inner_own, cotan_full = whole_tokens(inner_image), whole_tokens(inner_cotan)
    if batch == 1 and lc % 16 == 0:
        inner_own, cotan_full = inner_own[0], cotan_full[0]
    else:
        inner_own = lax.dynamic_index_in_dim(inner_own, s, 2, keepdims=False)
        inner_own = inner_own.reshape(own, width)
        cotan_full = jnp.transpose(cotan_full, (2, 0, 1, 3, 4)).reshape(ns, own, width)
    own_gains = [v.reshape(1, features) for v in (attn_gain, cross_gain, mlp_gain)]

    time_act = jax.nn.silu(time_embed(time_steps, channels))
    time_shift = jnp.dot(time_act, time_weight.astype(f32), precision=precise)
    fixed = jnp.stack([first_gain, first_bias, second_gain, second_bias])
    fixed = jnp.broadcast_to(fixed[None], (batch, 4, channels))
    empty = jnp.zeros((batch, 3, channels), f32)
    vectors = jnp.concatenate([fixed, time_shift[:, None, :], empty], axis=1)
    as_rows = lambda w: w.reshape(9 * channels, channels)
    text_rows = batch * text_states.shape[1]
    text = text_states.reshape(text_rows, -1)
    forward = [
        outer_forward(
            outer_image[b],
            as_rows(conv_first),
            as_rows(conv_second),
            vectors[b],
            own_gains,
            text,
            cross_key,
            cross_value,
            20 + b,
        )
        for b in range(batch)
    ]
    outer_out = jnp.stack([f[0] for f in forward])
    gains, cross_k, cross_v = forward[0][6:]
    pooled = jnp.concatenate([f[1] for f in forward], axis=0)

    flat = lambda v: v.reshape(-1, v.shape[-1])
    block, rows_all = ((own, width), f32), ((ns, own, width), bf16)
    stream_in, attn_in, query_t, kv = chain_call(
        enter_kernel,
        "enter",
        2,
        (
            block,
            rows_all,
            ((features, ns * own), bf16),
            ((ns * own, 2 * features), bf16),
        ),
        (inner_own, pooled, lift_weight, gains, query_weight, key_weight, value_weight),
        (),
        False,
        vmem=24,
        cost=LONG,
    )
    attn_in = flat(attn_in)

    def per_sample(values, tokens_last):
        if tokens_last:
            values = values.reshape(-1, ns, batch, lr * lc)
            return jnp.transpose(values, (2, 0, 1, 3)).reshape(batch, -1, length)
        values = values.reshape(ns, batch, lr * lc, -1)
        return jnp.transpose(values, (1, 0, 2, 3)).reshape(batch, length, -1)

    def all_samples(values, tokens_last):
        if tokens_last:
            values = values.reshape(batch, -1, ns, lr * lc)
            return jnp.transpose(values, (1, 2, 0, 3)).reshape(-1, ns * own)
        values = values.reshape(batch, ns, lr * lc, -1)
        return jnp.transpose(values, (1, 0, 2, 3)).reshape(ns * own, -1)

    mixed_t, head_q, head_kv, head_mixed_f, head_lse = self_attention(
        per_sample(query_t, True), per_sample(kv, False), 3
    )
    mixed_t = all_samples(mixed_t, True)
    after_attn, cross_in = chain_call(
        attn_out_kernel,
        "attn_out",
        5,
        (block, rows_all),
        (mixed_t, out_weight, stream_in, gains),
        [pltpu.VMEM((ns * own, features), bf16)],
        True,
        cost=LONG,
    )
    sample_of = lambda count: jnp.arange(batch * count) // count
    text_at = jnp.tile(jnp.arange(text_states.shape[1]), batch)
    good = text_at < jnp.repeat(text_lengths, text_states.shape[1])
    same = sample_of(lr * lc)[:, None] == sample_of(text_states.shape[1])[None, :]
    mask = jnp.where(same & good[None, :], 1.0, 0.0).astype(f32)
    head_rows = ((ns, own, features), bf16)
    after_cross, mlp_in, cross_q, cross_mixed = chain_call(
        cross_kernel,
        "cross",
        6,
        (block, rows_all, head_rows, head_rows),
        (cross_in, cross_query, cross_k, cross_v, mask, cross_out, after_attn, gains),
        (),
        True,
        cost=LONG,
    )

    units = up_weight.shape[1]
    one_row = ((1, width), f32)
    middle = pltpu.VMEM((ns * own, units), bf16)
    grad_after_cross, grad_cross_full, grad_mlp_gain, down, grad_up, grad_down = chain_call(
        mlp_kernel,
        "mlp",
        8,
        (
            block,
            rows_all,
            one_row,
            ((ns * own, width), bf16),
            ((width, units), bf16),
            ((units, width), bf16),
        ),
        (mlp_in, cotan_full, up_weight, down_weight, after_cross, gains),
        [middle, middle, pltpu.VMEM((ns, own, width), bf16)],
        True,
        vmem=56,
    )
    grad_down, grad_up = lax.psum((grad_down, grad_up), "tile")
    text_block = ((text_rows, features), bf16)
    (
        grad_after_attn,
        grad_attn_full,
        grad_cross_gain,
        grad_ck,
        grad_cv,
        grad_early,
    ) = chain_call(
        cross_back_kernel,
        "cross_back",
        10,
        (
            block,
            rows_all,
            one_row,
            text_block,
            text_block,
            ((2, features, width), bf16),
        ),
        (
            grad_cross_full,
            cross_out,
            cross_q,
            cross_k,
            cross_v,
            mask,
            cross_query,
            after_attn,
            gains,
            grad_after_cross,
            cross_in,
            cross_mixed,
        ),
        [pltpu.VMEM((text_rows, features), f32)] * 2
        + [pltpu.VMEM((ns * own, features), bf16)],
        True,
        vmem=56,
    )
    grad_attn_full = flat(grad_attn_full)
    grad_mixed_t = dot_t(out_weight, grad_attn_full).astype(bf16)
    grad_q_t, grad_kv, wide, down_own = attention_back(
        per_sample(grad_mixed_t, True),
        head_q,
        head_mixed_f,
        head_lse,
        head_kv,
        mixed_t,
        grad_attn_full,
        grad_early.reshape(2 * features, width),
        down,
        13,
    )
    grad_q_t, grad_kv = all_samples(grad_q_t, True), all_samples(grad_kv, False)
    grad_lifted, grad_attn_gain = chain_call(
        attn_back_kernel,
        "attn_back",
        15,
        (((own, width), bf16), one_row),
        (
            grad_q_t,
            grad_kv,
            query_weight,
            key_weight,
            value_weight,
            stream_in,
            gains,
            grad_after_attn,
        ),
        [
            pltpu.VMEM((ns * own, features), bf16),
            pltpu.VMEM((width, 2 * features), bf16),
            pltpu.VMEM((own, width), f32),
        ],
        True,
        False,
    )

    inner_sum = after_cross + down_own
    tokens = jnp.stack([inner_sum.astype(bf16), grad_lifted])
    tokens = tokens.reshape(2, own, ns, features).transpose(2, 0, 1, 3)
    gain_rows = jnp.stack([grad_attn_gain, grad_cross_gain, grad_mlp_gain]).reshape(-1, channels)
    by_tap = lambda w: w.reshape(9, channels, channels)
    backward = []
    for b in range(batch):
        once = (lambda v: v) if b == 0 else jnp.zeros_like
        sample = lambda v: v.reshape(batch, lr * lc, -1)[b]
        backward.append(
            outer_backward(
                outer_cotan[b],
                outer_image[b],
                by_tap(conv_second),
                by_tap(conv_first),
                vectors[b],
                forward[b][5],
                forward[b][4],
                once(wide),
                once(tokens),
                once(gain_rows),
                sample(pooled),
                sample(grad_lifted),
                lift_weight,
                attn_in,
                once(grad_q_t),
                once(grad_kv),
                once(grad_ck),
                once(grad_cv),
                forward[b][2],
                forward[b][3],
                20 + batch + b,
            )
        )
    outer_grad = jnp.stack([f[0] for f in backward])
    tall, wide, tokens = backward[0][1:4]
    tokens = tokens.reshape(ns, 2, batch, lr, lc, features).transpose(1, 2, 3, 0, 4, 5)
    inner_out, inner_grad = tokens.reshape(2, batch, length, features)
    inner_grad = inner_grad.astype(f32)
    if batch > 1:
        sum2, sum1 = (
            sum(f[k].astype(f32) for f in backward).astype(bf16) for k in (4, 5)
        )
    else:
        sum2, sum1 = backward[0][4:6]
    ends = finish_grads(
        text,
        grad_up,
        grad_down,
        tall,
        wide,
        sum2,
        sum1,
        9 * channels,
        text_rows,
    )
    grad_q_w, grad_k_w, grad_v_w, grad_o_w, grad_co_w = ends[:5]
    grad_conv_second, grad_conv_first = (v.reshape(conv_first.shape) for v in ends[5:7])
    grad_up, grad_down, grad_cq_w = ends[7:10]
    grad_ck_w, grad_cv_w, grad_lift = ends[10:]
    stats = jnp.stack([f[5] for f in forward])
    back = jnp.stack([f[6] for f in backward])
    grad_gains = back[0, 8:].reshape(3, width)
    center2, std2, hidden_total = stats[:, 2], stats[:, 3], stats[:, 4]
    hat2_total = std2 * (hidden_total - pixels * center2)
    hidden_sum = std2 * (
        second_gain * back[:, 2] - pixels * back[:, 4] - back[:, 5] * hat2_total
    )
    grad_time = jnp.dot(time_act.T, hidden_sum, precision=precise)
    back = jnp.sum(back, axis=0)
    grad_gains = lax.dynamic_slice_in_dim(grad_gains, s * features, features, axis=1)
    return (
        outer_out,
        inner_out,
        outer_grad,
        inner_grad,
        back[1],
        back[0],
        grad_conv_first,
        grad_time,
        back[3],
        back[2],
        grad_conv_second,
        grad_lift,
        grad_gains[0],
        grad_q_w,
        grad_k_w,
        grad_v_w,
        grad_o_w,
        grad_gains[1],
        grad_cq_w,
        grad_ck_w,
        grad_cv_w,
        grad_co_w,
        grad_gains[2],
        grad_up,
        grad_down,
    )


def solution(mesh):
    pixels = P(None, "tile", "sub", None)
    tokens = P(None, "tile", "sub")
    columns, rows, vector = P(None, "sub"), P("sub", None), P("sub")
    return jax.shard_map(
        local,
        mesh=mesh,
        in_specs=(pixels, tokens)
        + (P(),) * 11
        + (vector, columns, columns, columns, rows)
        + (vector, columns, columns, columns, rows)
        + (vector, columns, rows)
        + (pixels, tokens),
        out_specs=(pixels, tokens, pixels, tokens)
        + (P(),) * 8
        + (vector, columns, columns, columns, rows)
        + (vector, columns, columns, columns, rows)
        + (vector, columns, rows),
        check_vma=False,
    )
```

```python
import functools
import math

import jax
import jax.numpy as jnp
from jax import lax
from jax.experimental import pallas as pl
from jax.experimental.pallas import tpu as pltpu
from jax.sharding import PartitionSpec as P

G = 32
HD = 64
POOL = 4
EPSILON = 1e-05
MESH = pl.DeviceIdType.MESH
precise = lax.Precision.HIGHEST
f32 = jnp.float32
bf16 = jnp.bfloat16


def params(cid=None, vmem=56):
    if cid is None:
        return pltpu.CompilerParams(vmem_limit_bytes=vmem << 20)
    return pltpu.CompilerParams(
        collective_id=cid, has_side_effects=True, vmem_limit_bytes=vmem << 20
    )


SHORT = pl.CostEstimate(flops=1, transcendentals=0, bytes_accessed=1)
LONG = pl.CostEstimate(flops=20_000_000_000, transcendentals=0, bytes_accessed=60_000_000)


def in_vmem():
    return pl.BlockSpec(memory_space=pltpu.VMEM)


def anywhere():
    return pl.BlockSpec(memory_space=pl.ANY)


def dma(*shape):
    return pltpu.SemaphoreType.DMA(shape)


def remote(src, dst, send_sem, recv_sem, where):
    return pltpu.make_async_remote_copy(
        src_ref=src,
        dst_ref=dst,
        send_sem=send_sem,
        recv_sem=recv_sem,
        device_id=where,
        device_id_type=MESH,
    )


def arrived(dst, send_sem, recv_sem, me):
    remote(dst, dst, send_sem, recv_sem, me).wait_recv()


def greet(peers):
    barrier = pltpu.get_barrier_semaphore()
    for peer in peers:
        pl.semaphore_signal(barrier, inc=1, device_id=peer, device_id_type=MESH)
    pl.semaphore_wait(barrier, len(peers))


def dot(left, right):
    return jnp.dot(left, right, preferred_element_type=f32)


def dot_t(left, right):
    return lax.dot_general(left, right, (((1,), (1,)), ((), ())), preferred_element_type=f32)


def clear(*refs):
    for ref in refs:
        ref[...] = jnp.zeros_like(ref)


def round_up(rows, step):
    return (rows + step - 1) // step * step


def chunks_of(rows):
    return max(1, min(4, rows // 16))


class Copies:
    def __init__(self):
        self.started = []

    def send(self, src, dst, send_sem, recv_sem, where, when=None):
        copy = remote(src, dst, send_sem, recv_sem, where)
        if when is None:
            copy.start()
        else:
            pl.when(when)(copy.start)
        self.started.append((when, copy))

    def finish(self):
        for when, copy in self.started:
            if when is None:
                copy.wait_send()
            else:
                pl.when(when)(copy.wait_send)


class SubScatter:
    def __init__(self, ns, copies, x, got, stage, last, sems):
        t, s = lax.axis_index("tile"), lax.axis_index("sub")
        self.far, self.copies, self.x, self.s, self.t = ns // 2, copies, x, s, t
        self.got, self.stage, self.last = got, stage, last
        self.r, self.c = s // 2, lax.rem(s, 2)
        self.me, self.twin = (t, s), (t, self.r * 2 + 1 - self.c)
        self.count = chunks_of(x.shape[1])
        self.size = x.shape[1] // self.count
        self.s1, self.r1, self.s2, self.r2 = sems

    @staticmethod
    def scratch(ns, rows, width):
        far, count = ns // 2, chunks_of(rows)
        blocks = [pltpu.VMEM((far, rows, width), bf16) for _ in range(3)]
        return blocks + [dma(far, count) for _ in range(4)]

    def peers(self):
        return [self.twin] + [self.peer(k) for k in range(1, self.far)]

    def peer(self, k):
        return (self.t, lax.rem(self.r + k, self.far) * 2 + self.c)

    def part(self, j):
        return pl.ds(j * self.size, self.size)

    def over(self, k):
        return lax.rem(self.r + k, self.far) * 2 + 1 - self.c

    def start_one(self, k):
        for j in range(self.count):
            block, got = self.x.at[self.over(k), self.part(j)], self.got.at[k, self.part(j)]
            self.copies.send(block, got, self.s1.at[k, j], self.r1.at[k, j], self.twin)

    def start(self):
        for k in list(range(1, self.far)) + [0]:
            self.start_one(k)

    def run(self, make, out, meanwhile=None, then=None):
        for k in range(1, self.far):
            make(self.over(k))
            self.start_one(k)
        for k in range(1, self.far):
            make(self.peer(k)[1])
        make(self.over(0))
        self.start_one(0)
        self.cross()
        make(self.s)
        if meanwhile is not None:
            meanwhile()
        self.end(out, then)

    def cross(self):
        for j in range(self.count):
            part = self.part(j)
            for k in range(1, self.far):
                arrived(self.got.at[k, part], self.s1.at[k, j], self.r1.at[k, j], self.me)
                own = self.x[self.peer(k)[1], part].astype(f32)
                self.stage[k, part] = (own + self.got[k, part].astype(f32)).astype(bf16)
                src, dst = self.stage.at[k, part], self.last.at[k, part]
                self.copies.send(src, dst, self.s2.at[k, j], self.r2.at[k, j], self.peer(k))

    def end(self, out, then=None):
        for j in range(self.count):
            part = self.part(j)
            arrived(self.got.at[0, part], self.s1.at[0, j], self.r1.at[0, j], self.me)
            total = self.x[self.s, part].astype(f32) + self.got[0, part].astype(f32)
            for k in range(1, self.far):
                arrived(self.last.at[k, part], self.s2.at[k, j], self.r2.at[k, j], self.me)
                total = total + self.last[k, part].astype(f32)
            out[part] = total
            if then is not None:
                then(j, part)


class SubGather:
    def __init__(self, ns, copies, out, sems):
        t, s = lax.axis_index("tile"), lax.axis_index("sub")
        self.far, self.copies, self.out, self.t, self.s = ns // 2, copies, out, t, s
        self.r, self.c = s // 2, lax.rem(s, 2)
        self.me, self.twin = (t, s), (t, self.r * 2 + 1 - self.c)
        self.count = chunks_of(out.shape[1])
        self.size = out.shape[1] // self.count
        self.s1, self.r1, self.s2, self.r2 = sems

    @staticmethod
    def scratch(ns, rows):
        return [dma(ns // 2, chunks_of(rows)) for _ in range(4)]

    def block(self, r, c, j):
        return self.out.at[lax.rem(r, self.far) * 2 + c, pl.ds(j * self.size, self.size)]

    def start(self):
        for j in range(self.count):
            self.start_one(j)

    def start_one(self, j):
        block = self.block(self.r, self.c, j)
        for k in range(1, self.far):
            peer = (self.t, lax.rem(self.r + k, self.far) * 2 + self.c)
            self.copies.send(block, block, self.s1.at[k, j], self.r1.at[k, j], peer)
        self.copies.send(block, block, self.s2.at[0, j], self.r2.at[0, j], self.twin)

    def relay(self):
        for j in range(self.count):
            for k in range(1, self.far):
                block = self.block(self.r + self.far - k, self.c, j)
                arrived(block, self.s1.at[k, j], self.r1.at[k, j], self.me)
                self.copies.send(block, block, self.s2.at[k, j], self.r2.at[k, j], self.twin)

    def end(self):
        for j in range(self.count):
            for k in range(self.far):
                block = self.block(self.r + self.far - k, 1 - self.c, j)
                arrived(block, self.s2.at[k, j], self.r2.at[k, j], self.me)


def sub_peers(ns):
    t, s = lax.axis_index("tile"), lax.axis_index("sub")
    far, r, c = ns // 2, s // 2, lax.rem(s, 2)
    return [(t, r * 2 + 1 - c)] + [(t, lax.rem(r + k, far) * 2 + c) for k in range(1, far)]


def layer_hat(values):
    width = values.shape[1]
    center = jnp.sum(values, axis=1, keepdims=True) / width
    moved = values - center
    inv_std = lax.rsqrt(jnp.sum(moved * moved, axis=1, keepdims=True) / width + EPSILON)
    return moved * inv_std, inv_std


def layer_back(grad_out, values, gain):
    width = values.shape[1]
    hat, inv_std = layer_hat(values)
    scaled = grad_out * gain
    mean_grad = jnp.sum(scaled, axis=1, keepdims=True) / width
    mean_cross = jnp.sum(scaled * hat, axis=1, keepdims=True) / width
    grad_in = inv_std * (scaled - mean_grad - hat * mean_cross)
    return grad_in, jnp.sum(grad_out * hat, axis=0, keepdims=True)


def tokens_of(ref, p):
    return ref[:, p].reshape(-1, ref.shape[3]) if len(ref.shape) == 4 else ref[p]


def by_head(first, second):
    parts = []
    for h in range(first.shape[1] // HD):
        parts += [head_of(first, h), head_of(second, h)]
    return side_by_side(parts)


def enter_kernel(
    ns, inner, pooled, lift, gain, wq, wk, wv, stream, gathered, q_out, kv_out, *sems
):
    copies = Copies()
    gather = SubGather(ns, copies, gathered, sems)
    mine = tokens_of(inner, gather.s) if len(inner.shape) == 4 else inner[...]
    value = mine.astype(f32) + dot(pooled[...], lift[...]).astype(bf16).astype(f32)
    stream[...] = value
    gathered[gather.s] = (layer_hat(value)[0] * gain[0:1, :]).astype(bf16)
    greet(sub_peers(ns))
    gather.start()
    turned = wq[...].T
    gather.relay()
    gather.end()
    rows = gathered[...].reshape(-1, gathered.shape[2])
    q_out[...] = dot_t(turned, rows).astype(bf16)
    kv_out[...] = by_head(dot(rows, wk[...]), dot(rows, wv[...])).astype(bf16)
    copies.finish()


def attn_out_kernel(ns, mixed_t, weight, before, gain, after, gathered, turned, *scratch):
    copies = Copies()
    own = before.shape[0]
    scatter = SubScatter(ns, copies, *scratch[:4], scratch[4:8])
    gather = SubGather(ns, copies, gathered, scratch[8:])
    turned[...] = mixed_t[...].T

    def make(p):
        rows = turned[pl.ds(pl.multiple_of(p * own, 16), own), :]
        scatter.x[p] = dot(rows, weight[...]).astype(bf16)

    greet(sub_peers(ns))

    def normalize(j, part):
        value = before[part, :] + after[part, :]
        after[part, :] = value
        gathered[gather.s, part] = (layer_hat(value)[0] * gain[1:2, :]).astype(bf16)
        gather.start_one(j)

    scatter.run(make, after, None, normalize)
    gather.relay()
    gather.end()
    copies.finish()


def head_of(values, h):
    return values[:, h * HD : (h + 1) * HD]


def head_probs(queries, keys, mask, h):
    scores = dot_t(head_of(queries, h), head_of(keys, h)) * HD ** (-0.5)
    scores = jnp.where(mask > 0.5, scores, -1000000000.0)
    raised = jnp.exp(scores - jnp.max(scores, axis=1, keepdims=True))
    return raised / jnp.sum(raised, axis=1, keepdims=True)


def side_by_side(parts):
    return jnp.concatenate(parts, axis=1) if len(parts) > 1 else parts[0]


def cross_kernel(
    ns, cross_in, wq, ck, cv, mask, wo, before, gain, after, gathered, queries, mixed, *scratch
):
    copies = Copies()
    scatter = SubScatter(ns, copies, *scratch[:4], scratch[4:8])
    gather = SubGather(ns, copies, gathered, scratch[8:])
    heads = wq.shape[1] // HD

    def make(p):
        q = dot(cross_in[p], wq[...]).astype(bf16)
        queries[p] = q
        keys, values, masked = ck[...], cv[...], mask[...]
        parts = [
            dot(head_probs(q, keys, masked, h).astype(bf16), head_of(values, h))
            for h in range(heads)
        ]
        mixed[p] = side_by_side(parts).astype(bf16)
        scatter.x[p] = dot(mixed[p], wo[...]).astype(bf16)

    greet(sub_peers(ns))

    def normalize(j, part):
        value = before[part, :] + after[part, :]
        after[part, :] = value
        gathered[gather.s, part] = (layer_hat(value)[0] * gain[2:3, :]).astype(bf16)
        gather.start_one(j)

    scatter.run(make, after, None, normalize)
    gather.relay()
    gather.end()
    copies.finish()


def mlp_kernel(
    ns, mlp_in, cotan, w_up, w_down, before, gain,
    grad, gathered, gain_grad, down, up_grad, down_grad, activated, grad_up, cotans, *scratch
):
    copies = Copies()
    for p in range(ns):
        cotans[p] = tokens_of(cotan, p)
    cotan = cotans
    scatter = SubScatter(ns, copies, *scratch[:4], scratch[4:8])
    gather = SubGather(ns, copies, gathered, scratch[8:])
    own = before.shape[0]
    rate = math.sqrt(2.0 / math.pi)

    def make(p):
        up = dot(mlp_in[p], w_up[...])
        square = up * up
        bent = jnp.tanh(rate * (up + 0.044715 * up * square))
        rows = pl.ds(pl.multiple_of(p * own, 16), own)
        activated[rows, :] = (0.5 * up * (1.0 + bent)).astype(bf16)
        slope = 0.5 * (1.0 + bent) + 0.5 * up * (1.0 - bent * bent) * (
            rate * (1.0 + 3.0 * 0.044715 * square)
        )
        turned = (slope * dot_t(cotan[p], w_down[...])).astype(bf16)
        grad_up[rows, :] = turned
        scatter.x[p] = dot_t(turned, w_up[...]).astype(bf16)

    greet(sub_peers(ns))
    whole = lambda ref: ref[...].reshape(ns * own, ref.shape[2])

    def meanwhile():
        up_grad[...] = dot(whole(mlp_in).T, grad_up[...]).astype(bf16)

    gain_grad[...] = jnp.zeros_like(gain_grad)

    def normalize(j, part):
        back, gains = layer_back(grad[part, :], before[part, :], gain[2:3, :])
        gain_grad[...] += gains
        value = cotan[gather.s, part].astype(f32) + back
        grad[part, :] = value
        gathered[gather.s, part] = value.astype(bf16)
        gather.start_one(j)

    scatter.run(make, grad, meanwhile, normalize)
    down_grad[...] = dot(activated[...].T, whole(cotan)).astype(bf16)
    gather.relay()
    down[...] = dot(activated[...], w_down[...]).astype(bf16)
    gather.end()
    copies.finish()


def cross_back_kernel(
    ns, incoming, wo, queries, ck, cv, mask, wq, before, gain, residual, cross_in, mixed,
    grad, gathered, gain_grad, dk_out, dv_out, weights, dk, dv, dq, *scratch
):
    copies = Copies()
    scatter = SubScatter(ns, copies, *scratch[:4], scratch[4:8])
    gather = SubGather(ns, copies, gathered, scratch[8:])
    heads = wq.shape[1] // HD
    own = before.shape[0]
    clear(dk, dv)

    def make(p):
        grad_mixed = dot_t(incoming[p], wo[...]).astype(bf16)
        q, keys, values, masked = queries[p], ck[...], cv[...], mask[...]
        parts_q, parts_k, parts_v = [], [], []
        for h in range(heads):
            probs = head_probs(q, keys, masked, h)
            slope = dot_t(head_of(grad_mixed, h), head_of(values, h))
            lean = probs * (slope - jnp.sum(probs * slope, axis=1, keepdims=True))
            lean = lean.astype(bf16)
            parts_q.append(dot(lean, head_of(keys, h)))
            parts_k.append(dot(lean.T, head_of(q, h)))
            parts_v.append(dot(probs.astype(bf16).T, head_of(grad_mixed, h)))
        part = (side_by_side(parts_q) * HD ** (-0.5)).astype(bf16)
        dq[pl.ds(pl.multiple_of(p * own, 16), own), :] = part
        dk[...] += side_by_side(parts_k)
        dv[...] += side_by_side(parts_v)
        scatter.x[p] = dot_t(part, wq[...]).astype(bf16)

    greet(sub_peers(ns))
    whole = lambda ref: ref[...].reshape(ns * own, ref.shape[2])

    def meanwhile():
        weights[0] = dot(whole(mixed).T, whole(incoming)).astype(bf16)
        dk_out[...] = (dk[...] * HD ** (-0.5)).astype(bf16)
        dv_out[...] = dv[...].astype(bf16)

    gain_grad[...] = jnp.zeros_like(gain_grad)

    def normalize(j, part):
        back, gains = layer_back(grad[part, :], before[part, :], gain[1:2, :])
        gain_grad[...] += gains
        value = residual[part, :] + back
        grad[part, :] = value
        gathered[gather.s, part] = value.astype(bf16)
        gather.start_one(j)

    scatter.run(make, grad, meanwhile, normalize)
    weights[1] = dot(dq[...].T, whole(cross_in)).astype(bf16)
    gather.relay()
    gather.end()
    copies.finish()


def attn_back_kernel(
    ns, dq_t, dkv, wq, wk, wv, before, gain, residual, out, gain_grad, turned, wkv, *scratch
):
    copies = Copies()
    scatter = SubScatter(ns, copies, *scratch[1:5], scratch[5:9])
    total = scratch[0]
    own = before.shape[0]
    turned[...] = dq_t[...].T
    wkv[...] = by_head(wk[...], wv[...])

    def make(p):
        rows = pl.ds(pl.multiple_of(p * own, 16), own)
        value = dot_t(turned[rows, :], wq[...]) + dot_t(dkv[rows, :], wkv[...])
        scatter.x[p] = value.astype(bf16)

    greet(sub_peers(ns))
    scatter.run(make, total)
    back, gains = layer_back(total[...], before[...], gain[0:1, :])
    gain_grad[...] = gains
    out[...] = (residual[...] + back).astype(bf16)
    copies.finish()


def chain_call(kernel, name, cid, outs, args, extra, scatter, gather=True, vmem=16, cost=SHORT):
    ns = lax.axis_size("sub")
    own, width = outs[0][0]
    scratch = list(extra)
    if scatter:
        scratch += [pltpu.VMEM((ns, own, width), bf16)] + SubScatter.scratch(ns, own, width)
    if gather:
        scratch += SubGather.scratch(ns, own)
    return pl.pallas_call(
        functools.partial(kernel, ns),
        out_shape=tuple(jax.ShapeDtypeStruct(*out) for out in outs),
        in_specs=[in_vmem()] * len(args),
        out_specs=(in_vmem(),) * len(outs),
        scratch_shapes=scratch,
        cost_estimate=cost,
        compiler_params=params(cid, vmem),
        name=name,
    )(*args)


def deal(nt, u):
    t, s = lax.axis_index("tile"), lax.axis_index("sub")
    nb = nt // u
    a, b = t // nb, lax.rem(t, nb)
    a_peer = lambda k: (lax.rem(a + k, u) * nb + b, s)
    b_peer = lambda k: (a * nb + lax.rem(b + k, nb), s)
    peers = [a_peer(k) for k in range(1, u)] + [b_peer(k) for k in range(1, nb)]
    return t, s, nb, a, b, a_peer, b_peer, peers


def rows_of(ref, i, size):
    return ref.at[:, pl.ds(pl.multiple_of(i * size, size), size), :]


def lanes_of(ref, i, size):
    return ref.at[:, :, pl.ds(pl.multiple_of(i * size, size), size)]


class TileSum:
    PARTS = 4

    def __init__(self, nt, x, out, pair, line, share_sems):
        t, s = lax.axis_index("tile"), lax.axis_index("sub")
        self.na, self.x, self.out = nt // 2, x, out
        self.a, self.b, self.s = t // 2, lax.rem(t, 2), s
        self.me, self.pair = (t, s), (self.a * 2 + 1 - self.b, s)
        self.half = (out.shape[0] if x is None else x.shape[0]) // 2
        self.piece = self.half // 2 // self.PARTS
        self.folded = None
        if pair:
            self.got1, self.s1, self.r1 = pair
        if line:
            self.stage, self.got2, self.s2, self.r2 = line
        if share_sems:
            self.s3, self.r3, self.s4, self.r4 = share_sems

    @staticmethod
    def buffers(rows, width):
        return pltpu.VMEM((rows // 2, width), bf16)

    @staticmethod
    def sems():
        return [dma(2, TileSum.PARTS) for _ in range(2)]

    @staticmethod
    def pair_scratch(rows, width):
        return [TileSum.buffers(rows, width)] + TileSum.sems()

    @staticmethod
    def line_scratch(rows, width):
        return [TileSum.buffers(rows, width)] * 2 + TileSum.sems()

    def rows(self, b, e, j):
        start = b * self.half + (j * 2 + e) * self.piece
        return pl.ds(pl.multiple_of(start, 16), self.piece)

    def along(self, e):
        up, down = (self.a * 2 + 2 + self.b, self.s), (self.a * 2 - 2 + self.b, self.s)
        return (down, up, self.a) if e else (up, down, self.na - 1 - self.a)

    def start(self):
        for j in range(self.PARTS):
            for e in range(2):
                self.to_pair(e, j).start()

    def to_pair(self, e, j):
        src, dst = self.x.at[self.rows(1 - self.b, e, j)], self.got1.at[self.rows(0, e, j)]
        return remote(src, dst, self.s1.at[e, j], self.r1.at[e, j], self.pair)

    def steps(self):
        return range(self.PARTS + self.na - 1)

    def step_of(self, way, step, action):
        j = step - way
        pl.when((j >= 0) & (j < self.PARTS))(lambda: action(jnp.clip(j, 0, self.PARTS - 1)))

    def add(self, steps):
        for step in steps:
            for e in range(2):
                self.step_of(self.along(e)[2], step, functools.partial(self.add_one, e))

    def with_pair(self, e, j):
        here, mine = self.rows(0, e, j), self.rows(self.b, e, j)
        arrived(self.got1.at[here], self.s1.at[e, j], self.r1.at[e, j], self.me)
        return self.x[mine].astype(f32) + self.got1[here].astype(f32)

    def fold(self, half):
        for j in range(self.PARTS):
            for e in range(2):
                half[self.rows(0, e, j)] = self.with_pair(e, j).astype(bf16)
        for j in range(self.PARTS):
            for e in range(2):
                self.to_pair(e, j).wait_send()

    def add_one(self, e, j):
        _, after, way = self.along(e)
        here, mine = self.rows(0, e, j), self.rows(self.b, e, j)
        both = self.with_pair(e, j) if self.folded is None else self.folded[here].astype(f32)

        @pl.when(way == 0)
        def _():
            self.stage[here] = both.astype(bf16)

        @pl.when(way > 0)
        def _():
            arrived(self.got2.at[here], self.s2.at[e, j], self.r2.at[e, j], self.me)
            self.stage[here] = (both + self.got2[here].astype(f32)).astype(bf16)

        @pl.when(way < self.na - 1)
        def _():
            src, dst = self.stage.at[here], self.got2.at[here]
            remote(src, dst, self.s2.at[e, j], self.r2.at[e, j], after).start()

        @pl.when(way == self.na - 1)
        def _():
            self.out[mine] = self.stage[here]

    def share(self, steps):
        for step in steps:
            for e in range(2):
                way = self.na - 1 - self.along(e)[2]
                self.step_of(way, step, functools.partial(self.share_one, e))

    def share_one(self, e, j):
        before, _, way = self.along(e)
        block = self.out.at[self.rows(self.b, e, j)]

        @pl.when(way < self.na - 1)
        def _():
            arrived(block, self.s3.at[e, j], self.r3.at[e, j], self.me)

        @pl.when(way > 0)
        def _():
            remote(block, block, self.s3.at[e, j], self.r3.at[e, j], before).start()

        remote(block, block, self.s4.at[e, j], self.r4.at[e, j], self.pair).start()

    def end_add(self):
        for j in range(self.PARTS):
            for e in range(2):
                _, after, way = self.along(e)
                if self.folded is None:
                    self.to_pair(e, j).wait_send()
                stage = self.stage.at[self.rows(0, e, j)]
                sent = remote(stage, stage, self.s2.at[e, j], self.r2.at[e, j], after)
                pl.when(way < self.na - 1)(sent.wait_send)

    def end_share(self):
        for j in range(self.PARTS):
            for e in range(2):
                block = self.out.at[self.rows(1 - self.b, e, j)]
                arrived(block, self.s4.at[e, j], self.r4.at[e, j], self.me)
        for j in range(self.PARTS):
            for e in range(2):
                before, _, way = self.along(e)
                block = self.out.at[self.rows(self.b, e, j)]
                sent = remote(block, block, self.s3.at[e, j], self.r3.at[e, j], before)
                pl.when(way > 0)(sent.wait_send)
                remote(block, block, self.s4.at[e, j], self.r4.at[e, j], self.pair).wait_send()


def self_attention_kernel(
    nt, u, q_ref, kv_ref, home, qo, kvo, mixed_out, lse, top, total, mixed, low,
    qs, qr, ks, kr, fs, fr, hs, hr, own
):
    t, s, nb, a, b, a_peer, b_peer, peers = deal(nt, u)
    me = (t, s)
    batch, length = q_ref.shape[0], q_ref.shape[2]
    copies = Copies()
    qo[a] = q_ref[:, pl.ds(pl.multiple_of(a * HD, HD), HD), :]
    local = [pltpu.make_async_copy(lanes_of(kv_ref, a, 2 * HD), kvo.at[t], own.at[0])]
    local[0].start()
    greet(peers)
    for k in range(1, u):
        block = rows_of(q_ref, lax.rem(a + k, u), HD)
        copies.send(block, qo.at[a], qs.at[k], qr.at[k], a_peer(k))
    for k in range(1, u):
        block = lanes_of(kv_ref, lax.rem(a + k, u), 2 * HD)
        copies.send(block, kvo.at[t], ks.at[k], kr.at[k], a_peer(k))
    for m in range(1, nb):
        block = lanes_of(kv_ref, a, 2 * HD)
        copies.send(block, kvo.at[t], fs.at[0, m], fr.at[0, m], b_peer(m))
    clear(total, mixed)
    top[...] = jnp.full(top.shape, -jnp.inf, f32)

    def take(tile, i, n):
        q = qo[i, n] * 0.125
        padded = jnp.concatenate([q, jnp.zeros_like(q)], axis=0)
        keys = kvo[tile, n]
        scores = dot(keys, padded)
        new = jnp.maximum(top[i, n], jnp.max(scores, axis=0, keepdims=True))
        raised = jnp.exp(scores - new)
        scale = jnp.exp(top[i, n] - new)
        added = dot(keys.T[HD:], raised.astype(bf16))
        return (
            new,
            total[i, n] * scale + jnp.sum(raised, axis=0, keepdims=True),
            mixed[i, n] * scale + added,
        )

    def take_all(tile):
        for n in range(batch):
            for i in range(u):
                top[i, n], total[i, n], mixed[i, n] = take(tile, i, n)

    def tile_of(k, m):
        return lax.rem(a + u - k, u) * nb + lax.rem(b + nb - m, nb)

    for k in range(1, u):
        arrived(qo.at[lax.rem(a + u - k, u)], qs.at[k], qr.at[k], me)
    local[0].wait()
    near_first = sorted(range(1, u), key=lambda k: min(k, u - k))
    order = [(0, m) for m in range(nb)] + [(k, 0) for k in near_first]
    order += [(k, m) for k in near_first for m in range(1, nb)]
    for k, m in order[:-1]:
        tile = tile_of(k, m)
        if m:
            arrived(kvo.at[tile], fs.at[k, m], fr.at[k, m], me)
        elif k:
            arrived(kvo.at[tile], ks.at[k], kr.at[k], me)
            for n in range(1, nb):
                block = kvo.at[tile]
                copies.send(block, block, fs.at[k, n], fr.at[k, n], b_peer(n))
        take_all(tile)
    k, m = order[-1]
    tile = tile_of(k, m)
    if m:
        arrived(kvo.at[tile], fs.at[k, m], fr.at[k, m], me)
    elif k:
        arrived(kvo.at[tile], ks.at[k], kr.at[k], me)
    for k in list(range(1, u)) + [0]:
        i = lax.rem(a + k, u)
        for n in range(batch):
            peak, weight, value = take(tile, i, n)
            value = value / weight
            mixed_out[i, n] = value
            low[i, n] = value.astype(bf16)
            lse[i, n] = peak + jnp.log(weight)
        if k:
            copies.send(low.at[i], rows_of(home, a, HD), hs.at[k], hr.at[k], a_peer(k))
        else:
            local.append(pltpu.make_async_copy(low.at[i], rows_of(home, a, HD), own.at[1]))
            local[1].start()
    for k in range(1, u):
        arrived(rows_of(home, lax.rem(a + u - k, u), HD), hs.at[k], hr.at[k], me)
    local[1].wait()
    copies.finish()


def self_attention(q, kv, cid):
    nt = lax.axis_size("tile")
    batch, width, length = q.shape
    u = width // HD
    nb = nt // u
    shape = jax.ShapeDtypeStruct
    dealt = (u, batch, HD, length)
    return pl.pallas_call(
        functools.partial(self_attention_kernel, nt, u),
        out_shape=(
            shape(q.shape, bf16),
            shape(dealt, bf16),
            shape((nt, batch, length, 2 * HD), bf16),
            shape(dealt, f32),
            shape((u, batch, 1, length), f32),
        ),
        in_specs=[in_vmem()] * 2,
        out_specs=(in_vmem(),) * 5,
        scratch_shapes=[
            pltpu.VMEM((u, batch, 1, length), f32),
            pltpu.VMEM((u, batch, 1, length), f32),
            pltpu.VMEM(dealt, f32),
            pltpu.VMEM(dealt, bf16),
        ]
        + [dma(u) for _ in range(4)]
        + [dma(u, nb) for _ in range(2)]
        + [dma(u) for _ in range(2)]
        + [dma(2)],
        cost_estimate=LONG,
        compiler_params=params(cid, 24),
        name="self_attention",
    )(q, kv)


class Nothing:
    def __getattr__(self, name):
        return lambda *args: None


class FullSum:
    def __init__(self, nt, ns, copies, x, out, got1, stage, got2, mine, got3, sems):
        t, s = lax.axis_index("tile"), lax.axis_index("sub")
        self.nt, self.far, self.copies, self.x, self.out = nt, ns // 2, copies, x, out
        self.got1, self.stage, self.got2, self.mine, self.got3 = got1, stage, got2, mine, got3
        self.t, self.s, self.r, self.c = t, s, s // 2, lax.rem(s, 2)
        self.me, self.twin = (t, s), (t, self.r * 2 + 1 - self.c)
        self.part = x.shape[0] // ns
        self.piece = self.part // nt
        (self.s1, self.r1, self.s2, self.r2, self.s3, self.r3) = sems[:6]
        (self.s4, self.r4, self.s5, self.r5, self.s6, self.r6) = sems[6:]

    @staticmethod
    def scratch(nt, ns, rows, width):
        far, part = ns // 2, rows // ns
        return (
            [pltpu.VMEM((far, part, width), bf16) for _ in range(3)]
            + [pltpu.VMEM((part, width), bf16), pltpu.VMEM((nt, part // nt, width), bf16)]
            + [dma(far) for _ in range(4)]
            + [dma(nt) for _ in range(4)]
            + [dma(far) for _ in range(4)]
        )

    def rows(self, r, c):
        return pl.ds(pl.multiple_of((c * self.far + r) * self.part, 16), self.part)

    def slot(self, t):
        return pl.ds(pl.multiple_of(t * self.piece, 16), self.piece)

    def other(self, k):
        return lax.rem(self.r + k, self.far)

    def tile(self, k):
        return lax.rem(self.t + k, self.nt)

    def start(self):
        for k in list(range(1, self.far)) + [0]:
            src = self.x.at[self.rows(self.other(k), 1 - self.c)]
            self.copies.send(src, self.got1.at[k], self.s1.at[k], self.r1.at[k], self.twin)

    def cross(self):
        for k in range(1, self.far):
            arrived(self.got1.at[k], self.s1.at[k], self.r1.at[k], self.me)
            own = self.x[self.rows(self.other(k), self.c)].astype(f32)
            self.stage[k] = (own + self.got1[k].astype(f32)).astype(bf16)
            peer = (self.t, self.other(k) * 2 + self.c)
            self.copies.send(self.stage.at[k], self.got2.at[k], self.s2.at[k], self.r2.at[k], peer)

    def spread(self):
        arrived(self.got1.at[0], self.s1.at[0], self.r1.at[0], self.me)
        total = self.x[self.rows(self.r, self.c)].astype(f32) + self.got1[0].astype(f32)
        for k in range(1, self.far):
            arrived(self.got2.at[k], self.s2.at[k], self.r2.at[k], self.me)
            total = total + self.got2[k].astype(f32)
        self.mine[...] = total.astype(bf16)
        for k in range(1, self.nt):
            p = self.tile(k)
            src = self.mine.at[self.slot(p)]
            self.copies.send(src, self.got3.at[k], self.s3.at[k], self.r3.at[k], (p, self.s))

    def place(self, t, r, c):
        start = (c * self.far + r) * self.part + t * self.piece
        return pl.ds(pl.multiple_of(start, 16), self.piece)

    def settle(self):
        total = self.mine[self.slot(self.t)].astype(f32)
        for k in range(1, self.nt):
            arrived(self.got3.at[k], self.s3.at[k], self.r3.at[k], self.me)
            total = total + self.got3[k].astype(f32)
        here = self.place(self.t, self.r, self.c)
        self.out[here] = total.astype(bf16)
        block = self.out.at[here]
        for k in range(1, self.nt):
            self.copies.send(block, block, self.s4.at[k], self.r4.at[k], (self.tile(k), self.s))

    def share(self):
        for k in range(1, self.nt):
            block = self.out.at[self.place(self.tile(self.nt - k), self.r, self.c)]
            arrived(block, self.s4.at[k], self.r4.at[k], self.me)
        block = self.out.at[self.rows(self.r, self.c)]
        for k in range(1, self.far):
            peer = (self.t, self.other(k) * 2 + self.c)
            self.copies.send(block, block, self.s5.at[k], self.r5.at[k], peer)
        self.copies.send(block, block, self.s6.at[0], self.r6.at[0], self.twin)

    def relay(self):
        for k in range(1, self.far):
            block = self.out.at[self.rows(self.other(self.far - k), self.c)]
            arrived(block, self.s5.at[k], self.r5.at[k], self.me)
            self.copies.send(block, block, self.s6.at[k], self.r6.at[k], self.twin)

    def end(self):
        for k in range(self.far):
            block = self.out.at[self.rows(self.other(self.far - k), 1 - self.c)]
            arrived(block, self.s6.at[k], self.r6.at[k], self.me)


def attention_back_kernel(
    nt, ns, u, d_ref, q_ref, of_ref, lse_ref, kv_ref, mixed_t, grad_attn, early_ref, beside_ref,
    qo, kvo, early_out, beside_out,
    dealt, qd, rows, delta, acc, low, sent, kept, got, stage, mine,
    ds, dr, fs, fr, ks, kr, qs, qr, own, *scratch
):
    t, s, nb, a, b, a_peer, b_peer, peers = deal(nt, u)
    me = (t, s)
    batch, length = d_ref.shape[0], d_ref.shape[2]
    copies = Copies()
    early = TileSum(nt, mine, None, scratch[:3], None, None)
    beside = SubScatter(ns, copies, beside_ref, *scratch[3:6], scratch[6:])
    greet_all(nt, ns)
    dealt[a] = d_ref[:, pl.ds(pl.multiple_of(a * HD, HD), HD), :]
    for k in range(1, u):
        block = rows_of(d_ref, lax.rem(a + k, u), HD)
        copies.send(block, dealt.at[a], ds.at[k], dr.at[k], a_peer(k))
    features = mixed_t.shape[0]
    mine[pl.ds(0, features), :] = dot(mixed_t[...], grad_attn[...]).astype(bf16)
    mine[pl.ds(features, 2 * features), :] = early_ref[...]
    spare = mine.shape[0] - 3 * features
    if spare:
        mine[pl.ds(3 * features, spare), :] = jnp.zeros((spare, mine.shape[1]), bf16)
    early.start()
    beside.start()

    def prepare(i):
        for n in range(batch):
            q, d = q_ref[i, n], dealt[i, n]
            zero = jnp.zeros_like(q)
            qd[i, n, 0] = jnp.concatenate([q * 0.125, zero], axis=0)
            qd[i, n, 1] = jnp.concatenate([zero, d], axis=0)
            rows[i, n, 0] = qd[i, n, 0].T
            rows[i, n, 1] = qd[i, n, 1].T
            delta[i, n] = jnp.sum(d.astype(f32) * of_ref[i, n], axis=0, keepdims=True)

    clear(acc)
    for k in range(u):
        i = lax.rem(a + u - k, u)
        if k:
            arrived(dealt.at[i], ds.at[k], dr.at[k], me)
        prepare(i)

    def work(tile, n):
        kv = kv_ref[tile, n]
        kt = kv.T[:HD]
        total = jnp.zeros(kv.shape, f32)
        for i in range(u):
            probs = jnp.exp(dot(kv, qd[i, n, 0]) - lse_ref[i, n])
            slope = dot(kv, qd[i, n, 1])
            grads = (probs * (slope - delta[i, n])).astype(bf16)
            total = total + dot(probs.astype(bf16), rows[i, n, 1]) + dot(grads, rows[i, n, 0])
            acc[i, n] += dot(kt, grads)
        return total

    def settle(k):
        for n in range(batch):
            total = kept[k, n]
            for m in range(1, nb):
                if n == 0:
                    arrived(got.at[m, k], fs.at[k, m], fr.at[k, m], me)
                total = total + got[m, k, n].astype(f32)
            stage[k, n] = total.astype(bf16)
        if k:
            copies.send(stage.at[k], lanes_of(kvo, a, 2 * HD), ks.at[k], kr.at[k], a_peer(k))

    order = list(range(1, u)) + [0]
    for at, k in enumerate(order):
        for m in range(1, nb):
            tile = lax.rem(a + k, u) * nb + lax.rem(b + m, nb)
            for n in range(batch):
                sent[m, k, n] = work(tile, n).astype(bf16)
            copies.send(sent.at[m, k], got.at[m, k], fs.at[k, m], fr.at[k, m], b_peer(m))
        if at == min(1, u - 1):
            beside.cross()
        for n in range(batch):
            kept[k, n] = work(lax.rem(a + k, u) * nb + b, n)
        if at:
            settle(order[at - 1])
    for k in list(range(1, u)) + [0]:
        i = lax.rem(a + k, u)
        for n in range(batch):
            low[i, n] = (acc[i, n] * 0.125).astype(bf16)
        if k:
            copies.send(low.at[i], rows_of(qo, a, HD), qs.at[k], qr.at[k], a_peer(k))
    local = [pltpu.make_async_copy(low.at[a], rows_of(qo, a, HD), own.at[0])]
    local[0].start()
    beside.end(beside_out)
    settle(order[-1])
    local.append(pltpu.make_async_copy(stage.at[0], lanes_of(kvo, a, 2 * HD), own.at[1]))
    local[1].start()
    early.fold(early_out)
    for k in range(1, u):
        i = lax.rem(a + u - k, u)
        arrived(rows_of(qo, i, HD), qs.at[k], qr.at[k], me)
        arrived(lanes_of(kvo, i, 2 * HD), ks.at[k], kr.at[k], me)
    for copy in local:
        copy.wait()
    copies.finish()


def attention_back(d, q, of, lse, kv, mixed_t, grad_attn, early, beside, cid):
    nt, ns = lax.axis_size("tile"), lax.axis_size("sub")
    u, batch, _, length = q.shape
    nb = nt // u
    block = (batch, length, 2 * HD)
    sums = (round_up(3 * u * HD, 16 * nt), grad_attn.shape[1])
    beside = beside.reshape(ns, -1, beside.shape[1])
    shape = jax.ShapeDtypeStruct
    return pl.pallas_call(
        functools.partial(attention_back_kernel, nt, ns, u),
        out_shape=(
            shape(d.shape, bf16),
            shape((batch, length, u * 2 * HD), bf16),
            shape((sums[0] // 2, sums[1]), bf16),
            shape(beside.shape[1:], f32),
        ),
        in_specs=[in_vmem()] * 9,
        out_specs=(in_vmem(),) * 4,
        scratch_shapes=[
            pltpu.VMEM(q.shape, bf16),
            pltpu.VMEM((u, batch, 2, 2 * HD, length), bf16),
            pltpu.VMEM((u, batch, 2, length, 2 * HD), bf16),
            pltpu.VMEM((u, batch, 1, length), f32),
            pltpu.VMEM(q.shape, f32),
            pltpu.VMEM(q.shape, bf16),
            pltpu.VMEM((nb, u) + block, bf16),
            pltpu.VMEM((u,) + block, f32),
            pltpu.VMEM((nb, u) + block, bf16),
            pltpu.VMEM((u,) + block, bf16),
            pltpu.VMEM(sums, bf16),
            dma(u),
            dma(u),
            dma(u, nb),
            dma(u, nb),
            dma(u),
            dma(u),
            dma(u),
            dma(u),
            dma(2),
        ]
        + TileSum.pair_scratch(*sums)
        + SubScatter.scratch(ns, *beside.shape[1:]),
        cost_estimate=SHORT,
        compiler_params=params(cid, 40),
        name="attention_back",
    )(d, q, of, lse, kv, mixed_t, grad_attn, early, beside)


AROUND = [(-1, 0), (1, 0), (0, -1), (0, 1), (-1, -1), (-1, 1), (1, -1), (1, 1)]
DIAGONAL = AROUND[4:]


def present(nt, ns, t, s, dt, ds):
    y, x = t + dt, s + ds
    return (y >= 0) & (y < nt) & (x >= 0) & (x < ns)


def greet_all(nt, ns):
    t, s = lax.axis_index("tile"), lax.axis_index("sub")
    barrier = pltpu.get_barrier_semaphore()
    for k in range(1, ns):
        peer = (t, lax.rem(s + k, ns))
        pl.semaphore_signal(barrier, inc=1, device_id=peer, device_id_type=MESH)
    for k in range(1, nt):
        peer = (lax.rem(t + k, nt), s)
        pl.semaphore_signal(barrier, inc=1, device_id=peer, device_id_type=MESH)
    count = ns + nt - 2
    for dt, ds in DIAGONAL:
        there = present(nt, ns, t, s, dt, ds)
        count = count + jnp.where(there, 1, 0)

        @pl.when(there)
        def _():
            pl.semaphore_signal(
                barrier, inc=1, device_id=(t + dt, s + ds), device_id_type=MESH
            )

    pl.semaphore_wait(barrier, count)


def border_copies(nt, ns, src, top, bottom, left, right, ss, rs):
    t, s = lax.axis_index("tile"), lax.axis_index("sub")
    rows, cols = src.shape[0], src.shape[1]
    high, low = pl.ds(0, 2), pl.ds(rows - 2, 2)
    first, last = pl.ds(0, 16), pl.ds(cols - 16, 16)
    inner, before, after = pl.ds(2, rows), pl.ds(0, 2), pl.ds(rows + 2, 2)
    pairs = [
        (src.at[high], bottom),
        (src.at[low], top),
        (src.at[:, first], right.at[inner]),
        (src.at[:, last], left.at[inner]),
        (src.at[high, first], right.at[after]),
        (src.at[high, last], left.at[after]),
        (src.at[low, first], right.at[before]),
        (src.at[low, last], left.at[before]),
    ]
    copies = []
    for i, (dt, ds) in enumerate(AROUND):
        out = present(nt, ns, t, s, dt, ds)
        back = present(nt, ns, t, s, -dt, -ds)
        copies.append((out, back, remote(*pairs[i], ss.at[i], rs.at[i], (t + dt, s + ds))))
    return copies


def begin(copies):
    for out, _, copy in copies:
        pl.when(out)(copy.start)


def finish(copies):
    for out, back, copy in copies:
        pl.when(back)(copy.wait_recv)
        pl.when(out)(copy.wait_send)


def sum_near(nt, ns, value, first, ss, rs):
    t, s = lax.axis_index("tile"), lax.axis_index("sub")
    first[s] = value
    copies = []
    for k in range(1, ns):
        peer = (t, lax.rem(s + k, ns))
        copies.append(remote(first.at[s], first.at[s], ss.at[k], rs.at[s], peer))
        copies[-1].start()
    return copies


def sum_far(nt, ns, first, second, ss1, rs1, ss2, rs2):
    t, s = lax.axis_index("tile"), lax.axis_index("sub")
    for k in range(1, ns):
        p = lax.rem(s + k, ns)
        arrived(first.at[p], ss1.at[k], rs1.at[p], (t, s))
    total = first[0]
    for k in range(1, ns):
        total = total + first[k]
    second[t] = total
    copies = []
    for k in range(1, nt):
        peer = (lax.rem(t + k, nt), s)
        copies.append(remote(second.at[t], second.at[t], ss2.at[k], rs2.at[t], peer))
        copies[-1].start()
    return copies


def sum_end(nt, second, ss2, rs2):
    t, s = lax.axis_index("tile"), lax.axis_index("sub")
    for k in range(1, nt):
        p = lax.rem(t + k, nt)
        arrived(second.at[p], ss2.at[k], rs2.at[p], (t, s))
    total = second[0]
    for k in range(1, nt):
        total = total + second[k]
    return total


def sum_scratch(nt, ns, channels, rows=2):
    return [
        pltpu.VMEM((ns, rows, channels), f32),
        pltpu.VMEM((nt, rows, channels), f32),
        dma(ns),
        dma(ns),
        dma(nt),
        dma(nt),
    ]


def in_groups(values):
    count, channels = values.shape
    per = channels // G
    row = lax.broadcasted_iota(jnp.int32, (channels, channels), 0) // per
    col = lax.broadcasted_iota(jnp.int32, (channels, channels), 1) // per
    same = jnp.where(row == col, 1.0, 0.0).astype(bf16)
    parts, rest = [], values
    for _ in range(3):
        parts.append(rest.astype(bf16))
        rest = rest - parts[-1].astype(f32)
    out = [dot(part, same) for part in parts]
    return out[0] + out[1] + out[2]


def fold(values):
    return jnp.sum(values.reshape(-1, 8, values.shape[-1]), axis=0)


def row_sums(count, channels, pair):
    def step(i, carry):
        first, second = pair(i)
        return carry[0] + fold(first), carry[1] + fold(second)

    zero = jnp.zeros((8, channels), f32)
    first, second = lax.fori_loop(0, count, step, (zero, zero), unroll=2)
    return jnp.concatenate(
        [jnp.sum(first, axis=0, keepdims=True), jnp.sum(second, axis=0, keepdims=True)], axis=0
    )


def sigmoid(values):
    return 1.0 / (1.0 + jnp.exp(-values))


def silu_slope(values):
    sigma = sigmoid(values)
    return sigma * (1.0 + values * (1.0 - sigma))


def block_of(total, step, limit):
    return max(n for n in range(step, limit + 1, step) if total % n == 0)


def put_left_to_right(flat, triple):
    total, channels = triple.shape[0], flat.shape[1]
    size = block_of(total, 16, 256)
    for start in range(0, total, size):
        for j in range(3):
            piece = flat[pl.ds(8 + start + j - 1, size), :]
            triple[pl.ds(start, size), pl.ds(j * channels, channels)] = piece.astype(bf16)


def conv_rows(triple, weight, start, size, pitch, multiply=dot):
    taps = [triple[pl.ds(start + i * pitch, size), :] for i in range(3)]
    return multiply(jnp.concatenate(taps, axis=1), weight)


def turned_taps(weight):
    return jnp.concatenate([weight[8 - k] for k in range(9)], axis=1)


def list_length(rows, pitch):
    return 16 + rows * pitch + 16


def fill(flat, rows, cols, row_ok, left_ok, right_ok, body, ending, opening):
    pitch = cols + 16
    channels = flat.shape[1]
    place = lax.broadcasted_iota(jnp.int32, (16, channels), 0)
    flat[pl.ds(0, 8), :] = jnp.zeros((8, channels), f32)
    end = 8 + 16 + rows * pitch
    flat[pl.ds(end, 24), :] = jnp.zeros((24, channels), f32)

    def places(right_good, left_good):
        good = jnp.where(place < 8, jnp.where(right_good, 1, 0), jnp.where(left_good, 1, 0))
        return good > 0

    flat[pl.ds(8, 16), :] = jnp.where(
        places(False, left_ok & row_ok(0)), opening(), 0.0
    )

    def step(i, carry):
        start = pl.multiple_of(24 + i * pitch, 8)
        value = body(i)
        good = jnp.full(value.shape, jnp.where(row_ok(i), 1, 0), jnp.int32)
        flat[pl.ds(start, cols), :] = jnp.where(good > 0, value, 0.0)
        good = places(right_ok & row_ok(i), left_ok & row_ok(i + 1))
        flat[pl.ds(start + cols, 16), :] = jnp.where(good, ending(i), 0.0)
        return carry

    lax.fori_loop(0, rows, step, 0)


def sides(left, right, i):
    place = lax.broadcasted_iota(jnp.int32, right.shape[1:], 0)
    return jnp.where(place < 8, right[i].astype(f32), left[i + 1].astype(f32))


def outer_forward_kernel(
    nt, ns, img, w1, w2, vec, gain1, gain2, gain3, text_in, wk_in, wv_in,
    out, pooled, act1_out, act2_out, hidden, stats, gains_out, keys, values,
    body, left, right, flat, act1, act2, rowsum, gains, text, wk, wv,
    border_ss, border_rs, keep, gain_ss, gain_rs, *sums
):
    rows, cols, channels = img.shape
    pitch = cols + 16
    t, s = lax.axis_index("tile"), lax.axis_index("sub")
    sums1, sums2 = sums[:6], sums[6:]
    count = float(nt * ns * rows * cols * (channels // G))
    pairs = ((text_in, text), (wk_in, wk), (wv_in, wv))
    loads = [pltpu.make_async_copy(*pair, keep.at[2 + i]) for i, pair in enumerate(pairs)]
    clear(body, left, right)
    greet_all(nt, ns)
    top, bottom = body.at[pl.ds(0, 2)], body.at[pl.ds(rows + 2, 2)]
    border = border_copies(nt, ns, img, top, bottom, left, right, border_ss, border_rs)
    begin(border)
    pixel = lambda i: img[i].astype(f32)
    local1 = row_sums(rows, channels, lambda i: (pixel(i), pixel(i) * pixel(i)))
    copies = sum_near(nt, ns, local1, sums1[0], sums1[2], sums1[3])
    copies += sum_far(nt, ns, sums1[0], sums1[1], *sums1[2:])
    for copy in loads:
        copy.start()
    gains[s] = jnp.concatenate([gain1[...], gain2[...], gain3[...]], axis=0)
    for k in range(1, ns):
        block, peer = gains.at[s], (t, lax.rem(s + k, ns))
        copies.append(remote(block, block, gain_ss.at[k], gain_rs.at[s], peer))
        copies[-1].start()

    def inner(i, carry):
        body[i + 2] = img[i]
        return carry

    lax.fori_loop(0, rows, inner, 0)
    total1 = sum_end(nt, sums1[1], sums1[4], sums1[5])

    def moments(total):
        grouped = in_groups(total) / count
        center = grouped[0:1]
        return center, lax.rsqrt(grouped[1:2] - center * center + EPSILON)

    center1, std1 = moments(total1)
    scale1 = std1 * vec[0:1]
    shift1 = vec[1:2] - center1 * scale1
    finish(border)

    def first_act(values):
        normed = values.astype(f32) * scale1 + shift1
        return normed * sigmoid(normed)

    ok = lambda lift: (
        lambda i: (t * rows + i - lift >= 0) & (t * rows + i - lift < nt * rows)
    )
    fill(
        flat, rows + 4, cols, ok(2), s > 0, s < ns - 1,
        lambda i: first_act(body[i]),
        lambda i: first_act(sides(left, right, i)),
        lambda: first_act(left[0]),
    )
    put_left_to_right(flat, act1)
    saved = [pltpu.make_async_copy(act1, act1_out, keep.at[0])]
    saved[0].start()
    length = list_length(rows + 2, pitch)
    size = block_of(length, 16, 700)
    for start in range(0, length, size):
        hidden[pl.ds(start, size), :] = conv_rows(act1, w1[...], start, size, pitch) + vec[4:5]

    def hidden_row(i):
        return hidden[pl.ds(pl.multiple_of(16 + (i + 1) * pitch, 16), cols), :]

    local2 = row_sums(rows, channels, lambda i: (hidden_row(i), hidden_row(i) * hidden_row(i)))
    copies += sum_near(nt, ns, local2, sums2[0], sums2[2], sums2[3])
    copies += sum_far(nt, ns, sums2[0], sums2[1], *sums2[2:])
    for copy in loads:
        copy.wait()
    keys[...] = dot(text[...], wk[...]).astype(bf16)
    values[...] = dot(text[...], wv[...]).astype(bf16)
    total2 = sum_end(nt, sums2[1], sums2[4], sums2[5])
    center2, std2 = moments(total2)
    scale2 = std2 * vec[2:3]
    shift2 = vec[3:4] - center2 * scale2
    stats[...] = jnp.concatenate(
        [center1, std1, center2, std2, total2, jnp.zeros_like(total2)], axis=0
    )

    def second_act(start, amount):
        normed = hidden[pl.ds(start, amount), :] * scale2 + shift2
        return normed * sigmoid(normed)

    at = lambda i: pl.multiple_of(16 + i * pitch, 16)
    fill(
        flat, rows + 2, cols, ok(1), s > 0, s < ns - 1,
        lambda i: second_act(at(i), cols),
        lambda i: second_act(at(i) + cols, 16),
        lambda: second_act(0, 16),
    )
    put_left_to_right(flat, act2)
    saved.append(pltpu.make_async_copy(act2, act2_out, keep.at[1]))
    saved[1].start()
    lc = cols // POOL
    for start in range(0, rows, 2 * POOL):
        grown = conv_rows(act2, w2[...], 16 + start * pitch, 2 * POOL * pitch, pitch)
        grown = grown.reshape(2 * POOL, pitch, channels)[:, :cols]
        grown = grown + img[pl.ds(start, 2 * POOL)].astype(f32)
        out[pl.ds(start, 2 * POOL)] = grown.astype(bf16)
        for half in range(2):
            added = jnp.sum(grown[half * POOL : (half + 1) * POOL], axis=0)
            means = []
            for n in range(channels // 128):
                rowsum[n] = added[:, n * 128 : (n + 1) * 128]
                mean = rowsum[n, pl.ds(0, lc, stride=POOL), :]
                for k in range(1, POOL):
                    mean = mean + rowsum[n, pl.ds(k, lc, stride=POOL), :]
                means.append(mean * (1.0 / (POOL * POOL)))
            place = pl.ds((start // POOL + half) * lc, lc)
            pooled[place, :] = jnp.concatenate(means, axis=1).astype(bf16)
    for k in range(1, ns):
        p = lax.rem(s + k, ns)
        arrived(gains.at[p], gain_ss.at[k], gain_rs.at[p], (t, s))
    gains_out[...] = side_by_side([gains[i] for i in range(ns)])
    for copy in copies:
        copy.wait_send()
    for copy in saved:
        copy.wait()


def outer_forward(img, w1, w2, vec, gains, text, wk, wv, cid):
    nt, ns = lax.axis_size("tile"), lax.axis_size("sub")
    rows, cols, channels = img.shape
    pitch = cols + 16
    long1, long2 = list_length(rows + 4, pitch), list_length(rows + 2, pitch)
    shape = jax.ShapeDtypeStruct
    return pl.pallas_call(
        functools.partial(outer_forward_kernel, nt, ns),
        out_shape=(
            shape(img.shape, bf16),
            shape((rows // POOL * (cols // POOL), channels), bf16),
            shape((long1, 3 * channels), bf16),
            shape((long2, 3 * channels), bf16),
            shape((long2, channels), f32),
            shape((8, channels), f32),
            shape((3, ns * wk.shape[1]), f32),
            shape((text.shape[0], wk.shape[1]), bf16),
            shape((text.shape[0], wk.shape[1]), bf16),
        ),
        in_specs=[in_vmem()] * 7 + [anywhere()] * 3,
        out_specs=(in_vmem(),) * 2 + (anywhere(),) * 2 + (in_vmem(),) * 5,
        scratch_shapes=[
            pltpu.VMEM((rows + 4, cols, channels), bf16),
            pltpu.VMEM((rows + 5, 16, channels), bf16),
            pltpu.VMEM((rows + 5, 16, channels), bf16),
            pltpu.VMEM((long1 + 16, channels), f32),
            pltpu.VMEM((long1, 3 * channels), bf16),
            pltpu.VMEM((long2, 3 * channels), bf16),
            pltpu.VMEM((channels // 128, cols, 128), f32),
            pltpu.VMEM((ns, 3, wk.shape[1]), f32),
            pltpu.VMEM(text.shape, bf16),
            pltpu.VMEM(wk.shape, bf16),
            pltpu.VMEM(wv.shape, bf16),
            dma(8),
            dma(8),
            dma(5),
            dma(ns),
            dma(ns),
        ]
        + sum_scratch(nt, ns, channels) * 2,
        cost_estimate=LONG,
        compiler_params=params(cid),
        name="outer_forward",
    )(img, w1, w2, vec, *gains, text, wk, wv)


def kernel_grads(triple, grads_t, start, size, pitch, out, between=()):
    for i in range(3):
        rows = triple[pl.ds(start + i * pitch, size), :]
        taps = dot(grads_t[...], rows).T.astype(bf16)
        out[pl.ds(i * taps.shape[0], taps.shape[0]), :] = taps
        for action in between[i : i + 1]:
            action()


def outer_backward_kernel(
    nt, ns, cut, cot, img, w2, w1, vec, stats, hidden, wide, tokens, gains, pooled, lifted, lift_weight,
    attn_in, grad_q_t, grad_kv, grad_ck, grad_cv, act1_in, act2_in, outer_grad, tall_out, wide_out, tokens_out, sum2_out, sum1_out, back_out,
    spread, grad2, body, left, right, flat, act1, act2, triple, inner_t, slope, own2, own1, tall,
    border_ss, border_rs, keep, token_ss, token_rs, *scratch
):
    rows, cols, channels = img.shape
    pitch = cols + 16
    lr, lc = rows // POOL, cols // POOL
    t, s = lax.axis_index("tile"), lax.axis_index("sub")
    sums2, sums1, scratch = scratch[:6], scratch[6:12], scratch[12:]
    copies = Copies()
    early = TileSum(nt, None, wide_out, None, scratch[:4], scratch[4:8])
    early.folded = wide
    late = TileSum(nt, tall, tall_out, scratch[8:11], scratch[11:15], scratch[15:19])
    scratch = scratch[19:]
    second = FullSum(nt, ns, copies, own2, sum2_out, *scratch[:5], scratch[5:17])
    scratch = scratch[17:]
    first, rest = Nothing(), []
    for skip, rows_of_sum in ((0, cut), (cut, own1.shape[0] - cut)):
        if rows_of_sum:
            part = pl.ds(skip, rows_of_sum)
            views = own1.at[part], sum1_out.at[part]
            rest.append(FullSum(nt, ns, copies, *views, *scratch[:5], scratch[5:17]))
            scratch = scratch[17:]
    if len(rest) > 1:
        first = rest[0]
    rest = rest[-1]
    count = float(nt * ns * rows * cols * (channels // G))
    held = [
        pltpu.make_async_copy(act2_in, act2, keep.at[0]),
        pltpu.make_async_copy(act1_in, act1, keep.at[1]),
    ]
    for copy in held:
        copy.start()
    clear(body, left, right)
    greet_all(nt, ns)
    width = lifted.shape[1]
    shrunk = dot_t(lifted[...], lift_weight[...]) * (1.0 / (POOL * POOL))

    def widen(i):
        for n in range(channels // 128):
            part = shrunk[i * lc : (i + 1) * lc, n * 128 : (n + 1) * 128]
            for k in range(POOL):
                spread[i, n, pl.ds(k, lc, stride=POOL), :] = part

    for i in range(lr):
        widen(i)

    def outer(i):
        parts = [spread[i // POOL, n] for n in range(channels // 128)]
        return cot[i].astype(f32) + jnp.concatenate(parts, axis=1)

    def round_outer(i, carry):
        value = outer(i).astype(bf16)
        grad2[i] = value
        body[i + 2] = value
        return carry

    lax.fori_loop(0, rows, round_outer, 0)
    top, bottom = body.at[pl.ds(0, 2)], body.at[pl.ds(rows + 2, 2)]
    border = border_copies(nt, ns, grad2, top, bottom, left, right, border_ss, border_rs)
    begin(border)
    tokens_out[s] = tokens[s]
    for k in range(1, ns):
        p = lax.rem(s + k, ns)
        copies.send(tokens.at[p], tokens_out.at[s], token_ss.at[k], token_rs.at[k], (t, p))
    features = grad_q_t.shape[0]
    heads = features // HD
    attn_t = attn_in[...].T
    tall[pl.ds(0, width), :] = dot_t(attn_t, grad_q_t[...]).astype(bf16)
    both = dot(attn_t, grad_kv[...])
    for n in range(2):
        lanes = [both[:, (2 * h + n) * HD : (2 * h + n + 1) * HD] for h in range(heads)]
        part = jnp.concatenate(lanes, axis=1) if heads > 1 else lanes[0]
        tall[pl.ds((1 + n) * width, width), :] = part.astype(bf16)
    used = 3 * width
    for ref in (grad_ck, grad_cv):
        tall[pl.ds(used, ref.shape[0]), :] = ref[...]
        used += ref.shape[0]
    if used < tall.shape[0]:
        tall[pl.ds(used, tall.shape[0] - used), :] = jnp.zeros(
            (tall.shape[0] - used, features), bf16
        )
    late.start()
    steps = list(early.steps())
    early.add(steps[:1])
    total = rows * pitch

    def turned(row):
        for start in range(0, rows, 8):
            block = [row(start + k) for k in range(8)]
            gap = jnp.zeros((16, channels), bf16)
            piece = jnp.concatenate([p for b in block for p in (b, gap)], axis=0)
            inner_t[:, pl.ds(start * pitch, 8 * pitch)] = piece.T

    def pad_below(ref, used):
        if used < ref.shape[0]:
            ref[pl.ds(used, ref.shape[0] - used), :] = jnp.zeros(
                (ref.shape[0] - used, channels), bf16
            )

    taps = 9 * channels
    turned(lambda i: grad2[i])
    held[0].wait()
    between = [lambda k=k: early.add(steps[k : k + 1]) for k in (1, 2, 3)]
    kernel_grads(act2, inner_t, 16, total, pitch, own2, between)
    lift_grad = dot(pooled[...].T, lifted[...]).astype(bf16)
    for n in range(width // channels):
        own2[pl.ds(taps + n * channels, channels), :] = lift_grad[
            :, n * channels : (n + 1) * channels
        ]
    pad_below(own2, taps + width)
    second.start()
    early.add(steps[4:5])
    finish(border)
    ok = lambda lift_by: (
        lambda i: (t * rows + i - lift_by >= 0) & (t * rows + i - lift_by < nt * rows)
    )
    fill(
        flat, rows + 4, cols, ok(2), s > 0, s < ns - 1,
        lambda i: body[i].astype(f32),
        lambda i: sides(left, right, i),
        lambda: left[0].astype(f32),
    )
    put_left_to_right(flat, triple)
    second.cross()
    center1, std1, center2, std2 = (stats[k : k + 1] for k in range(4))
    gain1, bias1, gain2, bias2 = (vec[k : k + 1] for k in range(4))
    length = list_length(rows + 2, pitch)
    size = block_of(length, 16, 700)
    w2t = turned_taps(w2)
    for start in range(0, length, size):
        hat = (hidden[pl.ds(start, size), :] - center2) * std2
        slope[pl.ds(start, size), :] = conv_rows(
            triple, w2t, start, size, pitch, dot_t
        ) * silu_slope(hat * gain2 + bias2)
        if start == size:
            early.add(steps[5:6])
    early.add(steps[6:])

    at = lambda i: pl.multiple_of(16 + i * pitch, 16)

    def pair2(i):
        place = pl.ds(at(i + 1), cols)
        value = slope[place, :]
        return value, value * ((hidden[place, :] - center2) * std2)

    local2 = jnp.concatenate([row_sums(rows, channels, pair2), gains[...]], axis=0)
    plain = sum_near(nt, ns, local2, sums2[0], sums2[2], sums2[3])
    plain += sum_far(nt, ns, sums2[0], sums2[1], *sums2[2:])
    second.spread()
    early.share(steps[:2])
    late.add(steps[:2])
    back2 = sum_end(nt, sums2[1], sums2[4], sums2[5])
    back2, gains_total = back2[:2], back2[2:]
    means2 = in_groups(back2 * gain2) / count

    def grad_hidden(start, amount):
        hat = (hidden[pl.ds(start, amount), :] - center2) * std2
        value = slope[pl.ds(start, amount), :] * gain2 - means2[0:1] - hat * means2[1:2]
        return std2 * value

    fill(
        flat, rows + 2, cols, ok(1), s > 0, s < ns - 1,
        lambda i: grad_hidden(at(i), cols),
        lambda i: grad_hidden(at(i) + cols, 16),
        lambda: grad_hidden(0, 16),
    )
    early.share(steps[2:3])
    late.add(steps[2:3])
    turned(lambda i: flat[pl.ds(24 + (i + 1) * pitch, cols), :].astype(bf16))
    held[1].wait()
    between = [lambda: late.add(steps[3:4]), lambda: first.start(), lambda: late.add(steps[4:5])]
    between[0] = lambda: (early.share(steps[3:4]), late.add(steps[3:4]))
    kernel_grads(act1, inner_t, 16 + pitch, total, pitch, own1, between)
    pad_below(own1, taps)
    rest.start()
    early.share(steps[4:5])
    second.settle()
    first.cross()
    put_left_to_right(flat, triple.at[pl.ds(0, length)])
    rest.cross()
    hat1 = lambda i: (img[i].astype(f32) - center1) * std1
    step = 2 * POOL
    w1t = turned_taps(w1)
    for start in range(0, rows, step):
        value = conv_rows(triple, w1t, 16 + start * pitch, step * pitch, pitch, dot_t)
        value = value.reshape(step, pitch, channels)[:, :cols]
        hat = (img[pl.ds(start, step)].astype(f32) - center1) * std1
        outer_grad[pl.ds(start, step)] = value * silu_slope(hat * gain1 + bias1)
        if start == step:
            early.share(steps[5:6])
            late.add(steps[5:6])
    first.spread()
    early.share(steps[6:])
    late.add(steps[6:])
    late.share(steps[:1])
    local1 = row_sums(rows, channels, lambda i: (outer_grad[i], outer_grad[i] * hat1(i)))
    plain += sum_near(nt, ns, local1, sums1[0], sums1[2], sums1[3])
    rest.spread()
    plain += sum_far(nt, ns, sums1[0], sums1[1], *sums1[2:])
    late.share(steps[1:3])
    second.share()
    back1 = sum_end(nt, sums1[1], sums1[4], sums1[5])
    means1 = in_groups(back1 * gain1) / count
    first.settle()
    late.share(steps[3:4])

    def last(i, carry):
        value = outer_grad[i] * gain1 - means1[0:1] - hat1(i) * means1[1:2]
        outer_grad[i] = outer(i) + std1 * value
        return carry

    lax.fori_loop(0, rows, last, 0)
    back_out[...] = jnp.concatenate(
        [back1, back2, means2, jnp.zeros_like(means2), gains_total], axis=0
    )
    rest.settle()
    late.share(steps[4:5])
    first.share()
    late.share(steps[5:])
    second.relay()
    rest.share()
    first.relay()
    for k in range(1, ns):
        block = tokens_out.at[lax.rem(s + ns - k, ns)]
        arrived(block, token_ss.at[k], token_rs.at[k], (t, s))
    rest.relay()
    early.end_add()
    early.end_share()
    second.end()
    first.end()
    late.end_add()
    late.end_share()
    rest.end()
    copies.finish()
    for copy in plain:
        copy.wait_send()


def outer_backward(
    cot, img, w2, w1, vec, stats, hidden, wide, tokens, gains, pooled, lifted, lift_weight,
    attn_in, grad_q_t, grad_kv, grad_ck, grad_cv, act1, act2, cid
):
    nt, ns = lax.axis_size("tile"), lax.axis_size("sub")
    rows, cols, channels = img.shape
    pitch = cols + 16
    long1, long2 = list_length(rows + 4, pitch), list_length(rows + 2, pitch)
    shape = jax.ShapeDtypeStruct
    step = 16 * nt * ns
    width, features = attn_in.shape[1], grad_q_t.shape[0]
    rows2 = round_up(9 * channels + width, step)
    tall = (round_up(3 * width + 2 * grad_ck.shape[0], 16 * nt), features)
    cut = 6 * channels // step * step
    rows1 = round_up(9 * channels, step)
    return pl.pallas_call(
        functools.partial(outer_backward_kernel, nt, ns, cut),
        out_shape=(
            shape(img.shape, f32),
            shape(tall, bf16),
            shape((2 * wide.shape[0], wide.shape[1]), bf16),
            shape(tokens.shape, bf16),
            shape((rows2, channels), bf16),
            shape((rows1, channels), bf16),
            shape((8 + gains.shape[0], channels), f32),
        ),
        in_specs=[in_vmem()] * 18 + [anywhere()] * 2,
        out_specs=(in_vmem(),) * 7,
        scratch_shapes=[
            pltpu.VMEM((rows // POOL, channels // 128, cols, 128), f32),
            pltpu.VMEM((rows, cols, channels), bf16),
            pltpu.VMEM((rows + 4, cols, channels), bf16),
            pltpu.VMEM((rows + 5, 16, channels), bf16),
            pltpu.VMEM((rows + 5, 16, channels), bf16),
            pltpu.VMEM((long1 + 16, channels), f32),
            pltpu.VMEM((long1, 3 * channels), bf16),
            pltpu.VMEM((long2, 3 * channels), bf16),
            pltpu.VMEM((long1, 3 * channels), bf16),
            pltpu.VMEM((channels, rows * pitch), bf16),
            pltpu.VMEM((long2, channels), f32),
            pltpu.VMEM((rows2, channels), bf16),
            pltpu.VMEM((rows1, channels), bf16),
            pltpu.VMEM(tall, bf16),
            dma(8),
            dma(8),
            dma(2),
            dma(ns),
            dma(ns),
        ]
        + sum_scratch(nt, ns, channels, 2 + gains.shape[0])
        + sum_scratch(nt, ns, channels)
        + TileSum.line_scratch(2 * wide.shape[0], wide.shape[1])
        + TileSum.sems()
        + TileSum.sems()
        + TileSum.pair_scratch(*tall)
        + TileSum.line_scratch(*tall)
        + TileSum.sems()
        + TileSum.sems()
        + FullSum.scratch(nt, ns, rows2, channels)
        + (FullSum.scratch(nt, ns, cut, channels) if cut else [])
        + FullSum.scratch(nt, ns, rows1 - cut, channels),
        cost_estimate=SHORT,
        compiler_params=params(cid, 62),
        name="outer_backward",
    )(
        cot, img, w2, w1, vec, stats, hidden, wide, tokens, gains, pooled, lifted, lift_weight,
        attn_in, grad_q_t, grad_kv, grad_ck, grad_cv, act1, act2,
    )


def finish_kernel(text, up, down, *refs):
    q, k, v, ck, cv, o, co, cq, second, first = refs[:10]
    lift, refs = refs[10:-13], refs[-13:]
    for src, dst in zip((q, k, v, o, co, second, first, up, down), refs[:9]):
        dst[...] = src[...].astype(f32)
    refs[9][...] = cq[...].T.astype(f32)
    turned = text[...].T
    refs[10][...] = dot(turned, ck[...])
    refs[11][...] = dot(turned, cv[...])
    refs[12][...] = jnp.concatenate([part[...].astype(f32) for part in lift], axis=1)


def finish_grads(text, up, down, tall, wide, second, first, taps, text_rows):
    features, width = tall.shape[1], wide.shape[1]
    channels = first.shape[1]
    steps = features // 32
    row = lambda size, lanes, skip=0: pl.BlockSpec((size, lanes), lambda i: (skip + i, 0))
    size = width // steps
    tall_specs = [row(size, features, n * steps) for n in range(3)]
    start = 3 * width // text_rows
    tall_specs += [
        pl.BlockSpec((text_rows, features), lambda i, n=n: (start + n, 0)) for n in range(2)
    ]
    wide_specs = [row(32, width, n * steps) for n in range(2)]
    wide_specs.append(pl.BlockSpec((features, size), lambda i: (2, i)))
    size = taps // steps
    lift_size = channels // steps
    lift_specs = [
        row(lift_size, channels, taps // lift_size + n * steps) for n in range(width // channels)
    ]
    full = text.shape[1]
    up_specs = [row(w.shape[0] // steps, w.shape[1]) for w in (up, down)]
    in_specs = [pl.BlockSpec((text.shape[0], full // steps), lambda i: (0, i))] + up_specs
    in_specs += tall_specs + wide_specs + [row(size, channels)] * 2 + lift_specs
    shape = lambda *dims: jax.ShapeDtypeStruct(dims, f32)
    return pl.pallas_call(
        finish_kernel,
        grid=(steps,),
        out_shape=(shape(width, features),) * 3
        + (shape(features, width),) * 2
        + (shape(taps, channels),) * 2
        + (shape(*up.shape), shape(*down.shape), shape(width, features))
        + (shape(full, features), shape(full, features), shape(channels, width)),
        in_specs=in_specs,
        out_specs=[row(width // steps, features)] * 3
        + [row(32, width)] * 2
        + [row(size, channels)] * 2
        + up_specs
        + [row(width // steps, features)]
        + [row(full // steps, features)] * 2
        + [row(lift_size, width)],
        cost_estimate=SHORT,
        compiler_params=params(),
        name="finish_grads",
    )(text, up, down, *[tall] * 5, *[wide] * 3, second, first, *[second] * len(lift_specs))


def time_embed(time_steps, channels):
    half_width = channels // 2
    frequency = jnp.exp(
        -math.log(10000.0) * jnp.arange(half_width).astype(f32) / half_width
    )
    angles = time_steps.astype(f32)[:, None] * frequency[None, :]
    return jnp.concatenate([jnp.sin(angles), jnp.cos(angles)], axis=1)


def weight_grad(inputs, grads):
    return lax.dot_general(inputs, grads, (((0,), (0,)), ((), ())), preferred_element_type=f32)


def local(
    outer_image,
    inner_image,
    text_states,
    time_steps,
    text_lengths,
    first_gain,
    first_bias,
    conv_first,
    time_weight,
    second_gain,
    second_bias,
    conv_second,
    lift_weight,
    attn_gain,
    query_weight,
    key_weight,
    value_weight,
    out_weight,
    cross_gain,
    cross_query,
    cross_key,
    cross_value,
    cross_out,
    mlp_gain,
    up_weight,
    down_weight,
    outer_cotan,
    inner_cotan,
):
    nt, ns = lax.axis_size("tile"), lax.axis_size("sub")
    s = lax.axis_index("sub")
    batch, rows, cols, channels = outer_image.shape
    lr, lc = rows // POOL, cols // POOL
    width = inner_image.shape[2] * ns
    features = inner_image.shape[2]
    heads = features // HD
    own = batch * lr * lc
    length = ns * lr * lc
    pixels = rows * cols * nt * ns


    def whole_tokens(values):
        full = lax.all_gather(values, "sub", axis=2, tiled=True)
        return full.reshape(batch, lr, ns, lc, width)

    inner_own, cotan_full = whole_tokens(inner_image), whole_tokens(inner_cotan)
    if batch == 1 and lc % 16 == 0:
        inner_own, cotan_full = inner_own[0], cotan_full[0]
    else:
        inner_own = lax.dynamic_index_in_dim(inner_own, s, 2, keepdims=False)
        inner_own = inner_own.reshape(own, width)
        cotan_full = jnp.transpose(cotan_full, (2, 0, 1, 3, 4)).reshape(ns, own, width)
    own_gains = [v.reshape(1, features) for v in (attn_gain, cross_gain, mlp_gain)]

    time_act = jax.nn.silu(time_embed(time_steps, channels))
    time_shift = jnp.dot(time_act, time_weight.astype(f32), precision=precise)
    fixed = jnp.stack([first_gain, first_bias, second_gain, second_bias])
    fixed = jnp.broadcast_to(fixed[None], (batch, 4, channels))
    empty = jnp.zeros((batch, 3, channels), f32)
    vectors = jnp.concatenate([fixed, time_shift[:, None, :], empty], axis=1)
    as_rows = lambda w: w.reshape(9 * channels, channels)
    text_rows = batch * text_states.shape[1]
    text = text_states.reshape(text_rows, -1)
    forward = [
        outer_forward(
            outer_image[b],
            as_rows(conv_first),
            as_rows(conv_second),
            vectors[b],
            own_gains,
            text,
            cross_key,
            cross_value,
            20 + b,
        )
        for b in range(batch)
    ]
    outer_out = jnp.stack([f[0] for f in forward])
    gains, cross_k, cross_v = forward[0][6:]
    pooled = jnp.concatenate([f[1] for f in forward], axis=0)

    flat = lambda v: v.reshape(-1, v.shape[-1])
    block, rows_all = ((own, width), f32), ((ns, own, width), bf16)
    stream_in, attn_in, query_t, kv = chain_call(
        enter_kernel,
        "enter",
        2,
        (
            block,
            rows_all,
            ((features, ns * own), bf16),
            ((ns * own, 2 * features), bf16),
        ),
        (inner_own, pooled, lift_weight, gains, query_weight, key_weight, value_weight),
        (),
        False,
        vmem=24,
        cost=LONG,
    )
    attn_in = flat(attn_in)

    def per_sample(values, tokens_last):
        if tokens_last:
            values = values.reshape(-1, ns, batch, lr * lc)
            return jnp.transpose(values, (2, 0, 1, 3)).reshape(batch, -1, length)
        values = values.reshape(ns, batch, lr * lc, -1)
        return jnp.transpose(values, (1, 0, 2, 3)).reshape(batch, length, -1)

    def all_samples(values, tokens_last):
        if tokens_last:
            values = values.reshape(batch, -1, ns, lr * lc)
            return jnp.transpose(values, (1, 2, 0, 3)).reshape(-1, ns * own)
        values = values.reshape(batch, ns, lr * lc, -1)
        return jnp.transpose(values, (1, 0, 2, 3)).reshape(ns * own, -1)

    mixed_t, head_q, head_kv, head_mixed_f, head_lse = self_attention(
        per_sample(query_t, True), per_sample(kv, False), 3
    )
    mixed_t = all_samples(mixed_t, True)
    after_attn, cross_in = chain_call(
        attn_out_kernel,
        "attn_out",
        5,
        (block, rows_all),
        (mixed_t, out_weight, stream_in, gains),
        [pltpu.VMEM((ns * own, features), bf16)],
        True,
        cost=LONG,
    )
    sample_of = lambda count: jnp.arange(batch * count) // count
    text_at = jnp.tile(jnp.arange(text_states.shape[1]), batch)
    good = text_at < jnp.repeat(text_lengths, text_states.shape[1])
    same = sample_of(lr * lc)[:, None] == sample_of(text_states.shape[1])[None, :]
    mask = jnp.where(same & good[None, :], 1.0, 0.0).astype(f32)
    head_rows = ((ns, own, features), bf16)
    after_cross, mlp_in, cross_q, cross_mixed = chain_call(
        cross_kernel,
        "cross",
        6,
        (block, rows_all, head_rows, head_rows),
        (cross_in, cross_query, cross_k, cross_v, mask, cross_out, after_attn, gains),
        (),
        True,
        cost=LONG,
    )

    units = up_weight.shape[1]
    one_row = ((1, width), f32)
    middle = pltpu.VMEM((ns * own, units), bf16)
    grad_after_cross, grad_cross_full, grad_mlp_gain, down, grad_up, grad_down = chain_call(
        mlp_kernel,
        "mlp",
        8,
        (
            block,
            rows_all,
            one_row,
            ((ns * own, width), bf16),
            ((width, units), bf16),
            ((units, width), bf16),
        ),
        (mlp_in, cotan_full, up_weight, down_weight, after_cross, gains),
        [middle, middle, pltpu.VMEM((ns, own, width), bf16)],
        True,
        vmem=56,
    )
    grad_down, grad_up = lax.psum((grad_down, grad_up), "tile")
    text_block = ((text_rows, features), bf16)
    (
        grad_after_attn,
        grad_attn_full,
        grad_cross_gain,
        grad_ck,
        grad_cv,
        grad_early,
    ) = chain_call(
        cross_back_kernel,
        "cross_back",
        10,
        (
            block,
            rows_all,
            one_row,
            text_block,
            text_block,
            ((2, features, width), bf16),
        ),
        (
            grad_cross_full,
            cross_out,
            cross_q,
            cross_k,
            cross_v,
            mask,
            cross_query,
            after_attn,
            gains,
            grad_after_cross,
            cross_in,
            cross_mixed,
        ),
        [pltpu.VMEM((text_rows, features), f32)] * 2
        + [pltpu.VMEM((ns * own, features), bf16)],
        True,
        vmem=56,
    )
    grad_attn_full = flat(grad_attn_full)
    grad_mixed_t = dot_t(out_weight, grad_attn_full).astype(bf16)
    grad_q_t, grad_kv, wide, down_own = attention_back(
        per_sample(grad_mixed_t, True),
        head_q,
        head_mixed_f,
        head_lse,
        head_kv,
        mixed_t,
        grad_attn_full,
        grad_early.reshape(2 * features, width),
        down,
        13,
    )
    grad_q_t, grad_kv = all_samples(grad_q_t, True), all_samples(grad_kv, False)
    grad_lifted, grad_attn_gain = chain_call(
        attn_back_kernel,
        "attn_back",
        15,
        (((own, width), bf16), one_row),
        (
            grad_q_t,
            grad_kv,
            query_weight,
            key_weight,
            value_weight,
            stream_in,
            gains,
            grad_after_attn,
        ),
        [
            pltpu.VMEM((ns * own, features), bf16),
            pltpu.VMEM((width, 2 * features), bf16),
            pltpu.VMEM((own, width), f32),
        ],
        True,
        False,
    )

    inner_sum = after_cross + down_own
    tokens = jnp.stack([inner_sum.astype(bf16), grad_lifted])
    tokens = tokens.reshape(2, own, ns, features).transpose(2, 0, 1, 3)
    gain_rows = jnp.stack([grad_attn_gain, grad_cross_gain, grad_mlp_gain]).reshape(-1, channels)
    by_tap = lambda w: w.reshape(9, channels, channels)
    backward = []
    for b in range(batch):
        once = (lambda v: v) if b == 0 else jnp.zeros_like
        sample = lambda v: v.reshape(batch, lr * lc, -1)[b]
        backward.append(
            outer_backward(
                outer_cotan[b],
                outer_image[b],
                by_tap(conv_second),
                by_tap(conv_first),
                vectors[b],
                forward[b][5],
                forward[b][4],
                once(wide),
                once(tokens),
                once(gain_rows),
                sample(pooled),
                sample(grad_lifted),
                lift_weight,
                attn_in,
                once(grad_q_t),
                once(grad_kv),
                once(grad_ck),
                once(grad_cv),
                forward[b][2],
                forward[b][3],
                20 + batch + b,
            )
        )
    outer_grad = jnp.stack([f[0] for f in backward])
    tall, wide, tokens = backward[0][1:4]
    tokens = tokens.reshape(ns, 2, batch, lr, lc, features).transpose(1, 2, 3, 0, 4, 5)
    inner_out, inner_grad = tokens.reshape(2, batch, length, features)
    inner_grad = inner_grad.astype(f32)
    if batch > 1:
        sum2, sum1 = (
            sum(f[k].astype(f32) for f in backward).astype(bf16) for k in (4, 5)
        )
    else:
        sum2, sum1 = backward[0][4:6]
    ends = finish_grads(
        text,
        grad_up,
        grad_down,
        tall,
        wide,
        sum2,
        sum1,
        9 * channels,
        text_rows,
    )
    grad_q_w, grad_k_w, grad_v_w, grad_o_w, grad_co_w = ends[:5]
    grad_conv_second, grad_conv_first = (v.reshape(conv_first.shape) for v in ends[5:7])
    grad_up, grad_down, grad_cq_w = ends[7:10]
    grad_ck_w, grad_cv_w, grad_lift = ends[10:]
    stats = jnp.stack([f[5] for f in forward])
    back = jnp.stack([f[6] for f in backward])
    grad_gains = back[0, 8:].reshape(3, width)
    center2, std2, hidden_total = stats[:, 2], stats[:, 3], stats[:, 4]
    hat2_total = std2 * (hidden_total - pixels * center2)
    hidden_sum = std2 * (
        second_gain * back[:, 2] - pixels * back[:, 4] - back[:, 5] * hat2_total
    )
    grad_time = jnp.dot(time_act.T, hidden_sum, precision=precise)
    back = jnp.sum(back, axis=0)
    grad_gains = lax.dynamic_slice_in_dim(grad_gains, s * features, features, axis=1)
    return (
        outer_out,
        inner_out,
        outer_grad,
        inner_grad,
        back[1],
        back[0],
        grad_conv_first,
        grad_time,
        back[3],
        back[2],
        grad_conv_second,
        grad_lift,
        grad_gains[0],
        grad_q_w,
        grad_k_w,
        grad_v_w,
        grad_o_w,
        grad_gains[1],
        grad_cq_w,
        grad_ck_w,
        grad_cv_w,
        grad_co_w,
        grad_gains[2],
        grad_up,
        grad_down,
    )


def solution(mesh):
    pixels = P(None, "tile", "sub", None)
    tokens = P(None, "tile", "sub")
    columns, rows, vector = P(None, "sub"), P("sub", None), P("sub")
    return jax.shard_map(
        local,
        mesh=mesh,
        in_specs=(pixels, tokens)
        + (P(),) * 11
        + (vector, columns, columns, columns, rows)
        + (vector, columns, columns, columns, rows)
        + (vector, columns, rows)
        + (pixels, tokens),
        out_specs=(pixels, tokens, pixels, tokens)
        + (P(),) * 8
        + (vector, columns, columns, columns, rows)
        + (vector, columns, columns, columns, rows)
        + (vector, columns, rows),
        check_vma=False,
    )
```

```python
import functools
import math

import jax
import jax.numpy as jnp
from jax import lax
from jax.experimental import pallas as pl
from jax.experimental.pallas import tpu as pltpu
from jax.sharding import PartitionSpec as P

G = 32
HD = 64
POOL = 4
EPSILON = 1e-05
MESH = pl.DeviceIdType.MESH
precise = lax.Precision.HIGHEST
f32 = jnp.float32
bf16 = jnp.bfloat16


def params(cid=None, vmem=56):
    if cid is None:
        return pltpu.CompilerParams(vmem_limit_bytes=vmem << 20)
    return pltpu.CompilerParams(
        collective_id=cid, has_side_effects=True, vmem_limit_bytes=vmem << 20
    )


SHORT = pl.CostEstimate(flops=1, transcendentals=0, bytes_accessed=1)
LONG = pl.CostEstimate(flops=20_000_000_000, transcendentals=0, bytes_accessed=60_000_000)


def in_vmem():
    return pl.BlockSpec(memory_space=pltpu.VMEM)


def anywhere():
    return pl.BlockSpec(memory_space=pl.ANY)


def dma(*shape):
    return pltpu.SemaphoreType.DMA(shape)


def remote(src, dst, send_sem, recv_sem, where):
    return pltpu.make_async_remote_copy(
        src_ref=src,
        dst_ref=dst,
        send_sem=send_sem,
        recv_sem=recv_sem,
        device_id=where,
        device_id_type=MESH,
    )


def arrived(dst, send_sem, recv_sem, me):
    remote(dst, dst, send_sem, recv_sem, me).wait_recv()


def greet(peers):
    barrier = pltpu.get_barrier_semaphore()
    for peer in peers:
        pl.semaphore_signal(barrier, inc=1, device_id=peer, device_id_type=MESH)
    pl.semaphore_wait(barrier, len(peers))


def dot(left, right):
    return jnp.dot(left, right, preferred_element_type=f32)


def dot_t(left, right):
    return lax.dot_general(left, right, (((1,), (1,)), ((), ())), preferred_element_type=f32)


def clear(*refs):
    for ref in refs:
        ref[...] = jnp.zeros_like(ref)


def round_up(rows, step):
    return (rows + step - 1) // step * step


def chunks_of(rows):
    return max(1, min(4, rows // 16))


class Copies:
    def __init__(self):
        self.started = []

    def send(self, src, dst, send_sem, recv_sem, where, when=None):
        copy = remote(src, dst, send_sem, recv_sem, where)
        if when is None:
            copy.start()
        else:
            pl.when(when)(copy.start)
        self.started.append((when, copy))

    def finish(self):
        for when, copy in self.started:
            if when is None:
                copy.wait_send()
            else:
                pl.when(when)(copy.wait_send)


class SubScatter:
    def __init__(self, ns, copies, x, got, stage, last, sems):
        t, s = lax.axis_index("tile"), lax.axis_index("sub")
        self.far, self.copies, self.x, self.s, self.t = ns // 2, copies, x, s, t
        self.got, self.stage, self.last = got, stage, last
        self.r, self.c = s // 2, lax.rem(s, 2)
        self.me, self.twin = (t, s), (t, self.r * 2 + 1 - self.c)
        self.count = chunks_of(x.shape[1])
        self.size = x.shape[1] // self.count
        self.s1, self.r1, self.s2, self.r2 = sems

    @staticmethod
    def scratch(ns, rows, width):
        far, count = ns // 2, chunks_of(rows)
        blocks = [pltpu.VMEM((far, rows, width), bf16) for _ in range(3)]
        return blocks + [dma(far, count) for _ in range(4)]

    def peers(self):
        return [self.twin] + [self.peer(k) for k in range(1, self.far)]

    def peer(self, k):
        return (self.t, lax.rem(self.r + k, self.far) * 2 + self.c)

    def part(self, j):
        return pl.ds(j * self.size, self.size)

    def over(self, k):
        return lax.rem(self.r + k, self.far) * 2 + 1 - self.c

    def start_one(self, k):
        for j in range(self.count):
            block, got = self.x.at[self.over(k), self.part(j)], self.got.at[k, self.part(j)]
            self.copies.send(block, got, self.s1.at[k, j], self.r1.at[k, j], self.twin)

    def start(self):
        for k in list(range(1, self.far)) + [0]:
            self.start_one(k)

    def run(self, make, out, meanwhile=None, then=None):
        for k in range(1, self.far):
            make(self.over(k))
            self.start_one(k)
        for k in range(1, self.far):
            make(self.peer(k)[1])
        make(self.over(0))
        self.start_one(0)
        self.cross()
        make(self.s)
        if meanwhile is not None:
            meanwhile()
        self.end(out, then)

    def cross(self):
        for j in range(self.count):
            part = self.part(j)
            for k in range(1, self.far):
                arrived(self.got.at[k, part], self.s1.at[k, j], self.r1.at[k, j], self.me)
                own = self.x[self.peer(k)[1], part].astype(f32)
                self.stage[k, part] = (own + self.got[k, part].astype(f32)).astype(bf16)
                src, dst = self.stage.at[k, part], self.last.at[k, part]
                self.copies.send(src, dst, self.s2.at[k, j], self.r2.at[k, j], self.peer(k))

    def end(self, out, then=None):
        for j in range(self.count):
            part = self.part(j)
            arrived(self.got.at[0, part], self.s1.at[0, j], self.r1.at[0, j], self.me)
            total = self.x[self.s, part].astype(f32) + self.got[0, part].astype(f32)
            for k in range(1, self.far):
                arrived(self.last.at[k, part], self.s2.at[k, j], self.r2.at[k, j], self.me)
                total = total + self.last[k, part].astype(f32)
            out[part] = total
            if then is not None:
                then(j, part)


class SubGather:
    def __init__(self, ns, copies, out, sems):
        t, s = lax.axis_index("tile"), lax.axis_index("sub")
        self.far, self.copies, self.out, self.t, self.s = ns // 2, copies, out, t, s
        self.r, self.c = s // 2, lax.rem(s, 2)
        self.me, self.twin = (t, s), (t, self.r * 2 + 1 - self.c)
        self.count = chunks_of(out.shape[1])
        self.size = out.shape[1] // self.count
        self.s1, self.r1, self.s2, self.r2 = sems

    @staticmethod
    def scratch(ns, rows):
        return [dma(ns // 2, chunks_of(rows)) for _ in range(4)]

    def block(self, r, c, j):
        return self.out.at[lax.rem(r, self.far) * 2 + c, pl.ds(j * self.size, self.size)]

    def start(self):
        for j in range(self.count):
            self.start_one(j)

    def start_one(self, j):
        block = self.block(self.r, self.c, j)
        for k in range(1, self.far):
            peer = (self.t, lax.rem(self.r + k, self.far) * 2 + self.c)
            self.copies.send(block, block, self.s1.at[k, j], self.r1.at[k, j], peer)
        self.copies.send(block, block, self.s2.at[0, j], self.r2.at[0, j], self.twin)

    def relay(self):
        for j in range(self.count):
            for k in range(1, self.far):
                block = self.block(self.r + self.far - k, self.c, j)
                arrived(block, self.s1.at[k, j], self.r1.at[k, j], self.me)
                self.copies.send(block, block, self.s2.at[k, j], self.r2.at[k, j], self.twin)

    def end(self):
        for j in range(self.count):
            for k in range(self.far):
                block = self.block(self.r + self.far - k, 1 - self.c, j)
                arrived(block, self.s2.at[k, j], self.r2.at[k, j], self.me)


def sub_peers(ns):
    t, s = lax.axis_index("tile"), lax.axis_index("sub")
    far, r, c = ns // 2, s // 2, lax.rem(s, 2)
    return [(t, r * 2 + 1 - c)] + [(t, lax.rem(r + k, far) * 2 + c) for k in range(1, far)]


def layer_hat(values):
    width = values.shape[1]
    center = jnp.sum(values, axis=1, keepdims=True) / width
    moved = values - center
    inv_std = lax.rsqrt(jnp.sum(moved * moved, axis=1, keepdims=True) / width + EPSILON)
    return moved * inv_std, inv_std


def layer_back(grad_out, values, gain):
    width = values.shape[1]
    hat, inv_std = layer_hat(values)
    scaled = grad_out * gain
    mean_grad = jnp.sum(scaled, axis=1, keepdims=True) / width
    mean_cross = jnp.sum(scaled * hat, axis=1, keepdims=True) / width
    grad_in = inv_std * (scaled - mean_grad - hat * mean_cross)
    return grad_in, jnp.sum(grad_out * hat, axis=0, keepdims=True)


def tokens_of(ref, p):
    return ref[:, p].reshape(-1, ref.shape[3]) if len(ref.shape) == 4 else ref[p]


def by_head(first, second):
    parts = []
    for h in range(first.shape[1] // HD):
        parts += [head_of(first, h), head_of(second, h)]
    return side_by_side(parts)


def enter_kernel(
    ns, inner, pooled, lift, gain, wq, wk, wv, stream, gathered, q_out, kv_out, *sems
):
    copies = Copies()
    gather = SubGather(ns, copies, gathered, sems)
    mine = tokens_of(inner, gather.s) if len(inner.shape) == 4 else inner[...]
    value = mine.astype(f32) + dot(pooled[...], lift[...]).astype(bf16).astype(f32)
    stream[...] = value
    gathered[gather.s] = (layer_hat(value)[0] * gain[0:1, :]).astype(bf16)
    greet(sub_peers(ns))
    gather.start()
    turned = wq[...].T
    gather.relay()
    gather.end()
    rows = gathered[...].reshape(-1, gathered.shape[2])
    q_out[...] = dot_t(turned, rows).astype(bf16)
    kv_out[...] = by_head(dot(rows, wk[...]), dot(rows, wv[...])).astype(bf16)
    copies.finish()


def attn_out_kernel(ns, mixed_t, weight, before, gain, after, gathered, turned, *scratch):
    copies = Copies()
    own = before.shape[0]
    scatter = SubScatter(ns, copies, *scratch[:4], scratch[4:8])
    gather = SubGather(ns, copies, gathered, scratch[8:])
    turned[...] = mixed_t[...].T

    def make(p):
        rows = turned[pl.ds(pl.multiple_of(p * own, 16), own), :]
        scatter.x[p] = dot(rows, weight[...]).astype(bf16)

    greet(sub_peers(ns))

    def normalize(j, part):
        value = before[part, :] + after[part, :]
        after[part, :] = value
        gathered[gather.s, part] = (layer_hat(value)[0] * gain[1:2, :]).astype(bf16)
        gather.start_one(j)

    scatter.run(make, after, None, normalize)
    gather.relay()
    gather.end()
    copies.finish()


def head_of(values, h):
    return values[:, h * HD : (h + 1) * HD]


def head_probs(queries, keys, mask, h):
    scores = dot_t(head_of(queries, h), head_of(keys, h)) * HD ** (-0.5)
    scores = jnp.where(mask > 0.5, scores, -1000000000.0)
    raised = jnp.exp(scores - jnp.max(scores, axis=1, keepdims=True))
    return raised / jnp.sum(raised, axis=1, keepdims=True)


def side_by_side(parts):
    return jnp.concatenate(parts, axis=1) if len(parts) > 1 else parts[0]


def cross_kernel(
    ns, cross_in, wq, ck, cv, mask, wo, before, gain, after, gathered, queries, mixed, *scratch
):
    copies = Copies()
    scatter = SubScatter(ns, copies, *scratch[:4], scratch[4:8])
    gather = SubGather(ns, copies, gathered, scratch[8:])
    heads = wq.shape[1] // HD

    def make(p):
        q = dot(cross_in[p], wq[...]).astype(bf16)
        queries[p] = q
        keys, values, masked = ck[...], cv[...], mask[...]
        parts = [
            dot(head_probs(q, keys, masked, h).astype(bf16), head_of(values, h))
            for h in range(heads)
        ]
        mixed[p] = side_by_side(parts).astype(bf16)
        scatter.x[p] = dot(mixed[p], wo[...]).astype(bf16)

    greet(sub_peers(ns))

    def normalize(j, part):
        value = before[part, :] + after[part, :]
        after[part, :] = value
        gathered[gather.s, part] = (layer_hat(value)[0] * gain[2:3, :]).astype(bf16)
        gather.start_one(j)

    scatter.run(make, after, None, normalize)
    gather.relay()
    gather.end()
    copies.finish()


def mlp_kernel(
    ns, mlp_in, cotan, w_up, w_down, before, gain,
    grad, gathered, gain_grad, down, up_grad, down_grad, activated, grad_up, cotans, *scratch
):
    copies = Copies()
    for p in range(ns):
        cotans[p] = tokens_of(cotan, p)
    cotan = cotans
    scatter = SubScatter(ns, copies, *scratch[:4], scratch[4:8])
    gather = SubGather(ns, copies, gathered, scratch[8:])
    own = before.shape[0]
    rate = math.sqrt(2.0 / math.pi)

    def make(p):
        up = dot(mlp_in[p], w_up[...])
        square = up * up
        bent = jnp.tanh(rate * (up + 0.044715 * up * square))
        rows = pl.ds(pl.multiple_of(p * own, 16), own)
        activated[rows, :] = (0.5 * up * (1.0 + bent)).astype(bf16)
        slope = 0.5 * (1.0 + bent) + 0.5 * up * (1.0 - bent * bent) * (
            rate * (1.0 + 3.0 * 0.044715 * square)
        )
        turned = (slope * dot_t(cotan[p], w_down[...])).astype(bf16)
        grad_up[rows, :] = turned
        scatter.x[p] = dot_t(turned, w_up[...]).astype(bf16)

    greet(sub_peers(ns))
    whole = lambda ref: ref[...].reshape(ns * own, ref.shape[2])

    def meanwhile():
        up_grad[...] = dot(whole(mlp_in).T, grad_up[...]).astype(bf16)

    gain_grad[...] = jnp.zeros_like(gain_grad)

    def normalize(j, part):
        back, gains = layer_back(grad[part, :], before[part, :], gain[2:3, :])
        gain_grad[...] += gains
        value = cotan[gather.s, part].astype(f32) + back
        grad[part, :] = value
        gathered[gather.s, part] = value.astype(bf16)
        gather.start_one(j)

    scatter.run(make, grad, meanwhile, normalize)
    down_grad[...] = dot(activated[...].T, whole(cotan)).astype(bf16)
    gather.relay()
    down[...] = dot(activated[...], w_down[...]).astype(bf16)
    gather.end()
    copies.finish()


def cross_back_kernel(
    ns, incoming, wo, queries, ck, cv, mask, wq, before, gain, residual, cross_in, mixed,
    grad, gathered, gain_grad, dk_out, dv_out, weights, dk, dv, dq, *scratch
):
    copies = Copies()
    scatter = SubScatter(ns, copies, *scratch[:4], scratch[4:8])
    gather = SubGather(ns, copies, gathered, scratch[8:])
    heads = wq.shape[1] // HD
    own = before.shape[0]
    clear(dk, dv)

    def make(p):
        grad_mixed = dot_t(incoming[p], wo[...]).astype(bf16)
        q, keys, values, masked = queries[p], ck[...], cv[...], mask[...]
        parts_q, parts_k, parts_v = [], [], []
        for h in range(heads):
            probs = head_probs(q, keys, masked, h)
            slope = dot_t(head_of(grad_mixed, h), head_of(values, h))
            lean = probs * (slope - jnp.sum(probs * slope, axis=1, keepdims=True))
            lean = lean.astype(bf16)
            parts_q.append(dot(lean, head_of(keys, h)))
            parts_k.append(dot(lean.T, head_of(q, h)))
            parts_v.append(dot(probs.astype(bf16).T, head_of(grad_mixed, h)))
        part = (side_by_side(parts_q) * HD ** (-0.5)).astype(bf16)
        dq[pl.ds(pl.multiple_of(p * own, 16), own), :] = part
        dk[...] += side_by_side(parts_k)
        dv[...] += side_by_side(parts_v)
        scatter.x[p] = dot_t(part, wq[...]).astype(bf16)

    greet(sub_peers(ns))
    whole = lambda ref: ref[...].reshape(ns * own, ref.shape[2])

    def meanwhile():
        weights[0] = dot(whole(mixed).T, whole(incoming)).astype(bf16)
        dk_out[...] = (dk[...] * HD ** (-0.5)).astype(bf16)
        dv_out[...] = dv[...].astype(bf16)

    gain_grad[...] = jnp.zeros_like(gain_grad)

    def normalize(j, part):
        back, gains = layer_back(grad[part, :], before[part, :], gain[1:2, :])
        gain_grad[...] += gains
        value = residual[part, :] + back
        grad[part, :] = value
        gathered[gather.s, part] = value.astype(bf16)
        gather.start_one(j)

    scatter.run(make, grad, meanwhile, normalize)
    weights[1] = dot(dq[...].T, whole(cross_in)).astype(bf16)
    gather.relay()
    gather.end()
    copies.finish()


def attn_back_kernel(
    ns, dq_t, dkv, wq, wk, wv, before, gain, residual, out, gain_grad, turned, wkv, *scratch
):
    copies = Copies()
    scatter = SubScatter(ns, copies, *scratch[1:5], scratch[5:9])
    total = scratch[0]
    own = before.shape[0]
    turned[...] = dq_t[...].T
    wkv[...] = by_head(wk[...], wv[...])

    def make(p):
        rows = pl.ds(pl.multiple_of(p * own, 16), own)
        value = dot_t(turned[rows, :], wq[...]) + dot_t(dkv[rows, :], wkv[...])
        scatter.x[p] = value.astype(bf16)

    greet(sub_peers(ns))
    scatter.run(make, total)
    back, gains = layer_back(total[...], before[...], gain[0:1, :])
    gain_grad[...] = gains
    out[...] = (residual[...] + back).astype(bf16)
    copies.finish()


def chain_call(kernel, name, cid, outs, args, extra, scatter, gather=True, vmem=16, cost=SHORT):
    ns = lax.axis_size("sub")
    own, width = outs[0][0]
    scratch = list(extra)
    if scatter:
        scratch += [pltpu.VMEM((ns, own, width), bf16)] + SubScatter.scratch(ns, own, width)
    if gather:
        scratch += SubGather.scratch(ns, own)
    return pl.pallas_call(
        functools.partial(kernel, ns),
        out_shape=tuple(jax.ShapeDtypeStruct(*out) for out in outs),
        in_specs=[in_vmem()] * len(args),
        out_specs=(in_vmem(),) * len(outs),
        scratch_shapes=scratch,
        cost_estimate=cost,
        compiler_params=params(cid, vmem),
        name=name,
    )(*args)


def deal(nt, u):
    t, s = lax.axis_index("tile"), lax.axis_index("sub")
    nb = nt // u
    a, b = t // nb, lax.rem(t, nb)
    a_peer = lambda k: (lax.rem(a + k, u) * nb + b, s)
    b_peer = lambda k: (a * nb + lax.rem(b + k, nb), s)
    peers = [a_peer(k) for k in range(1, u)] + [b_peer(k) for k in range(1, nb)]
    return t, s, nb, a, b, a_peer, b_peer, peers


def rows_of(ref, i, size):
    return ref.at[:, pl.ds(pl.multiple_of(i * size, size), size), :]


def lanes_of(ref, i, size):
    return ref.at[:, :, pl.ds(pl.multiple_of(i * size, size), size)]


class TileSum:
    PARTS = 4

    def __init__(self, nt, x, out, pair, line, share_sems):
        t, s = lax.axis_index("tile"), lax.axis_index("sub")
        self.na, self.x, self.out = nt // 2, x, out
        self.a, self.b, self.s = t // 2, lax.rem(t, 2), s
        self.me, self.pair = (t, s), (self.a * 2 + 1 - self.b, s)
        self.half = (out.shape[0] if x is None else x.shape[0]) // 2
        self.piece = self.half // 2 // self.PARTS
        self.folded = None
        if pair:
            self.got1, self.s1, self.r1 = pair
        if line:
            self.stage, self.got2, self.s2, self.r2 = line
        if share_sems:
            self.s3, self.r3, self.s4, self.r4 = share_sems

    @staticmethod
    def buffers(rows, width):
        return pltpu.VMEM((rows // 2, width), bf16)

    @staticmethod
    def sems():
        return [dma(2, TileSum.PARTS) for _ in range(2)]

    @staticmethod
    def pair_scratch(rows, width):
        return [TileSum.buffers(rows, width)] + TileSum.sems()

    @staticmethod
    def line_scratch(rows, width):
        return [TileSum.buffers(rows, width)] * 2 + TileSum.sems()

    def rows(self, b, e, j):
        start = b * self.half + (j * 2 + e) * self.piece
        return pl.ds(pl.multiple_of(start, 16), self.piece)

    def along(self, e):
        up, down = (self.a * 2 + 2 + self.b, self.s), (self.a * 2 - 2 + self.b, self.s)
        return (down, up, self.a) if e else (up, down, self.na - 1 - self.a)

    def start(self):
        for j in range(self.PARTS):
            for e in range(2):
                self.to_pair(e, j).start()

    def to_pair(self, e, j):
        src, dst = self.x.at[self.rows(1 - self.b, e, j)], self.got1.at[self.rows(0, e, j)]
        return remote(src, dst, self.s1.at[e, j], self.r1.at[e, j], self.pair)

    def steps(self):
        return range(self.PARTS + self.na - 1)

    def step_of(self, way, step, action):
        j = step - way
        pl.when((j >= 0) & (j < self.PARTS))(lambda: action(jnp.clip(j, 0, self.PARTS - 1)))

    def add(self, steps):
        for step in steps:
            for e in range(2):
                self.step_of(self.along(e)[2], step, functools.partial(self.add_one, e))

    def with_pair(self, e, j):
        here, mine = self.rows(0, e, j), self.rows(self.b, e, j)
        arrived(self.got1.at[here], self.s1.at[e, j], self.r1.at[e, j], self.me)
        return self.x[mine].astype(f32) + self.got1[here].astype(f32)

    def fold(self, half):
        for j in range(self.PARTS):
            for e in range(2):
                half[self.rows(0, e, j)] = self.with_pair(e, j).astype(bf16)
        for j in range(self.PARTS):
            for e in range(2):
                self.to_pair(e, j).wait_send()

    def add_one(self, e, j):
        _, after, way = self.along(e)
        here, mine = self.rows(0, e, j), self.rows(self.b, e, j)
        both = self.with_pair(e, j) if self.folded is None else self.folded[here].astype(f32)

        @pl.when(way == 0)
        def _():
            self.stage[here] = both.astype(bf16)

        @pl.when(way > 0)
        def _():
            arrived(self.got2.at[here], self.s2.at[e, j], self.r2.at[e, j], self.me)
            self.stage[here] = (both + self.got2[here].astype(f32)).astype(bf16)

        @pl.when(way < self.na - 1)
        def _():
            src, dst = self.stage.at[here], self.got2.at[here]
            remote(src, dst, self.s2.at[e, j], self.r2.at[e, j], after).start()

        @pl.when(way == self.na - 1)
        def _():
            self.out[mine] = self.stage[here]

    def share(self, steps):
        for step in steps:
            for e in range(2):
                way = self.na - 1 - self.along(e)[2]
                self.step_of(way, step, functools.partial(self.share_one, e))

    def share_one(self, e, j):
        before, _, way = self.along(e)
        block = self.out.at[self.rows(self.b, e, j)]

        @pl.when(way < self.na - 1)
        def _():
            arrived(block, self.s3.at[e, j], self.r3.at[e, j], self.me)

        @pl.when(way > 0)
        def _():
            remote(block, block, self.s3.at[e, j], self.r3.at[e, j], before).start()

        remote(block, block, self.s4.at[e, j], self.r4.at[e, j], self.pair).start()

    def end_add(self):
        for j in range(self.PARTS):
            for e in range(2):
                _, after, way = self.along(e)
                if self.folded is None:
                    self.to_pair(e, j).wait_send()
                stage = self.stage.at[self.rows(0, e, j)]
                sent = remote(stage, stage, self.s2.at[e, j], self.r2.at[e, j], after)
                pl.when(way < self.na - 1)(sent.wait_send)

    def end_share(self):
        for j in range(self.PARTS):
            for e in range(2):
                block = self.out.at[self.rows(1 - self.b, e, j)]
                arrived(block, self.s4.at[e, j], self.r4.at[e, j], self.me)
        for j in range(self.PARTS):
            for e in range(2):
                before, _, way = self.along(e)
                block = self.out.at[self.rows(self.b, e, j)]
                sent = remote(block, block, self.s3.at[e, j], self.r3.at[e, j], before)
                pl.when(way > 0)(sent.wait_send)
                remote(block, block, self.s4.at[e, j], self.r4.at[e, j], self.pair).wait_send()


def self_attention_kernel(
    nt, u, q_ref, kv_ref, home, qo, kvo, mixed_out, lse, top, total, mixed, low,
    qs, qr, ks, kr, fs, fr, hs, hr, own
):
    t, s, nb, a, b, a_peer, b_peer, peers = deal(nt, u)
    me = (t, s)
    batch, length = q_ref.shape[0], q_ref.shape[2]
    copies = Copies()
    qo[a] = q_ref[:, pl.ds(pl.multiple_of(a * HD, HD), HD), :]
    local = [pltpu.make_async_copy(lanes_of(kv_ref, a, 2 * HD), kvo.at[t], own.at[0])]
    local[0].start()
    greet(peers)
    for k in range(1, u):
        block = rows_of(q_ref, lax.rem(a + k, u), HD)
        copies.send(block, qo.at[a], qs.at[k], qr.at[k], a_peer(k))
    for k in range(1, u):
        block = lanes_of(kv_ref, lax.rem(a + k, u), 2 * HD)
        copies.send(block, kvo.at[t], ks.at[k], kr.at[k], a_peer(k))
    for m in range(1, nb):
        block = lanes_of(kv_ref, a, 2 * HD)
        copies.send(block, kvo.at[t], fs.at[0, m], fr.at[0, m], b_peer(m))
    clear(total, mixed)
    top[...] = jnp.full(top.shape, -jnp.inf, f32)

    def take(tile, i, n):
        q = qo[i, n] * 0.125
        padded = jnp.concatenate([q, jnp.zeros_like(q)], axis=0)
        keys = kvo[tile, n]
        scores = dot(keys, padded)
        new = jnp.maximum(top[i, n], jnp.max(scores, axis=0, keepdims=True))
        raised = jnp.exp(scores - new)
        scale = jnp.exp(top[i, n] - new)
        added = dot(keys.T[HD:], raised.astype(bf16))
        return (
            new,
            total[i, n] * scale + jnp.sum(raised, axis=0, keepdims=True),
            mixed[i, n] * scale + added,
        )

    def take_all(tile):
        for n in range(batch):
            for i in range(u):
                top[i, n], total[i, n], mixed[i, n] = take(tile, i, n)

    def tile_of(k, m):
        return lax.rem(a + u - k, u) * nb + lax.rem(b + nb - m, nb)

    for k in range(1, u):
        arrived(qo.at[lax.rem(a + u - k, u)], qs.at[k], qr.at[k], me)
    local[0].wait()
    near_first = sorted(range(1, u), key=lambda k: min(k, u - k))
    order = [(0, m) for m in range(nb)] + [(k, 0) for k in near_first]
    order += [(k, m) for k in near_first for m in range(1, nb)]
    for k, m in order[:-1]:
        tile = tile_of(k, m)
        if m:
            arrived(kvo.at[tile], fs.at[k, m], fr.at[k, m], me)
        elif k:
            arrived(kvo.at[tile], ks.at[k], kr.at[k], me)
            for n in range(1, nb):
                block = kvo.at[tile]
                copies.send(block, block, fs.at[k, n], fr.at[k, n], b_peer(n))
        take_all(tile)
    k, m = order[-1]
    tile = tile_of(k, m)
    if m:
        arrived(kvo.at[tile], fs.at[k, m], fr.at[k, m], me)
    elif k:
        arrived(kvo.at[tile], ks.at[k], kr.at[k], me)
    for k in list(range(1, u)) + [0]:
        i = lax.rem(a + k, u)
        for n in range(batch):
            peak, weight, value = take(tile, i, n)
            value = value / weight
            mixed_out[i, n] = value
            low[i, n] = value.astype(bf16)
            lse[i, n] = peak + jnp.log(weight)
        if k:
            copies.send(low.at[i], rows_of(home, a, HD), hs.at[k], hr.at[k], a_peer(k))
        else:
            local.append(pltpu.make_async_copy(low.at[i], rows_of(home, a, HD), own.at[1]))
            local[1].start()
    for k in range(1, u):
        arrived(rows_of(home, lax.rem(a + u - k, u), HD), hs.at[k], hr.at[k], me)
    local[1].wait()
    copies.finish()


def self_attention(q, kv, cid):
    nt = lax.axis_size("tile")
    batch, width, length = q.shape
    u = width // HD
    nb = nt // u
    shape = jax.ShapeDtypeStruct
    dealt = (u, batch, HD, length)
    return pl.pallas_call(
        functools.partial(self_attention_kernel, nt, u),
        out_shape=(
            shape(q.shape, bf16),
            shape(dealt, bf16),
            shape((nt, batch, length, 2 * HD), bf16),
            shape(dealt, f32),
            shape((u, batch, 1, length), f32),
        ),
        in_specs=[in_vmem()] * 2,
        out_specs=(in_vmem(),) * 5,
        scratch_shapes=[
            pltpu.VMEM((u, batch, 1, length), f32),
            pltpu.VMEM((u, batch, 1, length), f32),
            pltpu.VMEM(dealt, f32),
            pltpu.VMEM(dealt, bf16),
        ]
        + [dma(u) for _ in range(4)]
        + [dma(u, nb) for _ in range(2)]
        + [dma(u) for _ in range(2)]
        + [dma(2)],
        cost_estimate=LONG,
        compiler_params=params(cid, 24),
        name="self_attention",
    )(q, kv)


class Nothing:
    def __getattr__(self, name):
        return lambda *args: None


class FullSum:
    def __init__(self, nt, ns, copies, x, out, got1, stage, got2, mine, got3, sems):
        t, s = lax.axis_index("tile"), lax.axis_index("sub")
        self.nt, self.far, self.copies, self.x, self.out = nt, ns // 2, copies, x, out
        self.got1, self.stage, self.got2, self.mine, self.got3 = got1, stage, got2, mine, got3
        self.t, self.s, self.r, self.c = t, s, s // 2, lax.rem(s, 2)
        self.me, self.twin = (t, s), (t, self.r * 2 + 1 - self.c)
        self.part = x.shape[0] // ns
        self.piece = self.part // nt
        (self.s1, self.r1, self.s2, self.r2, self.s3, self.r3) = sems[:6]
        (self.s4, self.r4, self.s5, self.r5, self.s6, self.r6) = sems[6:]

    @staticmethod
    def scratch(nt, ns, rows, width):
        far, part = ns // 2, rows // ns
        return (
            [pltpu.VMEM((far, part, width), bf16) for _ in range(3)]
            + [pltpu.VMEM((part, width), bf16), pltpu.VMEM((nt, part // nt, width), bf16)]
            + [dma(far) for _ in range(4)]
            + [dma(nt) for _ in range(4)]
            + [dma(far) for _ in range(4)]
        )

    def rows(self, r, c):
        return pl.ds(pl.multiple_of((c * self.far + r) * self.part, 16), self.part)

    def slot(self, t):
        return pl.ds(pl.multiple_of(t * self.piece, 16), self.piece)

    def other(self, k):
        return lax.rem(self.r + k, self.far)

    def tile(self, k):
        return lax.rem(self.t + k, self.nt)

    def start(self):
        for k in list(range(1, self.far)) + [0]:
            src = self.x.at[self.rows(self.other(k), 1 - self.c)]
            self.copies.send(src, self.got1.at[k], self.s1.at[k], self.r1.at[k], self.twin)

    def cross(self):
        for k in range(1, self.far):
            arrived(self.got1.at[k], self.s1.at[k], self.r1.at[k], self.me)
            own = self.x[self.rows(self.other(k), self.c)].astype(f32)
            self.stage[k] = (own + self.got1[k].astype(f32)).astype(bf16)
            peer = (self.t, self.other(k) * 2 + self.c)
            self.copies.send(self.stage.at[k], self.got2.at[k], self.s2.at[k], self.r2.at[k], peer)

    def spread(self):
        arrived(self.got1.at[0], self.s1.at[0], self.r1.at[0], self.me)
        total = self.x[self.rows(self.r, self.c)].astype(f32) + self.got1[0].astype(f32)
        for k in range(1, self.far):
            arrived(self.got2.at[k], self.s2.at[k], self.r2.at[k], self.me)
            total = total + self.got2[k].astype(f32)
        self.mine[...] = total.astype(bf16)
        for k in range(1, self.nt):
            p = self.tile(k)
            src = self.mine.at[self.slot(p)]
            self.copies.send(src, self.got3.at[k], self.s3.at[k], self.r3.at[k], (p, self.s))

    def place(self, t, r, c):
        start = (c * self.far + r) * self.part + t * self.piece
        return pl.ds(pl.multiple_of(start, 16), self.piece)

    def settle(self):
        total = self.mine[self.slot(self.t)].astype(f32)
        for k in range(1, self.nt):
            arrived(self.got3.at[k], self.s3.at[k], self.r3.at[k], self.me)
            total = total + self.got3[k].astype(f32)
        here = self.place(self.t, self.r, self.c)
        self.out[here] = total.astype(bf16)
        block = self.out.at[here]
        for k in range(1, self.nt):
            self.copies.send(block, block, self.s4.at[k], self.r4.at[k], (self.tile(k), self.s))

    def share(self):
        for k in range(1, self.nt):
            block = self.out.at[self.place(self.tile(self.nt - k), self.r, self.c)]
            arrived(block, self.s4.at[k], self.r4.at[k], self.me)
        block = self.out.at[self.rows(self.r, self.c)]
        for k in range(1, self.far):
            peer = (self.t, self.other(k) * 2 + self.c)
            self.copies.send(block, block, self.s5.at[k], self.r5.at[k], peer)
        self.copies.send(block, block, self.s6.at[0], self.r6.at[0], self.twin)

    def relay(self):
        for k in range(1, self.far):
            block = self.out.at[self.rows(self.other(self.far - k), self.c)]
            arrived(block, self.s5.at[k], self.r5.at[k], self.me)
            self.copies.send(block, block, self.s6.at[k], self.r6.at[k], self.twin)

    def end(self):
        for k in range(self.far):
            block = self.out.at[self.rows(self.other(self.far - k), 1 - self.c)]
            arrived(block, self.s6.at[k], self.r6.at[k], self.me)


def attention_back_kernel(
    nt, ns, u, d_ref, q_ref, of_ref, lse_ref, kv_ref, mixed_t, grad_attn, early_ref, beside_ref,
    qo, kvo, early_out, beside_out,
    dealt, qd, rows, delta, acc, low, sent, kept, got, stage, mine,
    ds, dr, fs, fr, ks, kr, qs, qr, own, *scratch
):
    t, s, nb, a, b, a_peer, b_peer, peers = deal(nt, u)
    me = (t, s)
    batch, length = d_ref.shape[0], d_ref.shape[2]
    copies = Copies()
    early = TileSum(nt, mine, None, scratch[:3], None, None)
    beside = SubScatter(ns, copies, beside_ref, *scratch[3:6], scratch[6:])
    greet_all(nt, ns)
    dealt[a] = d_ref[:, pl.ds(pl.multiple_of(a * HD, HD), HD), :]
    for k in range(1, u):
        block = rows_of(d_ref, lax.rem(a + k, u), HD)
        copies.send(block, dealt.at[a], ds.at[k], dr.at[k], a_peer(k))
    features = mixed_t.shape[0]
    mine[pl.ds(0, features), :] = dot(mixed_t[...], grad_attn[...]).astype(bf16)
    mine[pl.ds(features, 2 * features), :] = early_ref[...]
    spare = mine.shape[0] - 3 * features
    if spare:
        mine[pl.ds(3 * features, spare), :] = jnp.zeros((spare, mine.shape[1]), bf16)
    early.start()
    beside.start()

    def prepare(i):
        for n in range(batch):
            q, d = q_ref[i, n], dealt[i, n]
            zero = jnp.zeros_like(q)
            qd[i, n, 0] = jnp.concatenate([q * 0.125, zero], axis=0)
            qd[i, n, 1] = jnp.concatenate([zero, d], axis=0)
            rows[i, n, 0] = qd[i, n, 0].T
            rows[i, n, 1] = qd[i, n, 1].T
            delta[i, n] = jnp.sum(d.astype(f32) * of_ref[i, n], axis=0, keepdims=True)

    clear(acc)
    for k in range(u):
        i = lax.rem(a + u - k, u)
        if k:
            arrived(dealt.at[i], ds.at[k], dr.at[k], me)
        prepare(i)

    def work(tile, n):
        kv = kv_ref[tile, n]
        kt = kv.T[:HD]
        total = jnp.zeros(kv.shape, f32)
        for i in range(u):
            probs = jnp.exp(dot(kv, qd[i, n, 0]) - lse_ref[i, n])
            slope = dot(kv, qd[i, n, 1])
            grads = (probs * (slope - delta[i, n])).astype(bf16)
            total = total + dot(probs.astype(bf16), rows[i, n, 1]) + dot(grads, rows[i, n, 0])
            acc[i, n] += dot(kt, grads)
        return total

    def settle(k):
        for n in range(batch):
            total = kept[k, n]
            for m in range(1, nb):
                if n == 0:
                    arrived(got.at[m, k], fs.at[k, m], fr.at[k, m], me)
                total = total + got[m, k, n].astype(f32)
            stage[k, n] = total.astype(bf16)
        if k:
            copies.send(stage.at[k], lanes_of(kvo, a, 2 * HD), ks.at[k], kr.at[k], a_peer(k))

    order = list(range(1, u)) + [0]
    for at, k in enumerate(order):
        for m in range(1, nb):
            tile = lax.rem(a + k, u) * nb + lax.rem(b + m, nb)
            for n in range(batch):
                sent[m, k, n] = work(tile, n).astype(bf16)
            copies.send(sent.at[m, k], got.at[m, k], fs.at[k, m], fr.at[k, m], b_peer(m))
        if at == min(1, u - 1):
            beside.cross()
        for n in range(batch):
            kept[k, n] = work(lax.rem(a + k, u) * nb + b, n)
        if at:
            settle(order[at - 1])
    for k in list(range(1, u)) + [0]:
        i = lax.rem(a + k, u)
        for n in range(batch):
            low[i, n] = (acc[i, n] * 0.125).astype(bf16)
        if k:
            copies.send(low.at[i], rows_of(qo, a, HD), qs.at[k], qr.at[k], a_peer(k))
    local = [pltpu.make_async_copy(low.at[a], rows_of(qo, a, HD), own.at[0])]
    local[0].start()
    beside.end(beside_out)
    settle(order[-1])
    local.append(pltpu.make_async_copy(stage.at[0], lanes_of(kvo, a, 2 * HD), own.at[1]))
    local[1].start()
    early.fold(early_out)
    for k in range(1, u):
        i = lax.rem(a + u - k, u)
        arrived(rows_of(qo, i, HD), qs.at[k], qr.at[k], me)
        arrived(lanes_of(kvo, i, 2 * HD), ks.at[k], kr.at[k], me)
    for copy in local:
        copy.wait()
    copies.finish()


def attention_back(d, q, of, lse, kv, mixed_t, grad_attn, early, beside, cid):
    nt, ns = lax.axis_size("tile"), lax.axis_size("sub")
    u, batch, _, length = q.shape
    nb = nt // u
    block = (batch, length, 2 * HD)
    sums = (round_up(3 * u * HD, 16 * nt), grad_attn.shape[1])
    beside = beside.reshape(ns, -1, beside.shape[1])
    shape = jax.ShapeDtypeStruct
    return pl.pallas_call(
        functools.partial(attention_back_kernel, nt, ns, u),
        out_shape=(
            shape(d.shape, bf16),
            shape((batch, length, u * 2 * HD), bf16),
            shape((sums[0] // 2, sums[1]), bf16),
            shape(beside.shape[1:], f32),
        ),
        in_specs=[in_vmem()] * 9,
        out_specs=(in_vmem(),) * 4,
        scratch_shapes=[
            pltpu.VMEM(q.shape, bf16),
            pltpu.VMEM((u, batch, 2, 2 * HD, length), bf16),
            pltpu.VMEM((u, batch, 2, length, 2 * HD), bf16),
            pltpu.VMEM((u, batch, 1, length), f32),
            pltpu.VMEM(q.shape, f32),
            pltpu.VMEM(q.shape, bf16),
            pltpu.VMEM((nb, u) + block, bf16),
            pltpu.VMEM((u,) + block, f32),
            pltpu.VMEM((nb, u) + block, bf16),
            pltpu.VMEM((u,) + block, bf16),
            pltpu.VMEM(sums, bf16),
            dma(u),
            dma(u),
            dma(u, nb),
            dma(u, nb),
            dma(u),
            dma(u),
            dma(u),
            dma(u),
            dma(2),
        ]
        + TileSum.pair_scratch(*sums)
        + SubScatter.scratch(ns, *beside.shape[1:]),
        cost_estimate=SHORT,
        compiler_params=params(cid, 40),
        name="attention_back",
    )(d, q, of, lse, kv, mixed_t, grad_attn, early, beside)


AROUND = [(-1, 0), (1, 0), (0, -1), (0, 1), (-1, -1), (-1, 1), (1, -1), (1, 1)]
DIAGONAL = AROUND[4:]


def present(nt, ns, t, s, dt, ds):
    y, x = t + dt, s + ds
    return (y >= 0) & (y < nt) & (x >= 0) & (x < ns)


def greet_all(nt, ns):
    t, s = lax.axis_index("tile"), lax.axis_index("sub")
    barrier = pltpu.get_barrier_semaphore()
    for k in range(1, ns):
        peer = (t, lax.rem(s + k, ns))
        pl.semaphore_signal(barrier, inc=1, device_id=peer, device_id_type=MESH)
    for k in range(1, nt):
        peer = (lax.rem(t + k, nt), s)
        pl.semaphore_signal(barrier, inc=1, device_id=peer, device_id_type=MESH)
    count = ns + nt - 2
    for dt, ds in DIAGONAL:
        there = present(nt, ns, t, s, dt, ds)
        count = count + jnp.where(there, 1, 0)

        @pl.when(there)
        def _():
            pl.semaphore_signal(
                barrier, inc=1, device_id=(t + dt, s + ds), device_id_type=MESH
            )

    pl.semaphore_wait(barrier, count)


def border_copies(nt, ns, src, top, bottom, left, right, ss, rs):
    t, s = lax.axis_index("tile"), lax.axis_index("sub")
    rows, cols = src.shape[0], src.shape[1]
    high, low = pl.ds(0, 2), pl.ds(rows - 2, 2)
    first, last = pl.ds(0, 16), pl.ds(cols - 16, 16)
    inner, before, after = pl.ds(2, rows), pl.ds(0, 2), pl.ds(rows + 2, 2)
    pairs = [
        (src.at[high], bottom),
        (src.at[low], top),
        (src.at[:, first], right.at[inner]),
        (src.at[:, last], left.at[inner]),
        (src.at[high, first], right.at[after]),
        (src.at[high, last], left.at[after]),
        (src.at[low, first], right.at[before]),
        (src.at[low, last], left.at[before]),
    ]
    copies = []
    for i, (dt, ds) in enumerate(AROUND):
        out = present(nt, ns, t, s, dt, ds)
        back = present(nt, ns, t, s, -dt, -ds)
        copies.append((out, back, remote(*pairs[i], ss.at[i], rs.at[i], (t + dt, s + ds))))
    return copies


def begin(copies):
    for out, _, copy in copies:
        pl.when(out)(copy.start)


def finish(copies):
    for out, back, copy in copies:
        pl.when(back)(copy.wait_recv)
        pl.when(out)(copy.wait_send)


def sum_near(nt, ns, value, first, ss, rs):
    t, s = lax.axis_index("tile"), lax.axis_index("sub")
    first[s] = value
    copies = []
    for k in range(1, ns):
        peer = (t, lax.rem(s + k, ns))
        copies.append(remote(first.at[s], first.at[s], ss.at[k], rs.at[s], peer))
        copies[-1].start()
    return copies


def sum_far(nt, ns, first, second, ss1, rs1, ss2, rs2):
    t, s = lax.axis_index("tile"), lax.axis_index("sub")
    for k in range(1, ns):
        p = lax.rem(s + k, ns)
        arrived(first.at[p], ss1.at[k], rs1.at[p], (t, s))
    total = first[0]
    for k in range(1, ns):
        total = total + first[k]
    second[t] = total
    copies = []
    for k in range(1, nt):
        peer = (lax.rem(t + k, nt), s)
        copies.append(remote(second.at[t], second.at[t], ss2.at[k], rs2.at[t], peer))
        copies[-1].start()
    return copies


def sum_end(nt, second, ss2, rs2):
    t, s = lax.axis_index("tile"), lax.axis_index("sub")
    for k in range(1, nt):
        p = lax.rem(t + k, nt)
        arrived(second.at[p], ss2.at[k], rs2.at[p], (t, s))
    total = second[0]
    for k in range(1, nt):
        total = total + second[k]
    return total


def sum_scratch(nt, ns, channels, rows=2):
    return [
        pltpu.VMEM((ns, rows, channels), f32),
        pltpu.VMEM((nt, rows, channels), f32),
        dma(ns),
        dma(ns),
        dma(nt),
        dma(nt),
    ]


def in_groups(values):
    count, channels = values.shape
    per = channels // G
    row = lax.broadcasted_iota(jnp.int32, (channels, channels), 0) // per
    col = lax.broadcasted_iota(jnp.int32, (channels, channels), 1) // per
    same = jnp.where(row == col, 1.0, 0.0).astype(bf16)
    parts, rest = [], values
    for _ in range(3):
        parts.append(rest.astype(bf16))
        rest = rest - parts[-1].astype(f32)
    out = [dot(part, same) for part in parts]
    return out[0] + out[1] + out[2]


def fold(values):
    return jnp.sum(values.reshape(-1, 8, values.shape[-1]), axis=0)


def row_sums(count, channels, pair):
    def step(i, carry):
        first, second = pair(i)
        return carry[0] + fold(first), carry[1] + fold(second)

    zero = jnp.zeros((8, channels), f32)
    first, second = lax.fori_loop(0, count, step, (zero, zero), unroll=2)
    return jnp.concatenate(
        [jnp.sum(first, axis=0, keepdims=True), jnp.sum(second, axis=0, keepdims=True)], axis=0
    )


def sigmoid(values):
    return 1.0 / (1.0 + jnp.exp(-values))


def silu_slope(values):
    sigma = sigmoid(values)
    return sigma * (1.0 + values * (1.0 - sigma))


def block_of(total, step, limit):
    return max(n for n in range(step, limit + 1, step) if total % n == 0)


def put_left_to_right(flat, triple):
    total, channels = triple.shape[0], flat.shape[1]
    size = block_of(total, 16, 256)
    for start in range(0, total, size):
        for j in range(3):
            piece = flat[pl.ds(8 + start + j - 1, size), :]
            triple[pl.ds(start, size), pl.ds(j * channels, channels)] = piece.astype(bf16)


def conv_rows(triple, weight, start, size, pitch, multiply=dot):
    taps = [triple[pl.ds(start + i * pitch, size), :] for i in range(3)]
    return multiply(jnp.concatenate(taps, axis=1), weight)


def turned_taps(weight):
    return jnp.concatenate([weight[8 - k] for k in range(9)], axis=1)


def list_length(rows, pitch):
    return 16 + rows * pitch + 16


def fill(flat, rows, cols, row_ok, left_ok, right_ok, body, ending, opening):
    pitch = cols + 16
    channels = flat.shape[1]
    place = lax.broadcasted_iota(jnp.int32, (16, channels), 0)
    flat[pl.ds(0, 8), :] = jnp.zeros((8, channels), f32)
    end = 8 + 16 + rows * pitch
    flat[pl.ds(end, 24), :] = jnp.zeros((24, channels), f32)

    def places(right_good, left_good):
        good = jnp.where(place < 8, jnp.where(right_good, 1, 0), jnp.where(left_good, 1, 0))
        return good > 0

    flat[pl.ds(8, 16), :] = jnp.where(
        places(False, left_ok & row_ok(0)), opening(), 0.0
    )

    def step(i, carry):
        start = pl.multiple_of(24 + i * pitch, 8)
        value = body(i)
        good = jnp.full(value.shape, jnp.where(row_ok(i), 1, 0), jnp.int32)
        flat[pl.ds(start, cols), :] = jnp.where(good > 0, value, 0.0)
        good = places(right_ok & row_ok(i), left_ok & row_ok(i + 1))
        flat[pl.ds(start + cols, 16), :] = jnp.where(good, ending(i), 0.0)
        return carry

    lax.fori_loop(0, rows, step, 0)


def sides(left, right, i):
    place = lax.broadcasted_iota(jnp.int32, right.shape[1:], 0)
    return jnp.where(place < 8, right[i].astype(f32), left[i + 1].astype(f32))


def outer_forward_kernel(
    nt, ns, img, w1, w2, vec, gain1, gain2, gain3, text_in, wk_in, wv_in,
    out, pooled, act1_out, act2_out, hidden, stats, gains_out, keys, values,
    body, left, right, flat, act1, act2, rowsum, gains, text, wk, wv,
    border_ss, border_rs, keep, gain_ss, gain_rs, *sums
):
    rows, cols, channels = img.shape
    pitch = cols + 16
    t, s = lax.axis_index("tile"), lax.axis_index("sub")
    sums1, sums2 = sums[:6], sums[6:]
    count = float(nt * ns * rows * cols * (channels // G))
    pairs = ((text_in, text), (wk_in, wk), (wv_in, wv))
    loads = [pltpu.make_async_copy(*pair, keep.at[2 + i]) for i, pair in enumerate(pairs)]
    clear(body, left, right)
    greet_all(nt, ns)
    top, bottom = body.at[pl.ds(0, 2)], body.at[pl.ds(rows + 2, 2)]
    border = border_copies(nt, ns, img, top, bottom, left, right, border_ss, border_rs)
    begin(border)
    pixel = lambda i: img[i].astype(f32)
    local1 = row_sums(rows, channels, lambda i: (pixel(i), pixel(i) * pixel(i)))
    copies = sum_near(nt, ns, local1, sums1[0], sums1[2], sums1[3])
    copies += sum_far(nt, ns, sums1[0], sums1[1], *sums1[2:])
    for copy in loads:
        copy.start()
    gains[s] = jnp.concatenate([gain1[...], gain2[...], gain3[...]], axis=0)
    for k in range(1, ns):
        block, peer = gains.at[s], (t, lax.rem(s + k, ns))
        copies.append(remote(block, block, gain_ss.at[k], gain_rs.at[s], peer))
        copies[-1].start()

    def inner(i, carry):
        body[i + 2] = img[i]
        return carry

    lax.fori_loop(0, rows, inner, 0)
    total1 = sum_end(nt, sums1[1], sums1[4], sums1[5])

    def moments(total):
        grouped = in_groups(total) / count
        center = grouped[0:1]
        return center, lax.rsqrt(jnp.maximum(grouped[1:2] - center * center, 0.0) + EPSILON)

    center1, std1 = moments(total1)
    scale1 = std1 * vec[0:1]
    shift1 = vec[1:2] - center1 * scale1
    finish(border)

    def first_act(values):
        normed = values.astype(f32) * scale1 + shift1
        return normed * sigmoid(normed)

    ok = lambda lift: (
        lambda i: (t * rows + i - lift >= 0) & (t * rows + i - lift < nt * rows)
    )
    fill(
        flat, rows + 4, cols, ok(2), s > 0, s < ns - 1,
        lambda i: first_act(body[i]),
        lambda i: first_act(sides(left, right, i)),
        lambda: first_act(left[0]),
    )
    put_left_to_right(flat, act1)
    saved = [pltpu.make_async_copy(act1, act1_out, keep.at[0])]
    saved[0].start()
    length = list_length(rows + 2, pitch)
    size = block_of(length, 16, 700)
    for start in range(0, length, size):
        hidden[pl.ds(start, size), :] = conv_rows(act1, w1[...], start, size, pitch) + vec[4:5]

    def hidden_row(i):
        return hidden[pl.ds(pl.multiple_of(16 + (i + 1) * pitch, 16), cols), :]

    local2 = row_sums(rows, channels, lambda i: (hidden_row(i), hidden_row(i) * hidden_row(i)))
    copies += sum_near(nt, ns, local2, sums2[0], sums2[2], sums2[3])
    copies += sum_far(nt, ns, sums2[0], sums2[1], *sums2[2:])
    for copy in loads:
        copy.wait()
    keys[...] = dot(text[...], wk[...]).astype(bf16)
    values[...] = dot(text[...], wv[...]).astype(bf16)
    total2 = sum_end(nt, sums2[1], sums2[4], sums2[5])
    center2, std2 = moments(total2)
    scale2 = std2 * vec[2:3]
    shift2 = vec[3:4] - center2 * scale2
    stats[...] = jnp.concatenate(
        [center1, std1, center2, std2, total2, jnp.zeros_like(total2)], axis=0
    )

    def second_act(start, amount):
        normed = hidden[pl.ds(start, amount), :] * scale2 + shift2
        return normed * sigmoid(normed)

    at = lambda i: pl.multiple_of(16 + i * pitch, 16)
    fill(
        flat, rows + 2, cols, ok(1), s > 0, s < ns - 1,
        lambda i: second_act(at(i), cols),
        lambda i: second_act(at(i) + cols, 16),
        lambda: second_act(0, 16),
    )
    put_left_to_right(flat, act2)
    saved.append(pltpu.make_async_copy(act2, act2_out, keep.at[1]))
    saved[1].start()
    lc = cols // POOL
    for start in range(0, rows, 2 * POOL):
        grown = conv_rows(act2, w2[...], 16 + start * pitch, 2 * POOL * pitch, pitch)
        grown = grown.reshape(2 * POOL, pitch, channels)[:, :cols]
        grown = grown + img[pl.ds(start, 2 * POOL)].astype(f32)
        out[pl.ds(start, 2 * POOL)] = grown.astype(bf16)
        for half in range(2):
            added = jnp.sum(grown[half * POOL : (half + 1) * POOL], axis=0)
            means = []
            for n in range(channels // 128):
                rowsum[n] = added[:, n * 128 : (n + 1) * 128]
                mean = rowsum[n, pl.ds(0, lc, stride=POOL), :]
                for k in range(1, POOL):
                    mean = mean + rowsum[n, pl.ds(k, lc, stride=POOL), :]
                means.append(mean * (1.0 / (POOL * POOL)))
            place = pl.ds((start // POOL + half) * lc, lc)
            pooled[place, :] = jnp.concatenate(means, axis=1).astype(bf16)
    for k in range(1, ns):
        p = lax.rem(s + k, ns)
        arrived(gains.at[p], gain_ss.at[k], gain_rs.at[p], (t, s))
    gains_out[...] = side_by_side([gains[i] for i in range(ns)])
    for copy in copies:
        copy.wait_send()
    for copy in saved:
        copy.wait()


def outer_forward(img, w1, w2, vec, gains, text, wk, wv, cid):
    nt, ns = lax.axis_size("tile"), lax.axis_size("sub")
    rows, cols, channels = img.shape
    pitch = cols + 16
    long1, long2 = list_length(rows + 4, pitch), list_length(rows + 2, pitch)
    shape = jax.ShapeDtypeStruct
    return pl.pallas_call(
        functools.partial(outer_forward_kernel, nt, ns),
        out_shape=(
            shape(img.shape, bf16),
            shape((rows // POOL * (cols // POOL), channels), bf16),
            shape((long1, 3 * channels), bf16),
            shape((long2, 3 * channels), bf16),
            shape((long2, channels), f32),
            shape((8, channels), f32),
            shape((3, ns * wk.shape[1]), f32),
            shape((text.shape[0], wk.shape[1]), bf16),
            shape((text.shape[0], wk.shape[1]), bf16),
        ),
        in_specs=[in_vmem()] * 7 + [anywhere()] * 3,
        out_specs=(in_vmem(),) * 2 + (anywhere(),) * 2 + (in_vmem(),) * 5,
        scratch_shapes=[
            pltpu.VMEM((rows + 4, cols, channels), bf16),
            pltpu.VMEM((rows + 5, 16, channels), bf16),
            pltpu.VMEM((rows + 5, 16, channels), bf16),
            pltpu.VMEM((long1 + 16, channels), f32),
            pltpu.VMEM((long1, 3 * channels), bf16),
            pltpu.VMEM((long2, 3 * channels), bf16),
            pltpu.VMEM((channels // 128, cols, 128), f32),
            pltpu.VMEM((ns, 3, wk.shape[1]), f32),
            pltpu.VMEM(text.shape, bf16),
            pltpu.VMEM(wk.shape, bf16),
            pltpu.VMEM(wv.shape, bf16),
            dma(8),
            dma(8),
            dma(5),
            dma(ns),
            dma(ns),
        ]
        + sum_scratch(nt, ns, channels) * 2,
        cost_estimate=LONG,
        compiler_params=params(cid),
        name="outer_forward",
    )(img, w1, w2, vec, *gains, text, wk, wv)


def kernel_grads(triple, grads_t, start, size, pitch, out, between=()):
    for i in range(3):
        rows = triple[pl.ds(start + i * pitch, size), :]
        taps = dot(grads_t[...], rows).T.astype(bf16)
        out[pl.ds(i * taps.shape[0], taps.shape[0]), :] = taps
        for action in between[i : i + 1]:
            action()


def outer_backward_kernel(
    nt, ns, cut, cot, img, w2, w1, vec, stats, hidden, wide, tokens, gains, pooled, lifted, lift_weight,
    attn_in, grad_q_t, grad_kv, grad_ck, grad_cv, act1_in, act2_in, outer_grad, tall_out, wide_out, tokens_out, sum2_out, sum1_out, back_out,
    spread, grad2, body, left, right, flat, act1, act2, triple, inner_t, slope, own2, own1, tall,
    border_ss, border_rs, keep, token_ss, token_rs, *scratch
):
    rows, cols, channels = img.shape
    pitch = cols + 16
    lr, lc = rows // POOL, cols // POOL
    t, s = lax.axis_index("tile"), lax.axis_index("sub")
    sums2, sums1, scratch = scratch[:6], scratch[6:12], scratch[12:]
    copies = Copies()
    early = TileSum(nt, None, wide_out, None, scratch[:4], scratch[4:8])
    early.folded = wide
    late = TileSum(nt, tall, tall_out, scratch[8:11], scratch[11:15], scratch[15:19])
    scratch = scratch[19:]
    second = FullSum(nt, ns, copies, own2, sum2_out, *scratch[:5], scratch[5:17])
    scratch = scratch[17:]
    first, rest = Nothing(), []
    for skip, rows_of_sum in ((0, cut), (cut, own1.shape[0] - cut)):
        if rows_of_sum:
            part = pl.ds(skip, rows_of_sum)
            views = own1.at[part], sum1_out.at[part]
            rest.append(FullSum(nt, ns, copies, *views, *scratch[:5], scratch[5:17]))
            scratch = scratch[17:]
    if len(rest) > 1:
        first = rest[0]
    rest = rest[-1]
    count = float(nt * ns * rows * cols * (channels // G))
    held = [
        pltpu.make_async_copy(act2_in, act2, keep.at[0]),
        pltpu.make_async_copy(act1_in, act1, keep.at[1]),
    ]
    for copy in held:
        copy.start()
    clear(body, left, right)
    greet_all(nt, ns)
    width = lifted.shape[1]
    shrunk = dot_t(lifted[...], lift_weight[...]) * (1.0 / (POOL * POOL))

    def widen(i):
        for n in range(channels // 128):
            part = shrunk[i * lc : (i + 1) * lc, n * 128 : (n + 1) * 128]
            for k in range(POOL):
                spread[i, n, pl.ds(k, lc, stride=POOL), :] = part

    for i in range(lr):
        widen(i)

    def outer(i):
        parts = [spread[i // POOL, n] for n in range(channels // 128)]
        return cot[i].astype(f32) + jnp.concatenate(parts, axis=1)

    def round_outer(i, carry):
        value = outer(i).astype(bf16)
        grad2[i] = value
        body[i + 2] = value
        return carry

    lax.fori_loop(0, rows, round_outer, 0)
    top, bottom = body.at[pl.ds(0, 2)], body.at[pl.ds(rows + 2, 2)]
    border = border_copies(nt, ns, grad2, top, bottom, left, right, border_ss, border_rs)
    begin(border)
    tokens_out[s] = tokens[s]
    for k in range(1, ns):
        p = lax.rem(s + k, ns)
        copies.send(tokens.at[p], tokens_out.at[s], token_ss.at[k], token_rs.at[k], (t, p))
    features = grad_q_t.shape[0]
    heads = features // HD
    attn_t = attn_in[...].T
    tall[pl.ds(0, width), :] = dot_t(attn_t, grad_q_t[...]).astype(bf16)
    both = dot(attn_t, grad_kv[...])
    for n in range(2):
        lanes = [both[:, (2 * h + n) * HD : (2 * h + n + 1) * HD] for h in range(heads)]
        part = jnp.concatenate(lanes, axis=1) if heads > 1 else lanes[0]
        tall[pl.ds((1 + n) * width, width), :] = part.astype(bf16)
    used = 3 * width
    for ref in (grad_ck, grad_cv):
        tall[pl.ds(used, ref.shape[0]), :] = ref[...]
        used += ref.shape[0]
    if used < tall.shape[0]:
        tall[pl.ds(used, tall.shape[0] - used), :] = jnp.zeros(
            (tall.shape[0] - used, features), bf16
        )
    late.start()
    steps = list(early.steps())
    early.add(steps[:1])
    total = rows * pitch

    def turned(row):
        for start in range(0, rows, 8):
            block = [row(start + k) for k in range(8)]
            gap = jnp.zeros((16, channels), bf16)
            piece = jnp.concatenate([p for b in block for p in (b, gap)], axis=0)
            inner_t[:, pl.ds(start * pitch, 8 * pitch)] = piece.T

    def pad_below(ref, used):
        if used < ref.shape[0]:
            ref[pl.ds(used, ref.shape[0] - used), :] = jnp.zeros(
                (ref.shape[0] - used, channels), bf16
            )

    taps = 9 * channels
    turned(lambda i: grad2[i])
    held[0].wait()
    between = [lambda k=k: early.add(steps[k : k + 1]) for k in (1, 2, 3)]
    kernel_grads(act2, inner_t, 16, total, pitch, own2, between)
    lift_grad = dot(pooled[...].T, lifted[...]).astype(bf16)
    for n in range(width // channels):
        own2[pl.ds(taps + n * channels, channels), :] = lift_grad[
            :, n * channels : (n + 1) * channels
        ]
    pad_below(own2, taps + width)
    second.start()
    early.add(steps[4:5])
    finish(border)
    ok = lambda lift_by: (
        lambda i: (t * rows + i - lift_by >= 0) & (t * rows + i - lift_by < nt * rows)
    )
    fill(
        flat, rows + 4, cols, ok(2), s > 0, s < ns - 1,
        lambda i: body[i].astype(f32),
        lambda i: sides(left, right, i),
        lambda: left[0].astype(f32),
    )
    put_left_to_right(flat, triple)
    second.cross()
    center1, std1, center2, std2 = (stats[k : k + 1] for k in range(4))
    gain1, bias1, gain2, bias2 = (vec[k : k + 1] for k in range(4))
    length = list_length(rows + 2, pitch)
    size = block_of(length, 16, 700)
    w2t = turned_taps(w2)
    for start in range(0, length, size):
        hat = (hidden[pl.ds(start, size), :] - center2) * std2
        slope[pl.ds(start, size), :] = conv_rows(
            triple, w2t, start, size, pitch, dot_t
        ) * silu_slope(hat * gain2 + bias2)
        if start == size:
            early.add(steps[5:6])
    early.add(steps[6:])

    at = lambda i: pl.multiple_of(16 + i * pitch, 16)

    def pair2(i):
        place = pl.ds(at(i + 1), cols)
        value = slope[place, :]
        return value, value * ((hidden[place, :] - center2) * std2)

    local2 = jnp.concatenate([row_sums(rows, channels, pair2), gains[...]], axis=0)
    plain = sum_near(nt, ns, local2, sums2[0], sums2[2], sums2[3])
    plain += sum_far(nt, ns, sums2[0], sums2[1], *sums2[2:])
    second.spread()
    early.share(steps[:2])
    late.add(steps[:2])
    back2 = sum_end(nt, sums2[1], sums2[4], sums2[5])
    back2, gains_total = back2[:2], back2[2:]
    means2 = in_groups(back2 * gain2) / count

    def grad_hidden(start, amount):
        hat = (hidden[pl.ds(start, amount), :] - center2) * std2
        value = slope[pl.ds(start, amount), :] * gain2 - means2[0:1] - hat * means2[1:2]
        return std2 * value

    fill(
        flat, rows + 2, cols, ok(1), s > 0, s < ns - 1,
        lambda i: grad_hidden(at(i), cols),
        lambda i: grad_hidden(at(i) + cols, 16),
        lambda: grad_hidden(0, 16),
    )
    early.share(steps[2:3])
    late.add(steps[2:3])
    turned(lambda i: flat[pl.ds(24 + (i + 1) * pitch, cols), :].astype(bf16))
    held[1].wait()
    between = [lambda: late.add(steps[3:4]), lambda: first.start(), lambda: late.add(steps[4:5])]
    between[0] = lambda: (early.share(steps[3:4]), late.add(steps[3:4]))
    kernel_grads(act1, inner_t, 16 + pitch, total, pitch, own1, between)
    pad_below(own1, taps)
    rest.start()
    early.share(steps[4:5])
    second.settle()
    first.cross()
    put_left_to_right(flat, triple.at[pl.ds(0, length)])
    rest.cross()
    hat1 = lambda i: (img[i].astype(f32) - center1) * std1
    step = 2 * POOL
    w1t = turned_taps(w1)
    for start in range(0, rows, step):
        value = conv_rows(triple, w1t, 16 + start * pitch, step * pitch, pitch, dot_t)
        value = value.reshape(step, pitch, channels)[:, :cols]
        hat = (img[pl.ds(start, step)].astype(f32) - center1) * std1
        outer_grad[pl.ds(start, step)] = value * silu_slope(hat * gain1 + bias1)
        if start == step:
            early.share(steps[5:6])
            late.add(steps[5:6])
    first.spread()
    early.share(steps[6:])
    late.add(steps[6:])
    late.share(steps[:1])
    local1 = row_sums(rows, channels, lambda i: (outer_grad[i], outer_grad[i] * hat1(i)))
    plain += sum_near(nt, ns, local1, sums1[0], sums1[2], sums1[3])
    rest.spread()
    plain += sum_far(nt, ns, sums1[0], sums1[1], *sums1[2:])
    late.share(steps[1:3])
    second.share()
    back1 = sum_end(nt, sums1[1], sums1[4], sums1[5])
    means1 = in_groups(back1 * gain1) / count
    first.settle()
    late.share(steps[3:4])

    def last(i, carry):
        value = outer_grad[i] * gain1 - means1[0:1] - hat1(i) * means1[1:2]
        outer_grad[i] = outer(i) + std1 * value
        return carry

    lax.fori_loop(0, rows, last, 0)
    back_out[...] = jnp.concatenate(
        [back1, back2, means2, jnp.zeros_like(means2), gains_total], axis=0
    )
    rest.settle()
    late.share(steps[4:5])
    first.share()
    late.share(steps[5:])
    second.relay()
    rest.share()
    first.relay()
    for k in range(1, ns):
        block = tokens_out.at[lax.rem(s + ns - k, ns)]
        arrived(block, token_ss.at[k], token_rs.at[k], (t, s))
    rest.relay()
    early.end_add()
    early.end_share()
    second.end()
    first.end()
    late.end_add()
    late.end_share()
    rest.end()
    copies.finish()
    for copy in plain:
        copy.wait_send()


def outer_backward(
    cot, img, w2, w1, vec, stats, hidden, wide, tokens, gains, pooled, lifted, lift_weight,
    attn_in, grad_q_t, grad_kv, grad_ck, grad_cv, act1, act2, cid
):
    nt, ns = lax.axis_size("tile"), lax.axis_size("sub")
    rows, cols, channels = img.shape
    pitch = cols + 16
    long1, long2 = list_length(rows + 4, pitch), list_length(rows + 2, pitch)
    shape = jax.ShapeDtypeStruct
    step = 16 * nt * ns
    width, features = attn_in.shape[1], grad_q_t.shape[0]
    rows2 = round_up(9 * channels + width, step)
    tall = (round_up(3 * width + 2 * grad_ck.shape[0], 16 * nt), features)
    cut = 6 * channels // step * step
    rows1 = round_up(9 * channels, step)
    return pl.pallas_call(
        functools.partial(outer_backward_kernel, nt, ns, cut),
        out_shape=(
            shape(img.shape, f32),
            shape(tall, bf16),
            shape((2 * wide.shape[0], wide.shape[1]), bf16),
            shape(tokens.shape, bf16),
            shape((rows2, channels), bf16),
            shape((rows1, channels), bf16),
            shape((8 + gains.shape[0], channels), f32),
        ),
        in_specs=[in_vmem()] * 18 + [anywhere()] * 2,
        out_specs=(in_vmem(),) * 7,
        scratch_shapes=[
            pltpu.VMEM((rows // POOL, channels // 128, cols, 128), f32),
            pltpu.VMEM((rows, cols, channels), bf16),
            pltpu.VMEM((rows + 4, cols, channels), bf16),
            pltpu.VMEM((rows + 5, 16, channels), bf16),
            pltpu.VMEM((rows + 5, 16, channels), bf16),
            pltpu.VMEM((long1 + 16, channels), f32),
            pltpu.VMEM((long1, 3 * channels), bf16),
            pltpu.VMEM((long2, 3 * channels), bf16),
            pltpu.VMEM((long1, 3 * channels), bf16),
            pltpu.VMEM((channels, rows * pitch), bf16),
            pltpu.VMEM((long2, channels), f32),
            pltpu.VMEM((rows2, channels), bf16),
            pltpu.VMEM((rows1, channels), bf16),
            pltpu.VMEM(tall, bf16),
            dma(8),
            dma(8),
            dma(2),
            dma(ns),
            dma(ns),
        ]
        + sum_scratch(nt, ns, channels, 2 + gains.shape[0])
        + sum_scratch(nt, ns, channels)
        + TileSum.line_scratch(2 * wide.shape[0], wide.shape[1])
        + TileSum.sems()
        + TileSum.sems()
        + TileSum.pair_scratch(*tall)
        + TileSum.line_scratch(*tall)
        + TileSum.sems()
        + TileSum.sems()
        + FullSum.scratch(nt, ns, rows2, channels)
        + (FullSum.scratch(nt, ns, cut, channels) if cut else [])
        + FullSum.scratch(nt, ns, rows1 - cut, channels),
        cost_estimate=SHORT,
        compiler_params=params(cid, 62),
        name="outer_backward",
    )(
        cot, img, w2, w1, vec, stats, hidden, wide, tokens, gains, pooled, lifted, lift_weight,
        attn_in, grad_q_t, grad_kv, grad_ck, grad_cv, act1, act2,
    )


def finish_kernel(text, up, down, *refs):
    q, k, v, ck, cv, o, co, cq, second, first = refs[:10]
    lift, refs = refs[10:-13], refs[-13:]
    for src, dst in zip((q, k, v, o, co, second, first, up, down), refs[:9]):
        dst[...] = src[...].astype(f32)
    refs[9][...] = cq[...].T.astype(f32)
    turned = text[...].T
    refs[10][...] = dot(turned, ck[...])
    refs[11][...] = dot(turned, cv[...])
    refs[12][...] = jnp.concatenate([part[...].astype(f32) for part in lift], axis=1)


def finish_grads(text, up, down, tall, wide, second, first, taps, text_rows):
    features, width = tall.shape[1], wide.shape[1]
    channels = first.shape[1]
    steps = features // 32
    row = lambda size, lanes, skip=0: pl.BlockSpec((size, lanes), lambda i: (skip + i, 0))
    size = width // steps
    tall_specs = [row(size, features, n * steps) for n in range(3)]
    start = 3 * width // text_rows
    tall_specs += [
        pl.BlockSpec((text_rows, features), lambda i, n=n: (start + n, 0)) for n in range(2)
    ]
    wide_specs = [row(32, width, n * steps) for n in range(2)]
    wide_specs.append(pl.BlockSpec((features, size), lambda i: (2, i)))
    size = taps // steps
    lift_size = channels // steps
    lift_specs = [
        row(lift_size, channels, taps // lift_size + n * steps) for n in range(width // channels)
    ]
    full = text.shape[1]
    up_specs = [row(w.shape[0] // steps, w.shape[1]) for w in (up, down)]
    in_specs = [pl.BlockSpec((text.shape[0], full // steps), lambda i: (0, i))] + up_specs
    in_specs += tall_specs + wide_specs + [row(size, channels)] * 2 + lift_specs
    shape = lambda *dims: jax.ShapeDtypeStruct(dims, f32)
    return pl.pallas_call(
        finish_kernel,
        grid=(steps,),
        out_shape=(shape(width, features),) * 3
        + (shape(features, width),) * 2
        + (shape(taps, channels),) * 2
        + (shape(*up.shape), shape(*down.shape), shape(width, features))
        + (shape(full, features), shape(full, features), shape(channels, width)),
        in_specs=in_specs,
        out_specs=[row(width // steps, features)] * 3
        + [row(32, width)] * 2
        + [row(size, channels)] * 2
        + up_specs
        + [row(width // steps, features)]
        + [row(full // steps, features)] * 2
        + [row(lift_size, width)],
        cost_estimate=SHORT,
        compiler_params=params(),
        name="finish_grads",
    )(text, up, down, *[tall] * 5, *[wide] * 3, second, first, *[second] * len(lift_specs))


def time_embed(time_steps, channels):
    half_width = channels // 2
    frequency = jnp.exp(
        -math.log(10000.0) * jnp.arange(half_width).astype(f32) / half_width
    )
    angles = time_steps.astype(f32)[:, None] * frequency[None, :]
    return jnp.concatenate([jnp.sin(angles), jnp.cos(angles)], axis=1)


def weight_grad(inputs, grads):
    return lax.dot_general(inputs, grads, (((0,), (0,)), ((), ())), preferred_element_type=f32)


def local(
    outer_image,
    inner_image,
    text_states,
    time_steps,
    text_lengths,
    first_gain,
    first_bias,
    conv_first,
    time_weight,
    second_gain,
    second_bias,
    conv_second,
    lift_weight,
    attn_gain,
    query_weight,
    key_weight,
    value_weight,
    out_weight,
    cross_gain,
    cross_query,
    cross_key,
    cross_value,
    cross_out,
    mlp_gain,
    up_weight,
    down_weight,
    outer_cotan,
    inner_cotan,
):
    nt, ns = lax.axis_size("tile"), lax.axis_size("sub")
    s = lax.axis_index("sub")
    batch, rows, cols, channels = outer_image.shape
    lr, lc = rows // POOL, cols // POOL
    width = inner_image.shape[2] * ns
    features = inner_image.shape[2]
    heads = features // HD
    own = batch * lr * lc
    length = ns * lr * lc
    pixels = rows * cols * nt * ns


    def whole_tokens(values):
        full = lax.all_gather(values, "sub", axis=2, tiled=True)
        return full.reshape(batch, lr, ns, lc, width)

    inner_own, cotan_full = whole_tokens(inner_image), whole_tokens(inner_cotan)
    if batch == 1 and lc % 16 == 0:
        inner_own, cotan_full = inner_own[0], cotan_full[0]
    else:
        inner_own = lax.dynamic_index_in_dim(inner_own, s, 2, keepdims=False)
        inner_own = inner_own.reshape(own, width)
        cotan_full = jnp.transpose(cotan_full, (2, 0, 1, 3, 4)).reshape(ns, own, width)
    own_gains = [v.reshape(1, features) for v in (attn_gain, cross_gain, mlp_gain)]

    time_act = jax.nn.silu(time_embed(time_steps, channels))
    time_shift = jnp.dot(time_act, time_weight.astype(f32), precision=precise)
    fixed = jnp.stack([first_gain, first_bias, second_gain, second_bias])
    fixed = jnp.broadcast_to(fixed[None], (batch, 4, channels))
    empty = jnp.zeros((batch, 3, channels), f32)
    vectors = jnp.concatenate([fixed, time_shift[:, None, :], empty], axis=1)
    as_rows = lambda w: w.reshape(9 * channels, channels)
    text_rows = batch * text_states.shape[1]
    text = text_states.reshape(text_rows, -1)
    forward = [
        outer_forward(
            outer_image[b],
            as_rows(conv_first),
            as_rows(conv_second),
            vectors[b],
            own_gains,
            text,
            cross_key,
            cross_value,
            20 + b,
        )
        for b in range(batch)
    ]
    outer_out = jnp.stack([f[0] for f in forward])
    gains, cross_k, cross_v = forward[0][6:]
    pooled = jnp.concatenate([f[1] for f in forward], axis=0)

    flat = lambda v: v.reshape(-1, v.shape[-1])
    block, rows_all = ((own, width), f32), ((ns, own, width), bf16)
    stream_in, attn_in, query_t, kv = chain_call(
        enter_kernel,
        "enter",
        2,
        (
            block,
            rows_all,
            ((features, ns * own), bf16),
            ((ns * own, 2 * features), bf16),
        ),
        (inner_own, pooled, lift_weight, gains, query_weight, key_weight, value_weight),
        (),
        False,
        vmem=24,
        cost=LONG,
    )
    attn_in = flat(attn_in)

    def per_sample(values, tokens_last):
        if tokens_last:
            values = values.reshape(-1, ns, batch, lr * lc)
            return jnp.transpose(values, (2, 0, 1, 3)).reshape(batch, -1, length)
        values = values.reshape(ns, batch, lr * lc, -1)
        return jnp.transpose(values, (1, 0, 2, 3)).reshape(batch, length, -1)

    def all_samples(values, tokens_last):
        if tokens_last:
            values = values.reshape(batch, -1, ns, lr * lc)
            return jnp.transpose(values, (1, 2, 0, 3)).reshape(-1, ns * own)
        values = values.reshape(batch, ns, lr * lc, -1)
        return jnp.transpose(values, (1, 0, 2, 3)).reshape(ns * own, -1)

    mixed_t, head_q, head_kv, head_mixed_f, head_lse = self_attention(
        per_sample(query_t, True), per_sample(kv, False), 3
    )
    mixed_t = all_samples(mixed_t, True)
    after_attn, cross_in = chain_call(
        attn_out_kernel,
        "attn_out",
        5,
        (block, rows_all),
        (mixed_t, out_weight, stream_in, gains),
        [pltpu.VMEM((ns * own, features), bf16)],
        True,
        cost=LONG,
    )
    sample_of = lambda count: jnp.arange(batch * count) // count
    text_at = jnp.tile(jnp.arange(text_states.shape[1]), batch)
    good = text_at < jnp.repeat(text_lengths, text_states.shape[1])
    same = sample_of(lr * lc)[:, None] == sample_of(text_states.shape[1])[None, :]
    mask = jnp.where(same & good[None, :], 1.0, 0.0).astype(f32)
    head_rows = ((ns, own, features), bf16)
    after_cross, mlp_in, cross_q, cross_mixed = chain_call(
        cross_kernel,
        "cross",
        6,
        (block, rows_all, head_rows, head_rows),
        (cross_in, cross_query, cross_k, cross_v, mask, cross_out, after_attn, gains),
        (),
        True,
        cost=LONG,
    )

    units = up_weight.shape[1]
    one_row = ((1, width), f32)
    middle = pltpu.VMEM((ns * own, units), bf16)
    grad_after_cross, grad_cross_full, grad_mlp_gain, down, grad_up, grad_down = chain_call(
        mlp_kernel,
        "mlp",
        8,
        (
            block,
            rows_all,
            one_row,
            ((ns * own, width), bf16),
            ((width, units), bf16),
            ((units, width), bf16),
        ),
        (mlp_in, cotan_full, up_weight, down_weight, after_cross, gains),
        [middle, middle, pltpu.VMEM((ns, own, width), bf16)],
        True,
        vmem=56,
    )
    grad_down, grad_up = lax.psum((grad_down, grad_up), "tile")
    text_block = ((text_rows, features), bf16)
    (
        grad_after_attn,
        grad_attn_full,
        grad_cross_gain,
        grad_ck,
        grad_cv,
        grad_early,
    ) = chain_call(
        cross_back_kernel,
        "cross_back",
        10,
        (
            block,
            rows_all,
            one_row,
            text_block,
            text_block,
            ((2, features, width), bf16),
        ),
        (
            grad_cross_full,
            cross_out,
            cross_q,
            cross_k,
            cross_v,
            mask,
            cross_query,
            after_attn,
            gains,
            grad_after_cross,
            cross_in,
            cross_mixed,
        ),
        [pltpu.VMEM((text_rows, features), f32)] * 2
        + [pltpu.VMEM((ns * own, features), bf16)],
        True,
        vmem=56,
    )
    grad_attn_full = flat(grad_attn_full)
    grad_mixed_t = dot_t(out_weight, grad_attn_full).astype(bf16)
    grad_q_t, grad_kv, wide, down_own = attention_back(
        per_sample(grad_mixed_t, True),
        head_q,
        head_mixed_f,
        head_lse,
        head_kv,
        mixed_t,
        grad_attn_full,
        grad_early.reshape(2 * features, width),
        down,
        13,
    )
    grad_q_t, grad_kv = all_samples(grad_q_t, True), all_samples(grad_kv, False)
    grad_lifted, grad_attn_gain = chain_call(
        attn_back_kernel,
        "attn_back",
        15,
        (((own, width), bf16), one_row),
        (
            grad_q_t,
            grad_kv,
            query_weight,
            key_weight,
            value_weight,
            stream_in,
            gains,
            grad_after_attn,
        ),
        [
            pltpu.VMEM((ns * own, features), bf16),
            pltpu.VMEM((width, 2 * features), bf16),
            pltpu.VMEM((own, width), f32),
        ],
        True,
        False,
    )

    inner_sum = after_cross + down_own
    tokens = jnp.stack([inner_sum.astype(bf16), grad_lifted])
    tokens = tokens.reshape(2, own, ns, features).transpose(2, 0, 1, 3)
    gain_rows = jnp.stack([grad_attn_gain, grad_cross_gain, grad_mlp_gain]).reshape(-1, channels)
    by_tap = lambda w: w.reshape(9, channels, channels)
    backward = []
    for b in range(batch):
        once = (lambda v: v) if b == 0 else jnp.zeros_like
        sample = lambda v: v.reshape(batch, lr * lc, -1)[b]
        backward.append(
            outer_backward(
                outer_cotan[b],
                outer_image[b],
                by_tap(conv_second),
                by_tap(conv_first),
                vectors[b],
                forward[b][5],
                forward[b][4],
                once(wide),
                once(tokens),
                once(gain_rows),
                sample(pooled),
                sample(grad_lifted),
                lift_weight,
                attn_in,
                once(grad_q_t),
                once(grad_kv),
                once(grad_ck),
                once(grad_cv),
                forward[b][2],
                forward[b][3],
                20 + batch + b,
            )
        )
    outer_grad = jnp.stack([f[0] for f in backward])
    tall, wide, tokens = backward[0][1:4]
    tokens = tokens.reshape(ns, 2, batch, lr, lc, features).transpose(1, 2, 3, 0, 4, 5)
    inner_out, inner_grad = tokens.reshape(2, batch, length, features)
    inner_grad = inner_grad.astype(f32)
    if batch > 1:
        sum2, sum1 = (
            sum(f[k].astype(f32) for f in backward).astype(bf16) for k in (4, 5)
        )
    else:
        sum2, sum1 = backward[0][4:6]
    ends = finish_grads(
        text,
        grad_up,
        grad_down,
        tall,
        wide,
        sum2,
        sum1,
        9 * channels,
        text_rows,
    )
    grad_q_w, grad_k_w, grad_v_w, grad_o_w, grad_co_w = ends[:5]
    grad_conv_second, grad_conv_first = (v.reshape(conv_first.shape) for v in ends[5:7])
    grad_up, grad_down, grad_cq_w = ends[7:10]
    grad_ck_w, grad_cv_w, grad_lift = ends[10:]
    stats = jnp.stack([f[5] for f in forward])
    back = jnp.stack([f[6] for f in backward])
    grad_gains = back[0, 8:].reshape(3, width)
    center2, std2, hidden_total = stats[:, 2], stats[:, 3], stats[:, 4]
    hat2_total = std2 * (hidden_total - pixels * center2)
    hidden_sum = std2 * (
        second_gain * back[:, 2] - pixels * back[:, 4] - back[:, 5] * hat2_total
    )
    grad_time = jnp.dot(time_act.T, hidden_sum, precision=precise)
    back = jnp.sum(back, axis=0)
    grad_gains = lax.dynamic_slice_in_dim(grad_gains, s * features, features, axis=1)
    return (
        outer_out,
        inner_out,
        outer_grad,
        inner_grad,
        back[1],
        back[0],
        grad_conv_first,
        grad_time,
        back[3],
        back[2],
        grad_conv_second,
        grad_lift,
        grad_gains[0],
        grad_q_w,
        grad_k_w,
        grad_v_w,
        grad_o_w,
        grad_gains[1],
        grad_cq_w,
        grad_ck_w,
        grad_cv_w,
        grad_co_w,
        grad_gains[2],
        grad_up,
        grad_down,
    )


def solution(mesh):
    pixels = P(None, "tile", "sub", None)
    tokens = P(None, "tile", "sub")
    columns, rows, vector = P(None, "sub"), P("sub", None), P("sub")
    return jax.shard_map(
        local,
        mesh=mesh,
        in_specs=(pixels, tokens)
        + (P(),) * 11
        + (vector, columns, columns, columns, rows)
        + (vector, columns, columns, columns, rows)
        + (vector, columns, rows)
        + (pixels, tokens),
        out_specs=(pixels, tokens, pixels, tokens)
        + (P(),) * 8
        + (vector, columns, columns, columns, rows)
        + (vector, columns, columns, columns, rows)
        + (vector, columns, rows),
        check_vma=False,
    )
```
